32 devices in a mesh: batch: 16 (over z, y, core), seq: 2 (over x).
Axes of the slice: x: 2, y: 2, z: 4, core: 2. Of those that a mesh axis runs over, the one named last changes fastest.
Arguments:
- tokens_in: bfloat16 [32, 1024, 768], P('batch', 'seq'), may hold values from -6 to 6
- doc_starts: int32 [32, 4], P('batch'), may hold values from 0 to 1023, as said below
- norm1_gain: bfloat16 [768], P(('batch', 'seq')), may hold values from 0.5 to 1.5
- norm1_bias: bfloat16 [768], P(('batch', 'seq')), may hold values from -3 to 3
- qkv_weight: bfloat16 [768, 2304], P(('batch', 'seq')), may hold values from -0.3125 to 0.3125
- query_bias: bfloat16 [768], P(('batch', 'seq')), may hold values from -3 to 3
- value_bias: bfloat16 [768], P(('batch', 'seq')), may hold values from -3 to 3
- attn_weight: bfloat16 [768, 768], P(('batch', 'seq')), may hold values from -1.75 to 1.75
- attn_bias: bfloat16 [768], P(('batch', 'seq')), may hold values from -3 to 3
- norm2_gain: bfloat16 [768], P(('batch', 'seq')), may hold values from 0.5 to 1.5
- norm2_bias: bfloat16 [768], P(('batch', 'seq')), may hold values from -3 to 3
- fc_weight: bfloat16 [768, 3072], P(('batch', 'seq')), may hold values from -0.21875 to 0.21875
- fc_bias: bfloat16 [3072], P(('batch', 'seq')), may hold values from -3 to 3
- proj_weight: bfloat16 [3072, 768], P(('batch', 'seq')), may hold values from -0.109375 to 0.109375
- proj_bias: bfloat16 [768], P(('batch', 'seq')), may hold values from -4 to 4
- out_grad: bfloat16 [32, 1024, 768], P('batch', 'seq'), may hold values from -6 to 6
Outputs:
- block_out: bfloat16 [32, 1024, 768], P('batch', 'seq')
- tokens_grad: float32 [32, 1024, 768], P('batch', 'seq')
- norm1_gain_grad: float32 [768], P(('batch', 'seq'))
- norm1_bias_grad: float32 [768], P(('batch', 'seq'))
- qkv_weight_grad: float32 [768, 2304], P(('batch', 'seq'))
- query_bias_grad: float32 [768], P(('batch', 'seq'))
- value_bias_grad: float32 [768], P(('batch', 'seq'))
- attn_weight_grad: float32 [768, 768], P(('batch', 'seq'))
- attn_bias_grad: float32 [768], P(('batch', 'seq'))
- norm2_gain_grad: float32 [768], P(('batch', 'seq'))
- norm2_bias_grad: float32 [768], P(('batch', 'seq'))
- fc_weight_grad: float32 [768, 3072], P(('batch', 'seq'))
- fc_bias_grad: float32 [3072], P(('batch', 'seq'))
- proj_weight_grad: float32 [3072, 768], P(('batch', 'seq'))
- proj_bias_grad: float32 [768], P(('batch', 'seq'))
The draws below stay inside these ranges and needn't reach their ends.
Inputs may be any that keep to these rules, and one draw needn't show every extreme that they name: `doc_starts`: in every row the first start is 0 and the starts rise; for j >= 1 start j lies inside part j of the 4 equal parts of the row, counting parts from 0 and never on that part's first position. In one row of every draw the last start is 1023.
All inputs are finite; a program needn't handle non-finite values.
Results may differ from the reference program's by a relative error of at most 0.018.
Values may be sent and summed in bfloat16 or wider, within the bound.
A program may use at most 256 MiB of HBM per device.

```python
import math
import jax
import jax.numpy as jnp
from jax import lax

D = 768
H = 12
HD = 64
FF = 3072
SEQ_LEN = 1024
NDOC = 4
ROWS = 32


def draw_doc_starts(key, part):
    key = jax.random.fold_in(key, 11)
    stride = SEQ_LEN // NDOC
    offsets = jax.random.randint(key, (ROWS, NDOC), 1, stride, dtype=jnp.int32)
    chosen = jax.random.randint(jax.random.fold_in(key, 5), (), 0, ROWS, dtype=jnp.int32)
    index = jnp.arange(NDOC, dtype=jnp.int32)
    row_index = jnp.arange(ROWS, dtype=jnp.int32)
    starts = index[None, :] * stride + offsets
    last_spot = (row_index[:, None] == chosen) & (index[None, :] == NDOC - 1)
    starts = jnp.where(last_spot, SEQ_LEN - 1, starts)
    return jnp.where(index[None, :] == 0, 0, starts).astype(jnp.int32)


def block_levels(rng, dims, pieces, low, top_value):
    def one(position, shards_of):
        steps = jax.random.uniform(jax.random.fold_in(jax.random.fold_in(rng, 6), position), (shards_of,), jnp.float32, low / len(pieces), top_value / len(pieces))
        return jnp.repeat(jnp.exp(steps), dims[position] // shards_of).reshape((-1,) + (1,) * (len(dims) - position - 1))

    factor_of = one(*pieces[0])
    for cut in pieces[1:]:
        factor_of = factor_of * one(*cut)
    return factor_of


def bell_draw(rng, dims, width, reach, shards=(), kind=jnp.bfloat16):
    level = block_levels(rng, dims, shards, -0.22, 0.18) if shards else 1.0
    values = jax.random.normal(rng, dims, jnp.float32) * width * level
    return jnp.minimum(jnp.maximum(values, -reach), reach).astype(kind)


def setup_inputs(seed: int = 0) -> dict:
    splits = jax.random.split(jax.random.key(seed), 17)
    tokens_in = bell_draw(splits[0], (ROWS, SEQ_LEN, D), 1.0, 6.0, ((0, 16), (1, 2)))
    doc_starts = draw_doc_starts(jax.random.fold_in(splits[16], 71), 0)
    norm1_gain = jnp.clip(1.0 + 0.1 * jax.random.normal(splits[2], (D,), jnp.float32), 0.5, 1.5).astype(jnp.bfloat16)
    norm1_bias = bell_draw(splits[3], (D,), 0.3, 3.0, ((0, 32),))
    qkv_weight = bell_draw(splits[4], (D, 3 * D), (D // 2) ** -0.5, 0.3125, ((0, 32),))
    query_bias = bell_draw(splits[5], (D,), 0.5, 3.0, ((0, 32),))
    value_bias = bell_draw(splits[6], (D,), 0.5, 3.0, ((0, 32),))
    attn_weight = bell_draw(splits[7], (D, D), (D // 64) ** -0.5, 1.75, ((0, 32),))
    attn_bias = bell_draw(splits[8], (D,), 0.3, 3.0, ((0, 32),))
    norm2_gain = jnp.clip(1.0 + 0.1 * jax.random.normal(splits[9], (D,), jnp.float32), 0.5, 1.5).astype(jnp.bfloat16)
    norm2_bias = bell_draw(splits[10], (D,), 0.3, 3.0, ((0, 32),))
    fc_weight = bell_draw(splits[11], (D, FF), D ** -0.5, 0.21875, ((0, 32),))
    fc_bias = bell_draw(splits[12], (FF,), 0.5, 3.0, ((0, 32),))
    proj_weight = bell_draw(splits[13], (FF, D), FF ** -0.5, 0.109375, ((0, 32),))
    proj_bias = bell_draw(splits[14], (D,), 1.0, 4.0, ((0, 32),))
    out_grad = bell_draw(splits[15], (ROWS, SEQ_LEN, D), 1.0, 6.0, ((0, 16), (1, 2)))
    return dict(tokens_in=tokens_in, doc_starts=doc_starts, norm1_gain=norm1_gain, norm1_bias=norm1_bias, qkv_weight=qkv_weight, query_bias=query_bias, value_bias=value_bias, attn_weight=attn_weight, attn_bias=attn_bias, norm2_gain=norm2_gain, norm2_bias=norm2_bias, fc_weight=fc_weight, fc_bias=fc_bias, proj_weight=proj_weight, proj_bias=proj_bias, out_grad=out_grad)


@jax.custom_vjp
def low(v):
    return lax.optimization_barrier(v.astype(jnp.bfloat16)).astype(jnp.float32)

@jax.custom_vjp
def low_back(v):
    return v

def low_keep(v):
    return (low(v), None)

def low_pass(kept, grad):
    return (grad,)

def back_keep(v):
    return (v, None)

def back_low(kept, grad):
    return (low(grad),)
low.defvjp(low_keep, low_pass)
low_back.defvjp(back_keep, back_low)
EPSILON = 1e-05
GELU_SCALE = 0.7978845608028654
NEGATIVE = -1e+30
HIGHEST = lax.Precision.HIGHEST

def matmul(left, right):
    return jnp.dot(left, right, precision=HIGHEST)

def layer_norm(values, gain, shift):
    average = lax.optimization_barrier(jnp.mean(values, axis=-1, keepdims=True))
    centered = values - average
    variance = lax.optimization_barrier(jnp.mean(centered * centered, axis=-1, keepdims=True))
    return centered * lax.rsqrt(variance + EPSILON) * gain + shift

def gelu_tanh(values):
    return 0.5 * values * (1.0 + jnp.tanh(GELU_SCALE * (values + 0.044715 * values * values * values)))

def segment_ids(doc_starts):
    positions = jnp.arange(SEQ_LEN, dtype=jnp.int32)
    return lax.optimization_barrier(jnp.sum((doc_starts[:, None, :] <= positions[None, :, None]).astype(jnp.int32), axis=-1)) - 1

def attend_row(packed):
    queries, keys, values, segments = packed
    positions = jnp.arange(SEQ_LEN, dtype=jnp.int32)
    allowed = (positions[None, :] <= positions[:, None]) & (segments[None, :] == segments[:, None])
    heads_query = queries.reshape(SEQ_LEN, H, HD)
    heads_key = keys.reshape(SEQ_LEN, H, HD)
    heads_value = values.reshape(SEQ_LEN, H, HD)
    scores = jnp.einsum('qhd,khd->hqk', heads_query, heads_key, precision=HIGHEST) * (1.0 / math.sqrt(HD))
    scores = low_back(scores)
    scores = jnp.where(allowed[None], scores, NEGATIVE)
    probs = low(jax.nn.softmax(scores, axis=-1))
    mixed = jnp.einsum('hqk,khd->qhd', probs, heads_value, precision=HIGHEST)
    return mixed.reshape(SEQ_LEN, D)

def forward(segments, tokens, norm1_gain, norm1_bias, qkv_weight, query_bias, value_bias, attn_weight, attn_bias, norm2_gain, norm2_bias, fc_weight, fc_bias, proj_weight, proj_bias):
    flat = tokens.reshape(ROWS * SEQ_LEN, D)
    normed = low(layer_norm(flat, norm1_gain, norm1_bias))
    joined_bias = jnp.concatenate([query_bias, jnp.zeros_like(query_bias), value_bias])
    projected = low_back(matmul(normed, qkv_weight) + joined_bias)
    queries = low(projected[:, :D]).reshape(ROWS, SEQ_LEN, D)
    keys = low(projected[:, D:2 * D]).reshape(ROWS, SEQ_LEN, D)
    values = low(projected[:, 2 * D:]).reshape(ROWS, SEQ_LEN, D)
    mixed = lax.map(jax.checkpoint(attend_row), (queries, keys, values, segments))
    mixed = low(low_back(mixed.reshape(ROWS * SEQ_LEN, D)))
    branch = low_back(matmul(mixed, attn_weight) + attn_bias)
    middle = flat + branch
    normed2 = low(layer_norm(middle, norm2_gain, norm2_bias))
    pre_act = low_back(matmul(normed2, fc_weight) + fc_bias)
    hidden = low(gelu_tanh(pre_act))
    result = middle + matmul(hidden, proj_weight) + proj_bias
    return result.reshape(ROWS, SEQ_LEN, D)

def reference(tokens_in, doc_starts, norm1_gain, norm1_bias, qkv_weight, query_bias, value_bias, attn_weight, attn_bias, norm2_gain, norm2_bias, fc_weight, fc_bias, proj_weight, proj_bias, out_grad):
    segments = segment_ids(doc_starts)
    inputs = tuple((member.astype(jnp.float32) for member in (tokens_in, norm1_gain, norm1_bias, qkv_weight, query_bias, value_bias, attn_weight, attn_bias, norm2_gain, norm2_bias, fc_weight, fc_bias, proj_weight, proj_bias)))

    def forward_of(*floats):
        return forward(segments, *floats)
    result, pullback = jax.vjp(forward_of, *inputs)
    grads = pullback(out_grad.astype(jnp.float32))
    return (result.astype(jnp.bfloat16), grads[0], grads[1], grads[2], grads[3], grads[4], grads[5], grads[6], grads[7], grads[8], grads[9], grads[10], grads[11], grads[12], grads[13])
```

```python
import functools
import math

import jax
import jax.numpy as jnp
from jax import lax
from jax.experimental import pallas as pl
from jax.experimental.pallas import tpu as pltpu
from jax.sharding import PartitionSpec as P

H = 12
HD = 64


EPSILON = 1e-05
GELU_SCALE = 0.7978845608028654
NEGATIVE = -1e30


MESH_ID = pl.DeviceIdType.MESH
VMEM_LIMIT = 60 * 2**20


def place():
    batch, seq = lax.axis_index("batch"), lax.axis_index("seq")
    return (batch // 4, (batch // 2) % 2, batch % 2, seq)


def device(a, y, c, s):
    return (a * 4 + y * 2 + c, s)


def greet(outer):
    a, y, c, s = place()
    barrier = pltpu.get_barrier_semaphore()
    others = [device(lax.rem(a + k, outer), y, c, s) for k in range(1, outer)]
    others += [device(a, 1 - y, c, s), device(a, y, c, 1 - s), device(a, y, 1 - c, s)]
    for other in others:
        pl.semaphore_signal(barrier, inc=1, device_id=other, device_id_type=MESH_ID)
    pl.semaphore_wait(barrier, len(others))


def gather_kernel(outer, pieces, count, *refs):
    shards, outs = refs[:count], refs[count : 2 * count]
    own_sem, send_sem, recv_sem = refs[2 * count :]
    a, y, c, s = place()
    greet(outer)
    owns = []
    for i in range(count):
        own = pltpu.make_async_copy(shards[i], outs[i].at[a, y, c, s], own_sem.at[i])
        own.start()
        owns.append(own)

    def z_copies(p):
        i, start, width, order = pieces[p]
        columns = pl.ds(start, width)
        return [
            pltpu.make_async_remote_copy(
                src_ref=shards[i].at[:, columns],
                dst_ref=outs[i].at[a, y, c, s, :, columns],
                send_sem=send_sem.at[p, k - 1],
                recv_sem=recv_sem.at[p, k - 1],
                device_id=device(lax.rem(a + k, outer), y, c, s),
                device_id_type=MESH_ID,
            )
            for k in range(1, outer)
        ]

    def later_copy(p, phase):
        i, start, width, order = pieces[p]
        columns = pl.ds(start, width)
        every = slice(None)
        if phase == 2:
            index = (every, every, c, every)
            other = device(a, y, 1 - c, s)
        elif (phase == 0) == (order == 0):
            index = (every, y, c, s if phase == 0 else every)
            other = device(a, 1 - y, c, s)
        else:
            index = (every, y if phase == 0 else every, c, s)
            other = device(a, y, c, 1 - s)
        block = outs[i].at[index + (every, columns)]
        return pltpu.make_async_remote_copy(
            src_ref=block,
            dst_ref=block,
            send_sem=send_sem.at[p, outer - 1 + phase],
            recv_sem=recv_sem.at[p, outer - 1 + phase],
            device_id=other,
            device_id_type=MESH_ID,
        )

    z_all = [z_copies(p) for p in range(len(pieces))]
    later = [[later_copy(p, phase) for phase in range(3)] for p in range(len(pieces))]
    lag = (1, 2, 4, 6)
    for t in range(len(pieces) + lag[3]):
        if t == 0:
            for p in range(min(2, len(pieces))):
                for copy in z_all[p]:
                    copy.start()
            for own in owns:
                own.wait()
        elif t + 1 < len(pieces):
            for copy in z_all[t + 1]:
                copy.start()
        p = t - lag[0]
        if 0 <= p < len(pieces):
            for copy in z_all[p]:
                copy.wait_recv()
            later[p][0].start()
        for phase in range(2):
            p = t - lag[phase + 1]
            if 0 <= p < len(pieces):
                later[p][phase].wait_recv()
                later[p][phase + 1].start()
        p = t - lag[3]
        if 0 <= p < len(pieces):
            later[p][2].wait_recv()
    for p in range(len(pieces)):
        for copy in z_all[p] + later[p]:
            copy.wait_send()


def gather_all(outer, shards, pieces):
    count = len(shards)
    return pl.pallas_call(
        functools.partial(gather_kernel, outer, pieces, count),
        out_shape=[
            jax.ShapeDtypeStruct((outer, 2, 2, 2) + shard.shape, shard.dtype) for shard in shards
        ],
        in_specs=[pl.BlockSpec(memory_space=pl.ANY)] * count,
        out_specs=[pl.BlockSpec(memory_space=pl.ANY)] * count,
        scratch_shapes=[
            pltpu.SemaphoreType.DMA((count,)),
            pltpu.SemaphoreType.DMA((len(pieces), outer + 2)),
            pltpu.SemaphoreType.DMA((len(pieces), outer + 2)),
        ],
        compiler_params=pltpu.CompilerParams(collective_id=0, has_side_effects=True),
    )(*shards)


def scatter_kernel(outer, pieces, count, *refs):
    terms, outs = refs[:count], refs[count : 2 * count]
    rest = refs[2 * count :]
    n = len(pieces)
    held, first, second, third, fourth = (rest[k * n : (k + 1) * n] for k in range(5))
    own_sem, send_sem, recv_sem = rest[5 * n :]
    a, y, c, s = place()
    greet(outer)
    every = slice(None)

    def remote(p, k, src, dst, other):
        return pltpu.make_async_remote_copy(
            src_ref=src,
            dst_ref=dst,
            send_sem=send_sem.at[p, k],
            recv_sem=recv_sem.at[p, k],
            device_id=other,
            device_id_type=MESH_ID,
        )

    started = []

    def core_start(p):
        i, start, width, order = pieces[p]
        columns = pl.ds(start, width)
        own = pltpu.make_async_copy(
            terms[i].at[:, :, c, :, :, columns], held[p], own_sem.at[p]
        )
        own.start()
        copy = remote(
            p, 0, terms[i].at[:, :, 1 - c, :, :, columns], first[p], device(a, y, 1 - c, s)
        )
        copy.start()
        started.append(copy)
        return (own, copy)

    def add(target, other):
        lead = target.shape[:-2]
        total = math.prod(lead)

        def body(k, carry):
            index = []
            for size in reversed(lead):
                index.append(lax.rem(k, size))
                k = k // size
            index = tuple(reversed(index))
            value = target[index].astype(jnp.float32) + other[index].astype(jnp.float32)
            target[index] = value.astype(target.dtype)
            return carry

        lax.fori_loop(0, total, body, 0)

    def first_half(p):
        order = pieces[p][3]
        if order == 0:
            src, other = held[p].at[:, :, 1 - s], device(a, y, c, 1 - s)
        else:
            src, other = held[p].at[:, 1 - y], device(a, 1 - y, c, s)
        copy = remote(p, 1, src, second[p], other)
        copy.start()
        started.append(copy)
        return copy

    def second_half(p):
        order = pieces[p][3]
        if order == 0:
            src, other = held[p].at[:, 1 - y, s], device(a, 1 - y, c, s)
        else:
            src, other = held[p].at[:, y, 1 - s], device(a, y, c, 1 - s)
        copy = remote(p, 2, src, third[p], other)
        copy.start()
        started.append(copy)
        return copy

    def z_start(p):
        copies = []
        for k in range(1, outer):
            to = lax.rem(a + k, outer)
            copy = remote(
                p, 2 + k, held[p].at[to, y, s], fourth[p].at[k - 1], device(to, y, c, s)
            )
            copy.start()
            started.append(copy)
            copies.append(copy)
        return copies

    def finish(p):
        i, start, width, order = pieces[p]
        value = held[p][a, y, s].astype(jnp.float32)
        for k in range(1, outer):
            value = value + fourth[p][k - 1].astype(jnp.float32)
        outs[i][:, pl.ds(start, width)] = value

    core, one, two, z_all = {}, {}, {}, {}
    for t in range(n + 6):
        if t == 0:
            for p in range(min(2, n)):
                core[p] = core_start(p)
        elif t + 1 < n:
            core[t + 1] = core_start(t + 1)
        p = t - 1
        if 0 <= p < n:
            for copy in core[p][:1]:
                copy.wait()
            core[p][1].wait_recv()
            add(held[p], first[p])
            one[p] = first_half(p)
        p = t - 3
        if 0 <= p < n:
            one[p].wait_recv()
            if pieces[p][3] == 0:
                add(held[p].at[:, :, s], second[p])
            else:
                add(held[p].at[:, y], second[p])
            two[p] = second_half(p)
        p = t - 4
        if 0 <= p < n:
            two[p].wait_recv()
            add(held[p].at[:, y, s], third[p])
            z_all[p] = z_start(p)
        p = t - 5
        if 0 <= p < n:
            for copy in z_all[p]:
                copy.wait_recv()
            finish(p)
    for copy in started:
        copy.wait_send()


def scatter_all(outer, terms, pieces):
    count = len(terms)
    shape = lambda p, *lead: pltpu.VMEM(
        lead + (terms[pieces[p][0]].shape[-2], pieces[p][2]), terms[pieces[p][0]].dtype
    )
    n = range(len(pieces))
    return pl.pallas_call(
        functools.partial(scatter_kernel, outer, pieces, count),
        out_shape=[jax.ShapeDtypeStruct(term.shape[-2:], jnp.float32) for term in terms],
        in_specs=[pl.BlockSpec(memory_space=pl.ANY)] * count,
        out_specs=[pl.BlockSpec(memory_space=pltpu.VMEM)] * count,
        scratch_shapes=[shape(p, outer, 2, 2) for p in n]
        + [shape(p, outer, 2, 2) for p in n]
        + [shape(p, outer, 2) for p in n]
        + [shape(p, outer) for p in n]
        + [shape(p, max(outer - 1, 1)) for p in n]
        + [
            pltpu.SemaphoreType.DMA((len(pieces),)),
            pltpu.SemaphoreType.DMA((len(pieces), outer + 2)),
            pltpu.SemaphoreType.DMA((len(pieces), outer + 2)),
        ],
        compiler_params=pltpu.CompilerParams(
            collective_id=1, has_side_effects=True, vmem_limit_bytes=VMEM_LIMIT
        ),
    )(*terms)


def cut(shape_list):
    pieces = []
    for i, (rows, columns) in enumerate(shape_list):
        parts, blocks = 1, columns // 128
        if rows % 8 == 0:
            fits = [k for k in range(1, blocks + 1) if blocks % k == 0 and rows * columns // k <= 25000]
            parts = min(fits) if fits else 1
        width = columns // parts
        for k in range(parts):
            pieces.append((i, k * width, width, len(pieces) % 2))
    return pieces


def pack_shape(shape):
    rows, columns = shape
    return shape if rows % 8 == 0 else (rows * columns // 128, 128)


def pack_vectors(parts):
    joined = jnp.concatenate([part.astype(jnp.float32) for part in parts], axis=-1)
    size = -(-joined.shape[-1] // 1024) * 1024
    pad = [(0, 0)] * (joined.ndim - 1) + [(0, size - joined.shape[-1])]
    return jnp.pad(joined, pad).reshape(joined.shape[:-1] + (size // 128, 128))


def gather_weights(outer, weights, vectors):
    shards = [pack_vectors(vectors)] + [w.reshape(pack_shape(w.shape)) for w in weights]
    full = gather_all(outer, shards, cut([shard.shape for shard in shards]))
    devices = outer * 8
    packed = full[0].reshape(devices, -1)
    whole_vectors, at = [], 0
    for vector in vectors:
        size = vector.shape[0]
        whole_vectors.append(packed[:, at : at + size].reshape(devices * size))
        at += size
    whole = [f.reshape(devices * w.shape[0], w.shape[1]) for f, w in zip(full[1:], weights)]
    return whole, whole_vectors


def scatter_grads(outer, weight_terms, vector_terms):
    devices = outer * 8
    cuts = [term.reshape(devices, -1) for term in vector_terms]
    packed = pack_vectors(cuts)
    terms = [packed.reshape((outer, 2, 2, 2) + packed.shape[1:])]
    shapes = [(term.shape[0] // devices, term.shape[1]) for term in weight_terms]
    for term, shape in zip(weight_terms, shapes):
        terms.append(term.astype(jnp.bfloat16).reshape((outer, 2, 2, 2) + pack_shape(shape)))
    shares = scatter_all(outer, terms, cut([term.shape[-2:] for term in terms]))
    flat = shares[0].reshape(-1)
    vectors, at = [], 0
    for part in cuts:
        vectors.append(flat[at : at + part.shape[1]])
        at += part.shape[1]
    return [share.reshape(shape) for share, shape in zip(shares[1:], shapes)], vectors


def layer_norm(values, gain, shift):
    average = jnp.mean(values, axis=-1, keepdims=True)
    centered = values - average
    variance = jnp.mean(centered * centered, axis=-1, keepdims=True)
    return centered * lax.rsqrt(variance + EPSILON) * gain + shift


def gelu_tanh(values):
    return (
        0.5 * values * (1.0 + jnp.tanh(GELU_SCALE * (values + 0.044715 * values * values * values)))
    )


def segment_ids(doc_starts, length):
    positions = jnp.arange(length, dtype=jnp.int32)
    return (
        jnp.sum((doc_starts[:, None, :] <= positions[None, :, None]).astype(jnp.int32), axis=-1) - 1
    )


def contract_rows(left, right):
    return lax.dot_general(
        left, right, (((0,), (0,)), ((), ())), preferred_element_type=jnp.float32
    )


def contract_last(left, right):
    return lax.dot_general(
        left, right, (((1,), (1,)), ((), ())), preferred_element_type=jnp.float32
    )


def split_heads(block):
    return block.reshape(block.shape[0], block.shape[1], H, HD)


def merge_heads(block):
    return block.reshape(block.shape[0], block.shape[1], H * HD)


def take_block(values, block, length):
    return lax.dynamic_slice_in_dim(values, block * length, length, 1)


def block_scores(query_block, key_block, query_segments, key_segments, query_start, key_start):
    scores = jnp.einsum(
        "rqhd,rkhd->rhqk",
        split_heads(query_block),
        split_heads(key_block),
        preferred_element_type=jnp.float32,
    ) * (1.0 / math.sqrt(HD))
    query_places = query_start + jnp.arange(query_block.shape[1], dtype=jnp.int32)
    key_places = key_start + jnp.arange(key_block.shape[1], dtype=jnp.int32)
    allowed = (key_places[None, None, :] <= query_places[None, :, None]) & (
        key_segments[:, None, :] == query_segments[:, :, None]
    )
    return (scores, allowed[:, None, :, :])


def pair_grads(
    query_block,
    grad_block,
    log_block,
    delta_block,
    key_block,
    value_block,
    query_segments,
    key_segments,
    query_start,
    key_start,
):
    scores, allowed = block_scores(
        query_block, key_block, query_segments, key_segments, query_start, key_start
    )
    probs = jnp.where(allowed, jnp.exp(scores - log_block[..., None]), 0.0)
    probs_low = probs.astype(jnp.bfloat16)
    value_grad = jnp.einsum(
        "rhqk,rqhd->rkhd", probs_low, split_heads(grad_block), preferred_element_type=jnp.float32
    )
    prob_grad = jnp.einsum(
        "rqhd,rkhd->rhqk",
        split_heads(grad_block),
        split_heads(value_block),
        preferred_element_type=jnp.float32,
    )
    score_grad = (probs * (prob_grad - delta_block[..., None])).astype(jnp.bfloat16)
    query_grad = jnp.einsum(
        "rhqk,rkhd->rqhd", score_grad, split_heads(key_block), preferred_element_type=jnp.float32
    ) * (1.0 / math.sqrt(HD))
    key_grad = jnp.einsum(
        "rhqk,rqhd->rkhd", score_grad, split_heads(query_block), preferred_element_type=jnp.float32
    ) * (1.0 / math.sqrt(HD))
    return (merge_heads(query_grad), merge_heads(key_grad), merge_heads(value_grad))


def shards(
    tokens_in,
    doc_starts,
    norm1_gain,
    norm1_bias,
    qkv_weight,
    query_bias,
    value_bias,
    attn_weight,
    attn_bias,
    norm2_gain,
    norm2_bias,
    fc_weight,
    fc_bias,
    proj_weight,
    proj_bias,
    out_grad,
):
    outer = lax.axis_size("batch") // 4
    weights, vectors = gather_weights(
        outer,
        [qkv_weight, attn_weight, fc_weight, proj_weight],
        [norm1_gain, norm1_bias, query_bias, value_bias, attn_bias, norm2_gain, norm2_bias, proj_bias, fc_bias],
    )
    gathered = (vectors[0], vectors[1], weights[0], vectors[2], vectors[3], weights[1], vectors[4], vectors[5], vectors[6], weights[2], vectors[8], weights[3], vectors[7])
    gain_one = gathered[0].astype(jnp.float32)
    shift_one = gathered[1].astype(jnp.float32)
    qkv_full = gathered[2]
    attn_full = gathered[5]
    gain_two = gathered[7].astype(jnp.float32)
    shift_two = gathered[8].astype(jnp.float32)
    fc_full = gathered[9]
    proj_full = gathered[11]
    rows, local, width = tokens_in.shape
    seq_count = lax.axis_size("seq")
    seq_index = lax.axis_index("seq")
    offset = seq_index * local
    segments = segment_ids(doc_starts, local * seq_count)
    query_segments = lax.dynamic_slice_in_dim(segments, offset, local, 1)
    flat = tokens_in.reshape(rows * local, width).astype(jnp.float32)
    normed, norm_back_one = jax.vjp(layer_norm, flat, gain_one, shift_one)
    normed_low = normed.astype(jnp.bfloat16)
    joined_bias = jnp.concatenate([gathered[3], jnp.zeros_like(gathered[3]), gathered[4]]).astype(
        jnp.float32
    )
    projected = jnp.dot(normed_low, qkv_full, preferred_element_type=jnp.float32) + joined_bias
    queries = projected[:, :width].astype(jnp.bfloat16).reshape(rows, local, width)
    keys = projected[:, width : 2 * width].astype(jnp.bfloat16).reshape(rows, local, width)
    values = projected[:, 2 * width :].astype(jnp.bfloat16).reshape(rows, local, width)
    keys_all, values_all = (
        lax.all_gather(keys, "seq", axis=1, tiled=True),
        lax.all_gather(values, "seq", axis=1, tiled=True),
    )

    def max_step(block, carry):
        top, total = carry
        scores, allowed = block_scores(
            queries,
            take_block(keys_all, block, local),
            query_segments,
            take_block(segments, block, local),
            offset,
            block * local,
        )
        masked = jnp.where(allowed, scores, NEGATIVE)
        new_top = jnp.maximum(top, jnp.max(masked, axis=-1))
        added = jnp.sum(jnp.where(allowed, jnp.exp(masked - new_top[..., None]), 0.0), axis=-1)
        return (new_top, total * jnp.exp(top - new_top) + added)

    start_top = jnp.full((rows, H, local), NEGATIVE, jnp.float32)
    top, total = lax.fori_loop(
        0, seq_index + 1, max_step, (start_top, jnp.zeros((rows, H, local), jnp.float32))
    )
    log_total = top + jnp.log(total)

    def value_step(block, mixed):
        scores, allowed = block_scores(
            queries,
            take_block(keys_all, block, local),
            query_segments,
            take_block(segments, block, local),
            offset,
            block * local,
        )
        probs_low = jnp.where(allowed, jnp.exp(scores - log_total[..., None]), 0.0).astype(
            jnp.bfloat16
        )
        return mixed + jnp.einsum(
            "rhqk,rkhd->rqhd",
            probs_low,
            split_heads(take_block(values_all, block, local)),
            preferred_element_type=jnp.float32,
        )

    attended = lax.fori_loop(
        0, seq_index + 1, value_step, jnp.zeros((rows, local, H, HD), jnp.float32)
    )
    attended = attended.reshape(rows * local, width)
    attended_low = attended.astype(jnp.bfloat16)
    middle = (
        flat
        + jnp.dot(attended_low, attn_full, preferred_element_type=jnp.float32)
        + gathered[6].astype(jnp.float32)
    )
    normed_two, norm_back_two = jax.vjp(layer_norm, middle, gain_two, shift_two)
    normed_two_low = normed_two.astype(jnp.bfloat16)
    pre_act = jnp.dot(normed_two_low, fc_full, preferred_element_type=jnp.float32) + gathered[
        10
    ].astype(jnp.float32)
    hidden, gelu_back = jax.vjp(gelu_tanh, pre_act)
    hidden_low = hidden.astype(jnp.bfloat16)
    result = (
        middle
        + jnp.dot(hidden_low, proj_full, preferred_element_type=jnp.float32)
        + gathered[12].astype(jnp.float32)
    )
    block_out = result.astype(jnp.bfloat16).reshape(rows, local, width)
    upstream = out_grad.reshape(rows * local, width)
    upstream_float = upstream.astype(jnp.float32)
    proj_weight_grad = contract_rows(hidden_low, upstream)
    proj_bias_grad = jnp.sum(upstream_float, axis=0)
    hidden_grad = contract_last(upstream, proj_full)
    pre_grad = gelu_back(hidden_grad)[0].astype(jnp.bfloat16)
    fc_weight_grad = contract_rows(normed_two_low, pre_grad)
    fc_bias_grad = jnp.sum(pre_grad.astype(jnp.float32), axis=0)
    norm_two_input = contract_last(pre_grad, fc_full)
    middle_part, norm2_gain_grad, norm2_bias_grad = norm_back_two(norm_two_input)
    middle_grad = upstream_float + middle_part
    branch_grad = middle_grad.astype(jnp.bfloat16)
    attn_weight_grad = contract_rows(attended_low, branch_grad)
    attn_bias_grad = jnp.sum(branch_grad.astype(jnp.float32), axis=0)
    attended_grad = contract_last(branch_grad, attn_full).astype(jnp.bfloat16)
    delta = jnp.sum(
        (attended_grad.astype(jnp.float32) * attended).reshape(rows, local, H, HD), axis=-1
    )
    delta = jnp.swapaxes(delta, 1, 2)
    attended_grad = attended_grad.reshape(rows, local, width)

    def grad_step(block, carry):
        query_grad, key_full, value_full = carry
        part_query, part_key, part_value = pair_grads(
            queries,
            attended_grad,
            log_total,
            delta,
            take_block(keys_all, block, local),
            take_block(values_all, block, local),
            query_segments,
            take_block(segments, block, local),
            offset,
            block * local,
        )
        key_full = lax.dynamic_update_slice_in_dim(
            key_full, take_block(key_full, block, local) + part_key, block * local, 1
        )
        value_full = lax.dynamic_update_slice_in_dim(
            value_full, take_block(value_full, block, local) + part_value, block * local, 1
        )
        return (query_grad + part_query, key_full, value_full)

    empty_full = jnp.zeros((rows, local * seq_count, width), jnp.float32)
    query_grad, key_full, value_full = lax.fori_loop(
        0,
        seq_index + 1,
        grad_step,
        (jnp.zeros((rows, local, width), jnp.float32), empty_full, empty_full),
    )
    key_grad, value_grad = (
        lax.psum_scatter(
            key_full.astype(jnp.bfloat16), "seq", scatter_dimension=1, tiled=True
        ).astype(jnp.float32),
        lax.psum_scatter(
            value_full.astype(jnp.bfloat16), "seq", scatter_dimension=1, tiled=True
        ).astype(jnp.float32),
    )
    qkv_grad = (
        jnp.concatenate([query_grad, key_grad, value_grad], axis=-1)
        .astype(jnp.bfloat16)
        .reshape(rows * local, 3 * width)
    )
    qkv_weight_grad = contract_rows(normed_low, qkv_grad)
    qkv_grad_float = qkv_grad.astype(jnp.float32)
    query_bias_grad = jnp.sum(qkv_grad_float[:, :width], axis=0)
    value_bias_grad = jnp.sum(qkv_grad_float[:, 2 * width :], axis=0)
    normed_grad = contract_last(qkv_grad, qkv_full)
    flat_part, norm1_gain_grad, norm1_bias_grad = norm_back_one(normed_grad)
    tokens_grad = (middle_grad + flat_part).reshape(rows, local, width)
    weight_shares, vector_shares = scatter_grads(
        outer,
        [qkv_weight_grad, attn_weight_grad, fc_weight_grad, proj_weight_grad],
        [norm1_gain_grad, norm1_bias_grad, query_bias_grad, value_bias_grad, attn_bias_grad, norm2_gain_grad, norm2_bias_grad, proj_bias_grad, fc_bias_grad],
    )
    qkv_share, attn_share, fc_share, proj_share = weight_shares
    g1, b1, qb, vb, ab, g2, b2, pb, fb = vector_shares
    shares = (g1, b1, qkv_share, qb, vb, attn_share, ab, g2, b2, fc_share, fb, proj_share, pb)
    return (block_out, tokens_grad) + tuple(shares)


def solution(mesh):
    return jax.shard_map(
        shards,
        mesh=mesh,
        in_specs=(
            P("batch", "seq", None),
            P("batch", None),
            P(("batch", "seq")),
            P(("batch", "seq")),
            P(("batch", "seq"), None),
            P(("batch", "seq")),
            P(("batch", "seq")),
            P(("batch", "seq"), None),
            P(("batch", "seq")),
            P(("batch", "seq")),
            P(("batch", "seq")),
            P(("batch", "seq"), None),
            P(("batch", "seq")),
            P(("batch", "seq"), None),
            P(("batch", "seq")),
            P("batch", "seq", None),
        ),
        out_specs=(
            P("batch", "seq", None),
            P("batch", "seq", None),
            P(("batch", "seq")),
            P(("batch", "seq")),
            P(("batch", "seq"), None),
            P(("batch", "seq")),
            P(("batch", "seq")),
            P(("batch", "seq"), None),
            P(("batch", "seq")),
            P(("batch", "seq")),
            P(("batch", "seq")),
            P(("batch", "seq"), None),
            P(("batch", "seq")),
            P(("batch", "seq"), None),
            P(("batch", "seq")),
        ),
        check_vma=False,
    )
```

```python
import functools
import math

import jax
import jax.numpy as jnp
from jax import lax
from jax.experimental import pallas as pl
from jax.experimental.pallas import tpu as pltpu
from jax.sharding import PartitionSpec as P

HD = 64
EPSILON = 1e-05
GELU_SCALE = 0.7978845608028654
MESH_ID = pl.DeviceIdType.MESH
VMEM_LIMIT = 60 * 2**20


def place():
    batch, seq = lax.axis_index("batch"), lax.axis_index("seq")
    return (batch // 4, (batch // 2) % 2, batch % 2, seq)


def device(a, y, c, s):
    return (a * 4 + y * 2 + c, s)


def greet(outer):
    a, y, c, s = place()
    barrier = pltpu.get_barrier_semaphore()
    others = [device(lax.rem(a + k, outer), y, c, s) for k in range(1, outer)]
    others += [device(a, 1 - y, c, s), device(a, y, c, 1 - s), device(a, y, 1 - c, s)]
    for other in others:
        pl.semaphore_signal(barrier, inc=1, device_id=other, device_id_type=MESH_ID)
    pl.semaphore_wait(barrier, len(others))


def gather_kernel(outer, pieces, count, *refs):
    shards, outs = refs[:count], refs[count : 2 * count]
    own_sem, send_sem, recv_sem = refs[2 * count :]
    a, y, c, s = place()
    greet(outer)
    owns = []
    for i in range(count):
        own = pltpu.make_async_copy(shards[i], outs[i].at[a, y, c, s], own_sem.at[i])
        own.start()
        owns.append(own)

    def z_copies(p):
        i, start, width, order = pieces[p]
        columns = pl.ds(start, width)
        return [
            pltpu.make_async_remote_copy(
                src_ref=shards[i].at[:, columns],
                dst_ref=outs[i].at[a, y, c, s, :, columns],
                send_sem=send_sem.at[p, k - 1],
                recv_sem=recv_sem.at[p, k - 1],
                device_id=device(lax.rem(a + k, outer), y, c, s),
                device_id_type=MESH_ID,
            )
            for k in range(1, outer)
        ]

    def later_copy(p, phase):
        i, start, width, order = pieces[p]
        columns = pl.ds(start, width)
        every = slice(None)
        if phase == 2:
            index = (every, every, c, every)
            other = device(a, y, 1 - c, s)
        elif (phase == 0) == (order == 0):
            index = (every, y, c, s if phase == 0 else every)
            other = device(a, 1 - y, c, s)
        else:
            index = (every, y if phase == 0 else every, c, s)
            other = device(a, y, c, 1 - s)
        block = outs[i].at[index + (every, columns)]
        return pltpu.make_async_remote_copy(
            src_ref=block,
            dst_ref=block,
            send_sem=send_sem.at[p, outer - 1 + phase],
            recv_sem=recv_sem.at[p, outer - 1 + phase],
            device_id=other,
            device_id_type=MESH_ID,
        )

    z_all = [z_copies(p) for p in range(len(pieces))]
    later = [[later_copy(p, phase) for phase in range(3)] for p in range(len(pieces))]
    lag = (1, 2, 4, 6)
    for t in range(len(pieces) + lag[3]):
        if t == 0:
            for p in range(min(2, len(pieces))):
                for copy in z_all[p]:
                    copy.start()
            for own in owns:
                own.wait()
        elif t + 1 < len(pieces):
            for copy in z_all[t + 1]:
                copy.start()
        p = t - lag[0]
        if 0 <= p < len(pieces):
            for copy in z_all[p]:
                copy.wait_recv()
            later[p][0].start()
        for phase in range(2):
            p = t - lag[phase + 1]
            if 0 <= p < len(pieces):
                later[p][phase].wait_recv()
                later[p][phase + 1].start()
        p = t - lag[3]
        if 0 <= p < len(pieces):
            later[p][2].wait_recv()
    for p in range(len(pieces)):
        for copy in z_all[p] + later[p]:
            copy.wait_send()


def gather_all(outer, shards, pieces):
    count = len(shards)
    return pl.pallas_call(
        functools.partial(gather_kernel, outer, pieces, count),
        out_shape=[
            jax.ShapeDtypeStruct((outer, 2, 2, 2) + shard.shape, shard.dtype) for shard in shards
        ],
        in_specs=[pl.BlockSpec(memory_space=pl.ANY)] * count,
        out_specs=[pl.BlockSpec(memory_space=pl.ANY)] * count,
        scratch_shapes=[
            pltpu.SemaphoreType.DMA((count,)),
            pltpu.SemaphoreType.DMA((len(pieces), outer + 2)),
            pltpu.SemaphoreType.DMA((len(pieces), outer + 2)),
        ],
        compiler_params=pltpu.CompilerParams(collective_id=0, has_side_effects=True),
    )(*shards)


def scatter_kernel(outer, pieces, count, *refs):
    terms, outs = refs[:count], refs[count : 2 * count]
    rest = refs[2 * count :]
    n = len(pieces)
    held, first, second, third, fourth = (rest[k * n : (k + 1) * n] for k in range(5))
    own_sem, send_sem, recv_sem = rest[5 * n :]
    a, y, c, s = place()
    greet(outer)
    every = slice(None)

    def remote(p, k, src, dst, other):
        return pltpu.make_async_remote_copy(
            src_ref=src,
            dst_ref=dst,
            send_sem=send_sem.at[p, k],
            recv_sem=recv_sem.at[p, k],
            device_id=other,
            device_id_type=MESH_ID,
        )

    started = []

    def core_start(p):
        i, start, width, order = pieces[p]
        columns = pl.ds(start, width)
        own = pltpu.make_async_copy(
            terms[i].at[:, :, c, :, :, columns], held[p], own_sem.at[p]
        )
        own.start()
        copy = remote(
            p, 0, terms[i].at[:, :, 1 - c, :, :, columns], first[p], device(a, y, 1 - c, s)
        )
        copy.start()
        started.append(copy)
        return (own, copy)

    def add(target, other):
        lead = target.shape[:-2]
        total = math.prod(lead)

        def body(k, carry):
            index = []
            for size in reversed(lead):
                index.append(lax.rem(k, size))
                k = k // size
            index = tuple(reversed(index))
            value = target[index].astype(jnp.float32) + other[index].astype(jnp.float32)
            target[index] = value.astype(target.dtype)
            return carry

        lax.fori_loop(0, total, body, 0)

    def first_half(p):
        order = pieces[p][3]
        if order == 0:
            src, other = held[p].at[:, :, 1 - s], device(a, y, c, 1 - s)
        else:
            src, other = held[p].at[:, 1 - y], device(a, 1 - y, c, s)
        copy = remote(p, 1, src, second[p], other)
        copy.start()
        started.append(copy)
        return copy

    def second_half(p):
        order = pieces[p][3]
        if order == 0:
            src, other = held[p].at[:, 1 - y, s], device(a, 1 - y, c, s)
        else:
            src, other = held[p].at[:, y, 1 - s], device(a, y, c, 1 - s)
        copy = remote(p, 2, src, third[p], other)
        copy.start()
        started.append(copy)
        return copy

    def z_start(p):
        copies = []
        for k in range(1, outer):
            to = lax.rem(a + k, outer)
            copy = remote(
                p, 2 + k, held[p].at[to, y, s], fourth[p].at[k - 1], device(to, y, c, s)
            )
            copy.start()
            started.append(copy)
            copies.append(copy)
        return copies

    def finish(p):
        i, start, width, order = pieces[p]
        value = held[p][a, y, s].astype(jnp.float32)
        for k in range(1, outer):
            value = value + fourth[p][k - 1].astype(jnp.float32)
        outs[i][:, pl.ds(start, width)] = value

    core, one, two, z_all = {}, {}, {}, {}
    for t in range(n + 6):
        if t == 0:
            for p in range(min(2, n)):
                core[p] = core_start(p)
        elif t + 1 < n:
            core[t + 1] = core_start(t + 1)
        p = t - 1
        if 0 <= p < n:
            for copy in core[p][:1]:
                copy.wait()
            core[p][1].wait_recv()
            add(held[p], first[p])
            one[p] = first_half(p)
        p = t - 3
        if 0 <= p < n:
            one[p].wait_recv()
            if pieces[p][3] == 0:
                add(held[p].at[:, :, s], second[p])
            else:
                add(held[p].at[:, y], second[p])
            two[p] = second_half(p)
        p = t - 4
        if 0 <= p < n:
            two[p].wait_recv()
            add(held[p].at[:, y, s], third[p])
            z_all[p] = z_start(p)
        p = t - 5
        if 0 <= p < n:
            for copy in z_all[p]:
                copy.wait_recv()
            finish(p)
    for copy in started:
        copy.wait_send()


def scatter_all(outer, terms, pieces):
    count = len(terms)
    shape = lambda p, *lead: pltpu.VMEM(
        lead + (terms[pieces[p][0]].shape[-2], pieces[p][2]), terms[pieces[p][0]].dtype
    )
    n = range(len(pieces))
    return pl.pallas_call(
        functools.partial(scatter_kernel, outer, pieces, count),
        out_shape=[jax.ShapeDtypeStruct(term.shape[-2:], jnp.float32) for term in terms],
        in_specs=[pl.BlockSpec(memory_space=pl.ANY)] * count,
        out_specs=[pl.BlockSpec(memory_space=pltpu.VMEM)] * count,
        scratch_shapes=[shape(p, outer, 2, 2) for p in n]
        + [shape(p, outer, 2, 2) for p in n]
        + [shape(p, outer, 2) for p in n]
        + [shape(p, outer) for p in n]
        + [shape(p, max(outer - 1, 1)) for p in n]
        + [
            pltpu.SemaphoreType.DMA((len(pieces),)),
            pltpu.SemaphoreType.DMA((len(pieces), outer + 2)),
            pltpu.SemaphoreType.DMA((len(pieces), outer + 2)),
        ],
        compiler_params=pltpu.CompilerParams(
            collective_id=1, has_side_effects=True, vmem_limit_bytes=VMEM_LIMIT
        ),
    )(*terms)


def cut(shape_list):
    pieces = []
    for i, (rows, columns) in enumerate(shape_list):
        parts, blocks = 1, columns // 128
        if rows % 8 == 0:
            fits = [k for k in range(1, blocks + 1) if blocks % k == 0 and rows * columns // k <= 25000]
            parts = min(fits) if fits else 1
        width = columns // parts
        for k in range(parts):
            pieces.append((i, k * width, width, len(pieces) % 2))
    return pieces


def pack_shape(shape):
    rows, columns = shape
    return shape if rows % 8 == 0 else (rows * columns // 128, 128)


def pack_vectors(parts):
    joined = jnp.concatenate([part.astype(jnp.float32) for part in parts], axis=-1)
    size = -(-joined.shape[-1] // 1024) * 1024
    pad = [(0, 0)] * (joined.ndim - 1) + [(0, size - joined.shape[-1])]
    return jnp.pad(joined, pad).reshape(joined.shape[:-1] + (size // 128, 128))


TILE = 256
PAIR = 128
FIRM = 1e30


def dot_nn(left, right):
    return lax.dot_general(left, right, (((1,), (0,)), ((), ())), preferred_element_type=jnp.float32)


def dot_nt(left, right):
    return lax.dot_general(left, right, (((1,), (1,)), ((), ())), preferred_element_type=jnp.float32)


def dot_tn(left, right):
    return lax.dot_general(left, right, (((0,), (0,)), ((), ())), preferred_element_type=jnp.float32)


def normalize(values):
    average = jnp.mean(values, axis=-1, keepdims=True)
    centered = values - average
    variance = jnp.mean(centered * centered, axis=-1, keepdims=True)
    scale = lax.rsqrt(variance + EPSILON)
    return centered * scale, scale


def norm_grad(upstream, gain, normal, scale):
    inner = upstream * gain
    first = jnp.mean(inner, axis=-1, keepdims=True)
    second = jnp.mean(inner * normal, axis=-1, keepdims=True)
    return scale * (inner - first - normal * second)


def column_sum(values):
    return jnp.sum(values, axis=0, keepdims=True)


def project_kernel(x_ref, prev_ref, weight_ref, vectors_ref, normed_ref, q_ref, k_ref, v_ref):
    tile = pl.program_id(1)
    width = x_ref.shape[-1]
    x = jnp.where(tile == 0, prev_ref[0], x_ref[0]).astype(jnp.float32)
    normal, _ = normalize(x)
    normed = (normal * vectors_ref[0:1] + vectors_ref[1:2]).astype(jnp.bfloat16)
    normed_ref[0] = normed

    @pl.when(tile > 0)
    def _():
        queries = dot_nn(normed, weight_ref[:, :width]) + vectors_ref[2:3]
        q_ref[0] = queries.astype(jnp.bfloat16) * jnp.bfloat16(1.0 / math.sqrt(HD))

    k_ref[0] = dot_nn(normed, weight_ref[:, width : 2 * width]).astype(jnp.bfloat16)
    values = dot_nn(normed, weight_ref[:, 2 * width :]) + vectors_ref[3:4]
    v_ref[0] = values.astype(jnp.bfloat16)


def project(tokens, prev, weight, vectors):
    rows, local, width = tokens.shape
    tiles = local // TILE
    here = lambda r, t: (r, jnp.maximum(t - 1, 0), 0)
    extended = jax.ShapeDtypeStruct((rows, local + TILE, width), jnp.bfloat16)
    return pl.pallas_call(
        project_kernel,
        grid=(rows, tiles + 1),
        in_specs=[
            pl.BlockSpec((1, TILE, width), here),
            pl.BlockSpec((1, TILE, width), lambda r, t: (r, 0, 0)),
            pl.BlockSpec(weight.shape, lambda r, t: (0, 0)),
            pl.BlockSpec(vectors.shape, lambda r, t: (0, 0)),
        ],
        out_specs=[
            pl.BlockSpec((1, TILE, width), lambda r, t: (r, t, 0)),
            pl.BlockSpec((1, TILE, width), here),
            pl.BlockSpec((1, TILE, width), lambda r, t: (r, t, 0)),
            pl.BlockSpec((1, TILE, width), lambda r, t: (r, t, 0)),
        ],
        out_shape=[extended, jax.ShapeDtypeStruct(tokens.shape, jnp.bfloat16), extended, extended],
        compiler_params=pltpu.CompilerParams(vmem_limit_bytes=VMEM_LIMIT),
    )(tokens, prev, weight, vectors)


def lane_index(rows):
    return lax.broadcasted_iota(jnp.int32, (rows, PAIR), 1)


def mask_columns(starts_ref, row, q_cols, k_cols):
    place = lax.broadcasted_iota(jnp.int32, (TILE, PAIR), 0)
    lane = lane_index(TILE)
    for tile in range(2):
        before, start = starts_ref[row, tile], starts_ref[row, tile + 1]
        late = jnp.where(place >= start, 1.0, 0.0)
        q_cols[tile] = jnp.where(lane == 0, late, jnp.where(lane == 1, 1.0, 0.0)).astype(jnp.bfloat16)
        early = jnp.where(place < before, -FIRM, 0.0)
        k_cols[tile, 0] = jnp.where(
            lane == 0, -FIRM, jnp.where(lane == 1, early, 0.0)
        ).astype(jnp.bfloat16)
        early = jnp.where(place < start, -FIRM, 0.0)
        k_cols[tile, 1] = jnp.where(lane == 0, early, 0.0).astype(jnp.bfloat16)


def attend_kernel(starts_ref, q_ref, k_ref, v_ref, probs_ref, out_ref, inverse_ref, q_cols, k_cols):
    row = pl.program_id(0)

    @pl.when(pl.program_id(1) == 0)
    def _():
        mask_columns(starts_ref, row, q_cols, k_cols)

    lane = lane_index(TILE)
    causal = lax.broadcasted_iota(jnp.int32, (TILE, TILE), 1) <= lax.broadcasted_iota(
        jnp.int32, (TILE, TILE), 0
    )
    ones = jnp.ones((TILE, PAIR), jnp.bfloat16)
    for tile in range(2):
        queries = q_ref[0, pl.ds(tile * TILE, TILE)]
        keys = [
            jnp.concatenate([k_ref[0, pl.ds((tile + w) * TILE, TILE)], k_cols[tile, w]], axis=1)
            for w in range(2)
        ]
        values = [
            jnp.concatenate([v_ref[0, pl.ds((tile + w) * TILE, TILE)], ones], axis=1)
            for w in range(2)
        ]
        mixed, inverse = [], []
        for head in range(2):
            mine = (lane < HD) if head == 0 else (lane >= HD)
            left = jnp.concatenate([jnp.where(mine, queries, jnp.bfloat16(0)), q_cols[tile]], axis=1)
            far = dot_nt(left, keys[0])
            near = jnp.where(causal, dot_nt(left, keys[1]), -FIRM)
            top = jnp.max(jnp.maximum(far, near), axis=-1, keepdims=True)
            far = jnp.exp(far - top).astype(jnp.bfloat16)
            near = jnp.exp(near - top).astype(jnp.bfloat16)
            probs_ref[0, 0, tile, head, 0] = far
            probs_ref[0, 0, tile, head, 1] = near
            total = dot_nn(far, values[0]) + dot_nn(near, values[1])
            share = 1.0 / total[:, PAIR:]
            mixed.append(total[:, :PAIR] * share)
            inverse.append(share)
        out_ref[0, pl.ds(tile * TILE, TILE)] = jnp.where(lane < HD, mixed[0], mixed[1]).astype(
            jnp.bfloat16
        )
        inverse_ref[0, pl.ds(tile * TILE, TILE)] = jnp.where(lane < HD, inverse[0], inverse[1])


def attend(starts, q, k, v):
    rows, local, width = q.shape
    pairs = width // PAIR
    by_pair = lambda r, j: (r, 0, j)
    return pl.pallas_call(
        attend_kernel,
        grid=(rows, pairs),
        in_specs=[
            pl.BlockSpec(memory_space=pltpu.SMEM),
            pl.BlockSpec((1, local, PAIR), by_pair),
            pl.BlockSpec((1, local + TILE, PAIR), by_pair),
            pl.BlockSpec((1, local + TILE, PAIR), by_pair),
        ],
        out_specs=[
            pl.BlockSpec((1, 1, 2, 2, 2, TILE, TILE), lambda r, j: (r, j, 0, 0, 0, 0, 0)),
            pl.BlockSpec((1, local, PAIR), by_pair),
            pl.BlockSpec((1, local, PAIR), by_pair),
        ],
        out_shape=[
            jax.ShapeDtypeStruct((rows, pairs, 2, 2, 2, TILE, TILE), jnp.bfloat16),
            jax.ShapeDtypeStruct((rows, local, width), jnp.bfloat16),
            jax.ShapeDtypeStruct((rows, local, width), jnp.float32),
        ],
        scratch_shapes=[
            pltpu.VMEM((2, TILE, PAIR), jnp.bfloat16),
            pltpu.VMEM((2, 2, TILE, PAIR), jnp.bfloat16),
        ],
        compiler_params=pltpu.CompilerParams(vmem_limit_bytes=VMEM_LIMIT),
    )(starts, q, k, v)


def attend_grad_kernel(
    probs_ref, q_ref, k_ref, v_ref, grad_ref, out_ref, inverse_ref, dq_ref, dk_ref, dv_ref, dk_sum, dv_sum
):
    lane = lane_index(TILE)
    ones = jnp.ones((TILE, PAIR), jnp.bfloat16)
    for tile in range(2):
        span = pl.ds(tile * TILE, TILE)
        queries = q_ref[0, span]
        scaled = (grad_ref[0, span].astype(jnp.float32) * inverse_ref[0, span]).astype(jnp.bfloat16)
        product = scaled.astype(jnp.float32) * out_ref[0, span].astype(jnp.float32)
        d_queries = []
        for head in range(2):
            mine = (lane < HD) if head == 0 else (lane >= HD)
            delta = -jnp.sum(jnp.where(mine, product, 0.0), axis=-1, keepdims=True)
            high = delta.astype(jnp.bfloat16).astype(jnp.float32)
            extra = jnp.where(lane == 0, high, jnp.where(lane == 1, delta - high, 0.0))
            grads = jnp.where(mine, scaled, jnp.bfloat16(0))
            mine_queries = jnp.where(mine, queries, jnp.bfloat16(0))
            left = jnp.concatenate([grads, extra.astype(jnp.bfloat16)], axis=1)
            d_query = None
            for w in range(2):
                at = pl.ds((tile + w) * TILE, TILE)
                right = jnp.concatenate([v_ref[0, at], ones], axis=1)
                probs = probs_ref[0, 0, tile, head, w]
                d_score = (probs.astype(jnp.float32) * dot_nt(left, right)).astype(jnp.bfloat16)
                part = dot_nn(d_score, k_ref[0, at])
                d_query = part if w == 0 else d_query + part
                d_key = dot_tn(d_score, mine_queries)
                d_value = dot_tn(probs, grads)
                if head == 0 and (w == 1 or tile == 0):
                    dk_sum[at] = d_key
                    dv_sum[at] = d_value
                else:
                    dk_sum[at] += d_key
                    dv_sum[at] += d_value
            d_queries.append(d_query)
        dq = jnp.where(lane < HD, d_queries[0], d_queries[1]) * (1.0 / math.sqrt(HD))
        dq_ref[0, span] = dq.astype(jnp.bfloat16)
    dk_ref[0] = dk_sum[...].astype(jnp.bfloat16)
    dv_ref[0] = dv_sum[...].astype(jnp.bfloat16)


def attend_grad(probs, q, k, v, grad, out, inverse):
    rows, local, width = q.shape
    pairs = width // PAIR
    by_pair = lambda r, j: (r, 0, j)
    small = pl.BlockSpec((1, local, PAIR), by_pair)
    large = pl.BlockSpec((1, local + TILE, PAIR), by_pair)
    return pl.pallas_call(
        attend_grad_kernel,
        grid=(rows, pairs),
        in_specs=[
            pl.BlockSpec((1, 1, 2, 2, 2, TILE, TILE), lambda r, j: (r, j, 0, 0, 0, 0, 0)),
            small,
            large,
            large,
            small,
            small,
            small,
        ],
        out_specs=[small, large, large],
        out_shape=[
            jax.ShapeDtypeStruct(q.shape, jnp.bfloat16),
            jax.ShapeDtypeStruct(k.shape, jnp.bfloat16),
            jax.ShapeDtypeStruct(k.shape, jnp.bfloat16),
        ],
        scratch_shapes=[
            pltpu.VMEM((local + TILE, PAIR), jnp.float32),
            pltpu.VMEM((local + TILE, PAIR), jnp.float32),
        ],
        compiler_params=pltpu.CompilerParams(vmem_limit_bytes=VMEM_LIMIT),
    )(probs, q, k, v, grad, out, inverse)


def gelu_pair(v):
    square = v * v
    half = 0.5 + 0.5 * jnp.tanh(v * (GELU_SCALE + (GELU_SCALE * 0.044715) * square))
    hidden = v * half
    slope = half + hidden * (1.0 - half) * (2.0 * GELU_SCALE + (6.0 * GELU_SCALE * 0.044715) * square)
    return hidden, slope


MLP_TILE = 256
CHUNK = 768


def mlp_kernel(
    x_hbm, att_hbm, dy_hbm, attn_hbm, fc_hbm, proj_hbm, vectors,
    out_hbm, middle_grad_hbm, att_grad_hbm, attn_grad_hbm, fc_grad_hbm, proj_grad_hbm, sums_ref,
    x, att, dy, attn, fc, proj, hidden, pre_grad, normed, branch, out, middle_grad, att_grad,
    attn_grad, fc_grad, proj_grad, in_sem, out_sem,
):
    tokens, width = x.shape
    chunks = fc.shape[1] // CHUNK
    tiles = tokens // MLP_TILE
    loads = [
        pltpu.make_async_copy(src, dst, in_sem.at[i])
        for i, (src, dst) in enumerate(
            ((att_hbm, att), (attn_hbm, attn), (x_hbm, x), (fc_hbm, fc), (dy_hbm, dy), (proj_hbm, proj))
        )
    ]
    for load in loads:
        load.start()
    sums_ref[...] = jnp.zeros_like(sums_ref)
    for load in loads[:3]:
        load.wait()

    def tile_step(t, carry):
        span = pl.ds(pl.multiple_of(t * MLP_TILE, MLP_TILE), MLP_TILE)
        middle = x[span].astype(jnp.float32) + dot_nn(att[span], attn[...]) + vectors[4:5]
        normal, scale = normalize(middle)
        low = (normal * vectors[5:6] + vectors[6:7]).astype(jnp.bfloat16)
        normed[span] = low

        @pl.when(t == 0)
        def _():
            for load in loads[3:]:
                load.wait()

        upstream = dy[span]
        result = middle + vectors[7:8]
        back = None
        for j in range(chunks):
            columns = pl.ds(j * CHUNK, CHUNK)
            pre = dot_nn(low, fc[:, columns]) + vectors[8 + j : 9 + j]
            value, slope = gelu_pair(pre)
            value = value.astype(jnp.bfloat16)
            hidden[span, columns] = value
            grad = dot_nt(upstream, proj[columns]) * slope
            grad = grad.astype(jnp.bfloat16)
            pre_grad[span, columns] = grad
            sums_ref[4 + j : 5 + j] += column_sum(grad.astype(jnp.float32))
            result = result + dot_nn(value, proj[columns])
            part = dot_nt(grad, fc[:, columns])
            back = part if back is None else back + part
        out[span] = result.astype(jnp.bfloat16)
        upstream = upstream.astype(jnp.float32)
        sums_ref[0:1] += column_sum(upstream)
        sums_ref[1:2] += column_sum(back * normal)
        sums_ref[2:3] += column_sum(back)
        total = upstream + norm_grad(back, vectors[5:6], normal, scale)
        middle_grad[span] = total
        total = total.astype(jnp.bfloat16)
        branch[span] = total
        sums_ref[3:4] += column_sum(total.astype(jnp.float32))
        att_grad[span] = dot_nt(total, attn[...]).astype(jnp.bfloat16)
        return carry

    lax.fori_loop(0, tiles, tile_step, 0)
    stores = []

    def store(src, dst):
        copy = pltpu.make_async_copy(src, dst, out_sem.at[len(stores)])
        copy.start()
        stores.append(copy)

    store(out, out_hbm)
    store(middle_grad, middle_grad_hbm)
    store(att_grad, att_grad_hbm)
    for j in range(chunks):
        columns = pl.ds(j * CHUNK, CHUNK)
        proj_grad[columns] = dot_tn(hidden[:, columns], dy[...]).astype(jnp.bfloat16)
        store(proj_grad.at[columns], proj_grad_hbm.at[columns])
    for j in range(chunks):
        columns = pl.ds(j * CHUNK, CHUNK)
        fc_grad[:, columns] = dot_tn(normed[...], pre_grad[:, columns]).astype(jnp.bfloat16)
        store(fc_grad.at[:, columns], fc_grad_hbm.at[:, columns])
    attn_grad[...] = dot_tn(att[...], branch[...]).astype(jnp.bfloat16)
    store(attn_grad, attn_grad_hbm)
    for copy in stores:
        copy.wait()


def mlp(x, att, dy, attn, fc, proj, vectors):
    tokens, width = x.shape
    hidden = fc.shape[1]
    low, full = jnp.bfloat16, jnp.float32
    anywhere = pl.BlockSpec(memory_space=pl.ANY)
    vmem = pl.BlockSpec(memory_space=pltpu.VMEM)
    return pl.pallas_call(
        mlp_kernel,
        in_specs=[anywhere] * 6 + [vmem],
        out_specs=[anywhere] * 6 + [vmem],
        out_shape=[
            jax.ShapeDtypeStruct((tokens, width), low),
            jax.ShapeDtypeStruct((tokens, width), full),
            jax.ShapeDtypeStruct((tokens, width), low),
            jax.ShapeDtypeStruct(attn.shape, low),
            jax.ShapeDtypeStruct(fc.shape, low),
            jax.ShapeDtypeStruct(proj.shape, low),
            jax.ShapeDtypeStruct((8, width), full),
        ],
        scratch_shapes=[
            pltpu.VMEM((tokens, width), low),
            pltpu.VMEM((tokens, width), low),
            pltpu.VMEM((tokens, width), low),
            pltpu.VMEM(attn.shape, low),
            pltpu.VMEM(fc.shape, low),
            pltpu.VMEM(proj.shape, low),
            pltpu.VMEM((tokens, hidden), low),
            pltpu.VMEM((tokens, hidden), low),
            pltpu.VMEM((tokens, width), low),
            pltpu.VMEM((tokens, width), low),
            pltpu.VMEM((tokens, width), low),
            pltpu.VMEM((tokens, width), full),
            pltpu.VMEM((tokens, width), low),
            pltpu.VMEM(attn.shape, low),
            pltpu.VMEM(fc.shape, low),
            pltpu.VMEM(proj.shape, low),
            pltpu.SemaphoreType.DMA((6,)),
            pltpu.SemaphoreType.DMA((12,)),
        ],
        compiler_params=pltpu.CompilerParams(vmem_limit_bytes=VMEM_LIMIT),
    )(x, att, dy, attn, fc, proj, vectors)


def project_grad_kernel(normed, dq, dk, dv, weight, weight_grad, prev_grad, sums):
    rows, extended, width = normed.shape
    local = dq.shape[1]
    third = [pl.ds(i * width, width) for i in range(3)]
    for r in range(rows):
        head = pl.ds(0, TILE)
        prev_grad[r] = (
            dot_nt(dk[r, head], weight[:, third[1]]) + dot_nt(dv[r, head], weight[:, third[2]])
        ).astype(jnp.bfloat16)
    total = None
    for i, grads in enumerate((dq, dk, dv)):
        total = None
        for r in range(rows):
            left = normed[r, TILE:] if i == 0 else normed[r]
            part = dot_tn(left, grads[r])
            total = part if total is None else total + part
        weight_grad[:, third[i]] = total.astype(jnp.bfloat16)
    sums[...] = jnp.zeros_like(sums)
    for r in range(rows):
        sums[0:1] += column_sum(dq[r].astype(jnp.float32))
        sums[1:2] += column_sum(dv[r].astype(jnp.float32))


def project_grad(normed, dq, dk, dv, weight):
    rows, extended, width = normed.shape
    vmem = pl.BlockSpec(memory_space=pltpu.VMEM)
    return pl.pallas_call(
        project_grad_kernel,
        in_specs=[vmem] * 5,
        out_specs=[vmem] * 3,
        out_shape=[
            jax.ShapeDtypeStruct(weight.shape, jnp.bfloat16),
            jax.ShapeDtypeStruct((rows, TILE, width), jnp.bfloat16),
            jax.ShapeDtypeStruct((8, width), jnp.float32),
        ],
        compiler_params=pltpu.CompilerParams(vmem_limit_bytes=VMEM_LIMIT),
    )(normed, dq, dk, dv, weight)


def tokens_grad_kernel(x_ref, dq, dk, dv, weight, late, middle_grad, vectors, out_ref, sums):
    row, tile = pl.program_id(0), pl.program_id(1)
    width = x_ref.shape[-1]

    @pl.when((row == 0) & (tile == 0))
    def _():
        sums[...] = jnp.zeros_like(sums)

    back = dot_nt(dq[0], weight[:, :width])
    back = back + dot_nt(dk[0], weight[:, width : 2 * width])
    back = back + dot_nt(dv[0], weight[:, 2 * width :])
    back = back + jnp.where(tile == pl.num_programs(1) - 1, late[0].astype(jnp.float32), 0.0)
    normal, scale = normalize(x_ref[0].astype(jnp.float32))
    sums[0:1] += column_sum(back * normal)
    sums[1:2] += column_sum(back)
    out_ref[0] = middle_grad[0] + norm_grad(back, vectors[0:1], normal, scale)


def tokens_grad_of(x, dq, dk, dv, weight, late, middle_grad, vectors):
    rows, local, width = x.shape
    block = lambda shift: pl.BlockSpec((1, TILE, width), lambda r, t: (r, t + shift, 0))
    whole = lambda v: pl.BlockSpec(v.shape, lambda r, t: (0, 0))
    return pl.pallas_call(
        tokens_grad_kernel,
        grid=(rows, local // TILE),
        in_specs=[
            block(0),
            block(0),
            block(1),
            block(1),
            whole(weight),
            pl.BlockSpec((1, TILE, width), lambda r, t: (r, 0, 0)),
            block(0),
            whole(vectors),
        ],
        out_specs=[block(0), pl.BlockSpec((8, width), lambda r, t: (0, 0))],
        out_shape=[
            jax.ShapeDtypeStruct(x.shape, jnp.float32),
            jax.ShapeDtypeStruct((8, width), jnp.float32),
        ],
        compiler_params=pltpu.CompilerParams(vmem_limit_bytes=VMEM_LIMIT),
    )(x, dq, dk, dv, weight, late, middle_grad, vectors)


def gather_weights(outer, weights, vectors, fc_bias):
    devices = outer * 8
    shards = [pack_vectors(vectors + [fc_bias])]
    shards += [w.reshape(pack_shape(w.shape)) for w in weights]
    full = gather_all(outer, shards, cut([shard.shape for shard in shards]))
    packed = full[0].reshape(devices, -1)
    count, size = len(vectors), vectors[0].shape[0]
    first = packed[:, : count * size].reshape(devices, count, size)
    first = jnp.swapaxes(first, 0, 1).reshape(count, devices * size)
    second = packed[:, count * size : count * size + fc_bias.shape[0]].reshape(-1, devices * size)
    whole = [f.reshape(devices * w.shape[0], w.shape[1]) for f, w in zip(full[1:], weights)]
    return whole, jnp.concatenate([first, second], axis=0)


def scatter_grads(outer, weight_terms, vector_terms, fc_bias_term):
    devices = outer * 8
    count, width = vector_terms.shape
    first = jnp.swapaxes(vector_terms.reshape(count, devices, width // devices), 0, 1)
    first = first.reshape(devices, -1)
    second = fc_bias_term.reshape(devices, -1)
    packed = pack_vectors([first, second])
    terms = [packed.reshape((outer, 2, 2, 2) + packed.shape[1:])]
    shapes = [(term.shape[0] // devices, term.shape[1]) for term in weight_terms]
    for term, shape in zip(weight_terms, shapes):
        terms.append(term.reshape((outer, 2, 2, 2) + pack_shape(shape)))
    shares = scatter_all(outer, terms, cut([term.shape[-2:] for term in terms]))
    flat = shares[0].reshape(-1)
    size = width // devices
    vectors = [flat[i * size : (i + 1) * size] for i in range(count)]
    fc_bias = flat[count * size : count * size + second.shape[1]]
    return [share.reshape(shape) for share, shape in zip(shares[1:], shapes)], vectors, fc_bias


def shards(
    tokens_in,
    doc_starts,
    norm1_gain,
    norm1_bias,
    qkv_weight,
    query_bias,
    value_bias,
    attn_weight,
    attn_bias,
    norm2_gain,
    norm2_bias,
    fc_weight,
    fc_bias,
    proj_weight,
    proj_bias,
    out_grad,
):
    outer = lax.axis_size("batch") // 4
    rows, local, width = tokens_in.shape
    seq = lax.axis_index("seq")
    prev = lax.ppermute(tokens_in[:, local - TILE :], "seq", [(0, 1)])
    (qkv, attn, fc, proj), vectors = gather_weights(
        outer,
        [qkv_weight, attn_weight, fc_weight, proj_weight],
        [norm1_gain, norm1_bias, query_bias, value_bias, attn_bias, norm2_gain, norm2_bias, proj_bias],
        fc_bias,
    )
    first = 2 * seq
    padded = jnp.pad(doc_starts, ((0, 0), (1, 0)))
    starts = lax.dynamic_slice_in_dim(padded, first, 3, 1)
    starts = starts - TILE * (first - 1 + jnp.arange(3, dtype=jnp.int32))
    normed, q, k, v = project(tokens_in, prev, qkv, vectors)
    probs, att, inverse = attend(starts, q, k, v)
    flat = lambda value: value.reshape(rows * local, width)
    out, middle_grad, att_grad, attn_grad, fc_grad, proj_grad, mlp_sums = mlp(
        flat(tokens_in), flat(att), flat(out_grad), attn, fc, proj, vectors
    )
    block = lambda value: value.reshape(rows, local, width)
    dq, dk, dv = attend_grad(probs, q, k, v, block(att_grad), att, inverse)
    qkv_grad, prev_grad, project_sums = project_grad(normed, dq, dk, dv, qkv)
    late = lax.ppermute(prev_grad, "seq", [(1, 0)])
    tokens_grad, norm_sums = tokens_grad_of(
        tokens_in, dq, dk, dv, qkv, late, block(middle_grad), vectors
    )
    sums = jnp.concatenate([norm_sums[:2], project_sums[:2], mlp_sums[:4]], axis=0)
    weights, shares, fc_share = scatter_grads(
        outer, [qkv_grad, attn_grad, fc_grad, proj_grad], sums, mlp_sums[4:]
    )
    gain1, bias1, query, value, proj_b, gain2, bias2, attn_b = shares
    return (
        out.reshape(rows, local, width),
        tokens_grad,
        gain1,
        bias1,
        weights[0],
        query,
        value,
        weights[1],
        attn_b,
        gain2,
        bias2,
        weights[2],
        fc_share,
        weights[3],
        proj_b,
    )


def solution(mesh):
    return jax.shard_map(
        shards,
        mesh=mesh,
        in_specs=(
            P("batch", "seq", None),
            P("batch", None),
            P(("batch", "seq")),
            P(("batch", "seq")),
            P(("batch", "seq"), None),
            P(("batch", "seq")),
            P(("batch", "seq")),
            P(("batch", "seq"), None),
            P(("batch", "seq")),
            P(("batch", "seq")),
            P(("batch", "seq")),
            P(("batch", "seq"), None),
            P(("batch", "seq")),
            P(("batch", "seq"), None),
            P(("batch", "seq")),
            P("batch", "seq", None),
        ),
        out_specs=(
            P("batch", "seq", None),
            P("batch", "seq", None),
            P(("batch", "seq")),
            P(("batch", "seq")),
            P(("batch", "seq"), None),
            P(("batch", "seq")),
            P(("batch", "seq")),
            P(("batch", "seq"), None),
            P(("batch", "seq")),
            P(("batch", "seq")),
            P(("batch", "seq")),
            P(("batch", "seq"), None),
            P(("batch", "seq")),
            P(("batch", "seq"), None),
            P(("batch", "seq")),
        ),
        check_vma=False,
    )
```

```python
import functools
import math

import jax
import jax.numpy as jnp
from jax import lax
from jax.experimental import pallas as pl
from jax.experimental.pallas import tpu as pltpu
from jax.sharding import PartitionSpec as P

HD = 64
EPSILON = 1e-05
GELU_SCALE = 0.7978845608028654
MESH_ID = pl.DeviceIdType.MESH
VMEM_LIMIT = 60 * 2**20
EVERY = slice(None)


def place():
    batch, seq = lax.axis_index("batch"), lax.axis_index("seq")
    return (batch // 4, (batch // 2) % 2, batch % 2, seq)


def device(a, y, c, s):
    return (a * 4 + y * 2 + c, s)


def greet(outer):
    a, y, c, s = place()
    barrier = pltpu.get_barrier_semaphore()
    others = [device(lax.rem(a + k, outer), y, c, s) for k in range(1, outer)]
    others += [device(a, 1 - y, c, s), device(a, y, c, 1 - s), device(a, y, 1 - c, s)]
    for other in others:
        pl.semaphore_signal(barrier, inc=1, device_id=other, device_id_type=MESH_ID)
    pl.semaphore_wait(barrier, len(others))


def remote(src, dst, send_sem, recv_sem, other):
    return pltpu.make_async_remote_copy(
        src_ref=src,
        dst_ref=dst,
        send_sem=send_sem,
        recv_sem=recv_sem,
        device_id=other,
        device_id_type=MESH_ID,
    )


class Gather:
    lags, ahead = (1, 2, 4, 6), 2

    def __init__(self, outer, pieces, shards, outs, own_sem, send_sem, recv_sem):
        self.outer, self.pieces, self.shards, self.outs = outer, pieces, shards, outs
        self.own_sem, self.send_sem, self.recv_sem = own_sem, send_sem, recv_sem
        self.steps = len(pieces) + self.lags[3]
        self.place = place()

    def sems(self, p, k):
        return self.send_sem.at[p, k], self.recv_sem.at[p, k]

    def own(self, i):
        return pltpu.make_async_copy(
            self.shards[i], self.outs[i].at[self.place], self.own_sem.at[i]
        )

    def first(self, p, k):
        i, start, width, order = self.pieces[p]
        a, y, c, s = self.place
        columns = pl.ds(start, width)
        src = self.shards[i].at[:, columns]
        dst = self.outs[i].at[a, y, c, s, :, columns]
        if k == 0:
            return remote(src, dst, *self.sems(p, 0), self.near(order))
        return remote(src, dst, *self.sems(p, k), device(lax.rem(a + k, self.outer), y, c, s))

    def near(self, order):
        a, y, c, s = self.place
        return device(a, 1 - y, c, s) if order == 0 else device(a, y, c, 1 - s)

    def second(self, p, k):
        i, start, width, order = self.pieces[p]
        a, y, c, s = self.place
        source = lax.rem(a + self.outer - k, self.outer)
        block = self.outs[i].at[source, y, c, s, :, pl.ds(start, width)]
        return remote(block, block, *self.sems(p, self.outer - 1 + k), self.near(order))

    def third(self, p):
        i, start, width, order = self.pieces[p]
        a, y, c, s = self.place
        index = (EVERY, EVERY, c, s) if order == 0 else (EVERY, y, c, EVERY)
        block = self.outs[i].at[index + (EVERY, pl.ds(start, width))]
        return remote(block, block, *self.sems(p, 2 * self.outer - 1), self.near(1 - order))

    def fourth(self, p):
        i, start, width, order = self.pieces[p]
        a, y, c, s = self.place
        block = self.outs[i].at[EVERY, EVERY, c, EVERY, EVERY, pl.ds(start, width)]
        return remote(block, block, *self.sems(p, 2 * self.outer), device(a, y, 1 - c, s))

    def step(self, t):
        outer, count, lags = self.outer, len(self.pieces), self.lags
        for p in range(self.ahead + 1) if t == 0 else (t + self.ahead,):
            if p < count:
                for k in range(outer):
                    self.first(p, k).start()
        if t == 0:
            for i in range(len(self.shards)):
                self.own(i).start()
        p = t - lags[0]
        if 0 <= p < count:
            for k in range(1, outer):
                self.first(p, k).wait_recv()
                self.second(p, k).start()
        p = t - lags[1]
        if 0 <= p < count:
            if p == 0:
                for i in range(len(self.shards)):
                    self.own(i).wait()
            self.first(p, 0).wait_recv()
            for k in range(1, outer):
                self.second(p, k).wait_recv()
            self.third(p).start()
        p = t - lags[2]
        if 0 <= p < count:
            self.third(p).wait_recv()
            self.fourth(p).start()
        p = t - lags[3]
        if 0 <= p < count:
            self.fourth(p).wait_recv()

    def end(self):
        for p in range(len(self.pieces)):
            for k in range(self.outer):
                self.first(p, k).wait_send()
            for k in range(1, self.outer):
                self.second(p, k).wait_send()
            self.third(p).wait_send()
            self.fourth(p).wait_send()

    @staticmethod
    def semaphores(outer, arrays, pieces):
        return [
            pltpu.SemaphoreType.DMA((arrays,)),
            pltpu.SemaphoreType.DMA((pieces, 2 * outer + 1)),
            pltpu.SemaphoreType.DMA((pieces, 2 * outer + 1)),
        ]


def add_slots(target, other):
    lead = target.shape[:-2]

    def body(k, carry):
        index = []
        for size in reversed(lead):
            index.append(lax.rem(k, size))
            k = k // size
        index = tuple(reversed(index))
        value = target[index].astype(jnp.float32) + other[index].astype(jnp.float32)
        target[index] = value.astype(target.dtype)
        return carry

    lax.fori_loop(0, math.prod(lead), body, 0)


class Scatter:
    lags = (1, 3, 4, 5)

    def __init__(self, outer, pieces, terms, outs, slots, own_sem, send_sem, recv_sem):
        self.outer, self.pieces, self.terms, self.outs = outer, pieces, terms, outs
        n = len(pieces)
        self.held, self.got = slots[:n], [slots[k * n : (k + 1) * n] for k in range(1, 5)]
        self.own_sem, self.send_sem, self.recv_sem = own_sem, send_sem, recv_sem
        self.steps = n + self.lags[3]
        self.place = place()

    def sems(self, p, k):
        return self.send_sem.at[p, k], self.recv_sem.at[p, k]

    def own(self, p):
        i, start, width, order = self.pieces[p]
        a, y, c, s = self.place
        block = self.terms[i].at[EVERY, EVERY, c, EVERY, EVERY, pl.ds(start, width)]
        return pltpu.make_async_copy(block, self.held[p], self.own_sem.at[p])

    def first(self, p):
        i, start, width, order = self.pieces[p]
        a, y, c, s = self.place
        block = self.terms[i].at[EVERY, EVERY, 1 - c, EVERY, EVERY, pl.ds(start, width)]
        return remote(block, self.got[0][p], *self.sems(p, 0), device(a, y, 1 - c, s))

    def second(self, p):
        a, y, c, s = self.place
        if self.pieces[p][3] == 0:
            src, other = self.held[p].at[:, :, 1 - s], device(a, y, c, 1 - s)
        else:
            src, other = self.held[p].at[:, 1 - y], device(a, 1 - y, c, s)
        return remote(src, self.got[1][p], *self.sems(p, 1), other)

    def third(self, p):
        a, y, c, s = self.place
        if self.pieces[p][3] == 0:
            src, other = self.held[p].at[:, 1 - y, s], device(a, 1 - y, c, s)
        else:
            src, other = self.held[p].at[:, y, 1 - s], device(a, y, c, 1 - s)
        return remote(src, self.got[2][p], *self.sems(p, 2), other)

    def fourth(self, p, k):
        a, y, c, s = self.place
        to = lax.rem(a + k, self.outer)
        src = self.held[p].at[to, y, s]
        return remote(src, self.got[3][p].at[k - 1], *self.sems(p, 2 + k), device(to, y, c, s))

    def step(self, t):
        outer, count, lags = self.outer, len(self.pieces), self.lags
        a, y, c, s = self.place
        if t < count:
            self.own(t).start()
            self.first(t).start()
        p = t - lags[0]
        if 0 <= p < count:
            self.own(p).wait()
            self.first(p).wait_recv()
            add_slots(self.held[p], self.got[0][p])
            self.second(p).start()
        p = t - lags[1]
        if 0 <= p < count:
            self.second(p).wait_recv()
            mine = (EVERY, EVERY, s) if self.pieces[p][3] == 0 else (EVERY, y)
            add_slots(self.held[p].at[mine], self.got[1][p])
            self.third(p).start()
        p = t - lags[2]
        if 0 <= p < count:
            self.third(p).wait_recv()
            add_slots(self.held[p].at[:, y, s], self.got[2][p])
            for k in range(1, outer):
                self.fourth(p, k).start()
        p = t - lags[3]
        if 0 <= p < count:
            i, start, width, order = self.pieces[p]
            value = self.held[p][a, y, s].astype(jnp.float32)
            for k in range(1, outer):
                self.fourth(p, k).wait_recv()
                value = value + self.got[3][p][k - 1].astype(jnp.float32)
            self.outs[i][:, pl.ds(start, width)] = value

    def end(self):
        for p in range(len(self.pieces)):
            self.first(p).wait_send()
            self.second(p).wait_send()
            self.third(p).wait_send()
            for k in range(1, self.outer):
                self.fourth(p, k).wait_send()

    @staticmethod
    def scratch(outer, shapes, pieces):
        def slot(p, *lead):
            i, start, width, order = pieces[p]
            return pltpu.VMEM(lead + (shapes[i][0], width), shapes[i][2])

        n = range(len(pieces))
        leads = ((outer, 2, 2), (outer, 2, 2), (outer, 2), (outer,), (max(outer - 1, 1),))
        return [slot(p, *lead) for lead in leads for p in n] + [
            pltpu.SemaphoreType.DMA((len(pieces),)),
            pltpu.SemaphoreType.DMA((len(pieces), outer + 2)),
            pltpu.SemaphoreType.DMA((len(pieces), outer + 2)),
        ]


def gather_kernel(outer, pieces, count, *refs):
    greet(outer)
    work = Gather(outer, pieces, refs[:count], refs[count : 2 * count], *refs[2 * count :])
    for t in range(work.steps):
        work.step(t)
    work.end()


def gather_all(outer, shards, pieces):
    count = len(shards)
    return pl.pallas_call(
        functools.partial(gather_kernel, outer, pieces, count),
        out_shape=[
            jax.ShapeDtypeStruct((outer, 2, 2, 2) + shard.shape, shard.dtype) for shard in shards
        ],
        in_specs=[pl.BlockSpec(memory_space=pltpu.VMEM)] * count,
        out_specs=[pl.BlockSpec(memory_space=pl.ANY)] * count,
        scratch_shapes=Gather.semaphores(outer, count, len(pieces)),
        compiler_params=pltpu.CompilerParams(
            collective_id=0, has_side_effects=True, vmem_limit_bytes=VMEM_LIMIT
        ),
    )(*shards)


def scatter_kernel(outer, pieces, count, *refs):
    greet(outer)
    rest = refs[2 * count :]
    work = Scatter(outer, pieces, refs[:count], refs[count : 2 * count], rest[:-3], *rest[-3:])
    for t in range(work.steps):
        work.step(t)
    work.end()


def scatter_all(outer, terms, pieces):
    count = len(terms)
    shapes = [term.shape[-2:] + (term.dtype,) for term in terms]
    return pl.pallas_call(
        functools.partial(scatter_kernel, outer, pieces, count),
        out_shape=[jax.ShapeDtypeStruct(term.shape[-2:], jnp.float32) for term in terms],
        in_specs=[pl.BlockSpec(memory_space=pl.ANY)] * count,
        out_specs=[pl.BlockSpec(memory_space=pltpu.VMEM)] * count,
        scratch_shapes=Scatter.scratch(outer, shapes, pieces),
        compiler_params=pltpu.CompilerParams(
            collective_id=1, has_side_effects=True, vmem_limit_bytes=VMEM_LIMIT
        ),
    )(*terms)


def cut(shape_list):
    pieces = []
    for i, (rows, columns) in enumerate(shape_list):
        parts, blocks = 1, columns // 128
        if rows % 8 == 0:
            fits = [k for k in range(1, blocks + 1) if blocks % k == 0 and rows * columns // k <= 25000]
            parts = min(fits) if fits else 1
        width = columns // parts
        for k in range(parts):
            pieces.append((i, k * width, width, len(pieces) % 2))
    return pieces


def pack_shape(shape):
    rows, columns = shape
    return shape if rows % 8 == 0 else (rows * columns // 128, 128)


def pack_vectors(parts):
    joined = jnp.concatenate([part.astype(jnp.float32) for part in parts], axis=-1)
    size = -(-joined.shape[-1] // 1024) * 1024
    pad = [(0, 0)] * (joined.ndim - 1) + [(0, size - joined.shape[-1])]
    return jnp.pad(joined, pad).reshape(joined.shape[:-1] + (size // 128, 128))


TILE = 256
PAIR = 128
FIRM = 1e30


def dot_nn(left, right):
    return lax.dot_general(left, right, (((1,), (0,)), ((), ())), preferred_element_type=jnp.float32)


def dot_nt(left, right):
    return lax.dot_general(left, right, (((1,), (1,)), ((), ())), preferred_element_type=jnp.float32)


def dot_tn(left, right):
    return lax.dot_general(left, right, (((0,), (0,)), ((), ())), preferred_element_type=jnp.float32)


def normalize(values):
    average = jnp.mean(values, axis=-1, keepdims=True)
    centered = values - average
    variance = jnp.mean(centered * centered, axis=-1, keepdims=True)
    scale = lax.rsqrt(variance + EPSILON)
    return centered * scale, scale


def norm_grad(upstream, gain, normal, scale):
    inner = upstream * gain
    first = jnp.mean(inner, axis=-1, keepdims=True)
    second = jnp.mean(inner * normal, axis=-1, keepdims=True)
    return scale * (inner - first - normal * second)


def column_sum(values):
    return jnp.sum(values, axis=0, keepdims=True)


def project_kernel(x_ref, prev_ref, weight_ref, vectors_ref, normed_ref, q_ref, k_ref, v_ref):
    tile = pl.program_id(1)
    width = x_ref.shape[-1]
    x = jnp.where(tile == 0, prev_ref[0], x_ref[0]).astype(jnp.float32)
    normal, _ = normalize(x)
    normed = (normal * vectors_ref[0:1] + vectors_ref[1:2]).astype(jnp.bfloat16)
    normed_ref[0] = normed

    @pl.when(tile > 0)
    def _():
        queries = dot_nn(normed, weight_ref[:, :width]) + vectors_ref[2:3]
        q_ref[0] = queries.astype(jnp.bfloat16) * jnp.bfloat16(1.0 / math.sqrt(HD))

    k_ref[0] = dot_nn(normed, weight_ref[:, width : 2 * width]).astype(jnp.bfloat16)
    values = dot_nn(normed, weight_ref[:, 2 * width :]) + vectors_ref[3:4]
    v_ref[0] = values.astype(jnp.bfloat16)


def project(tokens, prev, weight, vectors):
    rows, local, width = tokens.shape
    tiles = local // TILE
    here = lambda r, t: (r, jnp.maximum(t - 1, 0), 0)
    extended = jax.ShapeDtypeStruct((rows, local + TILE, width), jnp.bfloat16)
    return pl.pallas_call(
        project_kernel,
        grid=(rows, tiles + 1),
        in_specs=[
            pl.BlockSpec((1, TILE, width), here),
            pl.BlockSpec((1, TILE, width), lambda r, t: (r, 0, 0)),
            pl.BlockSpec(weight.shape, lambda r, t: (0, 0)),
            pl.BlockSpec(vectors.shape, lambda r, t: (0, 0)),
        ],
        out_specs=[
            pl.BlockSpec((1, TILE, width), lambda r, t: (r, t, 0)),
            pl.BlockSpec((1, TILE, width), here),
            pl.BlockSpec((1, TILE, width), lambda r, t: (r, t, 0)),
            pl.BlockSpec((1, TILE, width), lambda r, t: (r, t, 0)),
        ],
        out_shape=[extended, jax.ShapeDtypeStruct(tokens.shape, jnp.bfloat16), extended, extended],
        compiler_params=pltpu.CompilerParams(vmem_limit_bytes=VMEM_LIMIT),
    )(tokens, prev, weight, vectors)


def lane_index(rows):
    return lax.broadcasted_iota(jnp.int32, (rows, PAIR), 1)


def mask_columns(starts_ref, row, q_cols, k_cols):
    place = lax.broadcasted_iota(jnp.int32, (TILE, PAIR), 0)
    lane = lane_index(TILE)
    for tile in range(2):
        before, start = starts_ref[row, tile], starts_ref[row, tile + 1]
        late = jnp.where(place >= start, 1.0, 0.0)
        q_cols[tile] = jnp.where(lane == 0, late, jnp.where(lane == 1, 1.0, 0.0)).astype(jnp.bfloat16)
        early = jnp.where(place < before, -FIRM, 0.0)
        k_cols[tile, 0] = jnp.where(
            lane == 0, -FIRM, jnp.where(lane == 1, early, 0.0)
        ).astype(jnp.bfloat16)
        early = jnp.where(place < start, -FIRM, 0.0)
        k_cols[tile, 1] = jnp.where(lane == 0, early, 0.0).astype(jnp.bfloat16)


def attend_kernel(starts_ref, q_ref, k_ref, v_ref, probs_ref, out_ref, inverse_ref, q_cols, k_cols):
    row = pl.program_id(0)

    @pl.when(pl.program_id(1) == 0)
    def _():
        mask_columns(starts_ref, row, q_cols, k_cols)

    lane = lane_index(TILE)
    causal = lax.broadcasted_iota(jnp.int32, (TILE, TILE), 1) <= lax.broadcasted_iota(
        jnp.int32, (TILE, TILE), 0
    )
    ones = jnp.ones((TILE, PAIR), jnp.bfloat16)
    for tile in range(2):
        queries = q_ref[0, pl.ds(tile * TILE, TILE)]
        keys = [
            jnp.concatenate([k_ref[0, pl.ds((tile + w) * TILE, TILE)], k_cols[tile, w]], axis=1)
            for w in range(2)
        ]
        values = [
            jnp.concatenate([v_ref[0, pl.ds((tile + w) * TILE, TILE)], ones], axis=1)
            for w in range(2)
        ]
        mixed, inverse = [], []
        for head in range(2):
            mine = (lane < HD) if head == 0 else (lane >= HD)
            left = jnp.concatenate([jnp.where(mine, queries, jnp.bfloat16(0)), q_cols[tile]], axis=1)
            far = dot_nt(left, keys[0])
            near = jnp.where(causal, dot_nt(left, keys[1]), -FIRM)
            top = jnp.max(jnp.maximum(far, near), axis=-1, keepdims=True)
            far = jnp.exp(far - top).astype(jnp.bfloat16)
            near = jnp.exp(near - top).astype(jnp.bfloat16)
            probs_ref[0, 0, tile, head, 0] = far
            probs_ref[0, 0, tile, head, 1] = near
            total = dot_nn(far, values[0]) + dot_nn(near, values[1])
            share = 1.0 / total[:, PAIR:]
            mixed.append(total[:, :PAIR] * share)
            inverse.append(share)
        out_ref[0, pl.ds(tile * TILE, TILE)] = jnp.where(lane < HD, mixed[0], mixed[1]).astype(
            jnp.bfloat16
        )
        inverse_ref[0, pl.ds(tile * TILE, TILE)] = jnp.where(lane < HD, inverse[0], inverse[1])


def attend(starts, q, k, v):
    rows, local, width = q.shape
    pairs = width // PAIR
    by_pair = lambda r, j: (r, 0, j)
    return pl.pallas_call(
        attend_kernel,
        grid=(rows, pairs),
        in_specs=[
            pl.BlockSpec(memory_space=pltpu.SMEM),
            pl.BlockSpec((1, local, PAIR), by_pair),
            pl.BlockSpec((1, local + TILE, PAIR), by_pair),
            pl.BlockSpec((1, local + TILE, PAIR), by_pair),
        ],
        out_specs=[
            pl.BlockSpec((1, 1, 2, 2, 2, TILE, TILE), lambda r, j: (r, j, 0, 0, 0, 0, 0)),
            pl.BlockSpec((1, local, PAIR), by_pair),
            pl.BlockSpec((1, local, PAIR), by_pair),
        ],
        out_shape=[
            jax.ShapeDtypeStruct((rows, pairs, 2, 2, 2, TILE, TILE), jnp.bfloat16),
            jax.ShapeDtypeStruct((rows, local, width), jnp.bfloat16),
            jax.ShapeDtypeStruct((rows, local, width), jnp.float32),
        ],
        scratch_shapes=[
            pltpu.VMEM((2, TILE, PAIR), jnp.bfloat16),
            pltpu.VMEM((2, 2, TILE, PAIR), jnp.bfloat16),
        ],
        compiler_params=pltpu.CompilerParams(vmem_limit_bytes=VMEM_LIMIT),
    )(starts, q, k, v)


def attend_grad_kernel(
    probs_ref, q_ref, k_ref, v_ref, grad_ref, out_ref, inverse_ref, dq_ref, dk_ref, dv_ref, dk_sum, dv_sum
):
    lane = lane_index(TILE)
    ones = jnp.ones((TILE, PAIR), jnp.bfloat16)
    for tile in range(2):
        span = pl.ds(tile * TILE, TILE)
        queries = q_ref[0, span]
        scaled = (grad_ref[0, span].astype(jnp.float32) * inverse_ref[0, span]).astype(jnp.bfloat16)
        product = scaled.astype(jnp.float32) * out_ref[0, span].astype(jnp.float32)
        d_queries = []
        for head in range(2):
            mine = (lane < HD) if head == 0 else (lane >= HD)
            delta = -jnp.sum(jnp.where(mine, product, 0.0), axis=-1, keepdims=True)
            high = delta.astype(jnp.bfloat16).astype(jnp.float32)
            extra = jnp.where(lane == 0, high, jnp.where(lane == 1, delta - high, 0.0))
            grads = jnp.where(mine, scaled, jnp.bfloat16(0))
            mine_queries = jnp.where(mine, queries, jnp.bfloat16(0))
            left = jnp.concatenate([grads, extra.astype(jnp.bfloat16)], axis=1)
            d_query = None
            for w in range(2):
                at = pl.ds((tile + w) * TILE, TILE)
                right = jnp.concatenate([v_ref[0, at], ones], axis=1)
                probs = probs_ref[0, 0, tile, head, w]
                d_score = (probs.astype(jnp.float32) * dot_nt(left, right)).astype(jnp.bfloat16)
                part = dot_nn(d_score, k_ref[0, at])
                d_query = part if w == 0 else d_query + part
                d_key = dot_tn(d_score, mine_queries)
                d_value = dot_tn(probs, grads)
                if head == 0 and (w == 1 or tile == 0):
                    dk_sum[at] = d_key
                    dv_sum[at] = d_value
                else:
                    dk_sum[at] += d_key
                    dv_sum[at] += d_value
            d_queries.append(d_query)
        dq = jnp.where(lane < HD, d_queries[0], d_queries[1]) * (1.0 / math.sqrt(HD))
        dq_ref[0, span] = dq.astype(jnp.bfloat16)
    dk_ref[0] = dk_sum[...].astype(jnp.bfloat16)
    dv_ref[0] = dv_sum[...].astype(jnp.bfloat16)


def attend_grad(probs, q, k, v, grad, out, inverse):
    rows, local, width = q.shape
    pairs = width // PAIR
    by_pair = lambda r, j: (r, 0, j)
    small = pl.BlockSpec((1, local, PAIR), by_pair)
    large = pl.BlockSpec((1, local + TILE, PAIR), by_pair)
    return pl.pallas_call(
        attend_grad_kernel,
        grid=(rows, pairs),
        in_specs=[
            pl.BlockSpec((1, 1, 2, 2, 2, TILE, TILE), lambda r, j: (r, j, 0, 0, 0, 0, 0)),
            small,
            large,
            large,
            small,
            small,
            small,
        ],
        out_specs=[small, large, large],
        out_shape=[
            jax.ShapeDtypeStruct(q.shape, jnp.bfloat16),
            jax.ShapeDtypeStruct(k.shape, jnp.bfloat16),
            jax.ShapeDtypeStruct(k.shape, jnp.bfloat16),
        ],
        scratch_shapes=[
            pltpu.VMEM((local + TILE, PAIR), jnp.float32),
            pltpu.VMEM((local + TILE, PAIR), jnp.float32),
        ],
        compiler_params=pltpu.CompilerParams(vmem_limit_bytes=VMEM_LIMIT),
    )(probs, q, k, v, grad, out, inverse)


def gelu_pair(v):
    square = v * v
    half = 0.5 + 0.5 * jnp.tanh(v * (GELU_SCALE + (GELU_SCALE * 0.044715) * square))
    hidden = v * half
    slope = half + hidden * (1.0 - half) * (2.0 * GELU_SCALE + (6.0 * GELU_SCALE * 0.044715) * square)
    return hidden, slope


MLP_TILE = 256
CHUNK = 768


def mlp_kernel(
    x_hbm, att_hbm, dy_hbm, attn_hbm, fc_hbm, proj_hbm, vectors,
    out_hbm, middle_grad_hbm, att_grad_hbm, attn_grad_hbm, fc_grad_hbm, proj_grad_hbm, sums_ref,
    x, att, dy, attn, fc, proj, hidden, pre_grad, normed, branch, out, middle_grad, att_grad,
    attn_grad, fc_grad, proj_grad, in_sem, out_sem,
):
    tokens, width = x.shape
    chunks = fc.shape[1] // CHUNK
    tiles = tokens // MLP_TILE
    loads = [
        pltpu.make_async_copy(src, dst, in_sem.at[i])
        for i, (src, dst) in enumerate(
            ((att_hbm, att), (attn_hbm, attn), (x_hbm, x), (fc_hbm, fc), (dy_hbm, dy), (proj_hbm, proj))
        )
    ]
    for load in loads:
        load.start()
    sums_ref[...] = jnp.zeros_like(sums_ref)
    for load in loads[:3]:
        load.wait()

    def tile_step(t, carry):
        span = pl.ds(pl.multiple_of(t * MLP_TILE, MLP_TILE), MLP_TILE)
        middle = x[span].astype(jnp.float32) + dot_nn(att[span], attn[...]) + vectors[4:5]
        normal, scale = normalize(middle)
        low = (normal * vectors[5:6] + vectors[6:7]).astype(jnp.bfloat16)
        normed[span] = low

        @pl.when(t == 0)
        def _():
            for load in loads[3:]:
                load.wait()

        upstream = dy[span]
        result = middle + vectors[7:8]
        back = None
        for j in range(chunks):
            columns = pl.ds(j * CHUNK, CHUNK)
            pre = dot_nn(low, fc[:, columns]) + vectors[8 + j : 9 + j]
            value, slope = gelu_pair(pre)
            value = value.astype(jnp.bfloat16)
            hidden[span, columns] = value
            grad = dot_nt(upstream, proj[columns]) * slope
            grad = grad.astype(jnp.bfloat16)
            pre_grad[span, columns] = grad
            sums_ref[4 + j : 5 + j] += column_sum(grad.astype(jnp.float32))
            result = result + dot_nn(value, proj[columns])
            part = dot_nt(grad, fc[:, columns])
            back = part if back is None else back + part
        out[span] = result.astype(jnp.bfloat16)
        upstream = upstream.astype(jnp.float32)
        sums_ref[0:1] += column_sum(upstream)
        sums_ref[1:2] += column_sum(back * normal)
        sums_ref[2:3] += column_sum(back)
        total = upstream + norm_grad(back, vectors[5:6], normal, scale)
        middle_grad[span] = total
        total = total.astype(jnp.bfloat16)
        branch[span] = total
        sums_ref[3:4] += column_sum(total.astype(jnp.float32))
        att_grad[span] = dot_nt(total, attn[...]).astype(jnp.bfloat16)
        return carry

    lax.fori_loop(0, tiles, tile_step, 0)
    stores = []

    def store(src, dst):
        copy = pltpu.make_async_copy(src, dst, out_sem.at[len(stores)])
        copy.start()
        stores.append(copy)

    store(out, out_hbm)
    store(middle_grad, middle_grad_hbm)
    store(att_grad, att_grad_hbm)
    for j in range(chunks):
        columns = pl.ds(j * CHUNK, CHUNK)
        proj_grad[columns] = dot_tn(hidden[:, columns], dy[...]).astype(jnp.bfloat16)
        store(proj_grad.at[columns], proj_grad_hbm.at[columns])
    for j in range(chunks):
        columns = pl.ds(j * CHUNK, CHUNK)
        fc_grad[:, columns] = dot_tn(normed[...], pre_grad[:, columns]).astype(jnp.bfloat16)
        store(fc_grad.at[:, columns], fc_grad_hbm.at[:, columns])
    attn_grad[...] = dot_tn(att[...], branch[...]).astype(jnp.bfloat16)
    store(attn_grad, attn_grad_hbm)
    for copy in stores:
        copy.wait()


def mlp(x, att, dy, attn, fc, proj, vectors):
    tokens, width = x.shape
    hidden = fc.shape[1]
    low, full = jnp.bfloat16, jnp.float32
    anywhere = pl.BlockSpec(memory_space=pl.ANY)
    vmem = pl.BlockSpec(memory_space=pltpu.VMEM)
    return pl.pallas_call(
        mlp_kernel,
        in_specs=[anywhere] * 6 + [vmem],
        out_specs=[anywhere] * 6 + [vmem],
        out_shape=[
            jax.ShapeDtypeStruct((tokens, width), low),
            jax.ShapeDtypeStruct((tokens, width), full),
            jax.ShapeDtypeStruct((tokens, width), low),
            jax.ShapeDtypeStruct(attn.shape, low),
            jax.ShapeDtypeStruct(fc.shape, low),
            jax.ShapeDtypeStruct(proj.shape, low),
            jax.ShapeDtypeStruct((8, width), full),
        ],
        scratch_shapes=[
            pltpu.VMEM((tokens, width), low),
            pltpu.VMEM((tokens, width), low),
            pltpu.VMEM((tokens, width), low),
            pltpu.VMEM(attn.shape, low),
            pltpu.VMEM(fc.shape, low),
            pltpu.VMEM(proj.shape, low),
            pltpu.VMEM((tokens, hidden), low),
            pltpu.VMEM((tokens, hidden), low),
            pltpu.VMEM((tokens, width), low),
            pltpu.VMEM((tokens, width), low),
            pltpu.VMEM((tokens, width), low),
            pltpu.VMEM((tokens, width), full),
            pltpu.VMEM((tokens, width), low),
            pltpu.VMEM(attn.shape, low),
            pltpu.VMEM(fc.shape, low),
            pltpu.VMEM(proj.shape, low),
            pltpu.SemaphoreType.DMA((6,)),
            pltpu.SemaphoreType.DMA((12,)),
        ],
        compiler_params=pltpu.CompilerParams(vmem_limit_bytes=VMEM_LIMIT),
    )(x, att, dy, attn, fc, proj, vectors)


def project_grad_kernel(normed, dq, dk, dv, weight, weight_grad, prev_grad, sums):
    rows, extended, width = normed.shape
    local = dq.shape[1]
    third = [pl.ds(i * width, width) for i in range(3)]
    for r in range(rows):
        head = pl.ds(0, TILE)
        prev_grad[r] = (
            dot_nt(dk[r, head], weight[:, third[1]]) + dot_nt(dv[r, head], weight[:, third[2]])
        ).astype(jnp.bfloat16)
    total = None
    for i, grads in enumerate((dq, dk, dv)):
        total = None
        for r in range(rows):
            left = normed[r, TILE:] if i == 0 else normed[r]
            part = dot_tn(left, grads[r])
            total = part if total is None else total + part
        weight_grad[:, third[i]] = total.astype(jnp.bfloat16)
    sums[...] = jnp.zeros_like(sums)
    for r in range(rows):
        sums[0:1] += column_sum(dq[r].astype(jnp.float32))
        sums[1:2] += column_sum(dv[r].astype(jnp.float32))


def project_grad(normed, dq, dk, dv, weight):
    rows, extended, width = normed.shape
    vmem = pl.BlockSpec(memory_space=pltpu.VMEM)
    return pl.pallas_call(
        project_grad_kernel,
        in_specs=[vmem] * 5,
        out_specs=[vmem] * 3,
        out_shape=[
            jax.ShapeDtypeStruct(weight.shape, jnp.bfloat16),
            jax.ShapeDtypeStruct((rows, TILE, width), jnp.bfloat16),
            jax.ShapeDtypeStruct((8, width), jnp.float32),
        ],
        compiler_params=pltpu.CompilerParams(vmem_limit_bytes=VMEM_LIMIT),
    )(normed, dq, dk, dv, weight)


def tokens_grad_kernel(x_ref, dq, dk, dv, weight, late, middle_grad, vectors, out_ref, sums):
    row, tile = pl.program_id(0), pl.program_id(1)
    width = x_ref.shape[-1]

    @pl.when((row == 0) & (tile == 0))
    def _():
        sums[...] = jnp.zeros_like(sums)

    back = dot_nt(dq[0], weight[:, :width])
    back = back + dot_nt(dk[0], weight[:, width : 2 * width])
    back = back + dot_nt(dv[0], weight[:, 2 * width :])
    back = back + jnp.where(tile == pl.num_programs(1) - 1, late[0].astype(jnp.float32), 0.0)
    normal, scale = normalize(x_ref[0].astype(jnp.float32))
    sums[0:1] += column_sum(back * normal)
    sums[1:2] += column_sum(back)
    out_ref[0] = middle_grad[0] + norm_grad(back, vectors[0:1], normal, scale)


def tokens_grad_of(x, dq, dk, dv, weight, late, middle_grad, vectors):
    rows, local, width = x.shape
    block = lambda shift: pl.BlockSpec((1, TILE, width), lambda r, t: (r, t + shift, 0))
    whole = lambda v: pl.BlockSpec(v.shape, lambda r, t: (0, 0))
    return pl.pallas_call(
        tokens_grad_kernel,
        grid=(rows, local // TILE),
        in_specs=[
            block(0),
            block(0),
            block(1),
            block(1),
            whole(weight),
            pl.BlockSpec((1, TILE, width), lambda r, t: (r, 0, 0)),
            block(0),
            whole(vectors),
        ],
        out_specs=[block(0), pl.BlockSpec((8, width), lambda r, t: (0, 0))],
        out_shape=[
            jax.ShapeDtypeStruct(x.shape, jnp.float32),
            jax.ShapeDtypeStruct((8, width), jnp.float32),
        ],
        compiler_params=pltpu.CompilerParams(vmem_limit_bytes=VMEM_LIMIT),
    )(x, dq, dk, dv, weight, late, middle_grad, vectors)


def spread_vectors(slots, size, fc_size, width):
    outer = slots.shape[0]
    zeros = jnp.zeros((8, width - PAIR), jnp.float32)
    first, second = None, None
    for d in range(outer * 8):
        index = (d // 8, (d // 4) % 2, (d // 2) % 2, d % 2)
        top = jnp.concatenate([slots[index + (slice(0, 8),)], zeros], axis=1)
        low = jnp.concatenate([slots[index + (slice(8, 16),)], zeros], axis=1)
        top = pltpu.roll(top, d * size, 1) if d else top
        row, lane = divmod(d * fc_size, width)
        low = pltpu.roll(low, lane, 1) if lane else low
        low = pltpu.roll(low, row, 0) if row else low
        first = top if first is None else first + top
        second = low if second is None else second + low
    return first, second


def join_rows(target, slots, columns):
    outer, rows = slots.shape[0], slots.shape[-2]

    def body(a, carry):
        for y in range(2):
            for c in range(2):
                both = [slots[a, y, c, s, :, columns].astype(jnp.float32) for s in range(2)]
                start = pl.multiple_of(((a * 2 + y) * 2 + c) * (2 * rows), 2 * rows)
                joined = jnp.concatenate(both, axis=0).astype(target.dtype)
                target[pl.ds(start, 2 * rows), columns] = joined
        return carry

    lax.fori_loop(0, outer, body, 0)


VECTORS = 9


def forward_kernel(outer, pieces, *refs):
    tokens_hbm, starts_ref = refs[:2]
    vector_refs = refs[2 : 2 + VECTORS]
    shards = refs[2 + VECTORS : 6 + VECTORS]
    outs = refs[6 + VECTORS : 17 + VECTORS]
    (
        normed_hbm, q_hbm, k_hbm, v_hbm, probs_hbm, att_hbm, inverse_hbm, weight_hbm, *slots_hbm,
    ) = outs
    vectors = refs[17 + VECTORS]
    (
        own, vector_slots, qkv_slots, weight, x, normed, q, k, v, probs, att, inverse,
        q_cols, k_cols, move_sem, out_sem, probs_sem, own_sem, send_sem, recv_sem,
    ) = refs[18 + VECTORS :]
    rows, local, width = q.shape
    a, y, c, s = place()
    size, fc_size = vector_refs[0].shape[1], vector_refs[-1].shape[1]

    load = pltpu.make_async_copy(tokens_hbm, x.at[:, pl.ds(TILE, local)], move_sem.at[0])
    load.start()
    own[...] = jnp.zeros_like(own)
    for i, ref in enumerate(vector_refs):
        own[i : i + 1, : ref.shape[1]] = ref[...].astype(jnp.float32)
    greet(outer)
    prev = remote(
        tokens_hbm.at[:, pl.ds(local - TILE, TILE)],
        x.at[:, pl.ds(0, TILE)],
        move_sem.at[1],
        move_sem.at[2],
        device(a, y, c, 1 - s),
    )
    work = Gather(
        outer, pieces, (own,) + shards, (vector_slots, qkv_slots) + tuple(slots_hbm), own_sem, send_sem, recv_sem
    )
    work.step(0)

    @pl.when(s == 0)
    def _():
        prev.start()
        for r in range(rows):
            x[r, 0:TILE] = jnp.zeros((TILE, width), x.dtype)

    load.wait()
    ready = work.lags[3]
    for t in range(1, ready + 1):
        work.step(t)
    first, second = spread_vectors(vector_slots, size, fc_size, width)
    vectors[0:8], vectors[8:16] = first, second

    @pl.when(s == 1)
    def _():
        prev.wait_recv()

    def norm_step(n, carry):
        r, t = n // (local // TILE + 1), lax.rem(n, local // TILE + 1)
        span = pl.ds(pl.multiple_of(t * TILE, TILE), TILE)
        normal, _ = normalize(x[r, span].astype(jnp.float32))
        normed[r, span] = (normal * vectors[0:1] + vectors[1:2]).astype(jnp.bfloat16)
        return carry

    lax.fori_loop(0, rows * (local // TILE + 1), norm_step, 0)
    stores = []

    def store(src, dst):
        copy = pltpu.make_async_copy(src, dst, out_sem.at[len(stores)])
        copy.start()
        stores.append(copy)

    store(normed, normed_hbm)
    for third in range(3):
        work.step(ready + 1 + third)
        columns = slice(third * width, (third + 1) * width)
        join_rows(weight, qkv_slots, columns)

        def row_step(r, carry):
            if third == 0:
                value = dot_nn(normed[r, TILE:], weight[:, columns]) + vectors[2:3]
                q[r] = value.astype(jnp.bfloat16) * jnp.bfloat16(1.0 / math.sqrt(HD))
            elif third == 1:
                k[r] = dot_nn(normed[r], weight[:, columns]).astype(jnp.bfloat16)
            else:
                v[r] = (dot_nn(normed[r], weight[:, columns]) + vectors[3:4]).astype(jnp.bfloat16)
            return carry

        lax.fori_loop(0, rows, row_step, 0)
        store((q, k, v)[third], (q_hbm, k_hbm, v_hbm)[third])
    store(weight, weight_hbm)
    for r in range(rows):
        mask_columns(starts_ref, r, q_cols.at[r], k_cols.at[r])
    lane = lane_index(TILE)
    causal = lax.broadcasted_iota(jnp.int32, (TILE, TILE), 1) <= lax.broadcasted_iota(
        jnp.int32, (TILE, TILE), 0
    )
    ones = jnp.ones((TILE, PAIR), jnp.bfloat16)
    pairs = width // PAIR
    done = ready + 4

    def probs_copy(slot, r, j):
        return pltpu.make_async_copy(probs.at[slot], probs_hbm.at[r, j], probs_sem.at[slot])

    def attend_step(n, carry):
        r, j = n // pairs, lax.rem(n, pairs)
        slot = lax.rem(n, 2)
        pair = pl.ds(pl.multiple_of(j * PAIR, PAIR), PAIR)
        for i, t in enumerate(range(done, work.steps)):

            @pl.when(n == 2 * i + 1)
            def _():
                work.step(t)

        @pl.when(n >= 2)
        def _():
            probs_copy(slot, r, j).wait()

        for tile in range(2):
            span = pl.ds(tile * TILE, TILE)
            queries = q[r, span, pair]
            around = [pl.ds((tile + w) * TILE, TILE) for w in range(2)]
            keys = [
                jnp.concatenate([k[r, around[w], pair], k_cols[r, tile, w]], axis=1) for w in range(2)
            ]
            values = [jnp.concatenate([v[r, around[w], pair], ones], axis=1) for w in range(2)]
            mixed, shares = [], []
            for head in range(2):
                mine = (lane < HD) if head == 0 else (lane >= HD)
                left = jnp.concatenate(
                    [jnp.where(mine, queries, jnp.bfloat16(0)), q_cols[r, tile]], axis=1
                )
                far = dot_nt(left, keys[0])
                near = jnp.where(causal, dot_nt(left, keys[1]), -FIRM)
                top = jnp.max(jnp.maximum(far, near), axis=-1, keepdims=True)
                far = jnp.exp(far - top).astype(jnp.bfloat16)
                near = jnp.exp(near - top).astype(jnp.bfloat16)
                probs[slot, tile, head, 0] = far
                probs[slot, tile, head, 1] = near
                total = dot_nn(far, values[0]) + dot_nn(near, values[1])
                share = 1.0 / total[:, PAIR:]
                mixed.append(total[:, :PAIR] * share)
                shares.append(share)
            att[r, span, pair] = jnp.where(lane < HD, mixed[0], mixed[1]).astype(jnp.bfloat16)
            inverse[r, span, pair] = jnp.where(lane < HD, shares[0], shares[1])
        probs_copy(slot, r, j).start()
        return carry

    steps = rows * pairs
    lax.fori_loop(0, steps, attend_step, 0)
    store(att, att_hbm)
    store(inverse, inverse_hbm)
    for t in range(done + steps // 2, work.steps):
        work.step(t)
    work.end()
    for n in range(2):
        probs_copy(n, 0, n).wait()
    for copy in stores:
        copy.wait()

    @pl.when(s == 0)
    def _():
        prev.wait_send()


def forward(outer, tokens, starts, vectors, weights):
    rows, local, width = tokens.shape
    devices = outer * 8
    low, full = jnp.bfloat16, jnp.float32
    pairs = width // PAIR
    pieces = [(0, 0, PAIR, 0)]
    pieces += [(1, i * width, width, (i + 1) % 2) for i in range(3)]
    for i, weight in enumerate(weights[1:]):
        parts = max(weight.shape[0] * weight.shape[1] // (weights[0].shape[0] * width), 1)
        parts = min(parts, weight.shape[1] // PAIR)
        while weight.shape[1] % (parts * PAIR):
            parts -= 1
        step = weight.shape[1] // parts
        pieces += [(2 + i, j * step, step, (len(pieces) + j) % 2) for j in range(parts)]
    anywhere = pl.BlockSpec(memory_space=pl.ANY)
    vmem = pl.BlockSpec(memory_space=pltpu.VMEM)
    extended = (rows, local + TILE, width)
    qkv = (devices * weights[0].shape[0], weights[0].shape[1])
    slots = [(outer, 2, 2, 2) + weight.shape for weight in weights]
    results = pl.pallas_call(
        functools.partial(forward_kernel, outer, pieces),
        in_specs=[anywhere, pl.BlockSpec(memory_space=pltpu.SMEM)] + [vmem] * (VECTORS + 4),
        out_specs=[anywhere] * 11 + [vmem],
        out_shape=[
            jax.ShapeDtypeStruct(extended, low),
            jax.ShapeDtypeStruct(tokens.shape, low),
            jax.ShapeDtypeStruct(extended, low),
            jax.ShapeDtypeStruct(extended, low),
            jax.ShapeDtypeStruct((rows, pairs, 2, 2, 2, TILE, TILE), low),
            jax.ShapeDtypeStruct(tokens.shape, low),
            jax.ShapeDtypeStruct(tokens.shape, full),
            jax.ShapeDtypeStruct(qkv, low),
        ]
        + [jax.ShapeDtypeStruct(slot, low) for slot in slots[1:]]
        + [jax.ShapeDtypeStruct((16, width), full)],
        scratch_shapes=[
            pltpu.VMEM((16, PAIR), full),
            pltpu.VMEM((outer, 2, 2, 2, 16, PAIR), full),
            pltpu.VMEM(slots[0], low),
            pltpu.VMEM(qkv, low),
            pltpu.VMEM(extended, low),
            pltpu.VMEM(extended, low),
            pltpu.VMEM(tokens.shape, low),
            pltpu.VMEM(extended, low),
            pltpu.VMEM(extended, low),
            pltpu.VMEM((2, 2, 2, 2, TILE, TILE), low),
            pltpu.VMEM(tokens.shape, low),
            pltpu.VMEM(tokens.shape, full),
            pltpu.VMEM((rows, 2, TILE, PAIR), low),
            pltpu.VMEM((rows, 2, 2, TILE, PAIR), low),
            pltpu.SemaphoreType.DMA((3,)),
            pltpu.SemaphoreType.DMA((8,)),
            pltpu.SemaphoreType.DMA((2,)),
        ]
        + Gather.semaphores(outer, 5, len(pieces)),
        compiler_params=pltpu.CompilerParams(
            collective_id=2, has_side_effects=True, vmem_limit_bytes=VMEM_LIMIT
        ),
    )(tokens, starts, *[vector.reshape(1, -1) for vector in vectors], *weights)
    normed, q, k, v, probs, att, inverse, weight, *slots, whole_vectors = results
    whole = [weight] + [
        slot.reshape(devices * w.shape[0], w.shape[1]) for slot, w in zip(slots, weights[1:])
    ]
    return whole, whole_vectors, normed, q, k, v, probs, att, inverse


def gather_weights(outer, weights, vectors, fc_bias):
    devices = outer * 8
    shards = [pack_vectors(vectors + [fc_bias])]
    shards += [w.reshape(pack_shape(w.shape)) for w in weights]
    full = gather_all(outer, shards, cut([shard.shape for shard in shards]))
    packed = full[0].reshape(devices, -1)
    count, size = len(vectors), vectors[0].shape[0]
    first = packed[:, : count * size].reshape(devices, count, size)
    first = jnp.swapaxes(first, 0, 1).reshape(count, devices * size)
    second = packed[:, count * size : count * size + fc_bias.shape[0]].reshape(-1, devices * size)
    whole = [f.reshape(devices * w.shape[0], w.shape[1]) for f, w in zip(full[1:], weights)]
    return whole, jnp.concatenate([first, second], axis=0)


def scatter_grads(outer, weight_terms, vector_terms, fc_bias_term):
    devices = outer * 8
    count, width = vector_terms.shape
    first = jnp.swapaxes(vector_terms.reshape(count, devices, width // devices), 0, 1)
    first = first.reshape(devices, -1)
    second = fc_bias_term.reshape(devices, -1)
    packed = pack_vectors([first, second])
    terms = [packed.reshape((outer, 2, 2, 2) + packed.shape[1:])]
    shapes = [(term.shape[0] // devices, term.shape[1]) for term in weight_terms]
    for term, shape in zip(weight_terms, shapes):
        terms.append(term.reshape((outer, 2, 2, 2) + pack_shape(shape)))
    shares = scatter_all(outer, terms, cut([term.shape[-2:] for term in terms]))
    flat = shares[0].reshape(-1)
    size = width // devices
    vectors = [flat[i * size : (i + 1) * size] for i in range(count)]
    fc_bias = flat[count * size : count * size + second.shape[1]]
    return [share.reshape(shape) for share, shape in zip(shares[1:], shapes)], vectors, fc_bias


def shards(
    tokens_in,
    doc_starts,
    norm1_gain,
    norm1_bias,
    qkv_weight,
    query_bias,
    value_bias,
    attn_weight,
    attn_bias,
    norm2_gain,
    norm2_bias,
    fc_weight,
    fc_bias,
    proj_weight,
    proj_bias,
    out_grad,
):
    outer = lax.axis_size("batch") // 4
    rows, local, width = tokens_in.shape
    seq = lax.axis_index("seq")
    first = 2 * seq
    padded = jnp.pad(doc_starts, ((0, 0), (1, 0)))
    starts = lax.dynamic_slice_in_dim(padded, first, 3, 1)
    starts = starts - TILE * (first - 1 + jnp.arange(3, dtype=jnp.int32))
    weights = [qkv_weight, attn_weight, fc_weight, proj_weight]
    vectors = [norm1_gain, norm1_bias, query_bias, value_bias, attn_bias, norm2_gain, norm2_bias, proj_bias]
    if qkv_weight.shape[0] % 8 == 0:
        (qkv, attn, fc, proj), vectors, normed, q, k, v, probs, att, inverse = forward(
            outer, tokens_in, starts, vectors + [fc_bias], weights
        )
    else:
        prev = lax.ppermute(tokens_in[:, local - TILE :], "seq", [(0, 1)])
        (qkv, attn, fc, proj), vectors = gather_weights(outer, weights, vectors, fc_bias)
        normed, q, k, v = project(tokens_in, prev, qkv, vectors)
        probs, att, inverse = attend(starts, q, k, v)
    flat = lambda value: value.reshape(rows * local, width)
    out, middle_grad, att_grad, attn_grad, fc_grad, proj_grad, mlp_sums = mlp(
        flat(tokens_in), flat(att), flat(out_grad), attn, fc, proj, vectors
    )
    block = lambda value: value.reshape(rows, local, width)
    dq, dk, dv = attend_grad(probs, q, k, v, block(att_grad), att, inverse)
    qkv_grad, prev_grad, project_sums = project_grad(normed, dq, dk, dv, qkv)
    late = lax.ppermute(prev_grad, "seq", [(1, 0)])
    tokens_grad, norm_sums = tokens_grad_of(
        tokens_in, dq, dk, dv, qkv, late, block(middle_grad), vectors
    )
    sums = jnp.concatenate([norm_sums[:2], project_sums[:2], mlp_sums[:4]], axis=0)
    weights, shares, fc_share = scatter_grads(
        outer, [qkv_grad, attn_grad, fc_grad, proj_grad], sums, mlp_sums[4:]
    )
    gain1, bias1, query, value, proj_b, gain2, bias2, attn_b = shares
    return (
        out.reshape(rows, local, width),
        tokens_grad,
        gain1,
        bias1,
        weights[0],
        query,
        value,
        weights[1],
        attn_b,
        gain2,
        bias2,
        weights[2],
        fc_share,
        weights[3],
        proj_b,
    )


def solution(mesh):
    return jax.shard_map(
        shards,
        mesh=mesh,
        in_specs=(
            P("batch", "seq", None),
            P("batch", None),
            P(("batch", "seq")),
            P(("batch", "seq")),
            P(("batch", "seq"), None),
            P(("batch", "seq")),
            P(("batch", "seq")),
            P(("batch", "seq"), None),
            P(("batch", "seq")),
            P(("batch", "seq")),
            P(("batch", "seq")),
            P(("batch", "seq"), None),
            P(("batch", "seq")),
            P(("batch", "seq"), None),
            P(("batch", "seq")),
            P("batch", "seq", None),
        ),
        out_specs=(
            P("batch", "seq", None),
            P("batch", "seq", None),
            P(("batch", "seq")),
            P(("batch", "seq")),
            P(("batch", "seq"), None),
            P(("batch", "seq")),
            P(("batch", "seq")),
            P(("batch", "seq"), None),
            P(("batch", "seq")),
            P(("batch", "seq")),
            P(("batch", "seq")),
            P(("batch", "seq"), None),
            P(("batch", "seq")),
            P(("batch", "seq"), None),
            P(("batch", "seq")),
        ),
        check_vma=False,
    )
```

```python
import functools
import math

import jax
import jax.numpy as jnp
from jax import lax
from jax.experimental import pallas as pl
from jax.experimental.pallas import tpu as pltpu
from jax.sharding import PartitionSpec as P

HD = 64
EPSILON = 1e-05
GELU_SCALE = 0.7978845608028654
MESH_ID = pl.DeviceIdType.MESH
VMEM_LIMIT = 60 * 2**20
EVERY = slice(None)


def place():
    batch, seq = lax.axis_index("batch"), lax.axis_index("seq")
    return (batch // 4, (batch // 2) % 2, batch % 2, seq)


def device(a, y, c, s):
    return (a * 4 + y * 2 + c, s)


def greet(outer):
    a, y, c, s = place()
    barrier = pltpu.get_barrier_semaphore()
    others = [device(lax.rem(a + k, outer), y, c, s) for k in range(1, outer)]
    others += [device(a, 1 - y, c, s), device(a, y, c, 1 - s), device(a, y, 1 - c, s)]
    for other in others:
        pl.semaphore_signal(barrier, inc=1, device_id=other, device_id_type=MESH_ID)
    pl.semaphore_wait(barrier, len(others))


def remote(src, dst, send_sem, recv_sem, other):
    return pltpu.make_async_remote_copy(
        src_ref=src,
        dst_ref=dst,
        send_sem=send_sem,
        recv_sem=recv_sem,
        device_id=other,
        device_id_type=MESH_ID,
    )


class Gather:
    lags, ahead = (1, 2, 4, 6), 2

    def __init__(self, outer, pieces, shards, outs, own_sem, send_sem, recv_sem):
        self.outer, self.pieces, self.shards, self.outs = outer, pieces, shards, outs
        self.own_sem, self.send_sem, self.recv_sem = own_sem, send_sem, recv_sem
        self.steps = len(pieces) + self.lags[3]
        self.place = place()

    def sems(self, p, k):
        return self.send_sem.at[p, k], self.recv_sem.at[p, k]

    def own(self, i):
        return pltpu.make_async_copy(
            self.shards[i], self.outs[i].at[self.place], self.own_sem.at[i]
        )

    def first(self, p, k):
        i, start, width, order = self.pieces[p]
        a, y, c, s = self.place
        columns = pl.ds(start, width)
        src = self.shards[i].at[:, columns]
        dst = self.outs[i].at[a, y, c, s, :, columns]
        if k == 0:
            return remote(src, dst, *self.sems(p, 0), self.near(order))
        return remote(src, dst, *self.sems(p, k), device(lax.rem(a + k, self.outer), y, c, s))

    def near(self, order):
        a, y, c, s = self.place
        return device(a, 1 - y, c, s) if order == 0 else device(a, y, c, 1 - s)

    def second(self, p, k):
        i, start, width, order = self.pieces[p]
        a, y, c, s = self.place
        source = lax.rem(a + self.outer - k, self.outer)
        block = self.outs[i].at[source, y, c, s, :, pl.ds(start, width)]
        return remote(block, block, *self.sems(p, self.outer - 1 + k), self.near(order))

    def third(self, p):
        i, start, width, order = self.pieces[p]
        a, y, c, s = self.place
        index = (EVERY, EVERY, c, s) if order == 0 else (EVERY, y, c, EVERY)
        block = self.outs[i].at[index + (EVERY, pl.ds(start, width))]
        return remote(block, block, *self.sems(p, 2 * self.outer - 1), self.near(1 - order))

    def fourth(self, p):
        i, start, width, order = self.pieces[p]
        a, y, c, s = self.place
        block = self.outs[i].at[EVERY, EVERY, c, EVERY, EVERY, pl.ds(start, width)]
        return remote(block, block, *self.sems(p, 2 * self.outer), device(a, y, 1 - c, s))

    def step(self, t):
        outer, count, lags = self.outer, len(self.pieces), self.lags
        for p in range(self.ahead + 1) if t == 0 else (t + self.ahead,):
            if p < count:
                for k in range(outer):
                    self.first(p, k).start()
        if t == 0:
            for i in range(len(self.shards)):
                self.own(i).start()
        p = t - lags[0]
        if 0 <= p < count:
            for k in range(1, outer):
                self.first(p, k).wait_recv()
                self.second(p, k).start()
        p = t - lags[1]
        if 0 <= p < count:
            if p == 0:
                for i in range(len(self.shards)):
                    self.own(i).wait()
            self.first(p, 0).wait_recv()
            for k in range(1, outer):
                self.second(p, k).wait_recv()
            self.third(p).start()
        p = t - lags[2]
        if 0 <= p < count:
            self.third(p).wait_recv()
            self.fourth(p).start()
        p = t - lags[3]
        if 0 <= p < count:
            self.fourth(p).wait_recv()

    def end(self):
        for p in range(len(self.pieces)):
            for k in range(self.outer):
                self.first(p, k).wait_send()
            for k in range(1, self.outer):
                self.second(p, k).wait_send()
            self.third(p).wait_send()
            self.fourth(p).wait_send()

    @staticmethod
    def semaphores(outer, arrays, pieces):
        return [
            pltpu.SemaphoreType.DMA((arrays,)),
            pltpu.SemaphoreType.DMA((pieces, 2 * outer + 1)),
            pltpu.SemaphoreType.DMA((pieces, 2 * outer + 1)),
        ]


def add_slots(target, other):
    lead = target.shape[:-2]

    def body(k, carry):
        index = []
        for size in reversed(lead):
            index.append(lax.rem(k, size))
            k = k // size
        index = tuple(reversed(index))
        value = target[index].astype(jnp.float32) + other[index].astype(jnp.float32)
        target[index] = value.astype(target.dtype)
        return carry

    lax.fori_loop(0, math.prod(lead), body, 0)


class Scatter:
    def __init__(self, outer, pieces, terms, outs, slots, own_sem, send_sem, recv_sem, times=None, places=None):
        self.outer, self.pieces, self.terms, self.outs = outer, pieces, terms, outs
        n = len(pieces)
        self.held, self.got = slots[:n], [slots[k * n : (k + 1) * n] for k in range(1, 5)]
        self.own_sem, self.send_sem, self.recv_sem = own_sem, send_sem, recv_sem
        self.times = times or [(p, p + 1, p + 3, p + 4, p + 5) for p in range(n)]
        self.places = places or {}
        self.steps = max(time[4] for time in self.times) + 1
        self.place = place()

    def sems(self, p, k):
        return self.send_sem.at[p, k], self.recv_sem.at[p, k]

    def own(self, p):
        i, start, width, order = self.pieces[p]
        a, y, c, s = self.place
        block = self.terms[i].at[EVERY, EVERY, c, EVERY, EVERY, pl.ds(start, width)]
        return pltpu.make_async_copy(block, self.held[p], self.own_sem.at[p])

    def first(self, p):
        i, start, width, order = self.pieces[p]
        a, y, c, s = self.place
        block = self.terms[i].at[EVERY, EVERY, 1 - c, EVERY, EVERY, pl.ds(start, width)]
        return remote(block, self.got[0][p], *self.sems(p, 0), device(a, y, 1 - c, s))

    def second(self, p):
        a, y, c, s = self.place
        if self.pieces[p][3] == 0:
            src, other = self.held[p].at[:, :, 1 - s], device(a, y, c, 1 - s)
        else:
            src, other = self.held[p].at[:, 1 - y], device(a, 1 - y, c, s)
        return remote(src, self.got[1][p], *self.sems(p, 1), other)

    def third(self, p):
        a, y, c, s = self.place
        if self.pieces[p][3] == 0:
            src, other = self.held[p].at[:, 1 - y, s], device(a, 1 - y, c, s)
        else:
            src, other = self.held[p].at[:, y, 1 - s], device(a, y, c, 1 - s)
        return remote(src, self.got[2][p], *self.sems(p, 2), other)

    def fourth(self, p, k):
        a, y, c, s = self.place
        to = lax.rem(a + k, self.outer)
        src = self.held[p].at[to, y, s]
        return remote(src, self.got[3][p].at[k - 1], *self.sems(p, 2 + k), device(to, y, c, s))

    def step(self, t):
        outer = self.outer
        a, y, c, s = self.place
        for p, times in enumerate(self.times):
            if t == times[4]:
                i, start, width, order = self.pieces[p]
                value = self.held[p][a, y, s].astype(jnp.float32)
                for k in range(1, outer):
                    self.fourth(p, k).wait_recv()
                    value = value + self.got[3][p][k - 1].astype(jnp.float32)
                for offset, size, to in self.places.get(p, [(0, width, start)]):
                    self.outs[i][:, to : to + size] = value[:, offset : offset + size]
            if t == times[3]:
                self.third(p).wait_recv()
                add_slots(self.held[p].at[:, y, s], self.got[2][p])
                for k in range(1, outer):
                    self.fourth(p, k).start()
            if t == times[2]:
                self.second(p).wait_recv()
                mine = (EVERY, EVERY, s) if self.pieces[p][3] == 0 else (EVERY, y)
                add_slots(self.held[p].at[mine], self.got[1][p])
                self.third(p).start()
            if t == times[1]:
                self.own(p).wait()
                self.first(p).wait_recv()
                add_slots(self.held[p], self.got[0][p])
                self.second(p).start()
            if t == times[0]:
                self.own(p).start()
                self.first(p).start()

    def end(self):
        for p in range(len(self.pieces)):
            self.first(p).wait_send()
            self.second(p).wait_send()
            self.third(p).wait_send()
            for k in range(1, self.outer):
                self.fourth(p, k).wait_send()

    @staticmethod
    def scratch(outer, shapes, pieces):
        def slot(p, *lead):
            i, start, width, order = pieces[p]
            return pltpu.VMEM(lead + (shapes[i][0], width), shapes[i][2])

        n = range(len(pieces))
        leads = ((outer, 2, 2), (outer, 2, 2), (outer, 2), (outer,), (max(outer - 1, 1),))
        return [slot(p, *lead) for lead in leads for p in n] + [
            pltpu.SemaphoreType.DMA((len(pieces),)),
            pltpu.SemaphoreType.DMA((len(pieces), outer + 2)),
            pltpu.SemaphoreType.DMA((len(pieces), outer + 2)),
        ]


def gather_kernel(outer, pieces, count, *refs):
    greet(outer)
    work = Gather(outer, pieces, refs[:count], refs[count : 2 * count], *refs[2 * count :])
    for t in range(work.steps):
        work.step(t)
    work.end()


def gather_all(outer, shards, pieces):
    count = len(shards)
    return pl.pallas_call(
        functools.partial(gather_kernel, outer, pieces, count),
        out_shape=[
            jax.ShapeDtypeStruct((outer, 2, 2, 2) + shard.shape, shard.dtype) for shard in shards
        ],
        in_specs=[pl.BlockSpec(memory_space=pltpu.VMEM)] * count,
        out_specs=[pl.BlockSpec(memory_space=pl.ANY)] * count,
        scratch_shapes=Gather.semaphores(outer, count, len(pieces)),
        compiler_params=pltpu.CompilerParams(
            collective_id=0, has_side_effects=True, vmem_limit_bytes=VMEM_LIMIT
        ),
    )(*shards)


def scatter_kernel(outer, pieces, count, *refs):
    greet(outer)
    rest = refs[2 * count :]
    work = Scatter(outer, pieces, refs[:count], refs[count : 2 * count], rest[:-3], *rest[-3:])
    for t in range(work.steps):
        work.step(t)
    work.end()


def scatter_all(outer, terms, pieces):
    count = len(terms)
    shapes = [term.shape[-2:] + (term.dtype,) for term in terms]
    return pl.pallas_call(
        functools.partial(scatter_kernel, outer, pieces, count),
        out_shape=[jax.ShapeDtypeStruct(term.shape[-2:], jnp.float32) for term in terms],
        in_specs=[pl.BlockSpec(memory_space=pl.ANY)] * count,
        out_specs=[pl.BlockSpec(memory_space=pltpu.VMEM)] * count,
        scratch_shapes=Scatter.scratch(outer, shapes, pieces),
        compiler_params=pltpu.CompilerParams(
            collective_id=1, has_side_effects=True, vmem_limit_bytes=VMEM_LIMIT
        ),
    )(*terms)


def cut(shape_list):
    pieces = []
    for i, (rows, columns) in enumerate(shape_list):
        parts, blocks = 1, columns // 128
        if rows % 8 == 0:
            fits = [k for k in range(1, blocks + 1) if blocks % k == 0 and rows * columns // k <= 25000]
            parts = min(fits) if fits else 1
        width = columns // parts
        for k in range(parts):
            pieces.append((i, k * width, width, len(pieces) % 2))
    return pieces


def pack_shape(shape):
    rows, columns = shape
    return shape if rows % 8 == 0 else (rows * columns // 128, 128)


def pack_vectors(parts):
    joined = jnp.concatenate([part.astype(jnp.float32) for part in parts], axis=-1)
    size = -(-joined.shape[-1] // 1024) * 1024
    pad = [(0, 0)] * (joined.ndim - 1) + [(0, size - joined.shape[-1])]
    return jnp.pad(joined, pad).reshape(joined.shape[:-1] + (size // 128, 128))


TILE = 256
PAIR = 128
FIRM = 1e30


def dot_nn(left, right):
    return lax.dot_general(left, right, (((1,), (0,)), ((), ())), preferred_element_type=jnp.float32)


def dot_nt(left, right):
    return lax.dot_general(left, right, (((1,), (1,)), ((), ())), preferred_element_type=jnp.float32)


def dot_tn(left, right):
    return lax.dot_general(left, right, (((0,), (0,)), ((), ())), preferred_element_type=jnp.float32)


def normalize(values):
    average = jnp.mean(values, axis=-1, keepdims=True)
    centered = values - average
    variance = jnp.mean(centered * centered, axis=-1, keepdims=True)
    scale = lax.rsqrt(variance + EPSILON)
    return centered * scale, scale


def norm_grad(upstream, gain, normal, scale):
    inner = upstream * gain
    first = jnp.mean(inner, axis=-1, keepdims=True)
    second = jnp.mean(inner * normal, axis=-1, keepdims=True)
    return scale * (inner - first - normal * second)


def column_sum(values):
    return jnp.sum(values, axis=0, keepdims=True)


def project_kernel(x_ref, prev_ref, weight_ref, vectors_ref, normed_ref, q_ref, k_ref, v_ref):
    tile = pl.program_id(1)
    width = x_ref.shape[-1]
    x = jnp.where(tile == 0, prev_ref[0], x_ref[0]).astype(jnp.float32)
    normal, _ = normalize(x)
    normed = (normal * vectors_ref[0:1] + vectors_ref[1:2]).astype(jnp.bfloat16)
    normed_ref[0] = normed

    @pl.when(tile > 0)
    def _():
        queries = dot_nn(normed, weight_ref[:, :width]) + vectors_ref[2:3]
        q_ref[0] = queries.astype(jnp.bfloat16) * jnp.bfloat16(1.0 / math.sqrt(HD))

    k_ref[0] = dot_nn(normed, weight_ref[:, width : 2 * width]).astype(jnp.bfloat16)
    values = dot_nn(normed, weight_ref[:, 2 * width :]) + vectors_ref[3:4]
    v_ref[0] = values.astype(jnp.bfloat16)


def project(tokens, prev, weight, vectors):
    rows, local, width = tokens.shape
    tiles = local // TILE
    here = lambda r, t: (r, jnp.maximum(t - 1, 0), 0)
    extended = jax.ShapeDtypeStruct((rows, local + TILE, width), jnp.bfloat16)
    return pl.pallas_call(
        project_kernel,
        grid=(rows, tiles + 1),
        in_specs=[
            pl.BlockSpec((1, TILE, width), here),
            pl.BlockSpec((1, TILE, width), lambda r, t: (r, 0, 0)),
            pl.BlockSpec(weight.shape, lambda r, t: (0, 0)),
            pl.BlockSpec(vectors.shape, lambda r, t: (0, 0)),
        ],
        out_specs=[
            pl.BlockSpec((1, TILE, width), lambda r, t: (r, t, 0)),
            pl.BlockSpec((1, TILE, width), here),
            pl.BlockSpec((1, TILE, width), lambda r, t: (r, t, 0)),
            pl.BlockSpec((1, TILE, width), lambda r, t: (r, t, 0)),
        ],
        out_shape=[extended, jax.ShapeDtypeStruct(tokens.shape, jnp.bfloat16), extended, extended],
        compiler_params=pltpu.CompilerParams(vmem_limit_bytes=VMEM_LIMIT),
    )(tokens, prev, weight, vectors)


def lane_index(rows):
    return lax.broadcasted_iota(jnp.int32, (rows, PAIR), 1)


def mask_columns(starts_ref, row, q_cols, k_cols):
    place = lax.broadcasted_iota(jnp.int32, (TILE, PAIR), 0)
    lane = lane_index(TILE)
    for tile in range(2):
        before, start = starts_ref[row, tile], starts_ref[row, tile + 1]
        late = jnp.where(place >= start, 1.0, 0.0)
        q_cols[tile] = jnp.where(lane == 0, late, jnp.where(lane == 1, 1.0, 0.0)).astype(jnp.bfloat16)
        early = jnp.where(place < before, -FIRM, 0.0)
        k_cols[tile, 0] = jnp.where(
            lane == 0, -FIRM, jnp.where(lane == 1, early, 0.0)
        ).astype(jnp.bfloat16)
        early = jnp.where(place < start, -FIRM, 0.0)
        k_cols[tile, 1] = jnp.where(lane == 0, early, 0.0).astype(jnp.bfloat16)


def attend_kernel(starts_ref, q_ref, k_ref, v_ref, probs_ref, out_ref, inverse_ref, q_cols, k_cols):
    row = pl.program_id(0)

    @pl.when(pl.program_id(1) == 0)
    def _():
        mask_columns(starts_ref, row, q_cols, k_cols)

    lane = lane_index(TILE)
    causal = lax.broadcasted_iota(jnp.int32, (TILE, TILE), 1) <= lax.broadcasted_iota(
        jnp.int32, (TILE, TILE), 0
    )
    ones = jnp.ones((TILE, PAIR), jnp.bfloat16)
    for tile in range(2):
        queries = q_ref[0, pl.ds(tile * TILE, TILE)]
        keys = [
            jnp.concatenate([k_ref[0, pl.ds((tile + w) * TILE, TILE)], k_cols[tile, w]], axis=1)
            for w in range(2)
        ]
        values = [
            jnp.concatenate([v_ref[0, pl.ds((tile + w) * TILE, TILE)], ones], axis=1)
            for w in range(2)
        ]
        mixed, inverse = [], []
        for head in range(2):
            mine = (lane < HD) if head == 0 else (lane >= HD)
            left = jnp.concatenate([jnp.where(mine, queries, jnp.bfloat16(0)), q_cols[tile]], axis=1)
            far = dot_nt(left, keys[0])
            near = jnp.where(causal, dot_nt(left, keys[1]), -FIRM)
            top = jnp.max(jnp.maximum(far, near), axis=-1, keepdims=True)
            far = jnp.exp(far - top).astype(jnp.bfloat16)
            near = jnp.exp(near - top).astype(jnp.bfloat16)
            probs_ref[0, 0, tile, head, 0] = far
            probs_ref[0, 0, tile, head, 1] = near
            total = dot_nn(far, values[0]) + dot_nn(near, values[1])
            share = 1.0 / total[:, PAIR:]
            mixed.append(total[:, :PAIR] * share)
            inverse.append(share)
        out_ref[0, pl.ds(tile * TILE, TILE)] = jnp.where(lane < HD, mixed[0], mixed[1]).astype(
            jnp.bfloat16
        )
        inverse_ref[0, pl.ds(tile * TILE, TILE)] = jnp.where(lane < HD, inverse[0], inverse[1])


def attend(starts, q, k, v):
    rows, local, width = q.shape
    pairs = width // PAIR
    by_pair = lambda r, j: (r, 0, j)
    return pl.pallas_call(
        attend_kernel,
        grid=(rows, pairs),
        in_specs=[
            pl.BlockSpec(memory_space=pltpu.SMEM),
            pl.BlockSpec((1, local, PAIR), by_pair),
            pl.BlockSpec((1, local + TILE, PAIR), by_pair),
            pl.BlockSpec((1, local + TILE, PAIR), by_pair),
        ],
        out_specs=[
            pl.BlockSpec((1, 1, 2, 2, 2, TILE, TILE), lambda r, j: (r, j, 0, 0, 0, 0, 0)),
            pl.BlockSpec((1, local, PAIR), by_pair),
            pl.BlockSpec((1, local, PAIR), by_pair),
        ],
        out_shape=[
            jax.ShapeDtypeStruct((rows, pairs, 2, 2, 2, TILE, TILE), jnp.bfloat16),
            jax.ShapeDtypeStruct((rows, local, width), jnp.bfloat16),
            jax.ShapeDtypeStruct((rows, local, width), jnp.float32),
        ],
        scratch_shapes=[
            pltpu.VMEM((2, TILE, PAIR), jnp.bfloat16),
            pltpu.VMEM((2, 2, TILE, PAIR), jnp.bfloat16),
        ],
        compiler_params=pltpu.CompilerParams(vmem_limit_bytes=VMEM_LIMIT),
    )(starts, q, k, v)


def attend_grad_kernel(
    probs_ref, q_ref, k_ref, v_ref, grad_ref, out_ref, inverse_ref, dq_ref, dk_ref, dv_ref, dk_sum, dv_sum
):
    lane = lane_index(TILE)
    ones = jnp.ones((TILE, PAIR), jnp.bfloat16)
    for tile in range(2):
        span = pl.ds(tile * TILE, TILE)
        queries = q_ref[0, span]
        scaled = (grad_ref[0, span].astype(jnp.float32) * inverse_ref[0, span]).astype(jnp.bfloat16)
        product = scaled.astype(jnp.float32) * out_ref[0, span].astype(jnp.float32)
        d_queries = []
        for head in range(2):
            mine = (lane < HD) if head == 0 else (lane >= HD)
            delta = -jnp.sum(jnp.where(mine, product, 0.0), axis=-1, keepdims=True)
            high = delta.astype(jnp.bfloat16).astype(jnp.float32)
            extra = jnp.where(lane == 0, high, jnp.where(lane == 1, delta - high, 0.0))
            grads = jnp.where(mine, scaled, jnp.bfloat16(0))
            mine_queries = jnp.where(mine, queries, jnp.bfloat16(0))
            left = jnp.concatenate([grads, extra.astype(jnp.bfloat16)], axis=1)
            d_query = None
            for w in range(2):
                at = pl.ds((tile + w) * TILE, TILE)
                right = jnp.concatenate([v_ref[0, at], ones], axis=1)
                probs = probs_ref[0, 0, tile, head, w]
                d_score = (probs.astype(jnp.float32) * dot_nt(left, right)).astype(jnp.bfloat16)
                part = dot_nn(d_score, k_ref[0, at])
                d_query = part if w == 0 else d_query + part
                d_key = dot_tn(d_score, mine_queries)
                d_value = dot_tn(probs, grads)
                if head == 0 and (w == 1 or tile == 0):
                    dk_sum[at] = d_key
                    dv_sum[at] = d_value
                else:
                    dk_sum[at] += d_key
                    dv_sum[at] += d_value
            d_queries.append(d_query)
        dq = jnp.where(lane < HD, d_queries[0], d_queries[1]) * (1.0 / math.sqrt(HD))
        dq_ref[0, span] = dq.astype(jnp.bfloat16)
    dk_ref[0] = dk_sum[...].astype(jnp.bfloat16)
    dv_ref[0] = dv_sum[...].astype(jnp.bfloat16)


def attend_grad(probs, q, k, v, grad, out, inverse):
    rows, local, width = q.shape
    pairs = width // PAIR
    by_pair = lambda r, j: (r, 0, j)
    small = pl.BlockSpec((1, local, PAIR), by_pair)
    large = pl.BlockSpec((1, local + TILE, PAIR), by_pair)
    return pl.pallas_call(
        attend_grad_kernel,
        grid=(rows, pairs),
        in_specs=[
            pl.BlockSpec((1, 1, 2, 2, 2, TILE, TILE), lambda r, j: (r, j, 0, 0, 0, 0, 0)),
            small,
            large,
            large,
            small,
            small,
            small,
        ],
        out_specs=[small, large, large],
        out_shape=[
            jax.ShapeDtypeStruct(q.shape, jnp.bfloat16),
            jax.ShapeDtypeStruct(k.shape, jnp.bfloat16),
            jax.ShapeDtypeStruct(k.shape, jnp.bfloat16),
        ],
        scratch_shapes=[
            pltpu.VMEM((local + TILE, PAIR), jnp.float32),
            pltpu.VMEM((local + TILE, PAIR), jnp.float32),
        ],
        compiler_params=pltpu.CompilerParams(vmem_limit_bytes=VMEM_LIMIT),
    )(probs, q, k, v, grad, out, inverse)


def gelu_pair(v):
    square = v * v
    half = 0.5 + 0.5 * jnp.tanh(v * (GELU_SCALE + (GELU_SCALE * 0.044715) * square))
    hidden = v * half
    slope = half + hidden * (1.0 - half) * (2.0 * GELU_SCALE + (6.0 * GELU_SCALE * 0.044715) * square)
    return hidden, slope


MLP_TILE = 256
CHUNK = 768


def mlp_kernel(
    x_hbm, att_hbm, dy_hbm, attn_hbm, fc_hbm, proj_hbm, vectors,
    out_hbm, middle_grad_hbm, att_grad_hbm, attn_grad_hbm, fc_grad_hbm, proj_grad_hbm, sums_ref,
    x, att, dy, attn, fc, proj, hidden, pre_grad, normed, branch, out, middle_grad, att_grad,
    attn_grad, fc_grad, proj_grad, in_sem, out_sem,
):
    tokens, width = x.shape
    chunks = fc.shape[1] // CHUNK
    tiles = tokens // MLP_TILE
    loads = [
        pltpu.make_async_copy(src, dst, in_sem.at[i])
        for i, (src, dst) in enumerate(
            ((att_hbm, att), (attn_hbm, attn), (x_hbm, x), (fc_hbm, fc), (dy_hbm, dy), (proj_hbm, proj))
        )
    ]
    for load in loads:
        load.start()
    sums_ref[...] = jnp.zeros_like(sums_ref)
    for load in loads[:3]:
        load.wait()

    def tile_step(t, carry):
        span = pl.ds(pl.multiple_of(t * MLP_TILE, MLP_TILE), MLP_TILE)
        middle = x[span].astype(jnp.float32) + dot_nn(att[span], attn[...]) + vectors[4:5]
        normal, scale = normalize(middle)
        low = (normal * vectors[5:6] + vectors[6:7]).astype(jnp.bfloat16)
        normed[span] = low

        @pl.when(t == 0)
        def _():
            for load in loads[3:]:
                load.wait()

        upstream = dy[span]
        result = middle + vectors[7:8]
        back = None
        for j in range(chunks):
            columns = pl.ds(j * CHUNK, CHUNK)
            pre = dot_nn(low, fc[:, columns]) + vectors[8 + j : 9 + j]
            value, slope = gelu_pair(pre)
            value = value.astype(jnp.bfloat16)
            hidden[span, columns] = value
            grad = dot_nt(upstream, proj[columns]) * slope
            grad = grad.astype(jnp.bfloat16)
            pre_grad[span, columns] = grad
            sums_ref[4 + j : 5 + j] += column_sum(grad.astype(jnp.float32))
            result = result + dot_nn(value, proj[columns])
            part = dot_nt(grad, fc[:, columns])
            back = part if back is None else back + part
        out[span] = result.astype(jnp.bfloat16)
        upstream = upstream.astype(jnp.float32)
        sums_ref[0:1] += column_sum(upstream)
        sums_ref[1:2] += column_sum(back * normal)
        sums_ref[2:3] += column_sum(back)
        total = upstream + norm_grad(back, vectors[5:6], normal, scale)
        middle_grad[span] = total
        total = total.astype(jnp.bfloat16)
        branch[span] = total
        sums_ref[3:4] += column_sum(total.astype(jnp.float32))
        att_grad[span] = dot_nt(total, attn[...]).astype(jnp.bfloat16)
        return carry

    lax.fori_loop(0, tiles, tile_step, 0)
    stores = []

    def store(src, dst):
        copy = pltpu.make_async_copy(src, dst, out_sem.at[len(stores)])
        copy.start()
        stores.append(copy)

    store(out, out_hbm)
    store(middle_grad, middle_grad_hbm)
    store(att_grad, att_grad_hbm)
    for j in range(chunks):
        columns = pl.ds(j * CHUNK, CHUNK)
        proj_grad[columns] = dot_tn(hidden[:, columns], dy[...]).astype(jnp.bfloat16)
        store(proj_grad.at[columns], proj_grad_hbm.at[columns])
    for j in range(chunks):
        columns = pl.ds(j * CHUNK, CHUNK)
        fc_grad[:, columns] = dot_tn(normed[...], pre_grad[:, columns]).astype(jnp.bfloat16)
        store(fc_grad.at[:, columns], fc_grad_hbm.at[:, columns])
    attn_grad[...] = dot_tn(att[...], branch[...]).astype(jnp.bfloat16)
    store(attn_grad, attn_grad_hbm)
    for copy in stores:
        copy.wait()


def mlp(x, att, dy, attn, fc, proj, vectors):
    tokens, width = x.shape
    hidden = fc.shape[1]
    low, full = jnp.bfloat16, jnp.float32
    anywhere = pl.BlockSpec(memory_space=pl.ANY)
    vmem = pl.BlockSpec(memory_space=pltpu.VMEM)
    return pl.pallas_call(
        mlp_kernel,
        in_specs=[anywhere] * 6 + [vmem],
        out_specs=[anywhere] * 6 + [vmem],
        out_shape=[
            jax.ShapeDtypeStruct((tokens, width), low),
            jax.ShapeDtypeStruct((tokens, width), full),
            jax.ShapeDtypeStruct((tokens, width), low),
            jax.ShapeDtypeStruct(attn.shape, low),
            jax.ShapeDtypeStruct(fc.shape, low),
            jax.ShapeDtypeStruct(proj.shape, low),
            jax.ShapeDtypeStruct((8, width), full),
        ],
        scratch_shapes=[
            pltpu.VMEM((tokens, width), low),
            pltpu.VMEM((tokens, width), low),
            pltpu.VMEM((tokens, width), low),
            pltpu.VMEM(attn.shape, low),
            pltpu.VMEM(fc.shape, low),
            pltpu.VMEM(proj.shape, low),
            pltpu.VMEM((tokens, hidden), low),
            pltpu.VMEM((tokens, hidden), low),
            pltpu.VMEM((tokens, width), low),
            pltpu.VMEM((tokens, width), low),
            pltpu.VMEM((tokens, width), low),
            pltpu.VMEM((tokens, width), full),
            pltpu.VMEM((tokens, width), low),
            pltpu.VMEM(attn.shape, low),
            pltpu.VMEM(fc.shape, low),
            pltpu.VMEM(proj.shape, low),
            pltpu.SemaphoreType.DMA((6,)),
            pltpu.SemaphoreType.DMA((12,)),
        ],
        compiler_params=pltpu.CompilerParams(vmem_limit_bytes=VMEM_LIMIT),
    )(x, att, dy, attn, fc, proj, vectors)


def project_grad_kernel(normed, dq, dk, dv, weight, weight_grad, prev_grad, sums):
    rows, extended, width = normed.shape
    local = dq.shape[1]
    third = [pl.ds(i * width, width) for i in range(3)]
    for r in range(rows):
        head = pl.ds(0, TILE)
        prev_grad[r] = (
            dot_nt(dk[r, head], weight[:, third[1]]) + dot_nt(dv[r, head], weight[:, third[2]])
        ).astype(jnp.bfloat16)
    total = None
    for i, grads in enumerate((dq, dk, dv)):
        total = None
        for r in range(rows):
            left = normed[r, TILE:] if i == 0 else normed[r]
            part = dot_tn(left, grads[r])
            total = part if total is None else total + part
        weight_grad[:, third[i]] = total.astype(jnp.bfloat16)
    sums[...] = jnp.zeros_like(sums)
    for r in range(rows):
        sums[0:1] += column_sum(dq[r].astype(jnp.float32))
        sums[1:2] += column_sum(dv[r].astype(jnp.float32))


def project_grad(normed, dq, dk, dv, weight):
    rows, extended, width = normed.shape
    vmem = pl.BlockSpec(memory_space=pltpu.VMEM)
    return pl.pallas_call(
        project_grad_kernel,
        in_specs=[vmem] * 5,
        out_specs=[vmem] * 3,
        out_shape=[
            jax.ShapeDtypeStruct(weight.shape, jnp.bfloat16),
            jax.ShapeDtypeStruct((rows, TILE, width), jnp.bfloat16),
            jax.ShapeDtypeStruct((8, width), jnp.float32),
        ],
        compiler_params=pltpu.CompilerParams(vmem_limit_bytes=VMEM_LIMIT),
    )(normed, dq, dk, dv, weight)


def tokens_grad_kernel(x_ref, dq, dk, dv, weight, late, middle_grad, vectors, out_ref, sums):
    row, tile = pl.program_id(0), pl.program_id(1)
    width = x_ref.shape[-1]

    @pl.when((row == 0) & (tile == 0))
    def _():
        sums[...] = jnp.zeros_like(sums)

    back = dot_nt(dq[0], weight[:, :width])
    back = back + dot_nt(dk[0], weight[:, width : 2 * width])
    back = back + dot_nt(dv[0], weight[:, 2 * width :])
    back = back + jnp.where(tile == pl.num_programs(1) - 1, late[0].astype(jnp.float32), 0.0)
    normal, scale = normalize(x_ref[0].astype(jnp.float32))
    sums[0:1] += column_sum(back * normal)
    sums[1:2] += column_sum(back)
    out_ref[0] = middle_grad[0] + norm_grad(back, vectors[0:1], normal, scale)


def tokens_grad_of(x, dq, dk, dv, weight, late, middle_grad, vectors):
    rows, local, width = x.shape
    block = lambda shift: pl.BlockSpec((1, TILE, width), lambda r, t: (r, t + shift, 0))
    whole = lambda v: pl.BlockSpec(v.shape, lambda r, t: (0, 0))
    return pl.pallas_call(
        tokens_grad_kernel,
        grid=(rows, local // TILE),
        in_specs=[
            block(0),
            block(0),
            block(1),
            block(1),
            whole(weight),
            pl.BlockSpec((1, TILE, width), lambda r, t: (r, 0, 0)),
            block(0),
            whole(vectors),
        ],
        out_specs=[block(0), pl.BlockSpec((8, width), lambda r, t: (0, 0))],
        out_shape=[
            jax.ShapeDtypeStruct(x.shape, jnp.float32),
            jax.ShapeDtypeStruct((8, width), jnp.float32),
        ],
        compiler_params=pltpu.CompilerParams(vmem_limit_bytes=VMEM_LIMIT),
    )(x, dq, dk, dv, weight, late, middle_grad, vectors)


def spread_vectors(slots, size, fc_size, width):
    outer = slots.shape[0]
    zeros = jnp.zeros((8, width - PAIR), jnp.float32)
    first, second = None, None
    for d in range(outer * 8):
        index = (d // 8, (d // 4) % 2, (d // 2) % 2, d % 2)
        top = jnp.concatenate([slots[index + (slice(0, 8),)], zeros], axis=1)
        low = jnp.concatenate([slots[index + (slice(8, 16),)], zeros], axis=1)
        top = pltpu.roll(top, d * size, 1) if d else top
        row, lane = divmod(d * fc_size, width)
        low = pltpu.roll(low, lane, 1) if lane else low
        low = pltpu.roll(low, row, 0) if row else low
        first = top if first is None else first + top
        second = low if second is None else second + low
    return first, second


def join_rows(target, slots, columns):
    outer, rows = slots.shape[0], slots.shape[-2]

    def body(a, carry):
        for y in range(2):
            for c in range(2):
                both = [slots[a, y, c, s, :, columns].astype(jnp.float32) for s in range(2)]
                start = pl.multiple_of(((a * 2 + y) * 2 + c) * (2 * rows), 2 * rows)
                joined = jnp.concatenate(both, axis=0).astype(target.dtype)
                target[pl.ds(start, 2 * rows), columns] = joined
        return carry

    lax.fori_loop(0, outer, body, 0)


VECTORS = 9


def forward_kernel(outer, pieces, *refs):
    tokens_hbm, starts_ref = refs[:2]
    vector_refs = refs[2 : 2 + VECTORS]
    shards = refs[2 + VECTORS : 6 + VECTORS]
    outs = refs[6 + VECTORS : 17 + VECTORS]
    (
        normed_hbm, q_hbm, k_hbm, v_hbm, probs_hbm, att_hbm, inverse_hbm, weight_hbm, *slots_hbm,
    ) = outs
    vectors = refs[17 + VECTORS]
    (
        own, vector_slots, qkv_slots, weight, x, normed, q, k, v, probs, att, inverse,
        q_cols, k_cols, move_sem, out_sem, probs_sem, own_sem, send_sem, recv_sem,
    ) = refs[18 + VECTORS :]
    rows, local, width = q.shape
    a, y, c, s = place()
    size, fc_size = vector_refs[0].shape[1], vector_refs[-1].shape[1]

    load = pltpu.make_async_copy(tokens_hbm, x.at[:, pl.ds(TILE, local)], move_sem.at[0])
    load.start()
    own[...] = jnp.zeros_like(own)
    for i, ref in enumerate(vector_refs):
        own[i : i + 1, : ref.shape[1]] = ref[...].astype(jnp.float32)
    greet(outer)
    prev = remote(
        tokens_hbm.at[:, pl.ds(local - TILE, TILE)],
        x.at[:, pl.ds(0, TILE)],
        move_sem.at[1],
        move_sem.at[2],
        device(a, y, c, 1 - s),
    )
    work = Gather(
        outer, pieces, (own,) + shards, (vector_slots, qkv_slots) + tuple(slots_hbm), own_sem, send_sem, recv_sem
    )
    work.step(0)

    @pl.when(s == 0)
    def _():
        prev.start()
        for r in range(rows):
            x[r, 0:TILE] = jnp.zeros((TILE, width), x.dtype)

    load.wait()
    ready = work.lags[3]
    for t in range(1, ready + 1):
        work.step(t)
    first, second = spread_vectors(vector_slots, size, fc_size, width)
    vectors[0:8], vectors[8:16] = first, second

    @pl.when(s == 1)
    def _():
        prev.wait_recv()

    def norm_step(n, carry):
        r, t = n // (local // TILE + 1), lax.rem(n, local // TILE + 1)
        span = pl.ds(pl.multiple_of(t * TILE, TILE), TILE)
        normal, _ = normalize(x[r, span].astype(jnp.float32))
        normed[r, span] = (normal * vectors[0:1] + vectors[1:2]).astype(jnp.bfloat16)
        return carry

    lax.fori_loop(0, rows * (local // TILE + 1), norm_step, 0)
    stores = []

    def store(src, dst):
        copy = pltpu.make_async_copy(src, dst, out_sem.at[len(stores)])
        copy.start()
        stores.append(copy)

    store(normed, normed_hbm)
    for third in range(3):
        work.step(ready + 1 + third)
        columns = slice(third * width, (third + 1) * width)
        join_rows(weight, qkv_slots, columns)

        def row_step(r, carry):
            if third == 0:
                value = dot_nn(normed[r, TILE:], weight[:, columns]) + vectors[2:3]
                q[r] = value.astype(jnp.bfloat16) * jnp.bfloat16(1.0 / math.sqrt(HD))
            elif third == 1:
                k[r] = dot_nn(normed[r], weight[:, columns]).astype(jnp.bfloat16)
            else:
                v[r] = (dot_nn(normed[r], weight[:, columns]) + vectors[3:4]).astype(jnp.bfloat16)
            return carry

        lax.fori_loop(0, rows, row_step, 0)
        store((q, k, v)[third], (q_hbm, k_hbm, v_hbm)[third])
    store(weight, weight_hbm)
    for r in range(rows):
        mask_columns(starts_ref, r, q_cols.at[r], k_cols.at[r])
    lane = lane_index(TILE)
    causal = lax.broadcasted_iota(jnp.int32, (TILE, TILE), 1) <= lax.broadcasted_iota(
        jnp.int32, (TILE, TILE), 0
    )
    ones = jnp.ones((TILE, PAIR), jnp.bfloat16)
    pairs = width // PAIR
    done = ready + 4

    def probs_copy(slot, r, j):
        return pltpu.make_async_copy(probs.at[slot], probs_hbm.at[r, j], probs_sem.at[slot])

    def attend_step(n, carry):
        r, j = n // pairs, lax.rem(n, pairs)
        slot = lax.rem(n, 2)
        pair = pl.ds(pl.multiple_of(j * PAIR, PAIR), PAIR)
        for i, t in enumerate(range(done, work.steps)):

            @pl.when(n == 2 * i + 1)
            def _():
                work.step(t)

        @pl.when(n >= 2)
        def _():
            probs_copy(slot, r, j).wait()

        for tile in range(2):
            span = pl.ds(tile * TILE, TILE)
            queries = q[r, span, pair]
            around = [pl.ds((tile + w) * TILE, TILE) for w in range(2)]
            keys = [
                jnp.concatenate([k[r, around[w], pair], k_cols[r, tile, w]], axis=1) for w in range(2)
            ]
            values = [jnp.concatenate([v[r, around[w], pair], ones], axis=1) for w in range(2)]
            mixed, shares = [], []
            for head in range(2):
                mine = (lane < HD) if head == 0 else (lane >= HD)
                left = jnp.concatenate(
                    [jnp.where(mine, queries, jnp.bfloat16(0)), q_cols[r, tile]], axis=1
                )
                far = dot_nt(left, keys[0])
                near = jnp.where(causal, dot_nt(left, keys[1]), -FIRM)
                top = jnp.max(jnp.maximum(far, near), axis=-1, keepdims=True)
                far = jnp.exp(far - top).astype(jnp.bfloat16)
                near = jnp.exp(near - top).astype(jnp.bfloat16)
                probs[slot, tile, head, 0] = far
                probs[slot, tile, head, 1] = near
                total = dot_nn(far, values[0]) + dot_nn(near, values[1])
                share = 1.0 / total[:, PAIR:]
                mixed.append(total[:, :PAIR] * share)
                shares.append(share)
            att[r, span, pair] = jnp.where(lane < HD, mixed[0], mixed[1]).astype(jnp.bfloat16)
            inverse[r, span, pair] = jnp.where(lane < HD, shares[0], shares[1])
        probs_copy(slot, r, j).start()
        return carry

    steps = rows * pairs
    lax.fori_loop(0, steps, attend_step, 0)
    store(att, att_hbm)
    store(inverse, inverse_hbm)
    for t in range(done + steps // 2, work.steps):
        work.step(t)
    work.end()
    for n in range(2):
        probs_copy(n, 0, n).wait()
    for copy in stores:
        copy.wait()

    @pl.when(s == 0)
    def _():
        prev.wait_send()


def forward(outer, tokens, starts, vectors, weights):
    rows, local, width = tokens.shape
    devices = outer * 8
    low, full = jnp.bfloat16, jnp.float32
    pairs = width // PAIR
    pieces = [(0, 0, PAIR, 0)]
    pieces += [(1, i * width, width, (i + 1) % 2) for i in range(3)]
    for i, weight in enumerate(weights[1:]):
        parts = max(weight.shape[0] * weight.shape[1] // (weights[0].shape[0] * width), 1)
        parts = min(parts, weight.shape[1] // PAIR)
        while weight.shape[1] % (parts * PAIR):
            parts -= 1
        step = weight.shape[1] // parts
        pieces += [(2 + i, j * step, step, (len(pieces) + j) % 2) for j in range(parts)]
    anywhere = pl.BlockSpec(memory_space=pl.ANY)
    vmem = pl.BlockSpec(memory_space=pltpu.VMEM)
    extended = (rows, local + TILE, width)
    qkv = (devices * weights[0].shape[0], weights[0].shape[1])
    slots = [(outer, 2, 2, 2) + weight.shape for weight in weights]
    results = pl.pallas_call(
        functools.partial(forward_kernel, outer, pieces),
        in_specs=[anywhere, pl.BlockSpec(memory_space=pltpu.SMEM)] + [vmem] * (VECTORS + 4),
        out_specs=[anywhere] * 11 + [vmem],
        out_shape=[
            jax.ShapeDtypeStruct(extended, low),
            jax.ShapeDtypeStruct(tokens.shape, low),
            jax.ShapeDtypeStruct(extended, low),
            jax.ShapeDtypeStruct(extended, low),
            jax.ShapeDtypeStruct((rows, pairs, 2, 2, 2, TILE, TILE), low),
            jax.ShapeDtypeStruct(tokens.shape, low),
            jax.ShapeDtypeStruct(tokens.shape, full),
            jax.ShapeDtypeStruct(qkv, low),
        ]
        + [jax.ShapeDtypeStruct(slot, low) for slot in slots[1:]]
        + [jax.ShapeDtypeStruct((16, width), full)],
        scratch_shapes=[
            pltpu.VMEM((16, PAIR), full),
            pltpu.VMEM((outer, 2, 2, 2, 16, PAIR), full),
            pltpu.VMEM(slots[0], low),
            pltpu.VMEM(qkv, low),
            pltpu.VMEM(extended, low),
            pltpu.VMEM(extended, low),
            pltpu.VMEM(tokens.shape, low),
            pltpu.VMEM(extended, low),
            pltpu.VMEM(extended, low),
            pltpu.VMEM((2, 2, 2, 2, TILE, TILE), low),
            pltpu.VMEM(tokens.shape, low),
            pltpu.VMEM(tokens.shape, full),
            pltpu.VMEM((rows, 2, TILE, PAIR), low),
            pltpu.VMEM((rows, 2, 2, TILE, PAIR), low),
            pltpu.SemaphoreType.DMA((3,)),
            pltpu.SemaphoreType.DMA((8,)),
            pltpu.SemaphoreType.DMA((2,)),
        ]
        + Gather.semaphores(outer, 5, len(pieces)),
        compiler_params=pltpu.CompilerParams(
            collective_id=2, has_side_effects=True, vmem_limit_bytes=VMEM_LIMIT
        ),
    )(tokens, starts, *[vector.reshape(1, -1) for vector in vectors], *weights)
    normed, q, k, v, probs, att, inverse, weight, *slots, whole_vectors = results
    whole = [weight] + [
        slot.reshape(devices * w.shape[0], w.shape[1]) for slot, w in zip(slots, weights[1:])
    ]
    return whole, whole_vectors, normed, q, k, v, probs, att, inverse


def shares_out(rows, columns):
    return jax.ShapeDtypeStruct((rows, columns), jnp.float32)


def column_pieces(array, columns, parts, orders):
    step = columns // parts
    return [(array, j * step, step, orders[j % len(orders)]) for j in range(parts)]


def mlp_scatter_kernel(
    outer, pieces, times,
    x_hbm, att_hbm, dy_hbm, attn_hbm, fc_hbm, proj_hbm, vectors,
    out_hbm, middle_grad_hbm, att_grad_hbm, attn_grad_hbm, fc_grad_hbm, sums_ref, proj_share,
    x, att, dy, attn, fc, proj, hidden, slope, normed, branch, middle, att_grad,
    attn_grad, proj_terms, in_sem, out_sem, *rest,
):
    tokens, width = x.shape
    chunks = fc.shape[1] // CHUNK
    tiles = tokens // MLP_TILE
    loads = [
        pltpu.make_async_copy(src, dst, in_sem.at[i])
        for i, (src, dst) in enumerate(
            ((att_hbm, att), (attn_hbm, attn), (x_hbm, x), (fc_hbm, fc), (dy_hbm, dy), (proj_hbm, proj))
        )
    ]
    for load in loads:
        load.start()
    greet(outer)
    work = Scatter(outer, pieces, (proj_terms,), (proj_share,), rest[:-3], *rest[-3:], times)
    sums_ref[...] = jnp.zeros_like(sums_ref)
    for load in loads[:3]:
        load.wait()

    def forward_step(t, carry):
        span = pl.ds(pl.multiple_of(t * MLP_TILE, MLP_TILE), MLP_TILE)
        value = x[span].astype(jnp.float32) + dot_nn(att[span], attn[...]) + vectors[4:5]
        middle[span] = value
        normal, _ = normalize(value)
        low = (normal * vectors[5:6] + vectors[6:7]).astype(jnp.bfloat16)
        normed[span] = low

        @pl.when(t == 0)
        def _():
            loads[3].wait()

        for j in range(chunks):
            columns = pl.ds(j * CHUNK, CHUNK)
            pre = dot_nn(low, fc[:, columns]) + vectors[8 + j : 9 + j]
            value, back = gelu_pair(pre)
            hidden[span, columns] = value.astype(jnp.bfloat16)
            slope[span, columns] = back.astype(jnp.bfloat16)
        return carry

    lax.fori_loop(0, tiles, forward_step, 0)
    loads[4].wait()
    share = proj_terms.shape[-2]
    each = CHUNK // (8 * share)
    for j in range(chunks):
        columns = pl.ds(j * CHUNK, CHUNK)
        grad = dot_tn(hidden[:, columns], dy[...]).astype(jnp.bfloat16)
        proj_terms[j * each : (j + 1) * each] = grad.reshape((each, 2, 2, 2, share, width))
    loads[5].wait()

    def backward_step(t, carry):
        span = pl.ds(pl.multiple_of(t * MLP_TILE, MLP_TILE), MLP_TILE)
        for i in range(work.steps):
            if i < 2 * tiles and i % 2 == 0:

                @pl.when(t == i // 2)
                def _():
                    work.step(i)

        upstream = dy[span]
        result = middle[span] + vectors[7:8]
        back = None
        for j in range(chunks):
            columns = pl.ds(j * CHUNK, CHUNK)
            grad = dot_nt(upstream, proj[columns]) * slope[span, columns].astype(jnp.float32)
            grad = grad.astype(jnp.bfloat16)
            slope[span, columns] = grad
            sums_ref[4 + j : 5 + j] += column_sum(grad.astype(jnp.float32))
            part = dot_nt(grad, fc[:, columns])
            back = part if back is None else back + part
            if j == chunks // 2 - 1:
                for i in range(1, 2 * tiles, 2):

                    @pl.when(t == i // 2)
                    def _():
                        work.step(i)

            result = result + dot_nn(hidden[span, columns], proj[columns])
        x[span] = result.astype(jnp.bfloat16)
        normal, scale = normalize(middle[span])
        upstream = upstream.astype(jnp.float32)
        sums_ref[0:1] += column_sum(upstream)
        sums_ref[1:2] += column_sum(back * normal)
        sums_ref[2:3] += column_sum(back)
        total = upstream + norm_grad(back, vectors[5:6], normal, scale)
        middle[span] = total
        total = total.astype(jnp.bfloat16)
        branch[span] = total
        sums_ref[3:4] += column_sum(total.astype(jnp.float32))
        att_grad[span] = dot_nt(total, attn[...]).astype(jnp.bfloat16)
        return carry

    lax.fori_loop(0, tiles, backward_step, 0)
    stores = []

    def store(src, dst):
        copy = pltpu.make_async_copy(src, dst, out_sem.at[len(stores)])
        copy.start()
        stores.append(copy)

    store(x, out_hbm)
    store(middle, middle_grad_hbm)
    store(att_grad, att_grad_hbm)
    t = 2 * tiles
    for j in range(chunks):
        columns = pl.ds(j * CHUNK, CHUNK)
        grad = dot_tn(normed[...], slope[:, columns]).astype(jnp.bfloat16)
        hidden[0:width, columns] = grad
        store(hidden.at[pl.ds(0, width), columns], fc_grad_hbm.at[:, columns])
        if t < work.steps:
            work.step(t)
            t += 1
    attn_grad[...] = dot_tn(att[...], branch[...]).astype(jnp.bfloat16)
    store(attn_grad, attn_grad_hbm)
    while t < work.steps:
        work.step(t)
        t += 1
    work.end()
    for copy in stores:
        copy.wait()


def mlp_scatter(outer, x, att, dy, attn, fc, proj, vectors):
    tokens, width = x.shape
    hidden = fc.shape[1]
    share = hidden // (outer * 8)
    low, full = jnp.bfloat16, jnp.float32
    anywhere = pl.BlockSpec(memory_space=pl.ANY)
    vmem = pl.BlockSpec(memory_space=pltpu.VMEM)
    pieces = column_pieces(0, width, 3, (0, 1))
    times = [(0, 1, 5, 8, 11), (0, 1, 5, 8, 11), (1, 3, 9, 11, 13)]
    return pl.pallas_call(
        functools.partial(mlp_scatter_kernel, outer, pieces, times),
        in_specs=[anywhere] * 6 + [vmem],
        out_specs=[anywhere] * 5 + [vmem] * 2,
        out_shape=[
            jax.ShapeDtypeStruct((tokens, width), low),
            jax.ShapeDtypeStruct((tokens, width), full),
            jax.ShapeDtypeStruct((tokens, width), low),
            jax.ShapeDtypeStruct(attn.shape, low),
            jax.ShapeDtypeStruct(fc.shape, low),
            jax.ShapeDtypeStruct((8, width), full),
            shares_out(share, width),
        ],
        scratch_shapes=[
            pltpu.VMEM((tokens, width), low),
            pltpu.VMEM((tokens, width), low),
            pltpu.VMEM((tokens, width), low),
            pltpu.VMEM(attn.shape, low),
            pltpu.VMEM(fc.shape, low),
            pltpu.VMEM(proj.shape, low),
            pltpu.VMEM((tokens, hidden), low),
            pltpu.VMEM((tokens, hidden), low),
            pltpu.VMEM((tokens, width), low),
            pltpu.VMEM((tokens, width), low),
            pltpu.VMEM((tokens, width), full),
            pltpu.VMEM((tokens, width), low),
            pltpu.VMEM(attn.shape, low),
            pltpu.VMEM((outer, 2, 2, 2, share, width), low),
            pltpu.SemaphoreType.DMA((6,)),
            pltpu.SemaphoreType.DMA((12,)),
        ]
        + Scatter.scratch(outer, [(share, width, low)], pieces),
        compiler_params=pltpu.CompilerParams(
            collective_id=3, has_side_effects=True, vmem_limit_bytes=VMEM_LIMIT
        ),
    )(x, att, dy, attn, fc, proj, vectors)


def pack_columns(values, start, lanes):
    width = values.shape[1]
    moved = pltpu.roll(values, (width - start) % width, 1) if start % width else values
    return jnp.where(lane_index(values.shape[0]) < lanes, moved[:, :PAIR], 0.0)


def backward_kernel(
    outer, pieces, times, places, count,
    probs_hbm, q_hbm, k_hbm, v_hbm, normed_hbm, grad_hbm, att_hbm, inverse_hbm, x_hbm, middle_hbm,
    weight_hbm, vectors, mlp_sums, *refs,
):
    terms, refs = refs[:count], refs[count:]
    tokens_grad_hbm, refs = refs[0], refs[1:]
    shares, refs = refs[: count + 2], refs[count + 2 :]
    (
        q, k, v, normed, grad, att, inverse, x, middle, weight, probs, dq, dk, dv, dq_part, dk_sum,
        dv_sum, prev, late, qkv_terms, vector_terms, sums, in_sem, probs_sem, out_sem, late_sem, *rest,
    ) = refs
    rows, local, width = q.shape
    pairs = width // PAIR
    a, y, c, s = place()
    loads = [
        pltpu.make_async_copy(src, dst, in_sem.at[i])
        for i, (src, dst) in enumerate(
            (
                (q_hbm, q), (k_hbm, k), (v_hbm, v), (grad_hbm, grad), (att_hbm, att), (inverse_hbm, inverse),
                (weight_hbm, weight), (normed_hbm, normed), (x_hbm, x), (middle_hbm, middle),
            )
        )
    ]

    def far_copy(slot, r, j):
        return pltpu.make_async_copy(
            probs_hbm.at[r, j, 0, :, 0], probs.at[slot, 0, :, 0], probs_sem.at[slot]
        )

    def near_copy(slot, r, j):
        return pltpu.make_async_copy(
            probs_hbm.at[r, j, :, :, 1], probs.at[slot, :, :, 1], probs_sem.at[slot]
        )

    def cross_copy(slot, r, j):
        return pltpu.make_async_copy(
            probs_hbm.at[r, j, 1, :, 0], probs.at[slot, 1, :, 0], probs_sem.at[2 + slot]
        )

    for load in loads[:6]:
        load.start()
    far_copy(0, 0, 0).start()
    for load in loads[6:]:
        load.start()
    greet(outer)
    work = Scatter(
        outer, pieces, terms + (qkv_terms, vector_terms), shares, rest[:-3], *rest[-3:], times, places
    )
    sums[...] = jnp.zeros_like(sums)
    for load in loads[:6]:
        load.wait()
    lane = lane_index(TILE)
    ones = jnp.ones((TILE, PAIR), jnp.bfloat16)

    def sides(r, pair, tile):
        span = pl.ds(tile * TILE, TILE)
        scaled = (grad[r, span, pair].astype(jnp.float32) * inverse[r, span, pair]).astype(jnp.bfloat16)
        product = scaled.astype(jnp.float32) * att[r, span, pair].astype(jnp.float32)
        queries = q[r, span, pair]
        both = []
        for head in range(2):
            mine = (lane < HD) if head == 0 else (lane >= HD)
            delta = -jnp.sum(jnp.where(mine, product, 0.0), axis=-1, keepdims=True)
            high = delta.astype(jnp.bfloat16).astype(jnp.float32)
            extra = jnp.where(lane == 0, high, jnp.where(lane == 1, delta - high, 0.0))
            grads = jnp.where(mine, scaled, jnp.bfloat16(0))
            mine_queries = jnp.where(mine, queries, jnp.bfloat16(0))
            both.append(
                (jnp.concatenate([grads, extra.astype(jnp.bfloat16)], axis=1), grads, mine_queries)
            )
        return both

    def unit(r, pair, side, chances, place_of):
        at = pl.ds(place_of * TILE, TILE)
        left, grads, mine_queries = side
        right = jnp.concatenate([v[r, at, pair], ones], axis=1)
        d_score = (chances.astype(jnp.float32) * dot_nt(left, right)).astype(jnp.bfloat16)
        return (
            dot_nn(d_score, k[r, at, pair]),
            dot_tn(d_score, mine_queries),
            dot_tn(chances, grads),
        )

    def far_step(n, carry):
        r, j = n // pairs, lax.rem(n, pairs)
        slot = lax.rem(n, 2)
        pair = pl.ds(pl.multiple_of(j * PAIR, PAIR), PAIR)
        for t in range(rows * pairs):

            @pl.when(n == t)
            def _():
                work.step(t)

        far_copy(slot, r, j).wait()

        @pl.when(n + 1 < rows * pairs)
        def _():
            far_copy(1 - slot, (n + 1) // pairs, lax.rem(n + 1, pairs)).start()

        first = unit(r, pair, sides(r, pair, 0)[0], probs[slot, 0, 0, 0], 0)
        second = unit(r, pair, sides(r, pair, 0)[1], probs[slot, 0, 1, 0], 0)
        dq_part[r, :, pair] = jnp.where(lane < HD, first[0], second[0])
        dk[r, 0:TILE, pair] = (first[1] + second[1]).astype(jnp.bfloat16)
        dv[r, 0:TILE, pair] = (first[2] + second[2]).astype(jnp.bfloat16)
        return carry

    far_steps = rows * pairs
    lax.fori_loop(0, far_steps, far_step, 0)
    near_copy(0, 0, 0).start()
    cross_copy(0, 0, 0).start()
    for load in loads[6:8]:
        load.wait()
    third = [slice(i * width, (i + 1) * width) for i in range(3)]
    for r in range(rows):
        head = slice(0, TILE)
        prev[r] = (
            dot_nt(dk[r, head], weight[:, third[1]]) + dot_nt(dv[r, head], weight[:, third[2]])
        ).astype(jnp.bfloat16)
    late_copy = remote(prev, late, late_sem.at[0], late_sem.at[1], device(a, y, c, 1 - s))

    @pl.when(s == 1)
    def _():
        late_copy.start()
        late[...] = jnp.zeros_like(late)

    def near_step(n, carry):
        j, r = n // rows, lax.rem(n, rows)
        slot = lax.rem(n, 2)
        pair = pl.ds(pl.multiple_of(j * PAIR, PAIR), PAIR)
        for t in range(rows * pairs):

            @pl.when(n == t)
            def _():
                work.step(far_steps + t)

        near_copy(slot, r, j).wait()
        cross_copy(slot, r, j).wait()

        @pl.when(n + 1 < rows * pairs)
        def _():
            near_copy(1 - slot, lax.rem(n + 1, rows), (n + 1) // rows).start()
            cross_copy(1 - slot, lax.rem(n + 1, rows), (n + 1) // rows).start()

        scale = 1.0 / math.sqrt(HD)
        parts = []
        for head, side in enumerate(sides(r, pair, 0)):
            parts.append(unit(r, pair, side, probs[slot, 0, head, 1], 1))
        total = dq_part[r, :, pair] + jnp.where(lane < HD, parts[0][0], parts[1][0])
        dq[r, 0:TILE, pair] = (total * scale).astype(jnp.bfloat16)
        dk_sum[...] = parts[0][1] + parts[1][1]
        dv_sum[...] = parts[0][2] + parts[1][2]
        queries = []
        for head, side in enumerate(sides(r, pair, 1)):
            cross = unit(r, pair, side, probs[slot, 1, head, 0], 1)
            dk_sum[...] += cross[1]
            dv_sum[...] += cross[2]
            near = unit(r, pair, side, probs[slot, 1, head, 1], 2)
            queries.append(cross[0] + near[0])
            if head == 0:
                dk[r, 2 * TILE : 3 * TILE, pair] = near[1].astype(jnp.bfloat16)
                dv[r, 2 * TILE : 3 * TILE, pair] = near[2].astype(jnp.bfloat16)
            else:
                last = dk[r, 2 * TILE : 3 * TILE, pair].astype(jnp.float32) + near[1]
                dk[r, 2 * TILE : 3 * TILE, pair] = last.astype(jnp.bfloat16)
                last = dv[r, 2 * TILE : 3 * TILE, pair].astype(jnp.float32) + near[2]
                dv[r, 2 * TILE : 3 * TILE, pair] = last.astype(jnp.bfloat16)
        total = jnp.where(lane < HD, queries[0], queries[1])
        dq[r, TILE : 2 * TILE, pair] = (total * scale).astype(jnp.bfloat16)
        dk[r, TILE : 2 * TILE, pair] = dk_sum[...].astype(jnp.bfloat16)
        dv[r, TILE : 2 * TILE, pair] = dv_sum[...].astype(jnp.bfloat16)

        @pl.when((r == rows - 1) & (lax.rem(j, 2) == 1))
        def _():
            block = pl.ds(pl.multiple_of((j // 2) * (2 * PAIR), 2 * PAIR), 2 * PAIR)
            share = qkv_terms.shape[-2]
            for i, grads in enumerate((dq, dk, dv)):
                total = None
                for row in range(rows):
                    left = normed[row, TILE:] if i == 0 else normed[row]
                    part = dot_tn(left, grads[row, :, block])
                    total = part if total is None else total + part
                to = pl.ds(pl.multiple_of((j // 2) * width + i * 2 * PAIR, 2 * PAIR), 2 * PAIR)
                qkv_terms[:, :, :, :, :, to] = total.astype(jnp.bfloat16).reshape(
                    (outer, 2, 2, 2, share, 2 * PAIR)
                )

        return carry

    near_steps = rows * pairs
    lax.fori_loop(0, near_steps, near_step, 0)
    at = far_steps + near_steps
    for load in loads[8:]:
        load.wait()
    stores = []
    tiles = local // TILE
    for t in range(tiles):
        if t == tiles - 1:

            @pl.when(s == 0)
            def _():
                late_copy.wait_recv()

        for r in range(rows):
            work.step(at)
            at += 1
            span = slice(t * TILE, (t + 1) * TILE)
            keys = slice((t + 1) * TILE, (t + 2) * TILE)
            back = dot_nt(dq[r, span], weight[:, third[0]])
            back = back + dot_nt(dk[r, keys], weight[:, third[1]])
            back = back + dot_nt(dv[r, keys], weight[:, third[2]])
            if t == tiles - 1:
                back = back + late[r].astype(jnp.float32)
            normal, scale = normalize(x[r, span].astype(jnp.float32))
            sums[0:1] += column_sum(back * normal)
            sums[1:2] += column_sum(back)
            middle[r, span] = middle[r, span] + norm_grad(back, vectors[0:1], normal, scale)
            store = pltpu.make_async_copy(
                middle.at[r, pl.ds(t * TILE, TILE)],
                tokens_grad_hbm.at[r, pl.ds(t * TILE, TILE)],
                out_sem.at[t * rows + r],
            )
            store.start()
            stores.append(store)
    for r in range(rows):
        sums[2:3] += column_sum(dq[r].astype(jnp.float32))
        sums[3:4] += column_sum(dv[r].astype(jnp.float32))
    sums[4:8] = mlp_sums[0:4]
    size = width // (outer * 8)
    fc_size = 4 * size
    total, fc_total = sums[...], mlp_sums[...]
    for d in range(outer * 8):
        row, start = divmod(d * fc_size, width)
        index = (d // 8, (d // 4) % 2, (d // 2) % 2, d % 2)
        vector_terms[index + (slice(0, 8),)] = pack_columns(total, d * size, size)
        vector_terms[index + (slice(8, 16),)] = pack_columns(
            jnp.broadcast_to(fc_total[4 + row : 5 + row], (8, width)), start, fc_size
        )
    for t in range(at, work.steps):
        work.step(t)
    work.end()
    for store in stores:
        store.wait()

    @pl.when(s == 1)
    def _():
        late_copy.wait_send()


def backward(outer, probs, q, k, v, normed, grad, att, inverse, x, middle_grad, weight, vectors, mlp_sums, fc_grad, attn_grad):
    rows, local, width = q.shape
    devices = outer * 8
    low, full = jnp.bfloat16, jnp.float32
    share = weight.shape[0] // devices
    anywhere = pl.BlockSpec(memory_space=pl.ANY)
    vmem = pl.BlockSpec(memory_space=pltpu.VMEM)
    terms = [
        fc_grad.reshape((outer, 2, 2, 2, share, fc_grad.shape[1])),
        attn_grad.reshape((outer, 2, 2, 2, share, width)),
    ]
    blocks = weight.shape[1] // width
    pieces = column_pieces(0, fc_grad.shape[1], 4, (1, 0, 1, 1)) + [(1, 0, width, 0)]
    pieces += column_pieces(2, weight.shape[1], 3, (1, 0, 1)) + [(3, 0, PAIR, 0)]
    part = width // 3
    places = {
        5 + b: [(i * part, part, i * width + b * part) for i in range(blocks)] for b in range(3)
    }
    times = BACKWARD_TIMES
    shapes = [(share, fc_grad.shape[1], low), (share, width, low), (share, weight.shape[1], low), (16, PAIR, full)]
    extended = (rows, local + TILE, width)
    results = pl.pallas_call(
        functools.partial(backward_kernel, outer, pieces, times, places, 2),
        in_specs=[anywhere] * 11 + [vmem] * 2 + [anywhere] * 2,
        out_specs=[anywhere] + [vmem] * 4,
        out_shape=[jax.ShapeDtypeStruct(x.shape, full)]
        + [shares_out(shape[0], shape[1]) for shape in shapes],
        scratch_shapes=[
            pltpu.VMEM(q.shape, low),
            pltpu.VMEM(extended, low),
            pltpu.VMEM(extended, low),
            pltpu.VMEM(extended, low),
            pltpu.VMEM(q.shape, low),
            pltpu.VMEM(q.shape, low),
            pltpu.VMEM(q.shape, full),
            pltpu.VMEM(q.shape, low),
            pltpu.VMEM(q.shape, full),
            pltpu.VMEM(weight.shape, low),
            pltpu.VMEM((2, 2, 2, 2, TILE, TILE), low),
            pltpu.VMEM(q.shape, low),
            pltpu.VMEM(extended, low),
            pltpu.VMEM(extended, low),
            pltpu.VMEM((rows, TILE, width), full),
            pltpu.VMEM((TILE, PAIR), full),
            pltpu.VMEM((TILE, PAIR), full),
            pltpu.VMEM((rows, TILE, width), low),
            pltpu.VMEM((rows, TILE, width), low),
            pltpu.VMEM((outer, 2, 2, 2, share, weight.shape[1]), low),
            pltpu.VMEM((outer, 2, 2, 2, 16, PAIR), full),
            pltpu.VMEM((8, width), full),
            pltpu.SemaphoreType.DMA((10,)),
            pltpu.SemaphoreType.DMA((4,)),
            pltpu.SemaphoreType.DMA((rows * local // TILE,)),
            pltpu.SemaphoreType.DMA((2,)),
        ]
        + Scatter.scratch(outer, shapes, pieces),
        compiler_params=pltpu.CompilerParams(
            collective_id=4, has_side_effects=True, vmem_limit_bytes=VMEM_LIMIT
        ),
    )(probs, q, k, v, normed, grad, att, inverse, x, middle_grad, weight, vectors, mlp_sums, *terms)
    tokens_grad, fc_share, attn_share, qkv_share, packed = results
    size = width // devices
    return tokens_grad, fc_share, attn_share, qkv_share, packed[:8, :size], packed[8, : 4 * size]


BACKWARD_TIMES = [
    (0, 4, 14, 17, 20),
    (0, 4, 14, 17, 20),
    (6, 11, 18, 21, 24),
    (6, 11, 18, 21, 24),
    (14, 16, 21, 23, 25),
    (16, 18, 23, 25, 27),
    (20, 22, 25, 27, 29),
    (24, 25, 27, 28, 29),
    (28, 29, 30, 31, 32),
]


def gather_weights(outer, weights, vectors, fc_bias):
    devices = outer * 8
    shards = [pack_vectors(vectors + [fc_bias])]
    shards += [w.reshape(pack_shape(w.shape)) for w in weights]
    full = gather_all(outer, shards, cut([shard.shape for shard in shards]))
    packed = full[0].reshape(devices, -1)
    count, size = len(vectors), vectors[0].shape[0]
    first = packed[:, : count * size].reshape(devices, count, size)
    first = jnp.swapaxes(first, 0, 1).reshape(count, devices * size)
    second = packed[:, count * size : count * size + fc_bias.shape[0]].reshape(-1, devices * size)
    whole = [f.reshape(devices * w.shape[0], w.shape[1]) for f, w in zip(full[1:], weights)]
    return whole, jnp.concatenate([first, second], axis=0)


def scatter_grads(outer, weight_terms, vector_terms, fc_bias_term):
    devices = outer * 8
    count, width = vector_terms.shape
    first = jnp.swapaxes(vector_terms.reshape(count, devices, width // devices), 0, 1)
    first = first.reshape(devices, -1)
    second = fc_bias_term.reshape(devices, -1)
    packed = pack_vectors([first, second])
    terms = [packed.reshape((outer, 2, 2, 2) + packed.shape[1:])]
    shapes = [(term.shape[0] // devices, term.shape[1]) for term in weight_terms]
    for term, shape in zip(weight_terms, shapes):
        terms.append(term.reshape((outer, 2, 2, 2) + pack_shape(shape)))
    shares = scatter_all(outer, terms, cut([term.shape[-2:] for term in terms]))
    flat = shares[0].reshape(-1)
    size = width // devices
    vectors = [flat[i * size : (i + 1) * size] for i in range(count)]
    fc_bias = flat[count * size : count * size + second.shape[1]]
    return [share.reshape(shape) for share, shape in zip(shares[1:], shapes)], vectors, fc_bias


def shards(
    tokens_in,
    doc_starts,
    norm1_gain,
    norm1_bias,
    qkv_weight,
    query_bias,
    value_bias,
    attn_weight,
    attn_bias,
    norm2_gain,
    norm2_bias,
    fc_weight,
    fc_bias,
    proj_weight,
    proj_bias,
    out_grad,
):
    outer = lax.axis_size("batch") // 4
    rows, local, width = tokens_in.shape
    seq = lax.axis_index("seq")
    first = 2 * seq
    padded = jnp.pad(doc_starts, ((0, 0), (1, 0)))
    starts = lax.dynamic_slice_in_dim(padded, first, 3, 1)
    starts = starts - TILE * (first - 1 + jnp.arange(3, dtype=jnp.int32))
    weights = [qkv_weight, attn_weight, fc_weight, proj_weight]
    vectors = [norm1_gain, norm1_bias, query_bias, value_bias, attn_bias, norm2_gain, norm2_bias, proj_bias]
    if qkv_weight.shape[0] % 8 == 0:
        (qkv, attn, fc, proj), vectors, normed, q, k, v, probs, att, inverse = forward(
            outer, tokens_in, starts, vectors + [fc_bias], weights
        )
    else:
        prev = lax.ppermute(tokens_in[:, local - TILE :], "seq", [(0, 1)])
        (qkv, attn, fc, proj), vectors = gather_weights(outer, weights, vectors, fc_bias)
        normed, q, k, v = project(tokens_in, prev, qkv, vectors)
        probs, att, inverse = attend(starts, q, k, v)
    flat = lambda value: value.reshape(rows * local, width)
    block = lambda value: value.reshape(rows, local, width)
    if qkv_weight.shape[0] % 8 == 0:
        out, middle_grad, att_grad, attn_grad, fc_grad, mlp_sums, proj_share = mlp_scatter(
            outer, flat(tokens_in), flat(att), flat(out_grad), attn, fc, proj, vectors
        )
        tokens_grad, fc_share, attn_share, qkv_share, packed, fc_bias_share = backward(
            outer, probs, q, k, v, normed, block(att_grad), att, inverse, tokens_in, block(middle_grad),
            qkv, vectors, mlp_sums, fc_grad, attn_grad,
        )
        weights = [qkv_share, attn_share, fc_share, proj_share]
        shares = [packed[i] for i in range(8)]
    else:
        out, middle_grad, att_grad, attn_grad, fc_grad, proj_grad, mlp_sums = mlp(
            flat(tokens_in), flat(att), flat(out_grad), attn, fc, proj, vectors
        )
        dq, dk, dv = attend_grad(probs, q, k, v, block(att_grad), att, inverse)
        qkv_grad, prev_grad, project_sums = project_grad(normed, dq, dk, dv, qkv)
        late = lax.ppermute(prev_grad, "seq", [(1, 0)])
        tokens_grad, norm_sums = tokens_grad_of(
            tokens_in, dq, dk, dv, qkv, late, block(middle_grad), vectors
        )
        sums = jnp.concatenate([norm_sums[:2], project_sums[:2], mlp_sums[:4]], axis=0)
        weights, shares, fc_bias_share = scatter_grads(
            outer, [qkv_grad, attn_grad, fc_grad, proj_grad], sums, mlp_sums[4:]
        )
    gain1, bias1, query, value, proj_b, gain2, bias2, attn_b = shares
    return (
        out.reshape(rows, local, width),
        tokens_grad,
        gain1,
        bias1,
        weights[0],
        query,
        value,
        weights[1],
        attn_b,
        gain2,
        bias2,
        weights[2],
        fc_bias_share,
        weights[3],
        proj_b,
    )


def solution(mesh):
    return jax.shard_map(
        shards,
        mesh=mesh,
        in_specs=(
            P("batch", "seq", None),
            P("batch", None),
            P(("batch", "seq")),
            P(("batch", "seq")),
            P(("batch", "seq"), None),
            P(("batch", "seq")),
            P(("batch", "seq")),
            P(("batch", "seq"), None),
            P(("batch", "seq")),
            P(("batch", "seq")),
            P(("batch", "seq")),
            P(("batch", "seq"), None),
            P(("batch", "seq")),
            P(("batch", "seq"), None),
            P(("batch", "seq")),
            P("batch", "seq", None),
        ),
        out_specs=(
            P("batch", "seq", None),
            P("batch", "seq", None),
            P(("batch", "seq")),
            P(("batch", "seq")),
            P(("batch", "seq"), None),
            P(("batch", "seq")),
            P(("batch", "seq")),
            P(("batch", "seq"), None),
            P(("batch", "seq")),
            P(("batch", "seq")),
            P(("batch", "seq")),
            P(("batch", "seq"), None),
            P(("batch", "seq")),
            P(("batch", "seq"), None),
            P(("batch", "seq")),
        ),
        check_vma=False,
    )
```

```python
import functools
import math

import jax
import jax.numpy as jnp
from jax import lax
from jax.experimental import pallas as pl
from jax.experimental.pallas import tpu as pltpu
from jax.sharding import PartitionSpec as P

HD = 64
EPSILON = 1e-05
GELU_SCALE = 0.7978845608028654
MESH_ID = pl.DeviceIdType.MESH
VMEM_LIMIT = 60 * 2**20
EVERY = slice(None)


def place():
    batch, seq = lax.axis_index("batch"), lax.axis_index("seq")
    return (batch // 4, (batch // 2) % 2, batch % 2, seq)


def device(a, y, c, s):
    return (a * 4 + y * 2 + c, s)


def greet(outer):
    a, y, c, s = place()
    barrier = pltpu.get_barrier_semaphore()
    others = [device(lax.rem(a + k, outer), y, c, s) for k in range(1, outer)]
    others += [device(a, 1 - y, c, s), device(a, y, c, 1 - s), device(a, y, 1 - c, s)]
    for other in others:
        pl.semaphore_signal(barrier, inc=1, device_id=other, device_id_type=MESH_ID)
    pl.semaphore_wait(barrier, len(others))


def everyone(outer):
    a, y, c, s = place()
    devices = outer * 8
    me = ((a * 2 + y) * 2 + c) * 2 + s
    split = lambda d: (d // 8, (d // 4) % 2, (d // 2) % 2, d % 2)
    return [
        (split(lax.rem(me + k, devices)), split(lax.rem(me + devices - k, devices)))
        for k in range(1, devices)
    ]


def greet_all(outer):
    barrier = pltpu.get_barrier_semaphore()
    others = everyone(outer)
    for other, _ in others:
        pl.semaphore_signal(barrier, inc=1, device_id=device(*other), device_id_type=MESH_ID)
    pl.semaphore_wait(barrier, len(others))


def remote(src, dst, send_sem, recv_sem, other):
    return pltpu.make_async_remote_copy(
        src_ref=src,
        dst_ref=dst,
        send_sem=send_sem,
        recv_sem=recv_sem,
        device_id=other,
        device_id_type=MESH_ID,
    )


def sites_of(work, plan):
    def comm(name):
        for phase, p in plan.get(name, ()):
            work.act(phase, p)
            if (phase, p) in work.after:
                work.after[(phase, p)]()

    def comm_at(n, name, count):
        for i in range(count):
            if f"{name}{i}" in plan:

                @pl.when(n == i)
                def _():
                    comm(f"{name}{i}")

    return comm, comm_at


class Gather:
    def __init__(self, outer, pieces, shards, outs, own_sem, send_sem, recv_sem, eager=99):
        self.outer, self.pieces, self.shards, self.outs = outer, pieces, shards, outs
        self.own_sem, self.send_sem, self.recv_sem = own_sem, send_sem, recv_sem
        self.owned, self.eager, self.after = set(), eager, {}
        self.place = place()

    def sems(self, p, k):
        return self.send_sem.at[p, k], self.recv_sem.at[p, k]

    def own(self, i):
        return pltpu.make_async_copy(
            self.shards[i], self.outs[i].at[self.place], self.own_sem.at[i]
        )

    def first(self, p, k):
        i, start, width, order = self.pieces[p]
        a, y, c, s = self.place
        columns = pl.ds(start, width)
        src = self.shards[i].at[:, columns]
        dst = self.outs[i].at[a, y, c, s, :, columns]
        if k == 0:
            return remote(src, dst, *self.sems(p, 0), self.near(order))
        return remote(src, dst, *self.sems(p, k), device(lax.rem(a + k, self.outer), y, c, s))

    def near(self, order):
        a, y, c, s = self.place
        return device(a, 1 - y, c, s) if order == 0 else device(a, y, c, 1 - s)

    def second(self, p, k):
        i, start, width, order = self.pieces[p]
        a, y, c, s = self.place
        source = lax.rem(a + self.outer - k, self.outer)
        block = self.outs[i].at[source, y, c, s, :, pl.ds(start, width)]
        return remote(block, block, *self.sems(p, self.outer - 1 + k), self.near(order))

    def third(self, p):
        i, start, width, order = self.pieces[p]
        a, y, c, s = self.place
        index = (EVERY, EVERY, c, s) if order == 0 else (EVERY, y, c, EVERY)
        block = self.outs[i].at[index + (EVERY, pl.ds(start, width))]
        return remote(block, block, *self.sems(p, 2 * self.outer - 1), self.near(1 - order))

    def fourth(self, p):
        i, start, width, order = self.pieces[p]
        a, y, c, s = self.place
        block = self.outs[i].at[EVERY, EVERY, c, EVERY, EVERY, pl.ds(start, width)]
        return remote(block, block, *self.sems(p, 2 * self.outer), device(a, y, 1 - c, s))

    def start(self):
        for p in range(len(self.pieces)):
            for k in range(1, self.outer):
                self.first(p, k).start()
            if p < self.eager:
                self.first(p, 0).start()
        for i in range(len(self.shards)):
            self.own(i).start()

    def act(self, phase, p):
        outer, i = self.outer, self.pieces[p][0]
        if phase == 1:
            if p >= self.eager:
                self.first(p, 0).start()
            for k in range(1, outer):
                self.first(p, k).wait_recv()
                self.second(p, k).start()
        elif phase == 2:
            if i not in self.owned:
                self.owned.add(i)
                self.own(i).wait()
            self.first(p, 0).wait_recv()
            for k in range(1, outer):
                self.second(p, k).wait_recv()
            self.third(p).start()
        elif phase == 3:
            self.third(p).wait_recv()
            self.fourth(p).start()
        else:
            self.fourth(p).wait_recv()

    def end(self):
        for p in range(len(self.pieces)):
            for k in range(self.outer):
                self.first(p, k).wait_send()
            for k in range(1, self.outer):
                self.second(p, k).wait_send()
            self.third(p).wait_send()
            self.fourth(p).wait_send()

    @staticmethod
    def semaphores(outer, arrays, pieces):
        return [
            pltpu.SemaphoreType.DMA((arrays,)),
            pltpu.SemaphoreType.DMA((pieces, 2 * outer + 1)),
            pltpu.SemaphoreType.DMA((pieces, 2 * outer + 1)),
        ]


def add_slots(target, other):
    lead = target.shape[:-2]

    def body(k, carry):
        index = []
        for size in reversed(lead):
            index.append(lax.rem(k, size))
            k = k // size
        index = tuple(reversed(index))
        target[index] = target[index] + other[index]
        return carry

    lax.fori_loop(0, math.prod(lead), body, 0)


class Scatter:
    def __init__(self, outer, pieces, terms, outs, slots, own_sem, send_sem, recv_sem, places=None):
        self.outer, self.pieces, self.terms, self.outs = outer, pieces, terms, outs
        n = len(pieces)
        self.held, self.got = slots[:n], [slots[k * n : (k + 1) * n] for k in range(1, 5)]
        self.own_sem, self.send_sem, self.recv_sem = own_sem, send_sem, recv_sem
        self.places, self.after = places or {}, {}
        self.place = place()

    def sems(self, p, k):
        return self.send_sem.at[p, k], self.recv_sem.at[p, k]

    def own(self, p):
        i, start, width, order = self.pieces[p]
        a, y, c, s = self.place
        block = self.terms[i].at[EVERY, EVERY, c, EVERY, EVERY, pl.ds(start, width)]
        return pltpu.make_async_copy(block, self.held[p], self.own_sem.at[p])

    def first(self, p):
        i, start, width, order = self.pieces[p]
        a, y, c, s = self.place
        block = self.terms[i].at[EVERY, EVERY, 1 - c, EVERY, EVERY, pl.ds(start, width)]
        return remote(block, self.got[0][p], *self.sems(p, 0), device(a, y, 1 - c, s))

    def second(self, p):
        a, y, c, s = self.place
        if self.pieces[p][3] == 0:
            src, other = self.held[p].at[:, :, 1 - s], device(a, y, c, 1 - s)
        else:
            src, other = self.held[p].at[:, 1 - y], device(a, 1 - y, c, s)
        return remote(src, self.got[1][p], *self.sems(p, 1), other)

    def third(self, p):
        a, y, c, s = self.place
        if self.pieces[p][3] == 0:
            src, other = self.held[p].at[:, 1 - y, s], device(a, 1 - y, c, s)
        else:
            src, other = self.held[p].at[:, y, 1 - s], device(a, y, c, 1 - s)
        return remote(src, self.got[2][p], *self.sems(p, 2), other)

    def fourth(self, p, k):
        a, y, c, s = self.place
        to = lax.rem(a + k, self.outer)
        src = self.held[p].at[to, y, s]
        return remote(src, self.got[3][p].at[k - 1], *self.sems(p, 2 + k), device(to, y, c, s))

    def act(self, phase, p):
        outer = self.outer
        a, y, c, s = self.place
        i, start, width, order = self.pieces[p]
        if phase == 0:
            self.own(p).start()
            self.first(p).start()
        elif phase == 1:
            self.own(p).wait()
            self.first(p).wait_recv()
            add_slots(self.held[p], self.got[0][p])
            self.second(p).start()
        elif phase == 2:
            self.second(p).wait_recv()
            mine = (EVERY, EVERY, s) if order == 0 else (EVERY, y)
            add_slots(self.held[p].at[mine], self.got[1][p])
            self.third(p).start()
        elif phase == 3:
            self.third(p).wait_recv()
            add_slots(self.held[p].at[:, y, s], self.got[2][p])
            for k in range(1, outer):
                self.fourth(p, k).start()
        else:
            value = self.held[p][a, y, s].astype(jnp.float32)
            for k in range(1, outer):
                self.fourth(p, k).wait_recv()
                value = value + self.got[3][p][k - 1].astype(jnp.float32)
            for offset, size, to in self.places.get(p, [(0, width, start)]):
                self.outs[i][:, to : to + size] = value[:, offset : offset + size]

    def end(self):
        for p in range(len(self.pieces)):
            self.first(p).wait_send()
            self.second(p).wait_send()
            self.third(p).wait_send()
            for k in range(1, self.outer):
                self.fourth(p, k).wait_send()

    @staticmethod
    def scratch(outer, shapes, pieces):
        def slot(p, *lead):
            i, start, width, order = pieces[p]
            return pltpu.VMEM(lead + (shapes[i][0], width), shapes[i][2])

        n = range(len(pieces))
        leads = ((outer, 2, 2), (outer, 2, 2), (outer, 2), (outer,), (max(outer - 1, 1),))
        return [slot(p, *lead) for lead in leads for p in n] + [
            pltpu.SemaphoreType.DMA((len(pieces),)),
            pltpu.SemaphoreType.DMA((len(pieces), outer + 2)),
            pltpu.SemaphoreType.DMA((len(pieces), outer + 2)),
        ]


def steps_in_order(count, lags):
    first = 5 - len(lags)
    steps = [(p + lag, k + first, p) for p in range(count) for k, lag in enumerate(lags)]
    return [(p, phase) for _, phase, p in sorted(steps)]


def gather_kernel(outer, pieces, count, *refs):
    greet(outer)
    work = Gather(outer, pieces, refs[:count], refs[count : 2 * count], *refs[2 * count :])
    work.start()
    for p, phase in steps_in_order(len(pieces), (1, 2, 4, 6)):
        work.act(phase, p)
    work.end()


def gather_all(outer, shards, pieces):
    count = len(shards)
    return pl.pallas_call(
        functools.partial(gather_kernel, outer, pieces, count),
        out_shape=[
            jax.ShapeDtypeStruct((outer, 2, 2, 2) + shard.shape, shard.dtype) for shard in shards
        ],
        in_specs=[pl.BlockSpec(memory_space=pltpu.VMEM)] * count,
        out_specs=[pl.BlockSpec(memory_space=pl.ANY)] * count,
        scratch_shapes=Gather.semaphores(outer, count, len(pieces)),
        compiler_params=pltpu.CompilerParams(
            collective_id=0, has_side_effects=True, vmem_limit_bytes=VMEM_LIMIT
        ),
    )(*shards)


def scatter_kernel(outer, pieces, count, *refs):
    greet(outer)
    rest = refs[2 * count :]
    work = Scatter(outer, pieces, refs[:count], refs[count : 2 * count], rest[:-3], *rest[-3:])
    for p, phase in steps_in_order(len(pieces), (0, 1, 3, 4, 5)):
        work.act(phase, p)
    work.end()


def scatter_all(outer, terms, pieces):
    count = len(terms)
    shapes = [term.shape[-2:] + (term.dtype,) for term in terms]
    return pl.pallas_call(
        functools.partial(scatter_kernel, outer, pieces, count),
        out_shape=[jax.ShapeDtypeStruct(term.shape[-2:], jnp.float32) for term in terms],
        in_specs=[pl.BlockSpec(memory_space=pl.ANY)] * count,
        out_specs=[pl.BlockSpec(memory_space=pltpu.VMEM)] * count,
        scratch_shapes=Scatter.scratch(outer, shapes, pieces),
        compiler_params=pltpu.CompilerParams(
            collective_id=1, has_side_effects=True, vmem_limit_bytes=VMEM_LIMIT
        ),
    )(*terms)


def cut(shape_list):
    pieces = []
    for i, (rows, columns) in enumerate(shape_list):
        parts, blocks = 1, columns // 128
        if rows % 8 == 0:
            fits = [k for k in range(1, blocks + 1) if blocks % k == 0 and rows * columns // k <= 25000]
            parts = min(fits) if fits else 1
        width = columns // parts
        for k in range(parts):
            pieces.append((i, k * width, width, len(pieces) % 2))
    return pieces


def pack_shape(shape):
    rows, columns = shape
    return shape if rows % 8 == 0 else (rows * columns // 128, 128)


def pack_vectors(parts):
    joined = jnp.concatenate([part.astype(jnp.float32) for part in parts], axis=-1)
    size = -(-joined.shape[-1] // 1024) * 1024
    pad = [(0, 0)] * (joined.ndim - 1) + [(0, size - joined.shape[-1])]
    return jnp.pad(joined, pad).reshape(joined.shape[:-1] + (size // 128, 128))


TILE = 256
PAIR = 128
FIRM = 1e30


def dot_nn(left, right):
    return lax.dot_general(left, right, (((1,), (0,)), ((), ())), preferred_element_type=jnp.float32)


def dot_nt(left, right):
    return lax.dot_general(left, right, (((1,), (1,)), ((), ())), preferred_element_type=jnp.float32)


def dot_tn(left, right):
    return lax.dot_general(left, right, (((0,), (0,)), ((), ())), preferred_element_type=jnp.float32)


def normalize(values):
    average = jnp.mean(values, axis=-1, keepdims=True)
    centered = values - average
    variance = jnp.mean(centered * centered, axis=-1, keepdims=True)
    scale = lax.rsqrt(variance + EPSILON)
    return centered * scale, scale


def norm_grad(upstream, gain, normal, scale):
    inner = upstream * gain
    first = jnp.mean(inner, axis=-1, keepdims=True)
    second = jnp.mean(inner * normal, axis=-1, keepdims=True)
    return scale * (inner - first - normal * second)


def column_sum(values):
    return jnp.sum(values, axis=0, keepdims=True)


def project_kernel(x_ref, prev_ref, weight_ref, vectors_ref, normed_ref, q_ref, k_ref, v_ref):
    tile = pl.program_id(1)
    width = x_ref.shape[-1]
    x = jnp.where(tile == 0, prev_ref[0], x_ref[0]).astype(jnp.float32)
    normal, _ = normalize(x)
    normed = (normal * vectors_ref[0:1] + vectors_ref[1:2]).astype(jnp.bfloat16)
    normed_ref[0] = normed

    @pl.when(tile > 0)
    def _():
        queries = dot_nn(normed, weight_ref[:, :width]) + vectors_ref[2:3]
        q_ref[0] = queries.astype(jnp.bfloat16) * jnp.bfloat16(1.0 / math.sqrt(HD))

    k_ref[0] = dot_nn(normed, weight_ref[:, width : 2 * width]).astype(jnp.bfloat16)
    values = dot_nn(normed, weight_ref[:, 2 * width :]) + vectors_ref[3:4]
    v_ref[0] = values.astype(jnp.bfloat16)


def project(tokens, prev, weight, vectors):
    rows, local, width = tokens.shape
    tiles = local // TILE
    here = lambda r, t: (r, jnp.maximum(t - 1, 0), 0)
    extended = jax.ShapeDtypeStruct((rows, local + TILE, width), jnp.bfloat16)
    return pl.pallas_call(
        project_kernel,
        grid=(rows, tiles + 1),
        in_specs=[
            pl.BlockSpec((1, TILE, width), here),
            pl.BlockSpec((1, TILE, width), lambda r, t: (r, 0, 0)),
            pl.BlockSpec(weight.shape, lambda r, t: (0, 0)),
            pl.BlockSpec(vectors.shape, lambda r, t: (0, 0)),
        ],
        out_specs=[
            pl.BlockSpec((1, TILE, width), lambda r, t: (r, t, 0)),
            pl.BlockSpec((1, TILE, width), here),
            pl.BlockSpec((1, TILE, width), lambda r, t: (r, t, 0)),
            pl.BlockSpec((1, TILE, width), lambda r, t: (r, t, 0)),
        ],
        out_shape=[extended, jax.ShapeDtypeStruct(tokens.shape, jnp.bfloat16), extended, extended],
        compiler_params=pltpu.CompilerParams(vmem_limit_bytes=VMEM_LIMIT),
    )(tokens, prev, weight, vectors)


def lane_index(rows):
    return lax.broadcasted_iota(jnp.int32, (rows, PAIR), 1)


def mask_columns(starts_ref, row, q_cols, k_cols):
    place = lax.broadcasted_iota(jnp.int32, (TILE, PAIR), 0)
    lane = lane_index(TILE)
    for tile in range(2):
        before, start = starts_ref[row, tile], starts_ref[row, tile + 1]
        late = jnp.where(place >= start, 1.0, 0.0)
        q_cols[tile] = jnp.where(lane == 0, late, jnp.where(lane == 1, 1.0, 0.0)).astype(jnp.bfloat16)
        early = jnp.where(place < before, -FIRM, 0.0)
        k_cols[tile, 0] = jnp.where(
            lane == 0, -FIRM, jnp.where(lane == 1, early, 0.0)
        ).astype(jnp.bfloat16)
        early = jnp.where(place < start, -FIRM, 0.0)
        k_cols[tile, 1] = jnp.where(lane == 0, early, 0.0).astype(jnp.bfloat16)


def attend_kernel(starts_ref, q_ref, k_ref, v_ref, probs_ref, out_ref, inverse_ref, q_cols, k_cols):
    row = pl.program_id(0)

    @pl.when(pl.program_id(1) == 0)
    def _():
        mask_columns(starts_ref, row, q_cols, k_cols)

    lane = lane_index(TILE)
    causal = lax.broadcasted_iota(jnp.int32, (TILE, TILE), 1) <= lax.broadcasted_iota(
        jnp.int32, (TILE, TILE), 0
    )
    ones = jnp.ones((TILE, PAIR), jnp.bfloat16)
    for tile in range(2):
        queries = q_ref[0, pl.ds(tile * TILE, TILE)]
        keys = [
            jnp.concatenate([k_ref[0, pl.ds((tile + w) * TILE, TILE)], k_cols[tile, w]], axis=1)
            for w in range(2)
        ]
        values = [
            jnp.concatenate([v_ref[0, pl.ds((tile + w) * TILE, TILE)], ones], axis=1)
            for w in range(2)
        ]
        mixed, inverse = [], []
        for head in range(2):
            mine = (lane < HD) if head == 0 else (lane >= HD)
            left = jnp.concatenate([jnp.where(mine, queries, jnp.bfloat16(0)), q_cols[tile]], axis=1)
            far = dot_nt(left, keys[0])
            near = jnp.where(causal, dot_nt(left, keys[1]), -FIRM)
            top = jnp.max(jnp.maximum(far, near), axis=-1, keepdims=True)
            far = jnp.exp(far - top).astype(jnp.bfloat16)
            near = jnp.exp(near - top).astype(jnp.bfloat16)
            probs_ref[0, 0, tile, head, 0] = far
            probs_ref[0, 0, tile, head, 1] = near
            total = dot_nn(far, values[0]) + dot_nn(near, values[1])
            share = 1.0 / total[:, PAIR:]
            mixed.append(total[:, :PAIR] * share)
            inverse.append(share)
        out_ref[0, pl.ds(tile * TILE, TILE)] = jnp.where(lane < HD, mixed[0], mixed[1]).astype(
            jnp.bfloat16
        )
        inverse_ref[0, pl.ds(tile * TILE, TILE)] = jnp.where(lane < HD, inverse[0], inverse[1])


def attend(starts, q, k, v):
    rows, local, width = q.shape
    pairs = width // PAIR
    by_pair = lambda r, j: (r, 0, j)
    return pl.pallas_call(
        attend_kernel,
        grid=(rows, pairs),
        in_specs=[
            pl.BlockSpec(memory_space=pltpu.SMEM),
            pl.BlockSpec((1, local, PAIR), by_pair),
            pl.BlockSpec((1, local + TILE, PAIR), by_pair),
            pl.BlockSpec((1, local + TILE, PAIR), by_pair),
        ],
        out_specs=[
            pl.BlockSpec((1, 1, 2, 2, 2, TILE, TILE), lambda r, j: (r, j, 0, 0, 0, 0, 0)),
            pl.BlockSpec((1, local, PAIR), by_pair),
            pl.BlockSpec((1, local, PAIR), by_pair),
        ],
        out_shape=[
            jax.ShapeDtypeStruct((rows, pairs, 2, 2, 2, TILE, TILE), jnp.bfloat16),
            jax.ShapeDtypeStruct((rows, local, width), jnp.bfloat16),
            jax.ShapeDtypeStruct((rows, local, width), jnp.float32),
        ],
        scratch_shapes=[
            pltpu.VMEM((2, TILE, PAIR), jnp.bfloat16),
            pltpu.VMEM((2, 2, TILE, PAIR), jnp.bfloat16),
        ],
        compiler_params=pltpu.CompilerParams(vmem_limit_bytes=VMEM_LIMIT),
    )(starts, q, k, v)


def attend_grad_kernel(
    probs_ref, q_ref, k_ref, v_ref, grad_ref, out_ref, inverse_ref, dq_ref, dk_ref, dv_ref, dk_sum, dv_sum
):
    lane = lane_index(TILE)
    ones = jnp.ones((TILE, PAIR), jnp.bfloat16)
    for tile in range(2):
        span = pl.ds(tile * TILE, TILE)
        queries = q_ref[0, span]
        scaled = (grad_ref[0, span].astype(jnp.float32) * inverse_ref[0, span]).astype(jnp.bfloat16)
        product = scaled.astype(jnp.float32) * out_ref[0, span].astype(jnp.float32)
        d_queries = []
        for head in range(2):
            mine = (lane < HD) if head == 0 else (lane >= HD)
            delta = -jnp.sum(jnp.where(mine, product, 0.0), axis=-1, keepdims=True)
            high = delta.astype(jnp.bfloat16).astype(jnp.float32)
            extra = jnp.where(lane == 0, high, jnp.where(lane == 1, delta - high, 0.0))
            grads = jnp.where(mine, scaled, jnp.bfloat16(0))
            mine_queries = jnp.where(mine, queries, jnp.bfloat16(0))
            left = jnp.concatenate([grads, extra.astype(jnp.bfloat16)], axis=1)
            d_query = None
            for w in range(2):
                at = pl.ds((tile + w) * TILE, TILE)
                right = jnp.concatenate([v_ref[0, at], ones], axis=1)
                probs = probs_ref[0, 0, tile, head, w]
                d_score = (probs.astype(jnp.float32) * dot_nt(left, right)).astype(jnp.bfloat16)
                part = dot_nn(d_score, k_ref[0, at])
                d_query = part if w == 0 else d_query + part
                d_key = dot_tn(d_score, mine_queries)
                d_value = dot_tn(probs, grads)
                if head == 0 and (w == 1 or tile == 0):
                    dk_sum[at] = d_key
                    dv_sum[at] = d_value
                else:
                    dk_sum[at] += d_key
                    dv_sum[at] += d_value
            d_queries.append(d_query)
        dq = jnp.where(lane < HD, d_queries[0], d_queries[1]) * (1.0 / math.sqrt(HD))
        dq_ref[0, span] = dq.astype(jnp.bfloat16)
    dk_ref[0] = dk_sum[...].astype(jnp.bfloat16)
    dv_ref[0] = dv_sum[...].astype(jnp.bfloat16)


def attend_grad(probs, q, k, v, grad, out, inverse):
    rows, local, width = q.shape
    pairs = width // PAIR
    by_pair = lambda r, j: (r, 0, j)
    small = pl.BlockSpec((1, local, PAIR), by_pair)
    large = pl.BlockSpec((1, local + TILE, PAIR), by_pair)
    return pl.pallas_call(
        attend_grad_kernel,
        grid=(rows, pairs),
        in_specs=[
            pl.BlockSpec((1, 1, 2, 2, 2, TILE, TILE), lambda r, j: (r, j, 0, 0, 0, 0, 0)),
            small,
            large,
            large,
            small,
            small,
            small,
        ],
        out_specs=[small, large, large],
        out_shape=[
            jax.ShapeDtypeStruct(q.shape, jnp.bfloat16),
            jax.ShapeDtypeStruct(k.shape, jnp.bfloat16),
            jax.ShapeDtypeStruct(k.shape, jnp.bfloat16),
        ],
        scratch_shapes=[
            pltpu.VMEM((local + TILE, PAIR), jnp.float32),
            pltpu.VMEM((local + TILE, PAIR), jnp.float32),
        ],
        compiler_params=pltpu.CompilerParams(vmem_limit_bytes=VMEM_LIMIT),
    )(probs, q, k, v, grad, out, inverse)


def gelu_pair(v):
    square = v * v
    half = 0.5 + 0.5 * jnp.tanh(v * (GELU_SCALE + (GELU_SCALE * 0.044715) * square))
    hidden = v * half
    slope = half + hidden * (1.0 - half) * (2.0 * GELU_SCALE + (6.0 * GELU_SCALE * 0.044715) * square)
    return hidden, slope


MLP_TILE = 256
CHUNK = 768


def mlp_kernel(
    x_hbm, att_hbm, dy_hbm, attn_hbm, fc_hbm, proj_hbm, vectors,
    out_hbm, middle_grad_hbm, att_grad_hbm, attn_grad_hbm, fc_grad_hbm, proj_grad_hbm, sums_ref,
    x, att, dy, attn, fc, proj, hidden, pre_grad, normed, branch, out, middle_grad, att_grad,
    attn_grad, fc_grad, proj_grad, in_sem, out_sem,
):
    tokens, width = x.shape
    chunks = fc.shape[1] // CHUNK
    tiles = tokens // MLP_TILE
    loads = [
        pltpu.make_async_copy(src, dst, in_sem.at[i])
        for i, (src, dst) in enumerate(
            ((att_hbm, att), (attn_hbm, attn), (x_hbm, x), (fc_hbm, fc), (dy_hbm, dy), (proj_hbm, proj))
        )
    ]
    for load in loads:
        load.start()
    sums_ref[...] = jnp.zeros_like(sums_ref)
    for load in loads[:3]:
        load.wait()

    def tile_step(t, carry):
        span = pl.ds(pl.multiple_of(t * MLP_TILE, MLP_TILE), MLP_TILE)
        middle = x[span].astype(jnp.float32) + dot_nn(att[span], attn[...]) + vectors[4:5]
        normal, scale = normalize(middle)
        low = (normal * vectors[5:6] + vectors[6:7]).astype(jnp.bfloat16)
        normed[span] = low

        @pl.when(t == 0)
        def _():
            for load in loads[3:]:
                load.wait()

        upstream = dy[span]
        result = middle + vectors[7:8]
        back = None
        for j in range(chunks):
            columns = pl.ds(j * CHUNK, CHUNK)
            pre = dot_nn(low, fc[:, columns]) + vectors[8 + j : 9 + j]
            value, slope = gelu_pair(pre)
            value = value.astype(jnp.bfloat16)
            hidden[span, columns] = value
            grad = dot_nt(upstream, proj[columns]) * slope
            grad = grad.astype(jnp.bfloat16)
            pre_grad[span, columns] = grad
            sums_ref[4 + j : 5 + j] += column_sum(grad.astype(jnp.float32))
            result = result + dot_nn(value, proj[columns])
            part = dot_nt(grad, fc[:, columns])
            back = part if back is None else back + part
        out[span] = result.astype(jnp.bfloat16)
        upstream = upstream.astype(jnp.float32)
        sums_ref[0:1] += column_sum(upstream)
        sums_ref[1:2] += column_sum(back * normal)
        sums_ref[2:3] += column_sum(back)
        total = upstream + norm_grad(back, vectors[5:6], normal, scale)
        middle_grad[span] = total
        total = total.astype(jnp.bfloat16)
        branch[span] = total
        sums_ref[3:4] += column_sum(total.astype(jnp.float32))
        att_grad[span] = dot_nt(total, attn[...]).astype(jnp.bfloat16)
        return carry

    lax.fori_loop(0, tiles, tile_step, 0)
    stores = []

    def store(src, dst):
        copy = pltpu.make_async_copy(src, dst, out_sem.at[len(stores)])
        copy.start()
        stores.append(copy)

    store(out, out_hbm)
    store(middle_grad, middle_grad_hbm)
    store(att_grad, att_grad_hbm)
    for j in range(chunks):
        columns = pl.ds(j * CHUNK, CHUNK)
        proj_grad[columns] = dot_tn(hidden[:, columns], dy[...]).astype(jnp.bfloat16)
        store(proj_grad.at[columns], proj_grad_hbm.at[columns])
    for j in range(chunks):
        columns = pl.ds(j * CHUNK, CHUNK)
        fc_grad[:, columns] = dot_tn(normed[...], pre_grad[:, columns]).astype(jnp.bfloat16)
        store(fc_grad.at[:, columns], fc_grad_hbm.at[:, columns])
    attn_grad[...] = dot_tn(att[...], branch[...]).astype(jnp.bfloat16)
    store(attn_grad, attn_grad_hbm)
    for copy in stores:
        copy.wait()


def mlp(x, att, dy, attn, fc, proj, vectors):
    tokens, width = x.shape
    hidden = fc.shape[1]
    low, full = jnp.bfloat16, jnp.float32
    anywhere = pl.BlockSpec(memory_space=pl.ANY)
    vmem = pl.BlockSpec(memory_space=pltpu.VMEM)
    return pl.pallas_call(
        mlp_kernel,
        in_specs=[anywhere] * 6 + [vmem],
        out_specs=[anywhere] * 6 + [vmem],
        out_shape=[
            jax.ShapeDtypeStruct((tokens, width), low),
            jax.ShapeDtypeStruct((tokens, width), full),
            jax.ShapeDtypeStruct((tokens, width), low),
            jax.ShapeDtypeStruct(attn.shape, low),
            jax.ShapeDtypeStruct(fc.shape, low),
            jax.ShapeDtypeStruct(proj.shape, low),
            jax.ShapeDtypeStruct((8, width), full),
        ],
        scratch_shapes=[
            pltpu.VMEM((tokens, width), low),
            pltpu.VMEM((tokens, width), low),
            pltpu.VMEM((tokens, width), low),
            pltpu.VMEM(attn.shape, low),
            pltpu.VMEM(fc.shape, low),
            pltpu.VMEM(proj.shape, low),
            pltpu.VMEM((tokens, hidden), low),
            pltpu.VMEM((tokens, hidden), low),
            pltpu.VMEM((tokens, width), low),
            pltpu.VMEM((tokens, width), low),
            pltpu.VMEM((tokens, width), low),
            pltpu.VMEM((tokens, width), full),
            pltpu.VMEM((tokens, width), low),
            pltpu.VMEM(attn.shape, low),
            pltpu.VMEM(fc.shape, low),
            pltpu.VMEM(proj.shape, low),
            pltpu.SemaphoreType.DMA((6,)),
            pltpu.SemaphoreType.DMA((12,)),
        ],
        compiler_params=pltpu.CompilerParams(vmem_limit_bytes=VMEM_LIMIT),
    )(x, att, dy, attn, fc, proj, vectors)


def project_grad_kernel(normed, dq, dk, dv, weight, weight_grad, prev_grad, sums):
    rows, extended, width = normed.shape
    local = dq.shape[1]
    third = [pl.ds(i * width, width) for i in range(3)]
    for r in range(rows):
        head = pl.ds(0, TILE)
        prev_grad[r] = (
            dot_nt(dk[r, head], weight[:, third[1]]) + dot_nt(dv[r, head], weight[:, third[2]])
        ).astype(jnp.bfloat16)
    total = None
    for i, grads in enumerate((dq, dk, dv)):
        total = None
        for r in range(rows):
            left = normed[r, TILE:] if i == 0 else normed[r]
            part = dot_tn(left, grads[r])
            total = part if total is None else total + part
        weight_grad[:, third[i]] = total.astype(jnp.bfloat16)
    sums[...] = jnp.zeros_like(sums)
    for r in range(rows):
        sums[0:1] += column_sum(dq[r].astype(jnp.float32))
        sums[1:2] += column_sum(dv[r].astype(jnp.float32))


def project_grad(normed, dq, dk, dv, weight):
    rows, extended, width = normed.shape
    vmem = pl.BlockSpec(memory_space=pltpu.VMEM)
    return pl.pallas_call(
        project_grad_kernel,
        in_specs=[vmem] * 5,
        out_specs=[vmem] * 3,
        out_shape=[
            jax.ShapeDtypeStruct(weight.shape, jnp.bfloat16),
            jax.ShapeDtypeStruct((rows, TILE, width), jnp.bfloat16),
            jax.ShapeDtypeStruct((8, width), jnp.float32),
        ],
        compiler_params=pltpu.CompilerParams(vmem_limit_bytes=VMEM_LIMIT),
    )(normed, dq, dk, dv, weight)


def tokens_grad_kernel(x_ref, dq, dk, dv, weight, late, middle_grad, vectors, out_ref, sums):
    row, tile = pl.program_id(0), pl.program_id(1)
    width = x_ref.shape[-1]

    @pl.when((row == 0) & (tile == 0))
    def _():
        sums[...] = jnp.zeros_like(sums)

    back = dot_nt(dq[0], weight[:, :width])
    back = back + dot_nt(dk[0], weight[:, width : 2 * width])
    back = back + dot_nt(dv[0], weight[:, 2 * width :])
    back = back + jnp.where(tile == pl.num_programs(1) - 1, late[0].astype(jnp.float32), 0.0)
    normal, scale = normalize(x_ref[0].astype(jnp.float32))
    sums[0:1] += column_sum(back * normal)
    sums[1:2] += column_sum(back)
    out_ref[0] = middle_grad[0] + norm_grad(back, vectors[0:1], normal, scale)


def tokens_grad_of(x, dq, dk, dv, weight, late, middle_grad, vectors):
    rows, local, width = x.shape
    block = lambda shift: pl.BlockSpec((1, TILE, width), lambda r, t: (r, t + shift, 0))
    whole = lambda v: pl.BlockSpec(v.shape, lambda r, t: (0, 0))
    return pl.pallas_call(
        tokens_grad_kernel,
        grid=(rows, local // TILE),
        in_specs=[
            block(0),
            block(0),
            block(1),
            block(1),
            whole(weight),
            pl.BlockSpec((1, TILE, width), lambda r, t: (r, 0, 0)),
            block(0),
            whole(vectors),
        ],
        out_specs=[block(0), pl.BlockSpec((8, width), lambda r, t: (0, 0))],
        out_shape=[
            jax.ShapeDtypeStruct(x.shape, jnp.float32),
            jax.ShapeDtypeStruct((8, width), jnp.float32),
        ],
        compiler_params=pltpu.CompilerParams(vmem_limit_bytes=VMEM_LIMIT),
    )(x, dq, dk, dv, weight, late, middle_grad, vectors)


def spread_vectors(slots, size, fc_size, width):
    outer = slots.shape[0]
    zeros = jnp.zeros((8, width - PAIR), jnp.float32)
    first, second = None, None
    for d in range(outer * 8):
        index = (d // 8, (d // 4) % 2, (d // 2) % 2, d % 2)
        top = jnp.concatenate([slots[index + (slice(0, 8),)], zeros], axis=1)
        low = jnp.concatenate([slots[index + (slice(8, 16),)], zeros], axis=1)
        top = pltpu.roll(top, d * size, 1) if d else top
        row, lane = divmod(d * fc_size, width)
        low = pltpu.roll(low, lane, 1) if lane else low
        low = pltpu.roll(low, row, 0) if row else low
        first = top if first is None else first + top
        second = low if second is None else second + low
    return first, second


def join_rows(target, slots, columns):
    outer, rows = slots.shape[0], slots.shape[-2]

    def body(a, carry):
        for y in range(2):
            for c in range(2):
                both = [slots[a, y, c, s, :, columns].astype(jnp.float32) for s in range(2)]
                start = pl.multiple_of(((a * 2 + y) * 2 + c) * (2 * rows), 2 * rows)
                joined = jnp.concatenate(both, axis=0).astype(target.dtype)
                target[pl.ds(start, 2 * rows), columns] = joined
        return carry

    lax.fori_loop(0, outer, body, 0)


VECTORS = 9


FORWARD_ORDERS = (0, 0, 1, 1, 1, 1, 1, 1, 1, 0, 0, 1, 1, 0, 1)
PREV_AFTER, EAGER = (2, 5), 99
FORWARD_PLAN = {'ln': [(1, 0), (1, 1), (1, 2), (1, 3), (2, 0), (1, 4), (2, 1), (2, 2), (1, 5), (2, 3), (1, 6), (3, 0), (2, 4), (1, 7), (4, 0)], 'q': [(3, 1), (3, 2), (3, 3), (2, 5), (1, 8), (2, 6), (1, 9), (4, 1), (2, 7), (4, 2), (3, 4)], 'k': [(4, 3), (4, 4), (1, 10)], 'v': [(3, 5), (1, 11), (3, 6), (4, 5), (2, 9), (4, 6)], 'b0': [(1, 12)], 'b3': [(1, 13), (3, 7)], 'b4': [(2, 10)], 'b5': [(4, 7), (1, 14), (2, 8), (2, 13), (2, 11)], 'a2': [(3, 8), (3, 9)], 'a4': [(4, 8), (2, 12), (4, 9)], 'a5': [(3, 11)], 'm1': [(3, 10), (4, 11)], 'm2': [(2, 14), (4, 10)], 'm4': [(3, 12)], 'm7': [(4, 12), (3, 13)], 'w1': [(3, 14)], 'w2': [(4, 13)], 'end': [(4, 14)]}


def forward_kernel(outer, pieces, *refs):
    tokens_hbm, dy_hbm, starts_ref = refs[:3]
    vector_refs = refs[3 : 3 + VECTORS]
    shards = refs[3 + VECTORS : 7 + VECTORS]
    (
        normed_hbm, q_hbm, k_hbm, v_hbm, probs_hbm, att_hbm, hidden_hbm, slope_hbm, middle_hbm,
        normed2_hbm, qkv_hbm, attn_hbm, fc_hbm, proj_slots, terms_hbm, vectors,
    ) = refs[7 + VECTORS : 23 + VECTORS]
    (
        own, vector_slots, qkv_slots, attn_slots, fc_slots, qkv, attn, fc, x, normed, q, k, v, probs, att,
        hidden, slope, middle, normed2, dy, terms, q_cols, k_cols,
        move_sem, out_sem, probs_sem, terms_sem, own_sem, send_sem, recv_sem,
    ) = refs[23 + VECTORS :]
    rows, local, width = q.shape
    a, y, c, s = place()
    size, fc_size = vector_refs[0].shape[1], vector_refs[-1].shape[1]
    pairs, chunks = width // PAIR, fc.shape[1] // CHUNK

    load = pltpu.make_async_copy(tokens_hbm, x.at[:, pl.ds(TILE, local)], move_sem.at[0])
    load_dy = pltpu.make_async_copy(dy_hbm, dy, move_sem.at[3])
    load.start()
    own[...] = jnp.zeros_like(own)
    for i, ref in enumerate(vector_refs):
        own[i : i + 1, : ref.shape[1]] = ref[...].astype(jnp.float32)
    greet(outer)
    prev = remote(
        tokens_hbm.at[:, pl.ds(local - TILE, TILE)],
        x.at[:, pl.ds(0, TILE)],
        move_sem.at[1],
        move_sem.at[2],
        device(a, y, c, 1 - s),
    )
    work = Gather(
        outer,
        pieces,
        (own,) + shards,
        (vector_slots, qkv_slots, attn_slots, fc_slots, proj_slots),
        own_sem,
        send_sem,
        recv_sem,
        EAGER,
    )
    work.start()
    load_dy.start()

    def start_prev():
        @pl.when(s == 0)
        def _():
            prev.start()

    work.after = {PREV_AFTER: start_prev}
    comm, comm_at = sites_of(work, FORWARD_PLAN)
    stores = []

    def store(src, dst):
        copy = pltpu.make_async_copy(src, dst, out_sem.at[len(stores)])
        copy.start()
        stores.append(copy)

    @pl.when(s == 0)
    def _():
        for r in range(rows):
            x[r, 0:TILE] = jnp.zeros((TILE, width), x.dtype)

    for r in range(rows):
        mask_columns(starts_ref, r, q_cols.at[r], k_cols.at[r])
    load.wait()
    comm("ln")
    first, second = spread_vectors(vector_slots, size, fc_size, width)
    vectors[0:8], vectors[8:16] = first, second

    def norm_tile(r, span):
        normal, _ = normalize(x[r, span].astype(jnp.float32))
        normed[r, span] = (normal * vectors[0:1] + vectors[1:2]).astype(jnp.bfloat16)

    def norm_step(n, carry):
        r, t = n // (local // TILE), lax.rem(n, local // TILE) + 1
        norm_tile(r, pl.ds(pl.multiple_of(t * TILE, TILE), TILE))
        return carry

    lax.fori_loop(0, rows * (local // TILE), norm_step, 0)
    third = [slice(i * width, (i + 1) * width) for i in range(3)]
    for i, site in enumerate(("q", "k", "v")):
        comm(site)
        join_rows(qkv, qkv_slots, third[i])

        def row_step(r, carry):
            value = dot_nn(normed[r, TILE:], qkv[:, third[i]])
            if i == 0:
                value = (value + vectors[2:3]).astype(jnp.bfloat16)
                q[r] = value * jnp.bfloat16(1.0 / math.sqrt(HD))
            elif i == 1:
                k[r, TILE:] = value.astype(jnp.bfloat16)
            else:
                v[r, TILE:] = (value + vectors[3:4]).astype(jnp.bfloat16)
            return carry

        lax.fori_loop(0, rows, row_step, 0)
    store(q, q_hbm)
    store(qkv, qkv_hbm)
    lane = lane_index(TILE)
    causal = lax.broadcasted_iota(jnp.int32, (TILE, 2 * TILE), 0) <= (
        lax.broadcasted_iota(jnp.int32, (TILE, 2 * TILE), 1) & (TILE - 1)
    )

    def probs_copy(slot, r, j, tile):
        part = probs_hbm.at[r, j, :, pl.ds(tile * 4 * TILE, 4 * TILE)]
        return pltpu.make_async_copy(probs.at[slot], part, probs_sem.at[slot])

    def attend_pair(r, j, tile, slot):
        pair = pl.ds(pl.multiple_of(j * PAIR, PAIR), PAIR)
        queries = q[r, tile * TILE : (tile + 1) * TILE, pair]
        left = []
        for head in range(2):
            mine = (lane < HD) if head == 0 else (lane >= HD)
            mine = jnp.where(mine, queries, jnp.bfloat16(0))
            left.append(jnp.concatenate([mine, q_cols[r, tile]], axis=1))
        left = jnp.concatenate(left, axis=0)
        scores = []
        for w in range(2):
            keys = k[r, (tile + w) * TILE : (tile + w + 1) * TILE, pair]
            scores.append(dot_nt(jnp.concatenate([keys, k_cols[r, tile, w]], axis=1), left))
        far, near = scores[0], jnp.where(causal, scores[1], -FIRM)
        top = jnp.max(jnp.maximum(far, near), axis=0, keepdims=True)
        far, near = jnp.exp(far - top), jnp.exp(near - top)
        share = 1.0 / jnp.sum(far + near, axis=0, keepdims=True)
        far, near = (far * share).astype(jnp.bfloat16), (near * share).astype(jnp.bfloat16)
        probs[slot, :, 0 : 2 * TILE], probs[slot, :, 2 * TILE :] = far, near
        values = v[r, tile * TILE : (tile + 2) * TILE, pair]
        mixed = []
        for head in range(2):
            part = slice(head * TILE, (head + 1) * TILE)
            mixed.append(dot_tn(jnp.concatenate([far[:, part], near[:, part]], axis=0), values))
        span = pl.ds(pl.multiple_of(r * local + tile * TILE, TILE), TILE)
        att[span, pair] = jnp.where(lane < HD, mixed[0], mixed[1]).astype(jnp.bfloat16)

    def attend_step(n, tile, index):
        r, j = n // (pairs // 2), lax.rem(n, pairs // 2) * 2
        slot = lax.rem(n, 2) * 2

        @pl.when(n + index * rows * pairs // 2 >= 2)
        def _():
            for i in range(2):
                probs_copy(slot + i, r, j + i, tile).wait()

        for i in range(2):
            attend_pair(r, j + i, tile, slot + i)
        for i in range(2):
            probs_copy(slot + i, r, j + i, tile).start()

    def late_step(n, carry):
        comm_at(n, "b", rows * pairs // 2)
        attend_step(n, 1, 0)
        return carry

    lax.fori_loop(0, rows * pairs // 2, late_step, 0)
    comm("prev")

    @pl.when(s == 1)
    def _():
        prev.wait_recv()

    for r in range(rows):
        norm_tile(r, slice(0, TILE))
        k[r, 0:TILE] = dot_nn(normed[r, 0:TILE], qkv[:, third[1]]).astype(jnp.bfloat16)
        value = dot_nn(normed[r, 0:TILE], qkv[:, third[2]]) + vectors[3:4]
        v[r, 0:TILE] = value.astype(jnp.bfloat16)
    store(normed, normed_hbm)
    store(k, k_hbm)
    store(v, v_hbm)

    def early_step(n, carry):
        comm_at(n, "a", rows * pairs // 2)
        attend_step(n, 0, 1)
        return carry

    lax.fori_loop(0, rows * pairs // 2, early_step, 0)
    store(att, att_hbm)
    comm("asm")
    join_rows(attn, attn_slots, slice(0, width))
    store(attn, attn_hbm)

    def mlp_step(r, carry):
        span = pl.ds(pl.multiple_of(r * local, TILE), local)
        value = x[r, TILE:].astype(jnp.float32) + dot_nn(att[span], attn[...]) + vectors[4:5]
        middle[span] = value
        normal, _ = normalize(value)
        low = (normal * vectors[5:6] + vectors[6:7]).astype(jnp.bfloat16)
        normed2[span] = low
        for j in range(chunks):
            for row in range(rows):
                if row == 0 or f"m{row * chunks + j}" in FORWARD_PLAN:

                    @pl.when(r == row)
                    def _():
                        comm(f"m{row * chunks + j}")
                        if row == 0:
                            join_rows(fc, fc_slots, slice(j * CHUNK, (j + 1) * CHUNK))

            columns = pl.ds(j * CHUNK, CHUNK)
            pre = dot_nn(low, fc[:, columns]) + vectors[8 + j : 9 + j]
            value, back = gelu_pair(pre)
            hidden[span, columns] = value.astype(jnp.bfloat16)
            slope[span, columns] = back.astype(jnp.bfloat16)
        return carry

    lax.fori_loop(0, rows, mlp_step, 0)
    store(slope, slope_hbm)
    store(hidden, hidden_hbm)
    store(middle, middle_hbm)
    store(normed2, normed2_hbm)
    store(fc, fc_hbm)
    load_dy.wait()
    share = terms.shape[-2]
    each = CHUNK // (8 * share)
    terms_copies = []
    for j in range(chunks):
        comm(f"w{j}")
        grad = dot_tn(hidden[:, j * CHUNK : (j + 1) * CHUNK], dy[...]).astype(jnp.bfloat16)
        if j >= 2:
            terms_copies[j - 2].wait()
        terms[j % 2] = grad.reshape((each, 2, 2, 2, share, width))
        copy = pltpu.make_async_copy(
            terms.at[j % 2], terms_hbm.at[pl.ds(j * each, each)], terms_sem.at[j % 2]
        )
        copy.start()
        terms_copies.append(copy)
    comm("end")
    work.end()
    for copy in terms_copies[-2:]:
        copy.wait()
    for n in range(4):
        probs_copy(n, 0, n, 0).wait()
    for copy in stores:
        copy.wait()

    @pl.when(s == 0)
    def _():
        prev.wait_send()


def forward(outer, tokens, dy, starts, vectors, weights):
    rows, local, width = tokens.shape
    devices = outer * 8
    low, full = jnp.bfloat16, jnp.float32
    pairs = width // PAIR
    qkv_weight, attn_weight, fc_weight, proj_weight = weights
    hidden = fc_weight.shape[1]
    half = width // 2
    pieces = [(0, 0, PAIR)] + [(1, i * half, half) for i in range(6)] + [(2, 0, width)]
    pieces += [(3, j * CHUNK, CHUNK) for j in range(hidden // CHUNK)]
    pieces += [(4, j * 2 * PAIR, 2 * PAIR) for j in range(width // (2 * PAIR))]
    pieces = [piece + (order,) for piece, order in zip(pieces, FORWARD_ORDERS)]
    anywhere = pl.BlockSpec(memory_space=pl.ANY)
    vmem = pl.BlockSpec(memory_space=pltpu.VMEM)
    extended = (rows, local + TILE, width)
    flat = (rows * local, width)
    whole = [(devices * weight.shape[0], weight.shape[1]) for weight in weights]
    slots = [(outer, 2, 2, 2) + weight.shape for weight in weights]
    shape = jax.ShapeDtypeStruct
    results = pl.pallas_call(
        functools.partial(forward_kernel, outer, pieces),
        in_specs=[anywhere] * 2 + [pl.BlockSpec(memory_space=pltpu.SMEM)] + [vmem] * (VECTORS + 4),
        out_specs=[anywhere] * 15 + [vmem],
        out_shape=[
            shape(extended, low),
            shape(tokens.shape, low),
            shape(extended, low),
            shape(extended, low),
            shape((rows, pairs, TILE, 8 * TILE), low),
            shape(flat, low),
            shape((rows * local, hidden), low),
            shape((rows * local, hidden), low),
            shape(flat, full),
            shape(flat, low),
            shape(whole[0], low),
            shape(whole[1], low),
            shape(whole[2], low),
            shape(slots[3], low),
            shape(slots[3], low),
            shape((16, width), full),
        ],
        scratch_shapes=[
            pltpu.VMEM((16, PAIR), full),
            pltpu.VMEM((outer, 2, 2, 2, 16, PAIR), full),
            pltpu.VMEM(slots[0], low),
            pltpu.VMEM(slots[1], low),
            pltpu.VMEM(slots[2], low),
            pltpu.VMEM(whole[0], low),
            pltpu.VMEM(whole[1], low),
            pltpu.VMEM(whole[2], low),
            pltpu.VMEM(extended, low),
            pltpu.VMEM(extended, low),
            pltpu.VMEM(tokens.shape, low),
            pltpu.VMEM(extended, low),
            pltpu.VMEM(extended, low),
            pltpu.VMEM((4, TILE, 4 * TILE), low),
            pltpu.VMEM(flat, low),
            pltpu.VMEM((rows * local, hidden), low),
            pltpu.VMEM((rows * local, hidden), low),
            pltpu.VMEM(flat, full),
            pltpu.VMEM(flat, low),
            pltpu.VMEM(flat, low),
            pltpu.VMEM((2, CHUNK // (8 * proj_weight.shape[0])) + slots[3][1:], low),
            pltpu.VMEM((rows, 2, TILE, PAIR), low),
            pltpu.VMEM((rows, 2, 2, TILE, PAIR), low),
            pltpu.SemaphoreType.DMA((4,)),
            pltpu.SemaphoreType.DMA((12,)),
            pltpu.SemaphoreType.DMA((4,)),
            pltpu.SemaphoreType.DMA((2,)),
        ]
        + Gather.semaphores(outer, 5, len(pieces)),
        compiler_params=pltpu.CompilerParams(
            collective_id=2, has_side_effects=True, vmem_limit_bytes=VMEM_LIMIT
        ),
    )(tokens, dy, starts, *[vector.reshape(1, -1) for vector in vectors], *weights)
    return results


def shares_out(rows, columns):
    return jax.ShapeDtypeStruct((rows, columns), jnp.float32)


def column_pieces(array, columns, parts, orders):
    step = columns // parts
    return [(array, j * step, step, orders[j % len(orders)]) for j in range(parts)]


def mlp_scatter_kernel(
    outer, pieces,
    hidden_hbm, slope_hbm, middle_hbm, normed_hbm, att_hbm, dy_hbm, attn_hbm, fc_hbm, proj_hbm, terms, vectors,
    out_hbm, middle_grad_hbm, att_grad_hbm, attn_grad_hbm, fc_grad_hbm, sums_ref, proj_share,
    hidden, slope, middle, normed, att, dy, attn, fc, proj, branch, out, att_grad, attn_grad,
    proj_sem, slope_sem, hidden_sem, fc_sem, in_sem, out_sem, *rest,
):
    tokens, width = dy.shape
    chunks = fc.shape[1] // CHUNK
    block = tokens // 2
    spans = [pl.ds(j * CHUNK, CHUNK) for j in range(chunks)]

    def copies(src, dst, sem, pick):
        return [
            pltpu.make_async_copy(src.at[pick(span)], dst.at[pick(span)], sem.at[j])
            for j, span in enumerate(spans)
        ]

    load_proj = copies(proj_hbm, proj, proj_sem, lambda span: (span,))
    load_slope = copies(slope_hbm, slope, slope_sem, lambda span: (EVERY, span))
    load_hidden = copies(hidden_hbm, hidden, hidden_sem, lambda span: (EVERY, span))
    load_fc = copies(fc_hbm, fc, fc_sem, lambda span: (EVERY, span))
    others = ((dy_hbm, dy), (middle_hbm, middle), (attn_hbm, attn), (normed_hbm, normed), (att_hbm, att))
    load_dy, load_middle, load_attn, load_normed, load_att = [
        pltpu.make_async_copy(src, dst, in_sem.at[i]) for i, (src, dst) in enumerate(others)
    ]
    load_dy.start()
    for j in range(chunks):
        for loads in (load_proj, load_slope, load_hidden, load_fc):
            loads[j].start()
    for load in (load_middle, load_attn, load_normed, load_att):
        load.start()
    greet(outer)
    work = Scatter(outer, pieces, (terms,), (proj_share,), rest[:-3], *rest[-3:])
    comm, comm_at = sites_of(work, MLP_PLAN)
    sums_ref[...] = jnp.zeros_like(sums_ref)
    comm("start")
    load_dy.wait()

    def backward_step(t, carry):
        span = pl.ds(pl.multiple_of(t * block, block), block)
        upstream = dy[span]
        result, back = None, None
        for j in range(chunks):
            @pl.when(t == 0)
            def _():
                for loads in (load_proj, load_slope, load_hidden, load_fc):
                    loads[j].wait()

            comm_at(t * chunks + j, "m", 2 * chunks)

            grad = dot_nt(upstream, proj[spans[j]]) * slope[span, spans[j]].astype(jnp.float32)
            grad = grad.astype(jnp.bfloat16)
            slope[span, spans[j]] = grad
            sums_ref[4 + j : 5 + j] += column_sum(grad.astype(jnp.float32))
            part = dot_nt(grad, fc[:, spans[j]])
            back = part if back is None else back + part
            part = dot_nn(hidden[span, spans[j]], proj[spans[j]])
            result = part if result is None else result + part

        @pl.when(t == 0)
        def _():
            load_middle.wait()
            load_attn.wait()

        value = middle[span]
        out[span] = (result + value + vectors[7:8]).astype(jnp.bfloat16)
        normal, scale = normalize(value)
        upstream = upstream.astype(jnp.float32)
        sums_ref[0:1] += column_sum(upstream)
        sums_ref[1:2] += column_sum(back * normal)
        sums_ref[2:3] += column_sum(back)
        total = upstream + norm_grad(back, vectors[5:6], normal, scale)
        middle[span] = total
        total = total.astype(jnp.bfloat16)
        branch[span] = total
        sums_ref[3:4] += column_sum(total.astype(jnp.float32))
        att_grad[span] = dot_nt(total, attn[...]).astype(jnp.bfloat16)
        return carry

    lax.fori_loop(0, 2, backward_step, 0)
    stores = []

    def store(src, dst):
        copy = pltpu.make_async_copy(src, dst, out_sem.at[len(stores)])
        copy.start()
        stores.append(copy)

    store(out, out_hbm)
    store(middle, middle_grad_hbm)
    store(att_grad, att_grad_hbm)
    load_normed.wait()
    for j in range(chunks):
        comm(f"f{j}")
        hidden[0:width, spans[j]] = dot_tn(normed[...], slope[:, spans[j]]).astype(jnp.bfloat16)
        store(hidden.at[pl.ds(0, width), spans[j]], fc_grad_hbm.at[:, spans[j]])
    load_att.wait()
    comm("attn")
    attn_grad[...] = dot_tn(att[...], branch[...]).astype(jnp.bfloat16)
    store(attn_grad, attn_grad_hbm)
    comm("end")
    work.end()
    for copy in stores:
        copy.wait()


MLP_ORDERS = (1, 0, 0)
MLP_PLAN = {'start': [(0, 0), (0, 1), (0, 2)], 'm2': [(1, 0), (1, 1)], 'm3': [(1, 2)], 'm6': [(2, 0), (2, 1)], 'f1': [(3, 1), (2, 2)], 'f3': [(3, 0)], 'end': [(4, 1), (3, 2), (4, 0), (4, 2)]}


def mlp_scatter(outer, hidden, slope, middle, normed, att, dy, attn, fc, proj, terms, vectors):
    tokens, width = dy.shape
    units = fc.shape[1]
    share = units // (outer * 8)
    chunks = units // CHUNK
    low, full = jnp.bfloat16, jnp.float32
    anywhere = pl.BlockSpec(memory_space=pl.ANY)
    vmem = pl.BlockSpec(memory_space=pltpu.VMEM)
    pieces = column_pieces(0, width, 3, MLP_ORDERS)
    shape = jax.ShapeDtypeStruct
    return pl.pallas_call(
        functools.partial(mlp_scatter_kernel, outer, pieces),
        in_specs=[anywhere] * 10 + [vmem],
        out_specs=[anywhere] * 5 + [vmem] * 2,
        out_shape=[
            shape((tokens, width), low),
            shape((tokens, width), full),
            shape((tokens, width), low),
            shape(attn.shape, low),
            shape(fc.shape, low),
            shape((8, width), full),
            shares_out(share, width),
        ],
        scratch_shapes=[
            pltpu.VMEM((tokens, units), low),
            pltpu.VMEM((tokens, units), low),
            pltpu.VMEM((tokens, width), full),
            pltpu.VMEM((tokens, width), low),
            pltpu.VMEM((tokens, width), low),
            pltpu.VMEM((tokens, width), low),
            pltpu.VMEM(attn.shape, low),
            pltpu.VMEM(fc.shape, low),
            pltpu.VMEM(proj.shape, low),
            pltpu.VMEM((tokens, width), low),
            pltpu.VMEM((tokens, width), low),
            pltpu.VMEM((tokens, width), low),
            pltpu.VMEM(attn.shape, low),
        ]
        + [pltpu.SemaphoreType.DMA((chunks,))] * 4
        + [pltpu.SemaphoreType.DMA((5,)), pltpu.SemaphoreType.DMA((12,))]
        + Scatter.scratch(outer, [(share, width, low)], pieces),
        compiler_params=pltpu.CompilerParams(
            collective_id=3, has_side_effects=True, vmem_limit_bytes=VMEM_LIMIT
        ),
    )(hidden, slope, middle, normed, att, dy, attn, fc, proj, terms, vectors)


def pack_columns(values, start, lanes):
    width = values.shape[1]
    moved = pltpu.roll(values, (width - start) % width, 1) if start % width else values
    return jnp.where(lane_index(values.shape[0]) < lanes, moved[:, :PAIR], 0.0)


def backward_kernel(
    outer, pieces, places, count,
    probs_hbm, q_hbm, k_hbm, v_hbm, normed_hbm, grad_hbm, att_hbm, x_hbm, middle_hbm, weight_hbm,
    vectors, mlp_sums, *refs,
):
    terms, refs = refs[:count], refs[count:]
    tokens_grad_hbm, refs = refs[0], refs[1:]
    shares, vector_share, refs = refs[: count + 1], refs[count + 1], refs[count + 2 :]
    (
        q, k, v, normed, grad, att, x, middle, weight, far_probs, near_probs, dq, dk, dv, dq_part,
        prev, late, qkv_terms, vector_terms, vector_got, sums, in_sem, far_sem, near_sem, out_sem, late_sem,
        vector_send, vector_recv, *rest,
    ) = refs
    rows, local, width = q.shape
    pairs = width // PAIR
    a, y, c, s = place()
    pairs_of_arrays = (
        (q_hbm, q), (k_hbm, k), (v_hbm, v), (grad_hbm, grad), (att_hbm, att),
        (weight_hbm, weight), (normed_hbm, normed), (x_hbm, x), (middle_hbm, middle),
    )
    loads = [
        [pltpu.make_async_copy(src.at[r], dst.at[r], in_sem.at[i, r]) for r in range(rows)]
        for i, (src, dst) in enumerate(pairs_of_arrays[:5])
    ]
    late_loads = [
        pltpu.make_async_copy(src, dst, in_sem.at[5 + i, 0])
        for i, (src, dst) in enumerate(pairs_of_arrays[5:])
    ]
    wide = 2 * TILE

    def far_copy(n):
        part = probs_hbm.at[n // pairs, lax.rem(n, pairs), :, pl.ds(0, wide)]
        return pltpu.make_async_copy(part, far_probs.at[n], far_sem.at[n])

    def near_copy(n):
        slot = lax.rem(n, 4)
        part = probs_hbm.at[lax.rem(n, rows), n // rows, :, pl.ds(wide, 3 * wide)]
        return pltpu.make_async_copy(part, near_probs.at[slot], near_sem.at[slot])

    for r in range(rows):
        for load in loads:
            load[r].start()
        for n in range(r * pairs, (r + 1) * pairs):
            far_copy(n).start()
    for load in late_loads:
        load.start()
    for n in range(4):
        near_copy(n).start()
    greet_all(outer)
    work = Scatter(
        outer, pieces, terms + (qkv_terms,), shares, rest[:-3], *rest[-3:], places
    )
    comm, comm_at = sites_of(work, BACKWARD_PLAN)
    sums[...] = jnp.zeros_like(sums)
    lane = lane_index(TILE)
    ones = jnp.ones((TILE, PAIR), jnp.bfloat16)

    def sides(r, pair, tile):
        span = slice(tile * TILE, (tile + 1) * TILE)
        grads, queries = grad[r, span, pair], q[r, span, pair]
        product = grads.astype(jnp.float32) * att[r, span, pair].astype(jnp.float32)
        left, mine_grads, mine_queries = [], [], []
        for head in range(2):
            mine = (lane < HD) if head == 0 else (lane >= HD)
            delta = -jnp.sum(jnp.where(mine, product, 0.0), axis=-1, keepdims=True)
            high = delta.astype(jnp.bfloat16).astype(jnp.float32)
            extra = jnp.where(lane == 0, high, jnp.where(lane == 1, delta - high, 0.0))
            mine_grads.append(jnp.where(mine, grads, jnp.bfloat16(0)))
            mine_queries.append(jnp.where(mine, queries, jnp.bfloat16(0)))
            left.append(jnp.concatenate([mine_grads[-1], extra.astype(jnp.bfloat16)], axis=1))
        return [jnp.concatenate(part, axis=0) for part in (left, mine_grads, mine_queries)]

    def unit(r, pair, tile, side, chances):
        values = jnp.concatenate([v[r, tile * TILE : (tile + 1) * TILE, pair], ones], axis=1)
        d_score = (chances.astype(jnp.float32) * dot_nt(values, side[0])).astype(jnp.bfloat16)
        span = slice(tile * TILE, (tile + 1) * TILE)
        dk[r, span, pair] = dot_nn(d_score, side[2]).astype(jnp.bfloat16)
        dv[r, span, pair] = dot_nn(chances, side[1]).astype(jnp.bfloat16)
        return d_score

    def heads(parts):
        return jnp.where(lane < HD, parts[0], parts[1])

    far_steps = rows * pairs // 2

    def far_step(n, carry):
        r, j = n // (pairs // 2), lax.rem(n, pairs // 2) * 2
        for row in range(rows):

            @pl.when(n == row * (pairs // 2))
            def _():
                for load in loads:
                    load[row].wait()

        comm_at(n, "f", far_steps)
        for i in range(2):
            far_copy(2 * n + i).wait()
        for i in range(2):
            pair = pl.ds(pl.multiple_of((j + i) * PAIR, PAIR), PAIR)
            d_score = unit(r, pair, 0, sides(r, pair, 0), far_probs[2 * n + i])
            keys = k[r, 0:TILE, pair]
            dq_part[r, :, pair] = heads(
                [dot_tn(d_score[:, h * TILE : (h + 1) * TILE], keys) for h in range(2)]
            )
        return carry

    lax.fori_loop(0, far_steps, far_step, 0)
    for load in late_loads[:2]:
        load.wait()
    comm("mm")
    third = [slice(i * width, (i + 1) * width) for i in range(3)]
    for r in range(rows):
        head = slice(0, TILE)
        prev[r] = (
            dot_nt(dk[r, head], weight[:, third[1]]) + dot_nt(dv[r, head], weight[:, third[2]])
        ).astype(jnp.bfloat16)
    late_copy = remote(prev, late, late_sem.at[0], late_sem.at[1], device(a, y, c, 1 - s))

    @pl.when(s == 1)
    def _():
        late_copy.start()
        late[...] = jnp.zeros_like(late)

    near_steps = rows * pairs // 2

    def near_pair(r, j, slot):
        pair = pl.ds(pl.multiple_of(j * PAIR, PAIR), PAIR)
        scale = 1.0 / math.sqrt(HD)
        one, two = sides(r, pair, 0), sides(r, pair, 1)
        both = [jnp.concatenate(part, axis=0) for part in zip(one, two)]
        first = unit(r, pair, 1, both, near_probs[slot, :, 0 : 2 * wide])
        second = unit(r, pair, 2, two, near_probs[slot, :, 2 * wide :])
        keys = k[r, TILE : 3 * TILE, pair]
        part = heads([dot_tn(first[:, h * TILE : (h + 1) * TILE], keys[:TILE]) for h in range(2)])
        dq[r, 0:TILE, pair] = ((dq_part[r, :, pair] + part) * scale).astype(jnp.bfloat16)
        crossed = jnp.concatenate([first[:, wide:], second], axis=0)
        part = heads([dot_tn(crossed[:, h * TILE : (h + 1) * TILE], keys) for h in range(2)])
        dq[r, TILE : 2 * TILE, pair] = (part * scale).astype(jnp.bfloat16)

    def near_step(n, carry):
        comm_at(n, "n", near_steps)
        for r in range(rows):
            near_copy(n * rows + r).wait()
        for r in range(rows):
            near_pair(r, n, lax.rem(n * rows + r, 4))

        @pl.when(n + 2 < near_steps)
        def _():
            for r in range(rows):
                near_copy((n + 2) * rows + r).start()

        @pl.when(lax.rem(n, 2) == 1)
        def _():
            block = pl.ds(pl.multiple_of((n // 2) * (2 * PAIR), 2 * PAIR), 2 * PAIR)
            share = qkv_terms.shape[-2]
            for i, grads in enumerate((dq, dk, dv)):
                total = None
                for row in range(rows):
                    left = normed[row, TILE:] if i == 0 else normed[row]
                    part = dot_tn(left, grads[row, :, block])
                    total = part if total is None else total + part
                to = pl.ds(pl.multiple_of((n // 2) * width + i * 2 * PAIR, 2 * PAIR), 2 * PAIR)
                qkv_terms[:, :, :, :, :, to] = total.astype(jnp.bfloat16).reshape(
                    (outer, 2, 2, 2, share, 2 * PAIR)
                )

        return carry

    lax.fori_loop(0, near_steps, near_step, 0)
    for load in late_loads[2:]:
        load.wait()
    stores = []
    tiles = local // TILE
    for t in range(tiles):
        for r in range(rows):
            comm(f"t{t * rows + r}")
            if t == tiles - 1 and r == 0:

                @pl.when(s == 0)
                def _():
                    late_copy.wait_recv()

            span = slice(t * TILE, (t + 1) * TILE)
            keys = slice((t + 1) * TILE, (t + 2) * TILE)
            back = dot_nt(dq[r, span], weight[:, third[0]])
            back = back + dot_nt(dk[r, keys], weight[:, third[1]])
            back = back + dot_nt(dv[r, keys], weight[:, third[2]])
            if t == tiles - 1:
                back = back + late[r].astype(jnp.float32)
            normal, scale = normalize(x[r, span].astype(jnp.float32))
            sums[0:1] += column_sum(back * normal)
            sums[1:2] += column_sum(back)
            middle[r, span] = middle[r, span] + norm_grad(back, vectors[0:1], normal, scale)
            store = pltpu.make_async_copy(
                middle.at[r, pl.ds(t * TILE, TILE)],
                tokens_grad_hbm.at[r, pl.ds(t * TILE, TILE)],
                out_sem.at[t * rows + r],
            )
            store.start()
            stores.append(store)
    for r in range(rows):
        sums[2:3] += column_sum(dq[r].astype(jnp.float32))
        sums[3:4] += column_sum(dv[r].astype(jnp.float32))
    sums[4:8] = mlp_sums[0:4]
    size = width // (outer * 8)
    fc_size = 4 * size
    total, fc_total = sums[...], mlp_sums[...]
    for d in range(outer * 8):
        row, start = divmod(d * fc_size, width)
        index = (d // 8, (d // 4) % 2, (d // 2) % 2, d % 2)
        vector_terms[index + (slice(0, 8),)] = pack_columns(total, d * size, size)
        vector_terms[index + (slice(8, 16),)] = pack_columns(
            jnp.broadcast_to(fc_total[4 + row : 5 + row], (8, width)), start, fc_size
        )
    vector_copies = [
        remote(
            vector_terms.at[to], vector_got.at[n], vector_send.at[n], vector_recv.at[n], device(*to)
        )
        for n, (to, _) in enumerate(everyone(outer))
    ]
    for copy in vector_copies:
        copy.start()
    comm("end")
    value = vector_terms[a, y, c, s]
    for n, copy in enumerate(vector_copies):
        copy.wait_recv()
        value = value + vector_got[n]
    vector_share[...] = value
    work.end()
    for copy in vector_copies:
        copy.wait_send()
    for store in stores:
        store.wait()

    @pl.when(s == 1)
    def _():
        late_copy.wait_send()


BACKWARD_ORDERS = (1, 0, 1, 1, 1, 1, 1, 1, 1, 1, 1, 1, 1, 1, 1, 0)
BACKWARD_PLAN = {'f0': [(0, 0), (0, 1), (0, 2), (0, 3), (0, 4), (0, 5), (0, 6), (0, 7), (0, 8), (0, 9)], 'mm': [(1, 0)], 'n0': [(1, 1), (1, 2), (1, 3), (1, 4), (1, 5), (1, 6)], 'n1': [(1, 7), (1, 8), (1, 9)], 'n2': [(2, 0), (2, 2), (0, 10), (0, 11)], 'n4': [(2, 3), (2, 4), (1, 10), (1, 11), (0, 12), (0, 13)], 't0': [(2, 5), (2, 6), (1, 12), (1, 13), (0, 14), (0, 15)], 't1': [(2, 1)], 't2': [(3, 0), (2, 7), (1, 14)], 't3': [(3, 2), (2, 8), (1, 15)], 'end': [(4, 0), (3, 3), (3, 4), (2, 9), (3, 5), (4, 2), (3, 6), (2, 10), (4, 3), (3, 7), (4, 4), (3, 8), (2, 11), (4, 5), (4, 6), (2, 15), (2, 12), (4, 7), (3, 9), (4, 8), (3, 10), (2, 13), (3, 11), (3, 1), (4, 9), (3, 12), (4, 10), (3, 13), (2, 14), (4, 11), (3, 15), (4, 1), (4, 12), (3, 14), (4, 13), (4, 15), (4, 14)]}


def backward(outer, probs, q, k, v, normed, grad, att, x, middle_grad, weight, vectors, mlp_sums, fc_grad, attn_grad):
    rows, local, width = q.shape
    devices = outer * 8
    low, full = jnp.bfloat16, jnp.float32
    share = weight.shape[0] // devices
    anywhere = pl.BlockSpec(memory_space=pl.ANY)
    vmem = pl.BlockSpec(memory_space=pltpu.VMEM)
    terms = [
        fc_grad.reshape((outer, 2, 2, 2, share, fc_grad.shape[1])),
        attn_grad.reshape((outer, 2, 2, 2, share, width)),
    ]
    blocks = weight.shape[1] // width
    pieces = column_pieces(0, fc_grad.shape[1], 2 * fc_grad.shape[1] // width, (0,))
    pieces += column_pieces(1, width, 2, (0,))
    first = len(pieces)
    pieces += column_pieces(2, weight.shape[1], 2 * blocks, (0,))
    pieces = [piece[:3] + (order,) for piece, order in zip(pieces, BACKWARD_ORDERS)]
    part, half = width // 3, width // 2
    places = {}
    for b in range(blocks):
        for h in range(2):
            begin, end = h * half, (h + 1) * half
            places[first + 2 * b + h] = [
                (max(i * part, begin) - begin, min((i + 1) * part, end) - max(i * part, begin),
                 i * width + b * part + max(i * part, begin) - i * part)
                for i in range(blocks)
                if max(i * part, begin) < min((i + 1) * part, end)
            ]
    shapes = [(share, fc_grad.shape[1], low), (share, width, low), (share, weight.shape[1], low)]
    extended = (rows, local + TILE, width)
    return pl.pallas_call(
        functools.partial(backward_kernel, outer, pieces, places, 2),
        in_specs=[anywhere] * 10 + [vmem] * 2 + [anywhere] * 2,
        out_specs=[anywhere] + [vmem] * 4,
        out_shape=[jax.ShapeDtypeStruct(x.shape, full)]
        + [shares_out(shape[0], shape[1]) for shape in shapes]
        + [shares_out(16, PAIR)],
        scratch_shapes=[
            pltpu.VMEM(q.shape, low),
            pltpu.VMEM(extended, low),
            pltpu.VMEM(extended, low),
            pltpu.VMEM(extended, low),
            pltpu.VMEM(q.shape, low),
            pltpu.VMEM(q.shape, low),
            pltpu.VMEM(q.shape, low),
            pltpu.VMEM(q.shape, full),
            pltpu.VMEM(weight.shape, low),
            pltpu.VMEM((rows * width // PAIR, TILE, 2 * TILE), low),
            pltpu.VMEM((4, TILE, 6 * TILE), low),
            pltpu.VMEM(q.shape, low),
            pltpu.VMEM(extended, low),
            pltpu.VMEM(extended, low),
            pltpu.VMEM((rows, TILE, width), full),
            pltpu.VMEM((rows, TILE, width), low),
            pltpu.VMEM((rows, TILE, width), low),
            pltpu.VMEM((outer, 2, 2, 2, share, weight.shape[1]), low),
            pltpu.VMEM((outer, 2, 2, 2, 16, PAIR), full),
            pltpu.VMEM((devices - 1, 16, PAIR), full),
            pltpu.VMEM((8, width), full),
            pltpu.SemaphoreType.DMA((9, rows)),
            pltpu.SemaphoreType.DMA((rows * width // PAIR,)),
            pltpu.SemaphoreType.DMA((4,)),
            pltpu.SemaphoreType.DMA((rows * local // TILE,)),
            pltpu.SemaphoreType.DMA((2,)),
            pltpu.SemaphoreType.DMA((devices - 1,)),
            pltpu.SemaphoreType.DMA((devices - 1,)),
        ]
        + Scatter.scratch(outer, shapes, pieces),
        compiler_params=pltpu.CompilerParams(
            collective_id=4, has_side_effects=True, vmem_limit_bytes=VMEM_LIMIT
        ),
    )(probs, q, k, v, normed, grad, att, x, middle_grad, weight, vectors, mlp_sums, *terms)


def gather_weights(outer, weights, vectors, fc_bias):
    devices = outer * 8
    shards = [pack_vectors(vectors + [fc_bias])]
    shards += [w.reshape(pack_shape(w.shape)) for w in weights]
    full = gather_all(outer, shards, cut([shard.shape for shard in shards]))
    packed = full[0].reshape(devices, -1)
    count, size = len(vectors), vectors[0].shape[0]
    first = packed[:, : count * size].reshape(devices, count, size)
    first = jnp.swapaxes(first, 0, 1).reshape(count, devices * size)
    second = packed[:, count * size : count * size + fc_bias.shape[0]].reshape(-1, devices * size)
    whole = [f.reshape(devices * w.shape[0], w.shape[1]) for f, w in zip(full[1:], weights)]
    return whole, jnp.concatenate([first, second], axis=0)


def scatter_grads(outer, weight_terms, vector_terms, fc_bias_term):
    devices = outer * 8
    count, width = vector_terms.shape
    first = jnp.swapaxes(vector_terms.reshape(count, devices, width // devices), 0, 1)
    first = first.reshape(devices, -1)
    second = fc_bias_term.reshape(devices, -1)
    packed = pack_vectors([first, second])
    terms = [packed.reshape((outer, 2, 2, 2) + packed.shape[1:])]
    shapes = [(term.shape[0] // devices, term.shape[1]) for term in weight_terms]
    for term, shape in zip(weight_terms, shapes):
        terms.append(term.reshape((outer, 2, 2, 2) + pack_shape(shape)))
    shares = scatter_all(outer, terms, cut([term.shape[-2:] for term in terms]))
    flat = shares[0].reshape(-1)
    size = width // devices
    vectors = [flat[i * size : (i + 1) * size] for i in range(count)]
    fc_bias = flat[count * size : count * size + second.shape[1]]
    return [share.reshape(shape) for share, shape in zip(shares[1:], shapes)], vectors, fc_bias


def shards(
    tokens_in,
    doc_starts,
    norm1_gain,
    norm1_bias,
    qkv_weight,
    query_bias,
    value_bias,
    attn_weight,
    attn_bias,
    norm2_gain,
    norm2_bias,
    fc_weight,
    fc_bias,
    proj_weight,
    proj_bias,
    out_grad,
):
    outer = lax.axis_size("batch") // 4
    rows, local, width = tokens_in.shape
    seq = lax.axis_index("seq")
    first = 2 * seq
    padded = jnp.pad(doc_starts, ((0, 0), (1, 0)))
    starts = lax.dynamic_slice_in_dim(padded, first, 3, 1)
    starts = starts - TILE * (first - 1 + jnp.arange(3, dtype=jnp.int32))
    weights = [qkv_weight, attn_weight, fc_weight, proj_weight]
    vectors = [norm1_gain, norm1_bias, query_bias, value_bias, attn_bias, norm2_gain, norm2_bias, proj_bias]
    flat = lambda value: value.reshape(rows * local, width)
    block = lambda value: value.reshape(rows, local, width)
    dy = flat(out_grad)
    devices = 8 * outer
    if qkv_weight.shape[0] % 8 == 0 and proj_weight.shape[0] % 16 == 0 and CHUNK % (8 * proj_weight.shape[0]) == 0:
        (
            normed, q, k, v, probs, att, hidden, slope, middle, normed2, qkv, attn, fc, proj, proj_terms, vectors,
        ) = forward(outer, tokens_in, dy, starts, vectors + [fc_bias], weights)
        proj = proj.reshape(devices * proj_weight.shape[0], width)
        out, middle_grad, att_grad, attn_grad, fc_grad, mlp_sums, proj_share = mlp_scatter(
            outer, hidden, slope, middle, normed2, att, dy, attn, fc, proj, proj_terms, vectors
        )
        tokens_grad, fc_share, attn_share, qkv_share, packed = backward(
            outer, probs, q, k, v, normed, block(att_grad), block(att), tokens_in, block(middle_grad),
            qkv, vectors, mlp_sums, fc_grad, attn_grad,
        )
        size = width // devices
        weights = [qkv_share, attn_share, fc_share, proj_share]
        shares = [packed[i, :size] for i in range(8)]
        fc_bias_share = packed[8, : 4 * size]
    else:
        prev = lax.ppermute(tokens_in[:, local - TILE :], "seq", [(0, 1)])
        (qkv, attn, fc, proj), vectors = gather_weights(outer, weights, vectors, fc_bias)
        normed, q, k, v = project(tokens_in, prev, qkv, vectors)
        probs, att, inverse = attend(starts, q, k, v)
        out, middle_grad, att_grad, attn_grad, fc_grad, proj_grad, mlp_sums = mlp(
            flat(tokens_in), flat(att), dy, attn, fc, proj, vectors
        )
        dq, dk, dv = attend_grad(probs, q, k, v, block(att_grad), att, inverse)
        qkv_grad, prev_grad, project_sums = project_grad(normed, dq, dk, dv, qkv)
        late = lax.ppermute(prev_grad, "seq", [(1, 0)])
        tokens_grad, norm_sums = tokens_grad_of(
            tokens_in, dq, dk, dv, qkv, late, block(middle_grad), vectors
        )
        sums = jnp.concatenate([norm_sums[:2], project_sums[:2], mlp_sums[:4]], axis=0)
        weights, shares, fc_bias_share = scatter_grads(
            outer, [qkv_grad, attn_grad, fc_grad, proj_grad], sums, mlp_sums[4:]
        )
    gain1, bias1, query, value, proj_b, gain2, bias2, attn_b = shares
    return (
        out.reshape(rows, local, width),
        tokens_grad,
        gain1,
        bias1,
        weights[0],
        query,
        value,
        weights[1],
        attn_b,
        gain2,
        bias2,
        weights[2],
        fc_bias_share,
        weights[3],
        proj_b,
    )


def solution(mesh):
    return jax.shard_map(
        shards,
        mesh=mesh,
        in_specs=(
            P("batch", "seq", None),
            P("batch", None),
            P(("batch", "seq")),
            P(("batch", "seq")),
            P(("batch", "seq"), None),
            P(("batch", "seq")),
            P(("batch", "seq")),
            P(("batch", "seq"), None),
            P(("batch", "seq")),
            P(("batch", "seq")),
            P(("batch", "seq")),
            P(("batch", "seq"), None),
            P(("batch", "seq")),
            P(("batch", "seq"), None),
            P(("batch", "seq")),
            P("batch", "seq", None),
        ),
        out_specs=(
            P("batch", "seq", None),
            P("batch", "seq", None),
            P(("batch", "seq")),
            P(("batch", "seq")),
            P(("batch", "seq"), None),
            P(("batch", "seq")),
            P(("batch", "seq")),
            P(("batch", "seq"), None),
            P(("batch", "seq")),
            P(("batch", "seq")),
            P(("batch", "seq")),
            P(("batch", "seq"), None),
            P(("batch", "seq")),
            P(("batch", "seq"), None),
            P(("batch", "seq")),
        ),
        check_vma=False,
    )
```

```python
import functools
import math

import jax
import jax.numpy as jnp
from jax import lax
from jax.experimental import pallas as pl
from jax.experimental.pallas import tpu as pltpu
from jax.sharding import PartitionSpec as P

HD = 64
EPSILON = 1e-05
GELU_SCALE = 0.7978845608028654
MESH_ID = pl.DeviceIdType.MESH
VMEM_LIMIT = 62 * 2**20
EVERY = slice(None)


def place():
    batch, seq = lax.axis_index("batch"), lax.axis_index("seq")
    return (batch // 4, (batch // 2) % 2, batch % 2, seq)


def device(a, y, c, s):
    return (a * 4 + y * 2 + c, s)


def greet(outer):
    a, y, c, s = place()
    barrier = pltpu.get_barrier_semaphore()
    others = [device(lax.rem(a + k, outer), y, c, s) for k in range(1, outer)]
    others += [device(a, 1 - y, c, s), device(a, y, c, 1 - s), device(a, y, 1 - c, s)]
    for other in others:
        pl.semaphore_signal(barrier, inc=1, device_id=other, device_id_type=MESH_ID)
    pl.semaphore_wait(barrier, len(others))


def everyone(outer):
    a, y, c, s = place()
    devices = outer * 8
    me = ((a * 2 + y) * 2 + c) * 2 + s
    split = lambda d: (d // 8, (d // 4) % 2, (d // 2) % 2, d % 2)
    return [
        (split(lax.rem(me + k, devices)), split(lax.rem(me + devices - k, devices)))
        for k in range(1, devices)
    ]


def greet_all(outer):
    barrier = pltpu.get_barrier_semaphore()
    others = everyone(outer)
    for other, _ in others:
        pl.semaphore_signal(barrier, inc=1, device_id=device(*other), device_id_type=MESH_ID)
    pl.semaphore_wait(barrier, len(others))


def remote(src, dst, send_sem, recv_sem, other):
    return pltpu.make_async_remote_copy(
        src_ref=src,
        dst_ref=dst,
        send_sem=send_sem,
        recv_sem=recv_sem,
        device_id=other,
        device_id_type=MESH_ID,
    )


def sites_of(work, plan):
    def comm(name):
        for phase, p in plan.get(name, ()):
            work.act(phase, p)
            if (phase, p) in work.after:
                work.after[(phase, p)]()

    def comm_at(n, name, count, stride=1, offset=0):
        for i in range(count):
            site = f"{name}{i * stride + offset}"
            if site in plan:

                @pl.when(n == i)
                def _():
                    comm(site)

    return comm, comm_at


class Gather:
    def __init__(self, outer, pieces, shards, outs, own_sem, send_sem, recv_sem, eager=99):
        self.outer, self.pieces, self.shards, self.outs = outer, pieces, shards, outs
        self.own_sem, self.send_sem, self.recv_sem = own_sem, send_sem, recv_sem
        self.owned, self.eager, self.after = set(), eager, {}
        self.place = place()

    def sems(self, p, k):
        return self.send_sem.at[p, k], self.recv_sem.at[p, k]

    def own(self, i):
        return pltpu.make_async_copy(
            self.shards[i], self.outs[i].at[self.place], self.own_sem.at[i]
        )

    def first(self, p, k):
        i, start, width, order = self.pieces[p]
        a, y, c, s = self.place
        columns = pl.ds(start, width)
        src = self.shards[i].at[:, columns]
        dst = self.outs[i].at[a, y, c, s, :, columns]
        if k == 0:
            return remote(src, dst, *self.sems(p, 0), self.near(order))
        return remote(src, dst, *self.sems(p, k), device(lax.rem(a + k, self.outer), y, c, s))

    def near(self, order):
        a, y, c, s = self.place
        return device(a, 1 - y, c, s) if order == 0 else device(a, y, c, 1 - s)

    def second(self, p, k):
        i, start, width, order = self.pieces[p]
        a, y, c, s = self.place
        source = lax.rem(a + self.outer - k, self.outer)
        block = self.outs[i].at[source, y, c, s, :, pl.ds(start, width)]
        return remote(block, block, *self.sems(p, self.outer - 1 + k), self.near(order))

    def third(self, p):
        i, start, width, order = self.pieces[p]
        a, y, c, s = self.place
        index = (EVERY, EVERY, c, s) if order == 0 else (EVERY, y, c, EVERY)
        block = self.outs[i].at[index + (EVERY, pl.ds(start, width))]
        return remote(block, block, *self.sems(p, 2 * self.outer - 1), self.near(1 - order))

    def fourth(self, p):
        i, start, width, order = self.pieces[p]
        a, y, c, s = self.place
        block = self.outs[i].at[EVERY, EVERY, c, EVERY, EVERY, pl.ds(start, width)]
        return remote(block, block, *self.sems(p, 2 * self.outer), device(a, y, 1 - c, s))

    def start(self):
        for p in range(len(self.pieces)):
            for k in range(1, self.outer):
                self.first(p, k).start()
            if p < self.eager:
                self.first(p, 0).start()
        for i in range(len(self.shards)):
            self.own(i).start()

    def act(self, phase, p):
        outer, i = self.outer, self.pieces[p][0]
        if phase == 1:
            if p >= self.eager:
                self.first(p, 0).start()
            for k in range(1, outer):
                self.first(p, k).wait_recv()
                self.second(p, k).start()
        elif phase == 2:
            if i not in self.owned:
                self.owned.add(i)
                self.own(i).wait()
            self.first(p, 0).wait_recv()
            for k in range(1, outer):
                self.second(p, k).wait_recv()
            self.third(p).start()
        elif phase == 3:
            self.third(p).wait_recv()
            self.fourth(p).start()
        else:
            self.fourth(p).wait_recv()

    def end(self):
        for p in range(len(self.pieces)):
            for k in range(self.outer):
                self.first(p, k).wait_send()
            for k in range(1, self.outer):
                self.second(p, k).wait_send()
            self.third(p).wait_send()
            self.fourth(p).wait_send()

    @staticmethod
    def semaphores(outer, arrays, pieces):
        return [
            pltpu.SemaphoreType.DMA((arrays,)),
            pltpu.SemaphoreType.DMA((pieces, 2 * outer + 1)),
            pltpu.SemaphoreType.DMA((pieces, 2 * outer + 1)),
        ]


def add_slots(target, other):
    target[...] = target[...] + other[...]


class Scatter:
    def __init__(self, outer, pieces, terms, outs, slots, own_sem, send_sem, recv_sem, places=None):
        self.outer, self.pieces, self.terms, self.outs = outer, pieces, terms, outs
        n = len(pieces)
        self.held, self.got = slots[:n], [slots[k * n : (k + 1) * n] for k in range(1, 5)]
        self.own_sem, self.send_sem, self.recv_sem = own_sem, send_sem, recv_sem
        self.places, self.before, self.after = places or {}, {}, {}
        self.place = place()

    def sems(self, p, k):
        return self.send_sem.at[p, k], self.recv_sem.at[p, k]

    def own(self, p):
        i, start, width, order = self.pieces[p]
        a, y, c, s = self.place
        block = self.terms[i].at[EVERY, EVERY, c, EVERY, EVERY, pl.ds(start, width)]
        return pltpu.make_async_copy(block, self.held[p], self.own_sem.at[p])

    def first(self, p):
        i, start, width, order = self.pieces[p]
        a, y, c, s = self.place
        block = self.terms[i].at[EVERY, EVERY, 1 - c, EVERY, EVERY, pl.ds(start, width)]
        return remote(block, self.got[0][p], *self.sems(p, 0), device(a, y, 1 - c, s))

    def second(self, p):
        a, y, c, s = self.place
        if self.pieces[p][3] == 0:
            src, other = self.held[p].at[:, :, 1 - s], device(a, y, c, 1 - s)
        else:
            src, other = self.held[p].at[:, 1 - y], device(a, 1 - y, c, s)
        return remote(src, self.got[1][p], *self.sems(p, 1), other)

    def third(self, p):
        a, y, c, s = self.place
        if self.pieces[p][3] == 0:
            src, other = self.held[p].at[:, 1 - y, s], device(a, 1 - y, c, s)
        else:
            src, other = self.held[p].at[:, y, 1 - s], device(a, y, c, 1 - s)
        return remote(src, self.got[2][p], *self.sems(p, 2), other)

    def fourth(self, p, k):
        a, y, c, s = self.place
        to = lax.rem(a + k, self.outer)
        src = self.held[p].at[to, y, s]
        return remote(src, self.got[3][p].at[k - 1], *self.sems(p, 2 + k), device(to, y, c, s))

    def act(self, phase, p):
        outer = self.outer
        a, y, c, s = self.place
        i, start, width, order = self.pieces[p]
        if phase == 0:
            if p in self.before:
                self.before[p]()
            self.own(p).start()
            self.first(p).start()
        elif phase == 1:
            self.own(p).wait()
            self.first(p).wait_recv()
            add_slots(self.held[p], self.got[0][p])
            self.second(p).start()
        elif phase == 2:
            self.second(p).wait_recv()
            mine = (EVERY, EVERY, s) if order == 0 else (EVERY, y)
            add_slots(self.held[p].at[mine], self.got[1][p])
            self.third(p).start()
        elif phase == 3:
            self.third(p).wait_recv()
            add_slots(self.held[p].at[:, y, s], self.got[2][p])
            for k in range(1, outer):
                self.fourth(p, k).start()
        else:
            value = self.held[p][a, y, s].astype(jnp.float32)
            for k in range(1, outer):
                self.fourth(p, k).wait_recv()
                value = value + self.got[3][p][k - 1].astype(jnp.float32)
            for offset, size, to in self.places.get(p, [(0, width, start)]):
                self.outs[i][:, to : to + size] = value[:, offset : offset + size]

    def end(self):
        for p in range(len(self.pieces)):
            self.first(p).wait_send()
            self.second(p).wait_send()
            self.third(p).wait_send()
            for k in range(1, self.outer):
                self.fourth(p, k).wait_send()

    @staticmethod
    def scratch(outer, shapes, pieces):
        def slot(p, *lead):
            i, start, width, order = pieces[p]
            return pltpu.VMEM(lead + (shapes[i][0], width), shapes[i][2])

        n = range(len(pieces))
        leads = ((outer, 2, 2), (outer, 2, 2), (outer, 2), (outer,), (max(outer - 1, 1),))
        return [slot(p, *lead) for lead in leads for p in n] + [
            pltpu.SemaphoreType.DMA((len(pieces),)),
            pltpu.SemaphoreType.DMA((len(pieces), outer + 2)),
            pltpu.SemaphoreType.DMA((len(pieces), outer + 2)),
        ]


def steps_in_order(count, lags):
    first = 5 - len(lags)
    steps = [(p + lag, k + first, p) for p in range(count) for k, lag in enumerate(lags)]
    return [(p, phase) for _, phase, p in sorted(steps)]


def gather_kernel(outer, pieces, count, *refs):
    greet(outer)
    work = Gather(outer, pieces, refs[:count], refs[count : 2 * count], *refs[2 * count :])
    work.start()
    for p, phase in steps_in_order(len(pieces), (1, 2, 4, 6)):
        work.act(phase, p)
    work.end()


def gather_all(outer, shards, pieces):
    count = len(shards)
    return pl.pallas_call(
        functools.partial(gather_kernel, outer, pieces, count),
        out_shape=[
            jax.ShapeDtypeStruct((outer, 2, 2, 2) + shard.shape, shard.dtype) for shard in shards
        ],
        in_specs=[pl.BlockSpec(memory_space=pltpu.VMEM)] * count,
        out_specs=[pl.BlockSpec(memory_space=pl.ANY)] * count,
        scratch_shapes=Gather.semaphores(outer, count, len(pieces)),
        compiler_params=pltpu.CompilerParams(
            collective_id=0, has_side_effects=True, vmem_limit_bytes=VMEM_LIMIT
        ),
    )(*shards)


def scatter_kernel(outer, pieces, count, *refs):
    greet(outer)
    rest = refs[2 * count :]
    work = Scatter(outer, pieces, refs[:count], refs[count : 2 * count], rest[:-3], *rest[-3:])
    for p, phase in steps_in_order(len(pieces), (0, 1, 3, 4, 5)):
        work.act(phase, p)
    work.end()


def scatter_all(outer, terms, pieces):
    count = len(terms)
    shapes = [term.shape[-2:] + (term.dtype,) for term in terms]
    return pl.pallas_call(
        functools.partial(scatter_kernel, outer, pieces, count),
        out_shape=[jax.ShapeDtypeStruct(term.shape[-2:], jnp.float32) for term in terms],
        in_specs=[pl.BlockSpec(memory_space=pl.ANY)] * count,
        out_specs=[pl.BlockSpec(memory_space=pltpu.VMEM)] * count,
        scratch_shapes=Scatter.scratch(outer, shapes, pieces),
        compiler_params=pltpu.CompilerParams(
            collective_id=1, has_side_effects=True, vmem_limit_bytes=VMEM_LIMIT
        ),
    )(*terms)


def cut(shape_list):
    pieces = []
    for i, (rows, columns) in enumerate(shape_list):
        parts, blocks = 1, columns // 128
        if rows % 8 == 0:
            fits = [k for k in range(1, blocks + 1) if blocks % k == 0 and rows * columns // k <= 25000]
            parts = min(fits) if fits else 1
        width = columns // parts
        for k in range(parts):
            pieces.append((i, k * width, width, len(pieces) % 2))
    return pieces


def pack_shape(shape):
    rows, columns = shape
    return shape if rows % 8 == 0 else (rows * columns // 128, 128)


def pack_vectors(parts):
    joined = jnp.concatenate([part.astype(jnp.float32) for part in parts], axis=-1)
    size = -(-joined.shape[-1] // 1024) * 1024
    pad = [(0, 0)] * (joined.ndim - 1) + [(0, size - joined.shape[-1])]
    return jnp.pad(joined, pad).reshape(joined.shape[:-1] + (size // 128, 128))


TILE = 256
PAIR = 128
FIRM = 1e30


def dot_nn(left, right):
    return lax.dot_general(left, right, (((1,), (0,)), ((), ())), preferred_element_type=jnp.float32)


def dot_nt(left, right):
    return lax.dot_general(left, right, (((1,), (1,)), ((), ())), preferred_element_type=jnp.float32)


def dot_tn(left, right):
    return lax.dot_general(left, right, (((0,), (0,)), ((), ())), preferred_element_type=jnp.float32)


def normalize(values):
    average = jnp.mean(values, axis=-1, keepdims=True)
    centered = values - average
    variance = jnp.mean(centered * centered, axis=-1, keepdims=True)
    scale = lax.rsqrt(variance + EPSILON)
    return centered * scale, scale


def norm_grad(upstream, gain, normal, scale):
    inner = upstream * gain
    first = jnp.mean(inner, axis=-1, keepdims=True)
    second = jnp.mean(inner * normal, axis=-1, keepdims=True)
    return scale * (inner - first - normal * second)


def column_sum(values):
    return jnp.sum(values, axis=0, keepdims=True)


def project_kernel(x_ref, prev_ref, weight_ref, vectors_ref, normed_ref, q_ref, k_ref, v_ref):
    tile = pl.program_id(1)
    width = x_ref.shape[-1]
    x = jnp.where(tile == 0, prev_ref[0], x_ref[0]).astype(jnp.float32)
    normal, _ = normalize(x)
    normed = (normal * vectors_ref[0:1] + vectors_ref[1:2]).astype(jnp.bfloat16)
    normed_ref[0] = normed

    @pl.when(tile > 0)
    def _():
        queries = dot_nn(normed, weight_ref[:, :width]) + vectors_ref[2:3]
        q_ref[0] = queries.astype(jnp.bfloat16) * jnp.bfloat16(1.0 / math.sqrt(HD))

    k_ref[0] = dot_nn(normed, weight_ref[:, width : 2 * width]).astype(jnp.bfloat16)
    values = dot_nn(normed, weight_ref[:, 2 * width :]) + vectors_ref[3:4]
    v_ref[0] = values.astype(jnp.bfloat16)


def project(tokens, prev, weight, vectors):
    rows, local, width = tokens.shape
    tiles = local // TILE
    here = lambda r, t: (r, jnp.maximum(t - 1, 0), 0)
    extended = jax.ShapeDtypeStruct((rows, local + TILE, width), jnp.bfloat16)
    return pl.pallas_call(
        project_kernel,
        grid=(rows, tiles + 1),
        in_specs=[
            pl.BlockSpec((1, TILE, width), here),
            pl.BlockSpec((1, TILE, width), lambda r, t: (r, 0, 0)),
            pl.BlockSpec(weight.shape, lambda r, t: (0, 0)),
            pl.BlockSpec(vectors.shape, lambda r, t: (0, 0)),
        ],
        out_specs=[
            pl.BlockSpec((1, TILE, width), lambda r, t: (r, t, 0)),
            pl.BlockSpec((1, TILE, width), here),
            pl.BlockSpec((1, TILE, width), lambda r, t: (r, t, 0)),
            pl.BlockSpec((1, TILE, width), lambda r, t: (r, t, 0)),
        ],
        out_shape=[extended, jax.ShapeDtypeStruct(tokens.shape, jnp.bfloat16), extended, extended],
        compiler_params=pltpu.CompilerParams(vmem_limit_bytes=VMEM_LIMIT),
    )(tokens, prev, weight, vectors)


def lane_index(rows):
    return lax.broadcasted_iota(jnp.int32, (rows, PAIR), 1)


def mask_columns(starts_ref, row, q_cols, k_cols):
    place = lax.broadcasted_iota(jnp.int32, (TILE, PAIR), 0)
    lane = lane_index(TILE)
    for tile in range(2):
        before, start = starts_ref[row, tile], starts_ref[row, tile + 1]
        late = jnp.where(place >= start, 1.0, 0.0)
        q_cols[tile] = jnp.where(lane == 0, late, jnp.where(lane == 1, 1.0, 0.0)).astype(jnp.bfloat16)
        early = jnp.where(place < before, -FIRM, 0.0)
        k_cols[tile, 0] = jnp.where(
            lane == 0, -FIRM, jnp.where(lane == 1, early, 0.0)
        ).astype(jnp.bfloat16)
        early = jnp.where(place < start, -FIRM, 0.0)
        k_cols[tile, 1] = jnp.where(lane == 0, early, 0.0).astype(jnp.bfloat16)


def attend_kernel(starts_ref, q_ref, k_ref, v_ref, probs_ref, out_ref, inverse_ref, q_cols, k_cols):
    row = pl.program_id(0)

    @pl.when(pl.program_id(1) == 0)
    def _():
        mask_columns(starts_ref, row, q_cols, k_cols)

    lane = lane_index(TILE)
    causal = lax.broadcasted_iota(jnp.int32, (TILE, TILE), 1) <= lax.broadcasted_iota(
        jnp.int32, (TILE, TILE), 0
    )
    ones = jnp.ones((TILE, PAIR), jnp.bfloat16)
    for tile in range(2):
        queries = q_ref[0, pl.ds(tile * TILE, TILE)]
        keys = [
            jnp.concatenate([k_ref[0, pl.ds((tile + w) * TILE, TILE)], k_cols[tile, w]], axis=1)
            for w in range(2)
        ]
        values = [
            jnp.concatenate([v_ref[0, pl.ds((tile + w) * TILE, TILE)], ones], axis=1)
            for w in range(2)
        ]
        mixed, inverse = [], []
        for head in range(2):
            mine = (lane < HD) if head == 0 else (lane >= HD)
            left = jnp.concatenate([jnp.where(mine, queries, jnp.bfloat16(0)), q_cols[tile]], axis=1)
            far = dot_nt(left, keys[0])
            near = jnp.where(causal, dot_nt(left, keys[1]), -FIRM)
            top = jnp.max(jnp.maximum(far, near), axis=-1, keepdims=True)
            far = jnp.exp(far - top).astype(jnp.bfloat16)
            near = jnp.exp(near - top).astype(jnp.bfloat16)
            probs_ref[0, 0, tile, head, 0] = far
            probs_ref[0, 0, tile, head, 1] = near
            total = dot_nn(far, values[0]) + dot_nn(near, values[1])
            share = 1.0 / total[:, PAIR:]
            mixed.append(total[:, :PAIR] * share)
            inverse.append(share)
        out_ref[0, pl.ds(tile * TILE, TILE)] = jnp.where(lane < HD, mixed[0], mixed[1]).astype(
            jnp.bfloat16
        )
        inverse_ref[0, pl.ds(tile * TILE, TILE)] = jnp.where(lane < HD, inverse[0], inverse[1])


def attend(starts, q, k, v):
    rows, local, width = q.shape
    pairs = width // PAIR
    by_pair = lambda r, j: (r, 0, j)
    return pl.pallas_call(
        attend_kernel,
        grid=(rows, pairs),
        in_specs=[
            pl.BlockSpec(memory_space=pltpu.SMEM),
            pl.BlockSpec((1, local, PAIR), by_pair),
            pl.BlockSpec((1, local + TILE, PAIR), by_pair),
            pl.BlockSpec((1, local + TILE, PAIR), by_pair),
        ],
        out_specs=[
            pl.BlockSpec((1, 1, 2, 2, 2, TILE, TILE), lambda r, j: (r, j, 0, 0, 0, 0, 0)),
            pl.BlockSpec((1, local, PAIR), by_pair),
            pl.BlockSpec((1, local, PAIR), by_pair),
        ],
        out_shape=[
            jax.ShapeDtypeStruct((rows, pairs, 2, 2, 2, TILE, TILE), jnp.bfloat16),
            jax.ShapeDtypeStruct((rows, local, width), jnp.bfloat16),
            jax.ShapeDtypeStruct((rows, local, width), jnp.float32),
        ],
        scratch_shapes=[
            pltpu.VMEM((2, TILE, PAIR), jnp.bfloat16),
            pltpu.VMEM((2, 2, TILE, PAIR), jnp.bfloat16),
        ],
        compiler_params=pltpu.CompilerParams(vmem_limit_bytes=VMEM_LIMIT),
    )(starts, q, k, v)


def attend_grad_kernel(
    probs_ref, q_ref, k_ref, v_ref, grad_ref, out_ref, inverse_ref, dq_ref, dk_ref, dv_ref, dk_sum, dv_sum
):
    lane = lane_index(TILE)
    ones = jnp.ones((TILE, PAIR), jnp.bfloat16)
    for tile in range(2):
        span = pl.ds(tile * TILE, TILE)
        queries = q_ref[0, span]
        scaled = (grad_ref[0, span].astype(jnp.float32) * inverse_ref[0, span]).astype(jnp.bfloat16)
        product = scaled.astype(jnp.float32) * out_ref[0, span].astype(jnp.float32)
        d_queries = []
        for head in range(2):
            mine = (lane < HD) if head == 0 else (lane >= HD)
            delta = -jnp.sum(jnp.where(mine, product, 0.0), axis=-1, keepdims=True)
            high = delta.astype(jnp.bfloat16).astype(jnp.float32)
            extra = jnp.where(lane == 0, high, jnp.where(lane == 1, delta - high, 0.0))
            grads = jnp.where(mine, scaled, jnp.bfloat16(0))
            mine_queries = jnp.where(mine, queries, jnp.bfloat16(0))
            left = jnp.concatenate([grads, extra.astype(jnp.bfloat16)], axis=1)
            d_query = None
            for w in range(2):
                at = pl.ds((tile + w) * TILE, TILE)
                right = jnp.concatenate([v_ref[0, at], ones], axis=1)
                probs = probs_ref[0, 0, tile, head, w]
                d_score = (probs.astype(jnp.float32) * dot_nt(left, right)).astype(jnp.bfloat16)
                part = dot_nn(d_score, k_ref[0, at])
                d_query = part if w == 0 else d_query + part
                d_key = dot_tn(d_score, mine_queries)
                d_value = dot_tn(probs, grads)
                if head == 0 and (w == 1 or tile == 0):
                    dk_sum[at] = d_key
                    dv_sum[at] = d_value
                else:
                    dk_sum[at] += d_key
                    dv_sum[at] += d_value
            d_queries.append(d_query)
        dq = jnp.where(lane < HD, d_queries[0], d_queries[1]) * (1.0 / math.sqrt(HD))
        dq_ref[0, span] = dq.astype(jnp.bfloat16)
    dk_ref[0] = dk_sum[...].astype(jnp.bfloat16)
    dv_ref[0] = dv_sum[...].astype(jnp.bfloat16)


def attend_grad(probs, q, k, v, grad, out, inverse):
    rows, local, width = q.shape
    pairs = width // PAIR
    by_pair = lambda r, j: (r, 0, j)
    small = pl.BlockSpec((1, local, PAIR), by_pair)
    large = pl.BlockSpec((1, local + TILE, PAIR), by_pair)
    return pl.pallas_call(
        attend_grad_kernel,
        grid=(rows, pairs),
        in_specs=[
            pl.BlockSpec((1, 1, 2, 2, 2, TILE, TILE), lambda r, j: (r, j, 0, 0, 0, 0, 0)),
            small,
            large,
            large,
            small,
            small,
            small,
        ],
        out_specs=[small, large, large],
        out_shape=[
            jax.ShapeDtypeStruct(q.shape, jnp.bfloat16),
            jax.ShapeDtypeStruct(k.shape, jnp.bfloat16),
            jax.ShapeDtypeStruct(k.shape, jnp.bfloat16),
        ],
        scratch_shapes=[
            pltpu.VMEM((local + TILE, PAIR), jnp.float32),
            pltpu.VMEM((local + TILE, PAIR), jnp.float32),
        ],
        compiler_params=pltpu.CompilerParams(vmem_limit_bytes=VMEM_LIMIT),
    )(probs, q, k, v, grad, out, inverse)


def gelu_pair(v):
    square = v * v
    half = 0.5 + 0.5 * jnp.tanh(v * (GELU_SCALE + (GELU_SCALE * 0.044715) * square))
    hidden = v * half
    slope = half + hidden * (1.0 - half) * (2.0 * GELU_SCALE + (6.0 * GELU_SCALE * 0.044715) * square)
    return hidden, slope


MLP_TILE = 256
CHUNK = 768


def mlp_kernel(
    x_hbm, att_hbm, dy_hbm, attn_hbm, fc_hbm, proj_hbm, vectors,
    out_hbm, middle_grad_hbm, att_grad_hbm, attn_grad_hbm, fc_grad_hbm, proj_grad_hbm, sums_ref,
    x, att, dy, attn, fc, proj, hidden, pre_grad, normed, branch, out, middle_grad, att_grad,
    attn_grad, fc_grad, proj_grad, in_sem, out_sem,
):
    tokens, width = x.shape
    chunks = fc.shape[1] // CHUNK
    tiles = tokens // MLP_TILE
    loads = [
        pltpu.make_async_copy(src, dst, in_sem.at[i])
        for i, (src, dst) in enumerate(
            ((att_hbm, att), (attn_hbm, attn), (x_hbm, x), (fc_hbm, fc), (dy_hbm, dy), (proj_hbm, proj))
        )
    ]
    for load in loads:
        load.start()
    sums_ref[...] = jnp.zeros_like(sums_ref)
    for load in loads[:3]:
        load.wait()

    def tile_step(t, carry):
        span = pl.ds(pl.multiple_of(t * MLP_TILE, MLP_TILE), MLP_TILE)
        middle = x[span].astype(jnp.float32) + dot_nn(att[span], attn[...]) + vectors[4:5]
        normal, scale = normalize(middle)
        low = (normal * vectors[5:6] + vectors[6:7]).astype(jnp.bfloat16)
        normed[span] = low

        @pl.when(t == 0)
        def _():
            for load in loads[3:]:
                load.wait()

        upstream = dy[span]
        result = middle + vectors[7:8]
        back = None
        for j in range(chunks):
            columns = pl.ds(j * CHUNK, CHUNK)
            pre = dot_nn(low, fc[:, columns]) + vectors[8 + j : 9 + j]
            value, slope = gelu_pair(pre)
            value = value.astype(jnp.bfloat16)
            hidden[span, columns] = value
            grad = dot_nt(upstream, proj[columns]) * slope
            grad = grad.astype(jnp.bfloat16)
            pre_grad[span, columns] = grad
            sums_ref[4 + j : 5 + j] += column_sum(grad.astype(jnp.float32))
            result = result + dot_nn(value, proj[columns])
            part = dot_nt(grad, fc[:, columns])
            back = part if back is None else back + part
        out[span] = result.astype(jnp.bfloat16)
        upstream = upstream.astype(jnp.float32)
        sums_ref[0:1] += column_sum(upstream)
        sums_ref[1:2] += column_sum(back * normal)
        sums_ref[2:3] += column_sum(back)
        total = upstream + norm_grad(back, vectors[5:6], normal, scale)
        middle_grad[span] = total
        total = total.astype(jnp.bfloat16)
        branch[span] = total
        sums_ref[3:4] += column_sum(total.astype(jnp.float32))
        att_grad[span] = dot_nt(total, attn[...]).astype(jnp.bfloat16)
        return carry

    lax.fori_loop(0, tiles, tile_step, 0)
    stores = []

    def store(src, dst):
        copy = pltpu.make_async_copy(src, dst, out_sem.at[len(stores)])
        copy.start()
        stores.append(copy)

    store(out, out_hbm)
    store(middle_grad, middle_grad_hbm)
    store(att_grad, att_grad_hbm)
    for j in range(chunks):
        columns = pl.ds(j * CHUNK, CHUNK)
        proj_grad[columns] = dot_tn(hidden[:, columns], dy[...]).astype(jnp.bfloat16)
        store(proj_grad.at[columns], proj_grad_hbm.at[columns])
    for j in range(chunks):
        columns = pl.ds(j * CHUNK, CHUNK)
        fc_grad[:, columns] = dot_tn(normed[...], pre_grad[:, columns]).astype(jnp.bfloat16)
        store(fc_grad.at[:, columns], fc_grad_hbm.at[:, columns])
    attn_grad[...] = dot_tn(att[...], branch[...]).astype(jnp.bfloat16)
    store(attn_grad, attn_grad_hbm)
    for copy in stores:
        copy.wait()


def mlp(x, att, dy, attn, fc, proj, vectors):
    tokens, width = x.shape
    hidden = fc.shape[1]
    low, full = jnp.bfloat16, jnp.float32
    anywhere = pl.BlockSpec(memory_space=pl.ANY)
    vmem = pl.BlockSpec(memory_space=pltpu.VMEM)
    return pl.pallas_call(
        mlp_kernel,
        in_specs=[anywhere] * 6 + [vmem],
        out_specs=[anywhere] * 6 + [vmem],
        out_shape=[
            jax.ShapeDtypeStruct((tokens, width), low),
            jax.ShapeDtypeStruct((tokens, width), full),
            jax.ShapeDtypeStruct((tokens, width), low),
            jax.ShapeDtypeStruct(attn.shape, low),
            jax.ShapeDtypeStruct(fc.shape, low),
            jax.ShapeDtypeStruct(proj.shape, low),
            jax.ShapeDtypeStruct((8, width), full),
        ],
        scratch_shapes=[
            pltpu.VMEM((tokens, width), low),
            pltpu.VMEM((tokens, width), low),
            pltpu.VMEM((tokens, width), low),
            pltpu.VMEM(attn.shape, low),
            pltpu.VMEM(fc.shape, low),
            pltpu.VMEM(proj.shape, low),
            pltpu.VMEM((tokens, hidden), low),
            pltpu.VMEM((tokens, hidden), low),
            pltpu.VMEM((tokens, width), low),
            pltpu.VMEM((tokens, width), low),
            pltpu.VMEM((tokens, width), low),
            pltpu.VMEM((tokens, width), full),
            pltpu.VMEM((tokens, width), low),
            pltpu.VMEM(attn.shape, low),
            pltpu.VMEM(fc.shape, low),
            pltpu.VMEM(proj.shape, low),
            pltpu.SemaphoreType.DMA((6,)),
            pltpu.SemaphoreType.DMA((12,)),
        ],
        compiler_params=pltpu.CompilerParams(vmem_limit_bytes=VMEM_LIMIT),
    )(x, att, dy, attn, fc, proj, vectors)


def project_grad_kernel(normed, dq, dk, dv, weight, weight_grad, prev_grad, sums):
    rows, extended, width = normed.shape
    local = dq.shape[1]
    third = [pl.ds(i * width, width) for i in range(3)]
    for r in range(rows):
        head = pl.ds(0, TILE)
        prev_grad[r] = (
            dot_nt(dk[r, head], weight[:, third[1]]) + dot_nt(dv[r, head], weight[:, third[2]])
        ).astype(jnp.bfloat16)
    total = None
    for i, grads in enumerate((dq, dk, dv)):
        total = None
        for r in range(rows):
            left = normed[r, TILE:] if i == 0 else normed[r]
            part = dot_tn(left, grads[r])
            total = part if total is None else total + part
        weight_grad[:, third[i]] = total.astype(jnp.bfloat16)
    sums[...] = jnp.zeros_like(sums)
    for r in range(rows):
        sums[0:1] += column_sum(dq[r].astype(jnp.float32))
        sums[1:2] += column_sum(dv[r].astype(jnp.float32))


def project_grad(normed, dq, dk, dv, weight):
    rows, extended, width = normed.shape
    vmem = pl.BlockSpec(memory_space=pltpu.VMEM)
    return pl.pallas_call(
        project_grad_kernel,
        in_specs=[vmem] * 5,
        out_specs=[vmem] * 3,
        out_shape=[
            jax.ShapeDtypeStruct(weight.shape, jnp.bfloat16),
            jax.ShapeDtypeStruct((rows, TILE, width), jnp.bfloat16),
            jax.ShapeDtypeStruct((8, width), jnp.float32),
        ],
        compiler_params=pltpu.CompilerParams(vmem_limit_bytes=VMEM_LIMIT),
    )(normed, dq, dk, dv, weight)


def tokens_grad_kernel(x_ref, dq, dk, dv, weight, late, middle_grad, vectors, out_ref, sums):
    row, tile = pl.program_id(0), pl.program_id(1)
    width = x_ref.shape[-1]

    @pl.when((row == 0) & (tile == 0))
    def _():
        sums[...] = jnp.zeros_like(sums)

    back = dot_nt(dq[0], weight[:, :width])
    back = back + dot_nt(dk[0], weight[:, width : 2 * width])
    back = back + dot_nt(dv[0], weight[:, 2 * width :])
    back = back + jnp.where(tile == pl.num_programs(1) - 1, late[0].astype(jnp.float32), 0.0)
    normal, scale = normalize(x_ref[0].astype(jnp.float32))
    sums[0:1] += column_sum(back * normal)
    sums[1:2] += column_sum(back)
    out_ref[0] = middle_grad[0] + norm_grad(back, vectors[0:1], normal, scale)


def tokens_grad_of(x, dq, dk, dv, weight, late, middle_grad, vectors):
    rows, local, width = x.shape
    block = lambda shift: pl.BlockSpec((1, TILE, width), lambda r, t: (r, t + shift, 0))
    whole = lambda v: pl.BlockSpec(v.shape, lambda r, t: (0, 0))
    return pl.pallas_call(
        tokens_grad_kernel,
        grid=(rows, local // TILE),
        in_specs=[
            block(0),
            block(0),
            block(1),
            block(1),
            whole(weight),
            pl.BlockSpec((1, TILE, width), lambda r, t: (r, 0, 0)),
            block(0),
            whole(vectors),
        ],
        out_specs=[block(0), pl.BlockSpec((8, width), lambda r, t: (0, 0))],
        out_shape=[
            jax.ShapeDtypeStruct(x.shape, jnp.float32),
            jax.ShapeDtypeStruct((8, width), jnp.float32),
        ],
        compiler_params=pltpu.CompilerParams(vmem_limit_bytes=VMEM_LIMIT),
    )(x, dq, dk, dv, weight, late, middle_grad, vectors)


def spread_vectors(slots, size, fc_size, width):
    outer = slots.shape[0]
    zeros = jnp.zeros((8, width - PAIR), jnp.float32)
    first, second = None, None
    for d in range(outer * 8):
        index = (d // 8, (d // 4) % 2, (d // 2) % 2, d % 2)
        top = jnp.concatenate([slots[index + (slice(0, 8),)], zeros], axis=1)
        low = jnp.concatenate([slots[index + (slice(8, 16),)], zeros], axis=1)
        top = pltpu.roll(top, d * size, 1) if d else top
        row, lane = divmod(d * fc_size, width)
        low = pltpu.roll(low, lane, 1) if lane else low
        low = pltpu.roll(low, row, 0) if row else low
        first = top if first is None else first + top
        second = low if second is None else second + low
    return first, second


def join_rows(target, slots, columns):
    outer, rows = slots.shape[0], slots.shape[-2]

    def body(a, carry):
        for y in range(2):
            for c in range(2):
                both = [slots[a, y, c, s, :, columns].astype(jnp.float32) for s in range(2)]
                start = pl.multiple_of(((a * 2 + y) * 2 + c) * (2 * rows), 2 * rows)
                joined = jnp.concatenate(both, axis=0).astype(target.dtype)
                target[pl.ds(start, 2 * rows), columns] = joined
        return carry

    lax.fori_loop(0, outer, body, 0)


VECTORS = 9


FORWARD_ORDERS = (0, 0, 1, 1, 1, 1, 1, 1, 1, 0, 0, 1, 1, 0, 1)
PREV_AFTER, EAGER = (2, 5), 99
FORWARD_PLAN = {'ln': [(1, 0), (1, 1), (1, 2), (1, 3), (2, 0), (1, 4), (2, 1), (2, 2), (1, 5), (2, 3), (1, 6), (3, 0), (2, 4), (1, 7), (4, 0)], 'q': [(3, 1), (3, 2), (3, 3), (2, 5), (1, 8), (2, 6), (1, 9), (4, 1), (2, 7), (4, 2), (3, 4)], 'k': [(4, 3), (4, 4), (1, 10)], 'v': [(3, 5), (1, 11), (3, 6), (4, 5), (2, 9), (4, 6)], 'b0': [(1, 12)], 'b3': [(1, 13), (3, 7)], 'b4': [(2, 10)], 'b5': [(4, 7), (1, 14), (2, 8), (2, 13), (2, 11)], 'a2': [(3, 8), (3, 9)], 'a4': [(4, 8), (2, 12), (4, 9)], 'a5': [(3, 11)], 'm1': [(3, 10), (4, 11)], 'm2': [(2, 14), (4, 10)], 'm4': [(3, 12)], 'm7': [(4, 12), (3, 13)], 'w1': [(3, 14)], 'w2': [(4, 13)], 'end': [(4, 14)]}


def forward_kernel(outer, pieces, *refs):
    tokens_hbm, dy_hbm, starts_ref = refs[:3]
    vector_refs = refs[3 : 3 + VECTORS]
    shards = refs[3 + VECTORS : 7 + VECTORS]
    (
        normed_hbm, q_hbm, k_hbm, v_hbm, probs_hbm, att_hbm, hidden_hbm, slope_hbm, middle_hbm,
        normed2_hbm, qkv_hbm, attn_hbm, fc_hbm, proj_slots, terms_hbm, vectors,
    ) = refs[7 + VECTORS : 23 + VECTORS]
    (
        own, vector_slots, qkv_slots, attn_slots, fc_slots, qkv, attn, fc, x, normed, q, k, v, probs, att,
        hidden, slope, middle, normed2, dy, terms, q_cols, k_cols,
        move_sem, out_sem, probs_sem, terms_sem, own_sem, send_sem, recv_sem,
    ) = refs[23 + VECTORS :]
    rows, local, width = q.shape
    a, y, c, s = place()
    size, fc_size = vector_refs[0].shape[1], vector_refs[-1].shape[1]
    pairs, chunks = width // PAIR, fc.shape[1] // CHUNK

    load = pltpu.make_async_copy(tokens_hbm, x.at[:, pl.ds(TILE, local)], move_sem.at[0])
    load_dy = pltpu.make_async_copy(dy_hbm, dy, move_sem.at[3])
    load.start()
    own[...] = jnp.zeros_like(own)
    for i, ref in enumerate(vector_refs):
        own[i : i + 1, : ref.shape[1]] = ref[...].astype(jnp.float32)
    greet(outer)
    prev = remote(
        tokens_hbm.at[:, pl.ds(local - TILE, TILE)],
        x.at[:, pl.ds(0, TILE)],
        move_sem.at[1],
        move_sem.at[2],
        device(a, y, c, 1 - s),
    )
    work = Gather(
        outer,
        pieces,
        (own,) + shards,
        (vector_slots, qkv_slots, attn_slots, fc_slots, proj_slots),
        own_sem,
        send_sem,
        recv_sem,
        EAGER,
    )
    work.start()
    load_dy.start()

    def start_prev():
        @pl.when(s == 0)
        def _():
            prev.start()

    work.after = {PREV_AFTER: start_prev}
    comm, comm_at = sites_of(work, FORWARD_PLAN)
    stores = []

    def store(src, dst):
        copy = pltpu.make_async_copy(src, dst, out_sem.at[len(stores)])
        copy.start()
        stores.append(copy)

    @pl.when(s == 0)
    def _():
        for r in range(rows):
            x[r, 0:TILE] = jnp.zeros((TILE, width), x.dtype)

    for r in range(rows):
        mask_columns(starts_ref, r, q_cols.at[r], k_cols.at[r])
    load.wait()
    comm("ln")
    first, second = spread_vectors(vector_slots, size, fc_size, width)
    vectors[0:8], vectors[8:16] = first, second

    def norm_tile(r, span):
        normal, _ = normalize(x[r, span].astype(jnp.float32))
        normed[r, span] = (normal * vectors[0:1] + vectors[1:2]).astype(jnp.bfloat16)

    def norm_step(n, carry):
        r, t = n // (local // TILE), lax.rem(n, local // TILE) + 1
        norm_tile(r, pl.ds(pl.multiple_of(t * TILE, TILE), TILE))
        return carry

    lax.fori_loop(0, rows * (local // TILE), norm_step, 0)
    third = [slice(i * width, (i + 1) * width) for i in range(3)]
    for i, site in enumerate(("q", "k", "v")):
        comm(site)
        join_rows(qkv, qkv_slots, third[i])

        def row_step(r, carry):
            value = dot_nn(normed[r, TILE:], qkv[:, third[i]])
            if i == 0:
                value = (value + vectors[2:3]).astype(jnp.bfloat16)
                q[r] = value * jnp.bfloat16(1.0 / math.sqrt(HD))
            elif i == 1:
                k[r, TILE:] = value.astype(jnp.bfloat16)
            else:
                v[r, TILE:] = (value + vectors[3:4]).astype(jnp.bfloat16)
            return carry

        lax.fori_loop(0, rows, row_step, 0)
    store(q, q_hbm)
    store(qkv, qkv_hbm)
    lane = lane_index(TILE)
    causal = lax.broadcasted_iota(jnp.int32, (TILE, 2 * TILE), 0) <= (
        lax.broadcasted_iota(jnp.int32, (TILE, 2 * TILE), 1) & (TILE - 1)
    )

    def probs_copy(slot, r, j, tile):
        part = probs_hbm.at[r, j, :, pl.ds(tile * 4 * TILE, 4 * TILE)]
        return pltpu.make_async_copy(probs.at[slot], part, probs_sem.at[slot])

    def attend_pair(r, j, tile, slot):
        pair = pl.ds(pl.multiple_of(j * PAIR, PAIR), PAIR)
        queries = q[r, tile * TILE : (tile + 1) * TILE, pair]
        left = []
        for head in range(2):
            mine = (lane < HD) if head == 0 else (lane >= HD)
            mine = jnp.where(mine, queries, jnp.bfloat16(0))
            left.append(jnp.concatenate([mine, q_cols[r, tile]], axis=1))
        left = jnp.concatenate(left, axis=0)
        scores = []
        for w in range(2):
            keys = k[r, (tile + w) * TILE : (tile + w + 1) * TILE, pair]
            scores.append(dot_nt(jnp.concatenate([keys, k_cols[r, tile, w]], axis=1), left))
        far, near = scores[0], jnp.where(causal, scores[1], -FIRM)
        top = jnp.max(jnp.maximum(far, near), axis=0, keepdims=True)
        far, near = jnp.exp(far - top), jnp.exp(near - top)
        share = 1.0 / jnp.sum(far + near, axis=0, keepdims=True)
        far, near = (far * share).astype(jnp.bfloat16), (near * share).astype(jnp.bfloat16)
        probs[slot, :, 0 : 2 * TILE], probs[slot, :, 2 * TILE :] = far, near
        values = v[r, tile * TILE : (tile + 2) * TILE, pair]
        mixed = []
        for head in range(2):
            part = slice(head * TILE, (head + 1) * TILE)
            mixed.append(dot_tn(jnp.concatenate([far[:, part], near[:, part]], axis=0), values))
        span = pl.ds(pl.multiple_of(r * local + tile * TILE, TILE), TILE)
        att[span, pair] = jnp.where(lane < HD, mixed[0], mixed[1]).astype(jnp.bfloat16)

    def attend_step(n, tile, index):
        r, j = n // (pairs // 2), lax.rem(n, pairs // 2) * 2
        slot = lax.rem(n, 2) * 2

        @pl.when(n + index * rows * pairs // 2 >= 2)
        def _():
            for i in range(2):
                probs_copy(slot + i, r, j + i, tile).wait()

        for i in range(2):
            attend_pair(r, j + i, tile, slot + i)
        for i in range(2):
            probs_copy(slot + i, r, j + i, tile).start()

    def late_step(n, carry):
        comm_at(n, "b", rows * pairs // 2)
        attend_step(n, 1, 0)
        return carry

    lax.fori_loop(0, rows * pairs // 2, late_step, 0)
    comm("prev")

    @pl.when(s == 1)
    def _():
        prev.wait_recv()

    for r in range(rows):
        norm_tile(r, slice(0, TILE))
        k[r, 0:TILE] = dot_nn(normed[r, 0:TILE], qkv[:, third[1]]).astype(jnp.bfloat16)
        value = dot_nn(normed[r, 0:TILE], qkv[:, third[2]]) + vectors[3:4]
        v[r, 0:TILE] = value.astype(jnp.bfloat16)
    store(normed, normed_hbm)
    store(k, k_hbm)
    store(v, v_hbm)

    def early_step(n, carry):
        comm_at(n, "a", rows * pairs // 2)
        attend_step(n, 0, 1)
        return carry

    lax.fori_loop(0, rows * pairs // 2, early_step, 0)
    store(att, att_hbm)
    comm("asm")
    join_rows(attn, attn_slots, slice(0, width))
    store(attn, attn_hbm)

    def mlp_step(r, carry):
        span = pl.ds(pl.multiple_of(r * local, TILE), local)
        value = x[r, TILE:].astype(jnp.float32) + dot_nn(att[span], attn[...]) + vectors[4:5]
        middle[span] = value
        normal, _ = normalize(value)
        low = (normal * vectors[5:6] + vectors[6:7]).astype(jnp.bfloat16)
        normed2[span] = low
        for j in range(chunks):
            for row in range(rows):
                if row == 0 or f"m{row * chunks + j}" in FORWARD_PLAN:

                    @pl.when(r == row)
                    def _():
                        comm(f"m{row * chunks + j}")
                        if row == 0:
                            join_rows(fc, fc_slots, slice(j * CHUNK, (j + 1) * CHUNK))

            columns = pl.ds(j * CHUNK, CHUNK)
            pre = dot_nn(low, fc[:, columns]) + vectors[8 + j : 9 + j]
            value, back = gelu_pair(pre)
            hidden[span, columns] = value.astype(jnp.bfloat16)
            slope[span, columns] = back.astype(jnp.bfloat16)
        return carry

    lax.fori_loop(0, rows, mlp_step, 0)
    store(slope, slope_hbm)
    store(hidden, hidden_hbm)
    store(middle, middle_hbm)
    store(normed2, normed2_hbm)
    store(fc, fc_hbm)
    load_dy.wait()
    share = terms.shape[-2]
    each = CHUNK // (8 * share)
    terms_copies = []
    for j in range(chunks):
        comm(f"w{j}")
        grad = dot_tn(hidden[:, j * CHUNK : (j + 1) * CHUNK], dy[...]).astype(jnp.bfloat16)
        if j >= 2:
            terms_copies[j - 2].wait()
        terms[j % 2] = grad.reshape((each, 2, 2, 2, share, width))
        copy = pltpu.make_async_copy(
            terms.at[j % 2], terms_hbm.at[pl.ds(j * each, each)], terms_sem.at[j % 2]
        )
        copy.start()
        terms_copies.append(copy)
    comm("end")
    work.end()
    for copy in terms_copies[-2:]:
        copy.wait()
    for n in range(4):
        probs_copy(n, 0, n, 0).wait()
    for copy in stores:
        copy.wait()

    @pl.when(s == 0)
    def _():
        prev.wait_send()


def forward(outer, tokens, dy, starts, vectors, weights):
    rows, local, width = tokens.shape
    devices = outer * 8
    low, full = jnp.bfloat16, jnp.float32
    pairs = width // PAIR
    qkv_weight, attn_weight, fc_weight, proj_weight = weights
    hidden = fc_weight.shape[1]
    half = width // 2
    pieces = [(0, 0, PAIR)] + [(1, i * half, half) for i in range(6)] + [(2, 0, width)]
    pieces += [(3, j * CHUNK, CHUNK) for j in range(hidden // CHUNK)]
    pieces += [(4, j * 2 * PAIR, 2 * PAIR) for j in range(width // (2 * PAIR))]
    pieces = [piece + (order,) for piece, order in zip(pieces, FORWARD_ORDERS)]
    anywhere = pl.BlockSpec(memory_space=pl.ANY)
    vmem = pl.BlockSpec(memory_space=pltpu.VMEM)
    extended = (rows, local + TILE, width)
    flat = (rows * local, width)
    whole = [(devices * weight.shape[0], weight.shape[1]) for weight in weights]
    slots = [(outer, 2, 2, 2) + weight.shape for weight in weights]
    shape = jax.ShapeDtypeStruct
    results = pl.pallas_call(
        functools.partial(forward_kernel, outer, pieces),
        in_specs=[anywhere] * 2 + [pl.BlockSpec(memory_space=pltpu.SMEM)] + [vmem] * (VECTORS + 4),
        out_specs=[anywhere] * 15 + [vmem],
        out_shape=[
            shape(extended, low),
            shape(tokens.shape, low),
            shape(extended, low),
            shape(extended, low),
            shape((rows, pairs, TILE, 8 * TILE), low),
            shape(flat, low),
            shape((rows * local, hidden), low),
            shape((rows * local, hidden), low),
            shape(flat, full),
            shape(flat, low),
            shape(whole[0], low),
            shape(whole[1], low),
            shape(whole[2], low),
            shape(slots[3], low),
            shape(slots[3], low),
            shape((16, width), full),
        ],
        scratch_shapes=[
            pltpu.VMEM((16, PAIR), full),
            pltpu.VMEM((outer, 2, 2, 2, 16, PAIR), full),
            pltpu.VMEM(slots[0], low),
            pltpu.VMEM(slots[1], low),
            pltpu.VMEM(slots[2], low),
            pltpu.VMEM(whole[0], low),
            pltpu.VMEM(whole[1], low),
            pltpu.VMEM(whole[2], low),
            pltpu.VMEM(extended, low),
            pltpu.VMEM(extended, low),
            pltpu.VMEM(tokens.shape, low),
            pltpu.VMEM(extended, low),
            pltpu.VMEM(extended, low),
            pltpu.VMEM((4, TILE, 4 * TILE), low),
            pltpu.VMEM(flat, low),
            pltpu.VMEM((rows * local, hidden), low),
            pltpu.VMEM((rows * local, hidden), low),
            pltpu.VMEM(flat, full),
            pltpu.VMEM(flat, low),
            pltpu.VMEM(flat, low),
            pltpu.VMEM((2, CHUNK // (8 * proj_weight.shape[0])) + slots[3][1:], low),
            pltpu.VMEM((rows, 2, TILE, PAIR), low),
            pltpu.VMEM((rows, 2, 2, TILE, PAIR), low),
            pltpu.SemaphoreType.DMA((4,)),
            pltpu.SemaphoreType.DMA((12,)),
            pltpu.SemaphoreType.DMA((4,)),
            pltpu.SemaphoreType.DMA((2,)),
        ]
        + Gather.semaphores(outer, 5, len(pieces)),
        compiler_params=pltpu.CompilerParams(
            collective_id=2, has_side_effects=True, vmem_limit_bytes=VMEM_LIMIT
        ),
    )(tokens, dy, starts, *[vector.reshape(1, -1) for vector in vectors], *weights)
    return results


def shares_out(rows, columns):
    return jax.ShapeDtypeStruct((rows, columns), jnp.float32)


def column_pieces(array, columns, parts, orders):
    step = columns // parts
    return [(array, j * step, step, orders[j % len(orders)]) for j in range(parts)]


def pack_columns(values, start, lanes):
    width = values.shape[1]
    moved = pltpu.roll(values, (width - start) % width, 1) if start % width else values
    return jnp.where(lane_index(values.shape[0]) < lanes, moved[:, :PAIR], 0.0)


def mlp_backward(refs, fc_terms, attn_terms, vectors, att, att_grad, middle, sums, work, comm, comm_at):
    slope_hbm, normed_hbm, dy_hbm, attn_hbm, fc_hbm, proj_hbm, load_middle, load_att = refs

    def body(dy, slope, normed, attn, fc, proj, branch, stage, proj_sem, slope_sem, fc_sem, in_sem, stage_sem):
        tokens, width = dy.shape
        chunks = fc.shape[1] // CHUNK
        block = tokens // 2
        spans = [pl.ds(j * CHUNK, CHUNK) for j in range(chunks)]
        share = fc_terms.shape[-2]

        copies = lambda src, dst, sem: [
            pltpu.make_async_copy(src.at[:, span], dst.at[:, span], sem.at[j])
            for j, span in enumerate(spans)
        ]
        load_proj = [
            pltpu.make_async_copy(proj_hbm.at[span], proj.at[span], proj_sem.at[j])
            for j, span in enumerate(spans)
        ]
        load_slope, load_fc = copies(slope_hbm, slope, slope_sem), copies(fc_hbm, fc, fc_sem)
        others = ((dy_hbm, dy), (normed_hbm, normed), (attn_hbm, attn))
        load_dy, load_normed, load_attn = [
            pltpu.make_async_copy(src, dst, in_sem.at[i]) for i, (src, dst) in enumerate(others)
        ]
        load_dy.start()
        for j in range(chunks):
            load_proj[j].start()
            load_slope[j].start()
        load_normed.start()
        for j in range(chunks):
            load_fc[j].start()
        for load in (load_middle, load_attn, load_att):
            load.start()
        comm("start")
        load_dy.wait()

        def grad_step(t, carry):
            span = pl.ds(pl.multiple_of(t * block, block), block)
            for j in range(chunks):

                @pl.when(t == 0)
                def _():
                    load_proj[j].wait()
                    load_slope[j].wait()

                comm_at(t, "m", 2, chunks, j)
                grad = dot_nt(dy[span], proj[spans[j]]) * slope[span, spans[j]].astype(jnp.float32)
                grad = grad.astype(jnp.bfloat16)
                slope[span, spans[j]] = grad
                sums[12 + j : 13 + j] += column_sum(grad.astype(jnp.float32))
            return carry

        lax.fori_loop(0, 2, grad_step, 0)
        load_normed.wait()
        waited = set()

        def stage_copy(n):
            to = fc_terms.at[:, :, :, :, :, spans[n]] if n < chunks else attn_terms
            return pltpu.make_async_copy(stage.at[n % 2], to, stage_sem.at[n])

        def settle(n):
            if n not in waited:
                waited.add(n)
                stage_copy(n).wait()

        def put(n, grad):
            if n >= 2:
                settle(n - 2)
            stage[n % 2] = grad.astype(jnp.bfloat16).reshape(stage.shape[1:])
            stage_copy(n).start()

        for p, piece in enumerate(work.pieces):
            if piece[0] in (1, 2):
                work.before[p] = functools.partial(settle, piece[1] // CHUNK if piece[0] == 1 else chunks)
        for j in range(chunks):
            comm(f"w{j}")
            put(j, dot_tn(normed[...], slope[:, spans[j]]))

        def back_step(t, carry):
            span = pl.ds(pl.multiple_of(t * block, block), block)
            back = None
            for j in range(chunks):

                @pl.when(t == 0)
                def _():
                    load_fc[j].wait()

                comm_at(t, "o", 2, chunks, j)
                more = dot_nt(slope[span, spans[j]], fc[:, spans[j]])
                back = more if back is None else back + more

            @pl.when(t == 0)
            def _():
                load_middle.wait()
                load_attn.wait()

            upstream = dy[span].astype(jnp.float32)
            value = middle[span]
            normal, scale = normalize(value)
            sums[4:5] += column_sum(upstream)
            sums[5:6] += column_sum(back * normal)
            sums[6:7] += column_sum(back)
            total = upstream + norm_grad(back, vectors[5:6], normal, scale)
            middle[span] = total
            total = total.astype(jnp.bfloat16)
            branch[span] = total
            sums[7:8] += column_sum(total.astype(jnp.float32))
            att_grad[span] = dot_nt(total, attn[...]).astype(jnp.bfloat16)
            return carry

        lax.fori_loop(0, 2, back_step, 0)
        load_att.wait()
        comm("attn")
        put(chunks, dot_tn(att[...], branch[...]))
        comm("rest")
        for n in range(chunks + 1):
            settle(n)

    tokens, width = att.shape
    hidden, chunks = fc_hbm.shape[1], fc_hbm.shape[1] // CHUNK
    low = jnp.bfloat16
    dma = lambda n: pltpu.SemaphoreType.DMA((n,))
    pl.run_scoped(
        body,
        pltpu.VMEM((tokens, width), low),
        pltpu.VMEM((tokens, hidden), low),
        pltpu.VMEM((tokens, width), low),
        pltpu.VMEM(attn_hbm.shape, low),
        pltpu.VMEM(fc_hbm.shape, low),
        pltpu.VMEM(proj_hbm.shape, low),
        pltpu.VMEM((tokens, width), low),
        pltpu.VMEM((2,) + attn_terms.shape, low),
        dma(chunks),
        dma(chunks),
        dma(chunks),
        dma(3),
        dma(chunks + 1),
    )


def backward_kernel(outer, pieces, places, *refs):
    (
        hidden_hbm, slope_hbm, middle_hbm, normed2_hbm, att_hbm, dy_hbm, attn_hbm, fc_hbm, proj_hbm, proj_terms,
        probs_hbm, q_hbm, k_hbm, v_hbm, normed_hbm, x_hbm, weight_hbm, vectors,
        out_hbm, tokens_grad_hbm, fc_terms, attn_terms, proj_share, fc_share, attn_share, qkv_share, vector_share,
        flat_att, flat_grad, flat_middle, prev, late, vector_terms, vector_got, sums,
        main_sem, late_sem, vector_send, vector_recv, *rest,
    ) = refs
    rows, local, width = q_hbm.shape
    pairs = width // PAIR
    a, y, c, s = place()
    load_middle = pltpu.make_async_copy(middle_hbm, flat_middle, main_sem.at[0])
    load_att = pltpu.make_async_copy(att_hbm, flat_att, main_sem.at[1])
    sums[...] = jnp.zeros_like(sums)
    greet_all(outer)
    work = Scatter(
        outer, pieces, [proj_terms, fc_terms, attn_terms, None],
        [proj_share, fc_share, attn_share, qkv_share], rest[:-3], *rest[-3:], places,
    )
    comm, comm_at = sites_of(work, BACKWARD_PLAN)
    mlp_refs = (
        slope_hbm, normed2_hbm, dy_hbm, attn_hbm, fc_hbm, proj_hbm, load_middle, load_att,
    )
    mlp_backward(
        mlp_refs, fc_terms, attn_terms, vectors, flat_att, flat_grad, flat_middle, sums,
        work, comm, comm_at,
    )
    low, full = jnp.bfloat16, jnp.float32
    extended = (rows, local + TILE, width)
    dma = lambda *n: pltpu.SemaphoreType.DMA(n)
    pl.run_scoped(
        functools.partial(
            attend_backward, outer, work, comm, comm_at,
            (probs_hbm, q_hbm, k_hbm, v_hbm, normed_hbm, x_hbm, weight_hbm, hidden_hbm, proj_hbm, middle_hbm),
            vectors, tokens_grad_hbm, out_hbm,
            vector_share, flat_att, flat_grad, flat_middle, prev, late, vector_terms, vector_got, sums,
            late_sem, vector_send, vector_recv,
        ),
        pltpu.VMEM(q_hbm.shape, low),
        pltpu.VMEM(extended, low),
        pltpu.VMEM(extended, low),
        pltpu.VMEM(extended, low),
        pltpu.VMEM(weight_hbm.shape, low),
        pltpu.VMEM((6, TILE, 2 * TILE), low),
        pltpu.VMEM((4, TILE, 6 * TILE), low),
        pltpu.VMEM(q_hbm.shape, low),
        pltpu.VMEM(extended, low),
        pltpu.VMEM(extended, low),
        pltpu.VMEM((rows, TILE, width), full),
        pltpu.VMEM((outer, 2, 2, 2, weight_hbm.shape[0] // (outer * 8), weight_hbm.shape[1]), low),
        dma(3, rows),
        dma(3),
        dma(6),
        dma(4),
        dma(rows * local // TILE),
        dma(4),
        dma(2, 4),
        dma(2),
        dma(2),
    )


def attend_backward(
    outer, work, comm, comm_at, arrays, vectors, tokens_grad_hbm, out_hbm, vector_share, att, grad, middle,
    prev, late, vector_terms, vector_got, sums, late_sem, vector_send, vector_recv,
    q, k, v, normed, weight, far_probs, near_probs, dq, dk, dv, dq_part, qkv_terms,
    in_sem, after_sem, far_sem, near_sem, out_sem, proj_sem, hidden_sem, middle_sem, result_sem,
):
    probs_hbm, q_hbm, k_hbm, v_hbm, normed_hbm, x_hbm, weight_hbm, hidden_hbm, proj_hbm, middle_hbm = arrays
    rows, local, width = q.shape
    pairs = width // PAIR
    a, y, c, s = place()
    work.terms[3] = qkv_terms
    loads = [
        [pltpu.make_async_copy(src.at[r], dst.at[r], in_sem.at[i, r]) for r in range(rows)]
        for i, (src, dst) in enumerate(((q_hbm, q), (k_hbm, k), (v_hbm, v)))
    ]
    load_weight = pltpu.make_async_copy(weight_hbm, weight, after_sem.at[0])
    load_normed = pltpu.make_async_copy(normed_hbm, normed, after_sem.at[1])
    load_x = pltpu.make_async_copy(x_hbm, q, after_sem.at[2])
    wide = 2 * TILE

    def far_copy(n):
        part = probs_hbm.at[n // pairs, lax.rem(n, pairs), :, pl.ds(0, wide)]
        slot = lax.rem(n, 6)
        return pltpu.make_async_copy(part, far_probs.at[slot], far_sem.at[slot])

    def near_copy(n):
        slot = lax.rem(n, 4)
        part = probs_hbm.at[lax.rem(n, rows), n // rows, :, pl.ds(wide, 3 * wide)]
        return pltpu.make_async_copy(part, near_probs.at[slot], near_sem.at[slot])

    for r in range(rows):
        for load in loads:
            load[r].start()
        if r == 0:
            for n in range(6):
                far_copy(n).start()
    load_weight.start()
    load_normed.start()
    for n in range(4):
        near_copy(n).start()
    lane = lane_index(TILE)
    ones = jnp.ones((TILE, PAIR), jnp.bfloat16)

    def sides(r, pair, tile):
        span = pl.ds(pl.multiple_of(r * local + tile * TILE, TILE), TILE)
        grads, queries = grad[span, pair], q[r, tile * TILE : (tile + 1) * TILE, pair]
        product = grads.astype(jnp.float32) * att[span, pair].astype(jnp.float32)
        left, mine_grads, mine_queries = [], [], []
        for head in range(2):
            mine = (lane < HD) if head == 0 else (lane >= HD)
            delta = -jnp.sum(jnp.where(mine, product, 0.0), axis=-1, keepdims=True)
            high = delta.astype(jnp.bfloat16).astype(jnp.float32)
            extra = jnp.where(lane == 0, high, jnp.where(lane == 1, delta - high, 0.0))
            mine_grads.append(jnp.where(mine, grads, jnp.bfloat16(0)))
            mine_queries.append(jnp.where(mine, queries, jnp.bfloat16(0)))
            left.append(jnp.concatenate([mine_grads[-1], extra.astype(jnp.bfloat16)], axis=1))
        return [jnp.concatenate(part, axis=0) for part in (left, mine_grads, mine_queries)]

    def unit(r, pair, tile, side, chances):
        values = jnp.concatenate([v[r, tile * TILE : (tile + 1) * TILE, pair], ones], axis=1)
        d_score = (chances.astype(jnp.float32) * dot_nt(values, side[0])).astype(jnp.bfloat16)
        span = slice(tile * TILE, (tile + 1) * TILE)
        dk[r, span, pair] = dot_nn(d_score, side[2]).astype(jnp.bfloat16)
        dv[r, span, pair] = dot_nn(chances, side[1]).astype(jnp.bfloat16)
        return d_score

    def heads(parts):
        return jnp.where(lane < HD, parts[0], parts[1])

    far_steps = rows * pairs // 2

    def far_step(n, carry):
        r, j = n // (pairs // 2), lax.rem(n, pairs // 2) * 2
        for row in range(rows):

            @pl.when(n == row * (pairs // 2))
            def _():
                for load in loads:
                    load[row].wait()

        comm_at(n, "f", far_steps)
        for i in range(2):
            far_copy(2 * n + i).wait()
        for i in range(2):
            pair = pl.ds(pl.multiple_of((j + i) * PAIR, PAIR), PAIR)
            d_score = unit(r, pair, 0, sides(r, pair, 0), far_probs[lax.rem(2 * n + i, 6)])
            keys = k[r, 0:TILE, pair]
            dq_part[r, :, pair] = heads(
                [dot_tn(d_score[:, h * TILE : (h + 1) * TILE], keys) for h in range(2)]
            )

        @pl.when(2 * n + 6 < rows * pairs)
        def _():
            for i in range(2):
                far_copy(2 * n + 6 + i).start()

        return carry

    lax.fori_loop(0, far_steps, far_step, 0)
    load_weight.wait()
    comm("mm")
    third = [slice(i * width, (i + 1) * width) for i in range(3)]
    for r in range(rows):
        head = slice(0, TILE)
        prev[r] = (
            dot_nt(dk[r, head], weight[:, third[1]]) + dot_nt(dv[r, head], weight[:, third[2]])
        ).astype(jnp.bfloat16)
    late_copy = remote(prev, late, late_sem.at[0], late_sem.at[1], device(a, y, c, 1 - s))

    @pl.when(s == 1)
    def _():
        late_copy.start()
        late[...] = jnp.zeros_like(late)

    load_normed.wait()
    near_steps = rows * pairs // 2

    def near_pair(r, j, slot):
        pair = pl.ds(pl.multiple_of(j * PAIR, PAIR), PAIR)
        scale = 1.0 / math.sqrt(HD)
        one, two = sides(r, pair, 0), sides(r, pair, 1)
        both = [jnp.concatenate(part, axis=0) for part in zip(one, two)]
        first = unit(r, pair, 1, both, near_probs[slot, :, 0 : 2 * wide])
        second = unit(r, pair, 2, two, near_probs[slot, :, 2 * wide :])
        keys = k[r, TILE : 3 * TILE, pair]
        part = heads([dot_tn(first[:, h * TILE : (h + 1) * TILE], keys[:TILE]) for h in range(2)])
        dq[r, 0:TILE, pair] = ((dq_part[r, :, pair] + part) * scale).astype(jnp.bfloat16)
        crossed = jnp.concatenate([first[:, wide:], second], axis=0)
        part = heads([dot_tn(crossed[:, h * TILE : (h + 1) * TILE], keys) for h in range(2)])
        dq[r, TILE : 2 * TILE, pair] = (part * scale).astype(jnp.bfloat16)

    def near_step(n, carry):
        comm_at(n, "n", near_steps)
        for r in range(rows):
            near_copy(n * rows + r).wait()
        near_pair(0, n, lax.rem(n * rows, 4))
        comm_at(n, "h", near_steps)
        for r in range(1, rows):
            near_pair(r, n, lax.rem(n * rows + r, 4))

        @pl.when(n + 2 < near_steps)
        def _():
            for r in range(rows):
                near_copy((n + 2) * rows + r).start()

        @pl.when(lax.rem(n, 2) == 1)
        def _():
            comm_at(n, "g", near_steps)
            block = pl.ds(pl.multiple_of((n // 2) * (2 * PAIR), 2 * PAIR), 2 * PAIR)
            share = qkv_terms.shape[-2]
            for i, grads in enumerate((dq, dk, dv)):
                total = None
                for row in range(rows):
                    left = normed[row, TILE:] if i == 0 else normed[row]
                    part = dot_tn(left, grads[row, :, block])
                    total = part if total is None else total + part
                to = pl.ds(pl.multiple_of((n // 2) * width + i * 2 * PAIR, 2 * PAIR), 2 * PAIR)
                qkv_terms[:, :, :, :, :, to] = total.astype(jnp.bfloat16).reshape(
                    (outer, 2, 2, 2, share, 2 * PAIR)
                )

        return carry

    lax.fori_loop(0, near_steps, near_step, 0)
    load_x.start()
    chunks = hidden_hbm.shape[1] // CHUNK
    places = [(k, 0), (k, 1), (v, 0), (v, 1)]
    load_proj = [
        pltpu.make_async_copy(
            proj_hbm.at[pl.ds(j * CHUNK, CHUNK)], places[j][0].at[places[j][1]], proj_sem.at[j]
        )
        for j in range(chunks)
    ]

    def hidden_copy(u, j):
        lanes = pl.ds((u % 2) * CHUNK, CHUNK)
        src = hidden_hbm.at[pl.ds(u * TILE, TILE), pl.ds(j * CHUNK, CHUNK)]
        return pltpu.make_async_copy(src, near_probs.at[j, :, lanes], hidden_sem.at[u % 2, j])

    def middle_copy(u):
        src = middle_hbm.at[pl.ds(u * TILE, TILE)]
        return pltpu.make_async_copy(src, dq_part.at[u % 2], middle_sem.at[u % 2])

    def result_copy(u):
        dst = out_hbm.at[pl.ds(u * TILE, TILE)]
        return pltpu.make_async_copy(normed.at[u % 2, pl.ds(0, TILE)], dst, result_sem.at[u % 2])

    for load in load_proj:
        load.start()
    for u in range(2):
        middle_copy(u).start()
        for j in range(chunks):
            hidden_copy(u, j).start()
    for r in range(rows):
        sums[2:3] += column_sum(dq[r].astype(jnp.float32))
        sums[3:4] += column_sum(dv[r].astype(jnp.float32))
    load_x.wait()
    stores = []
    tiles = local // TILE
    for t in range(tiles):
        for r in range(rows):
            comm(f"t{t * rows + r}")
            if t == tiles - 1 and r == 0:

                @pl.when(s == 0)
                def _():
                    late_copy.wait_recv()

            span = slice(t * TILE, (t + 1) * TILE)
            keys = slice((t + 1) * TILE, (t + 2) * TILE)
            back = dot_nt(dq[r, span], weight[:, third[0]])
            back = back + dot_nt(dk[r, keys], weight[:, third[1]])
            back = back + dot_nt(dv[r, keys], weight[:, third[2]])
            if t == tiles - 1:
                back = back + late[r].astype(jnp.float32)
            normal, scale = normalize(q[r, span].astype(jnp.float32))
            sums[0:1] += column_sum(back * normal)
            sums[1:2] += column_sum(back)
            flat = pl.ds(r * local + t * TILE, TILE)
            middle[flat] = middle[flat] + norm_grad(back, vectors[0:1], normal, scale)
            store = pltpu.make_async_copy(
                middle.at[flat],
                tokens_grad_hbm.at[r, pl.ds(t * TILE, TILE)],
                out_sem.at[t * rows + r],
            )
            store.start()
            stores.append(store)
    size = width // (outer * 8)
    fc_size = 4 * size
    total, fc_total = sums[0:8], sums[8:16]
    for d in range(outer * 8):
        row, start = divmod(d * fc_size, width)
        index = (d // 8, (d // 4) % 2, (d // 2) % 2, d % 2)
        vector_terms[index + (slice(0, 8),)] = pack_columns(total, d * size, size)
        vector_terms[index + (slice(8, 16),)] = pack_columns(
            jnp.broadcast_to(fc_total[4 + row : 5 + row], (8, width)), start, fc_size
        )
    vector_copies = [
        remote(
            vector_terms.at[to], vector_got.at[n], vector_send.at[n], vector_recv.at[n], device(*to)
        )
        for n, (to, _) in enumerate(everyone(outer))
    ]
    for copy in vector_copies:
        copy.start()
    for load in load_proj:
        load.wait()
    out_tiles = rows * local // TILE
    for u in range(out_tiles):
        comm(f"u{u}")
        middle_copy(u).wait()
        result = dq_part[u % 2] + vectors[7:8]
        for j in range(chunks):
            hidden_copy(u, j).wait()
            lanes = slice((u % 2) * CHUNK, (u % 2 + 1) * CHUNK)
            result = result + dot_nn(near_probs[j, :, lanes], places[j][0][places[j][1]])
        if u >= 2:
            result_copy(u - 2).wait()
        normed[u % 2, 0:TILE] = result.astype(jnp.bfloat16)
        result_copy(u).start()
        if u + 2 < out_tiles:
            middle_copy(u + 2).start()
            for j in range(chunks):
                hidden_copy(u + 2, j).start()
    for u in range(out_tiles - 2, out_tiles):
        result_copy(u).wait()
    comm("end")
    value = vector_terms[a, y, c, s]
    for n, copy in enumerate(vector_copies):
        copy.wait_recv()
        value = value + vector_got[n]
    vector_share[...] = value
    work.end()
    for copy in vector_copies:
        copy.wait_send()
    for store in stores:
        store.wait()

    @pl.when(s == 1)
    def _():
        late_copy.wait_send()


BACKWARD_ORDERS = (0, 1, 1, 0, 1, 1, 0, 1, 0, 1, 1, 0, 1, 1, 1, 0, 1, 0, 1)
BACKWARD_PLAN = {'start': [(0, 0), (0, 1), (0, 2)], 'm3': [(1, 0)], 'm4': [(1, 1), (1, 2)], 'w2': [(0, 3), (0, 4)], 'w3': [(2, 0), (0, 5), (0, 6)], 'o0': [(2, 1), (1, 3), (1, 4), (0, 7), (0, 8)], 'o1': [(0, 9), (0, 10)], 'o2': [(1, 5), (1, 6)], 'o4': [(1, 7), (1, 8), (1, 9), (3, 1), (2, 2), (1, 10)], 'o7': [(2, 3)], 'attn': [(3, 0), (2, 6)], 'rest': [(4, 1), (2, 4)], 'f0': [(2, 5), (2, 8), (0, 11), (0, 12)], 'f3': [(4, 0), (3, 2), (2, 7)], 'mm': [(3, 4), (1, 11)], 'n0': [(3, 5), (2, 9), (1, 12), (3, 7)], 'n1': [(4, 2), (2, 10)], 'h1': [(3, 3), (2, 11), (4, 4)], 'g1': [(3, 6)], 'n2': [(4, 5), (4, 7), (3, 8), (0, 13), (0, 14)], 'h2': [(4, 3)], 'n3': [(2, 12)], 'h3': [(4, 6)], 'g3': [(4, 8), (3, 11), (1, 13), (1, 14)], 'n4': [(0, 15), (0, 16)], 'n5': [(4, 11)], 'g5': [(2, 13), (1, 15), (1, 16)], 't0': [(0, 17), (0, 18)], 't1': [(3, 9), (3, 10), (2, 14)], 't2': [(3, 12), (2, 16), (1, 17), (1, 18), (3, 13)], 't3': [(4, 9)], 'u0': [(4, 10), (2, 15)], 'u1': [(4, 12), (4, 13), (3, 14), (3, 16), (2, 18)], 'u2': [(3, 15), (2, 17)], 'u3': [(4, 14), (3, 18)], 'end': [(4, 15), (4, 16), (3, 17), (4, 18), (4, 17)]}


def backward(outer, hidden, slope, middle, normed2, att, dy, attn, fc, proj, proj_terms, probs, q, k, v, normed, x, weight, vectors):
    rows, local, width = q.shape
    devices = outer * 8
    low, full = jnp.bfloat16, jnp.float32
    share = weight.shape[0] // devices
    units = fc.shape[1]
    anywhere = pl.BlockSpec(memory_space=pl.ANY)
    vmem = pl.BlockSpec(memory_space=pltpu.VMEM)
    blocks = weight.shape[1] // width
    pieces = column_pieces(0, width, 3, (0,))
    pieces += column_pieces(1, units, 2 * units // width, (0,)) + column_pieces(2, width, 2, (0,))
    first = len(pieces)
    pieces += column_pieces(3, weight.shape[1], 2 * blocks, (0,))
    pieces = [piece[:3] + (order,) for piece, order in zip(pieces, BACKWARD_ORDERS)]
    part, half = width // 3, width // 2
    places = {}
    for b in range(blocks):
        for h in range(2):
            begin, end = h * half, (h + 1) * half
            places[first + 2 * b + h] = [
                (max(i * part, begin) - begin, min((i + 1) * part, end) - max(i * part, begin),
                 i * width + b * part + max(i * part, begin) - i * part)
                for i in range(blocks)
                if max(i * part, begin) < min((i + 1) * part, end)
            ]
    shapes = [(units // devices, width, low), (share, units, low), (share, width, low), (share, weight.shape[1], low)]
    slots = lambda columns: jax.ShapeDtypeStruct((outer, 2, 2, 2, share, columns), low)
    flat = dy.shape
    return pl.pallas_call(
        functools.partial(backward_kernel, outer, pieces, places),
        in_specs=[anywhere] * 17 + [vmem],
        out_specs=[anywhere] * 4 + [vmem] * 5,
        out_shape=[
            jax.ShapeDtypeStruct(flat, low),
            jax.ShapeDtypeStruct(x.shape, full),
            slots(units),
            slots(width),
        ]
        + [shares_out(shape[0], shape[1]) for shape in shapes]
        + [shares_out(16, PAIR)],
        scratch_shapes=[
            pltpu.VMEM(flat, low),
            pltpu.VMEM(flat, low),
            pltpu.VMEM(flat, full),
            pltpu.VMEM((rows, TILE, width), low),
            pltpu.VMEM((rows, TILE, width), low),
            pltpu.VMEM((outer, 2, 2, 2, 16, PAIR), full),
            pltpu.VMEM((devices - 1, 16, PAIR), full),
            pltpu.VMEM((16, width), full),
            pltpu.SemaphoreType.DMA((2,)),
            pltpu.SemaphoreType.DMA((2,)),
            pltpu.SemaphoreType.DMA((devices - 1,)),
            pltpu.SemaphoreType.DMA((devices - 1,)),
        ]
        + Scatter.scratch(outer, shapes, pieces),
        compiler_params=pltpu.CompilerParams(
            collective_id=4, has_side_effects=True, vmem_limit_bytes=VMEM_LIMIT
        ),
    )(
        hidden, slope, middle, normed2, att, dy, attn, fc, proj, proj_terms,
        probs, q, k, v, normed, x, weight, vectors,
    )


def gather_weights(outer, weights, vectors, fc_bias):
    devices = outer * 8
    shards = [pack_vectors(vectors + [fc_bias])]
    shards += [w.reshape(pack_shape(w.shape)) for w in weights]
    full = gather_all(outer, shards, cut([shard.shape for shard in shards]))
    packed = full[0].reshape(devices, -1)
    count, size = len(vectors), vectors[0].shape[0]
    first = packed[:, : count * size].reshape(devices, count, size)
    first = jnp.swapaxes(first, 0, 1).reshape(count, devices * size)
    second = packed[:, count * size : count * size + fc_bias.shape[0]].reshape(-1, devices * size)
    whole = [f.reshape(devices * w.shape[0], w.shape[1]) for f, w in zip(full[1:], weights)]
    return whole, jnp.concatenate([first, second], axis=0)


def scatter_grads(outer, weight_terms, vector_terms, fc_bias_term):
    devices = outer * 8
    count, width = vector_terms.shape
    first = jnp.swapaxes(vector_terms.reshape(count, devices, width // devices), 0, 1)
    first = first.reshape(devices, -1)
    second = fc_bias_term.reshape(devices, -1)
    packed = pack_vectors([first, second])
    terms = [packed.reshape((outer, 2, 2, 2) + packed.shape[1:])]
    shapes = [(term.shape[0] // devices, term.shape[1]) for term in weight_terms]
    for term, shape in zip(weight_terms, shapes):
        terms.append(term.reshape((outer, 2, 2, 2) + pack_shape(shape)))
    shares = scatter_all(outer, terms, cut([term.shape[-2:] for term in terms]))
    flat = shares[0].reshape(-1)
    size = width // devices
    vectors = [flat[i * size : (i + 1) * size] for i in range(count)]
    fc_bias = flat[count * size : count * size + second.shape[1]]
    return [share.reshape(shape) for share, shape in zip(shares[1:], shapes)], vectors, fc_bias


def shards(
    tokens_in,
    doc_starts,
    norm1_gain,
    norm1_bias,
    qkv_weight,
    query_bias,
    value_bias,
    attn_weight,
    attn_bias,
    norm2_gain,
    norm2_bias,
    fc_weight,
    fc_bias,
    proj_weight,
    proj_bias,
    out_grad,
):
    outer = lax.axis_size("batch") // 4
    rows, local, width = tokens_in.shape
    seq = lax.axis_index("seq")
    first = 2 * seq
    padded = jnp.pad(doc_starts, ((0, 0), (1, 0)))
    starts = lax.dynamic_slice_in_dim(padded, first, 3, 1)
    starts = starts - TILE * (first - 1 + jnp.arange(3, dtype=jnp.int32))
    weights = [qkv_weight, attn_weight, fc_weight, proj_weight]
    vectors = [norm1_gain, norm1_bias, query_bias, value_bias, attn_bias, norm2_gain, norm2_bias, proj_bias]
    flat = lambda value: value.reshape(rows * local, width)
    block = lambda value: value.reshape(rows, local, width)
    dy = flat(out_grad)
    devices = 8 * outer
    if qkv_weight.shape[0] % 8 == 0 and proj_weight.shape[0] % 16 == 0 and CHUNK % (8 * proj_weight.shape[0]) == 0:
        (
            normed, q, k, v, probs, att, hidden, slope, middle, normed2, qkv, attn, fc, proj, proj_terms, vectors,
        ) = forward(outer, tokens_in, dy, starts, vectors + [fc_bias], weights)
        proj = proj.reshape(devices * proj_weight.shape[0], width)
        out, tokens_grad, _, _, proj_share, fc_share, attn_share, qkv_share, packed = backward(
            outer, hidden, slope, middle, normed2, att, dy, attn, fc, proj, proj_terms,
            probs, q, k, v, normed, tokens_in, qkv, vectors,
        )
        size = width // devices
        weights = [qkv_share, attn_share, fc_share, proj_share]
        shares = [packed[i, :size] for i in range(8)]
        fc_bias_share = packed[8, : 4 * size]
    else:
        prev = lax.ppermute(tokens_in[:, local - TILE :], "seq", [(0, 1)])
        (qkv, attn, fc, proj), vectors = gather_weights(outer, weights, vectors, fc_bias)
        normed, q, k, v = project(tokens_in, prev, qkv, vectors)
        probs, att, inverse = attend(starts, q, k, v)
        out, middle_grad, att_grad, attn_grad, fc_grad, proj_grad, mlp_sums = mlp(
            flat(tokens_in), flat(att), dy, attn, fc, proj, vectors
        )
        dq, dk, dv = attend_grad(probs, q, k, v, block(att_grad), att, inverse)
        qkv_grad, prev_grad, project_sums = project_grad(normed, dq, dk, dv, qkv)
        late = lax.ppermute(prev_grad, "seq", [(1, 0)])
        tokens_grad, norm_sums = tokens_grad_of(
            tokens_in, dq, dk, dv, qkv, late, block(middle_grad), vectors
        )
        sums = jnp.concatenate([norm_sums[:2], project_sums[:2], mlp_sums[:4]], axis=0)
        weights, shares, fc_bias_share = scatter_grads(
            outer, [qkv_grad, attn_grad, fc_grad, proj_grad], sums, mlp_sums[4:]
        )
    gain1, bias1, query, value, proj_b, gain2, bias2, attn_b = shares
    return (
        out.reshape(rows, local, width),
        tokens_grad,
        gain1,
        bias1,
        weights[0],
        query,
        value,
        weights[1],
        attn_b,
        gain2,
        bias2,
        weights[2],
        fc_bias_share,
        weights[3],
        proj_b,
    )


def solution(mesh):
    return jax.shard_map(
        shards,
        mesh=mesh,
        in_specs=(
            P("batch", "seq", None),
            P("batch", None),
            P(("batch", "seq")),
            P(("batch", "seq")),
            P(("batch", "seq"), None),
            P(("batch", "seq")),
            P(("batch", "seq")),
            P(("batch", "seq"), None),
            P(("batch", "seq")),
            P(("batch", "seq")),
            P(("batch", "seq")),
            P(("batch", "seq"), None),
            P(("batch", "seq")),
            P(("batch", "seq"), None),
            P(("batch", "seq")),
            P("batch", "seq", None),
        ),
        out_specs=(
            P("batch", "seq", None),
            P("batch", "seq", None),
            P(("batch", "seq")),
            P(("batch", "seq")),
            P(("batch", "seq"), None),
            P(("batch", "seq")),
            P(("batch", "seq")),
            P(("batch", "seq"), None),
            P(("batch", "seq")),
            P(("batch", "seq")),
            P(("batch", "seq")),
            P(("batch", "seq"), None),
            P(("batch", "seq")),
            P(("batch", "seq"), None),
            P(("batch", "seq")),
        ),
        check_vma=False,
    )
```

```python
import functools
import math

import jax
import jax.numpy as jnp
from jax import lax
from jax.experimental import pallas as pl
from jax.experimental.pallas import tpu as pltpu
from jax.sharding import PartitionSpec as P

HD = 64
EPSILON = 1e-05
GELU_SCALE = 0.7978845608028654
MESH_ID = pl.DeviceIdType.MESH
VMEM_LIMIT = 62 * 2**20
EVERY = slice(None)


def place():
    batch, seq = lax.axis_index("batch"), lax.axis_index("seq")
    return (batch // 4, (batch // 2) % 2, batch % 2, seq)


def device(a, y, c, s):
    return (a * 4 + y * 2 + c, s)


def greet(outer):
    a, y, c, s = place()
    barrier = pltpu.get_barrier_semaphore()
    others = [device(lax.rem(a + k, outer), y, c, s) for k in range(1, outer)]
    others += [device(a, 1 - y, c, s), device(a, y, c, 1 - s), device(a, y, 1 - c, s)]
    for other in others:
        pl.semaphore_signal(barrier, inc=1, device_id=other, device_id_type=MESH_ID)
    pl.semaphore_wait(barrier, len(others))


def everyone(outer):
    a, y, c, s = place()
    devices = outer * 8
    me = ((a * 2 + y) * 2 + c) * 2 + s
    split = lambda d: (d // 8, (d // 4) % 2, (d // 2) % 2, d % 2)
    return [
        (split(lax.rem(me + k, devices)), split(lax.rem(me + devices - k, devices)))
        for k in range(1, devices)
    ]


def greet_all(outer):
    barrier = pltpu.get_barrier_semaphore()
    others = everyone(outer)
    for other, _ in others:
        pl.semaphore_signal(barrier, inc=1, device_id=device(*other), device_id_type=MESH_ID)
    pl.semaphore_wait(barrier, len(others))


def remote(src, dst, send_sem, recv_sem, other):
    return pltpu.make_async_remote_copy(
        src_ref=src,
        dst_ref=dst,
        send_sem=send_sem,
        recv_sem=recv_sem,
        device_id=other,
        device_id_type=MESH_ID,
    )


def sites_of(work, plan):
    def comm(name):
        for phase, p in plan.get(name, ()):
            work.act(phase, p)
            if (phase, p) in work.after:
                work.after[(phase, p)]()

    def comm_at(n, name, count, stride=1, offset=0):
        for i in range(count):
            site = f"{name}{i * stride + offset}"
            if site in plan:

                @pl.when(n == i)
                def _():
                    comm(site)

    return comm, comm_at


class Gather:
    def __init__(self, outer, pieces, shards, outs, own_sem, send_sem, recv_sem, eager=99):
        self.outer, self.pieces, self.shards, self.outs = outer, pieces, shards, outs
        self.own_sem, self.send_sem, self.recv_sem = own_sem, send_sem, recv_sem
        self.eager, self.after = eager, {}
        self.place = place()

    def sems(self, p, k):
        return self.send_sem.at[p, k], self.recv_sem.at[p, k]

    def own(self, i):
        return pltpu.make_async_copy(
            self.shards[i], self.outs[i].at[self.place], self.own_sem.at[i]
        )

    def first(self, p, k):
        i, start, width, order = self.pieces[p]
        a, y, c, s = self.place
        columns = pl.ds(start, width)
        src = self.shards[i].at[:, columns]
        dst = self.outs[i].at[a, y, c, s, :, columns]
        if k == 0:
            return remote(src, dst, *self.sems(p, 0), self.near(order))
        return remote(src, dst, *self.sems(p, k), device(lax.rem(a + k, self.outer), y, c, s))

    def near(self, order):
        a, y, c, s = self.place
        return device(a, 1 - y, c, s) if order == 0 else device(a, y, c, 1 - s)

    def second(self, p, k):
        i, start, width, order = self.pieces[p]
        a, y, c, s = self.place
        source = lax.rem(a + self.outer - k, self.outer)
        block = self.outs[i].at[source, y, c, s, :, pl.ds(start, width)]
        return remote(block, block, *self.sems(p, self.outer - 1 + k), self.near(order))

    def third(self, p):
        i, start, width, order = self.pieces[p]
        a, y, c, s = self.place
        index = (EVERY, EVERY, c, s) if order == 0 else (EVERY, y, c, EVERY)
        block = self.outs[i].at[index + (EVERY, pl.ds(start, width))]
        return remote(block, block, *self.sems(p, 2 * self.outer - 1), self.near(1 - order))

    def fourth(self, p):
        i, start, width, order = self.pieces[p]
        a, y, c, s = self.place
        block = self.outs[i].at[EVERY, EVERY, c, EVERY, EVERY, pl.ds(start, width)]
        return remote(block, block, *self.sems(p, 2 * self.outer), device(a, y, 1 - c, s))

    def start(self):
        for p in range(len(self.pieces)):
            for k in range(1, self.outer):
                self.first(p, k).start()
            if p < self.eager:
                self.first(p, 0).start()
        for i in range(len(self.shards)):
            self.own(i).start()

    def act(self, phase, p):
        outer = self.outer
        if phase == 1:
            if p >= self.eager:
                self.first(p, 0).start()
            for k in range(1, outer):
                self.first(p, k).wait_recv()
                self.second(p, k).start()
        elif phase == 2:
            if p == 0:
                for n in range(len(self.shards)):
                    self.own(n).wait()
            self.first(p, 0).wait_recv()
            for k in range(1, outer):
                self.second(p, k).wait_recv()
            self.third(p).start()
        elif phase == 3:
            self.third(p).wait_recv()
            self.fourth(p).start()
        else:
            self.fourth(p).wait_recv()

    def end(self):
        for p in range(len(self.pieces)):
            for k in range(self.outer):
                self.first(p, k).wait_send()
            for k in range(1, self.outer):
                self.second(p, k).wait_send()
            self.third(p).wait_send()
            self.fourth(p).wait_send()

    @staticmethod
    def semaphores(outer, arrays, pieces):
        return [
            pltpu.SemaphoreType.DMA((arrays,)),
            pltpu.SemaphoreType.DMA((pieces, 2 * outer + 1)),
            pltpu.SemaphoreType.DMA((pieces, 2 * outer + 1)),
        ]


def add_slots(target, other):
    target[...] = target[...] + other[...]


class Scatter:
    def __init__(self, outer, pieces, terms, outs, slots, own_sem, send_sem, recv_sem, places=None):
        self.outer, self.pieces, self.terms, self.outs = outer, pieces, terms, outs
        n = len(pieces)
        self.held, self.got = slots[:n], [slots[k * n : (k + 1) * n] for k in range(1, 5)]
        self.own_sem, self.send_sem, self.recv_sem = own_sem, send_sem, recv_sem
        self.places, self.before, self.after = places or {}, {}, {}
        self.place = place()

    def sems(self, p, k):
        return self.send_sem.at[p, k], self.recv_sem.at[p, k]

    def own(self, p):
        i, start, width, order = self.pieces[p]
        a, y, c, s = self.place
        block = self.terms[i].at[EVERY, EVERY, c, EVERY, EVERY, pl.ds(start, width)]
        return pltpu.make_async_copy(block, self.held[p], self.own_sem.at[p])

    def first(self, p):
        i, start, width, order = self.pieces[p]
        a, y, c, s = self.place
        block = self.terms[i].at[EVERY, EVERY, 1 - c, EVERY, EVERY, pl.ds(start, width)]
        return remote(block, self.got[0][p], *self.sems(p, 0), device(a, y, 1 - c, s))

    def second(self, p):
        a, y, c, s = self.place
        if self.pieces[p][3] == 0:
            src, other = self.held[p].at[:, :, 1 - s], device(a, y, c, 1 - s)
        else:
            src, other = self.held[p].at[:, 1 - y], device(a, 1 - y, c, s)
        return remote(src, self.got[1][p], *self.sems(p, 1), other)

    def third(self, p):
        a, y, c, s = self.place
        if self.pieces[p][3] == 0:
            src, other = self.held[p].at[:, 1 - y, s], device(a, 1 - y, c, s)
        else:
            src, other = self.held[p].at[:, y, 1 - s], device(a, y, c, 1 - s)
        return remote(src, self.got[2][p], *self.sems(p, 2), other)

    def fourth(self, p, k):
        a, y, c, s = self.place
        to = lax.rem(a + k, self.outer)
        src = self.held[p].at[to, y, s]
        return remote(src, self.got[3][p].at[k - 1], *self.sems(p, 2 + k), device(to, y, c, s))

    def act(self, phase, p):
        outer = self.outer
        a, y, c, s = self.place
        i, start, width, order = self.pieces[p]
        if phase == 0:
            if p in self.before:
                self.before[p]()
            self.own(p).start()
            self.first(p).start()
        elif phase == 1:
            self.own(p).wait()
            self.first(p).wait_recv()
            add_slots(self.held[p], self.got[0][p])
            self.second(p).start()
        elif phase == 2:
            self.second(p).wait_recv()
            mine = (EVERY, EVERY, s) if order == 0 else (EVERY, y)
            add_slots(self.held[p].at[mine], self.got[1][p])
            self.third(p).start()
        elif phase == 3:
            self.third(p).wait_recv()
            add_slots(self.held[p].at[:, y, s], self.got[2][p])
            for k in range(1, outer):
                self.fourth(p, k).start()
        else:
            value = self.held[p][a, y, s].astype(jnp.float32)
            for k in range(1, outer):
                self.fourth(p, k).wait_recv()
                value = value + self.got[3][p][k - 1].astype(jnp.float32)
            for offset, size, to in self.places.get(p, [(0, width, start)]):
                self.outs[i][:, to : to + size] = value[:, offset : offset + size]

    def end(self):
        for p in range(len(self.pieces)):
            self.first(p).wait_send()
            self.second(p).wait_send()
            self.third(p).wait_send()
            for k in range(1, self.outer):
                self.fourth(p, k).wait_send()

    @staticmethod
    def scratch(outer, shapes, pieces):
        def slot(p, *lead):
            i, start, width, order = pieces[p]
            return pltpu.VMEM(lead + (shapes[i][0], width), shapes[i][2])

        n = range(len(pieces))
        leads = ((outer, 2, 2), (outer, 2, 2), (outer, 2), (outer,), (max(outer - 1, 1),))
        return [slot(p, *lead) for lead in leads for p in n] + [
            pltpu.SemaphoreType.DMA((len(pieces),)),
            pltpu.SemaphoreType.DMA((len(pieces), outer + 2)),
            pltpu.SemaphoreType.DMA((len(pieces), outer + 2)),
        ]


def steps_in_order(count, lags):
    first = 5 - len(lags)
    steps = [(p + lag, k + first, p) for p in range(count) for k, lag in enumerate(lags)]
    return [(p, phase) for _, phase, p in sorted(steps)]


def gather_kernel(outer, pieces, count, *refs):
    greet(outer)
    work = Gather(outer, pieces, refs[:count], refs[count : 2 * count], *refs[2 * count :])
    work.start()
    for p, phase in steps_in_order(len(pieces), (1, 2, 4, 6)):
        work.act(phase, p)
    work.end()


def gather_all(outer, shards, pieces):
    count = len(shards)
    return pl.pallas_call(
        functools.partial(gather_kernel, outer, pieces, count),
        out_shape=[
            jax.ShapeDtypeStruct((outer, 2, 2, 2) + shard.shape, shard.dtype) for shard in shards
        ],
        in_specs=[pl.BlockSpec(memory_space=pltpu.VMEM)] * count,
        out_specs=[pl.BlockSpec(memory_space=pl.ANY)] * count,
        scratch_shapes=Gather.semaphores(outer, count, len(pieces)),
        compiler_params=pltpu.CompilerParams(
            collective_id=0, has_side_effects=True, vmem_limit_bytes=VMEM_LIMIT
        ),
    )(*shards)


def scatter_kernel(outer, pieces, count, *refs):
    greet(outer)
    rest = refs[2 * count :]
    work = Scatter(outer, pieces, refs[:count], refs[count : 2 * count], rest[:-3], *rest[-3:])
    for p, phase in steps_in_order(len(pieces), (0, 1, 3, 4, 5)):
        work.act(phase, p)
    work.end()


def scatter_all(outer, terms, pieces):
    count = len(terms)
    shapes = [term.shape[-2:] + (term.dtype,) for term in terms]
    return pl.pallas_call(
        functools.partial(scatter_kernel, outer, pieces, count),
        out_shape=[jax.ShapeDtypeStruct(term.shape[-2:], jnp.float32) for term in terms],
        in_specs=[pl.BlockSpec(memory_space=pl.ANY)] * count,
        out_specs=[pl.BlockSpec(memory_space=pltpu.VMEM)] * count,
        scratch_shapes=Scatter.scratch(outer, shapes, pieces),
        compiler_params=pltpu.CompilerParams(
            collective_id=1, has_side_effects=True, vmem_limit_bytes=VMEM_LIMIT
        ),
    )(*terms)


def cut(shape_list):
    pieces = []
    for i, (rows, columns) in enumerate(shape_list):
        parts, blocks = 1, columns // 128
        if rows % 8 == 0:
            fits = [k for k in range(1, blocks + 1) if blocks % k == 0 and rows * columns // k <= 25000]
            parts = min(fits) if fits else 1
        width = columns // parts
        for k in range(parts):
            pieces.append((i, k * width, width, len(pieces) % 2))
    return pieces


def pack_shape(shape):
    rows, columns = shape
    return shape if rows % 8 == 0 else (rows * columns // 128, 128)


def pack_vectors(parts):
    joined = jnp.concatenate([part.astype(jnp.float32) for part in parts], axis=-1)
    size = -(-joined.shape[-1] // 1024) * 1024
    pad = [(0, 0)] * (joined.ndim - 1) + [(0, size - joined.shape[-1])]
    return jnp.pad(joined, pad).reshape(joined.shape[:-1] + (size // 128, 128))


TILE = 256
PAIR = 128
FIRM = 1e30


def dot_nn(left, right):
    return lax.dot_general(left, right, (((1,), (0,)), ((), ())), preferred_element_type=jnp.float32)


def dot_nt(left, right):
    return lax.dot_general(left, right, (((1,), (1,)), ((), ())), preferred_element_type=jnp.float32)


def dot_tn(left, right):
    return lax.dot_general(left, right, (((0,), (0,)), ((), ())), preferred_element_type=jnp.float32)


def normalize(values):
    average = jnp.mean(values, axis=-1, keepdims=True)
    centered = values - average
    variance = jnp.mean(centered * centered, axis=-1, keepdims=True)
    scale = lax.rsqrt(variance + EPSILON)
    return centered * scale, scale


def norm_grad(upstream, gain, normal, scale):
    inner = upstream * gain
    first = jnp.mean(inner, axis=-1, keepdims=True)
    second = jnp.mean(inner * normal, axis=-1, keepdims=True)
    return scale * (inner - first - normal * second)


def column_sum(values):
    return jnp.sum(values, axis=0, keepdims=True)


def project_kernel(x_ref, prev_ref, weight_ref, vectors_ref, normed_ref, q_ref, k_ref, v_ref):
    tile = pl.program_id(1)
    width = x_ref.shape[-1]
    x = jnp.where(tile == 0, prev_ref[0], x_ref[0]).astype(jnp.float32)
    normal, _ = normalize(x)
    normed = (normal * vectors_ref[0:1] + vectors_ref[1:2]).astype(jnp.bfloat16)
    normed_ref[0] = normed

    @pl.when(tile > 0)
    def _():
        queries = dot_nn(normed, weight_ref[:, :width]) + vectors_ref[2:3]
        q_ref[0] = queries.astype(jnp.bfloat16) * jnp.bfloat16(1.0 / math.sqrt(HD))

    k_ref[0] = dot_nn(normed, weight_ref[:, width : 2 * width]).astype(jnp.bfloat16)
    values = dot_nn(normed, weight_ref[:, 2 * width :]) + vectors_ref[3:4]
    v_ref[0] = values.astype(jnp.bfloat16)


def project(tokens, prev, weight, vectors):
    rows, local, width = tokens.shape
    tiles = local // TILE
    here = lambda r, t: (r, jnp.maximum(t - 1, 0), 0)
    extended = jax.ShapeDtypeStruct((rows, local + TILE, width), jnp.bfloat16)
    return pl.pallas_call(
        project_kernel,
        grid=(rows, tiles + 1),
        in_specs=[
            pl.BlockSpec((1, TILE, width), here),
            pl.BlockSpec((1, TILE, width), lambda r, t: (r, 0, 0)),
            pl.BlockSpec(weight.shape, lambda r, t: (0, 0)),
            pl.BlockSpec(vectors.shape, lambda r, t: (0, 0)),
        ],
        out_specs=[
            pl.BlockSpec((1, TILE, width), lambda r, t: (r, t, 0)),
            pl.BlockSpec((1, TILE, width), here),
            pl.BlockSpec((1, TILE, width), lambda r, t: (r, t, 0)),
            pl.BlockSpec((1, TILE, width), lambda r, t: (r, t, 0)),
        ],
        out_shape=[extended, jax.ShapeDtypeStruct(tokens.shape, jnp.bfloat16), extended, extended],
        compiler_params=pltpu.CompilerParams(vmem_limit_bytes=VMEM_LIMIT),
    )(tokens, prev, weight, vectors)


def lane_index(rows):
    return lax.broadcasted_iota(jnp.int32, (rows, PAIR), 1)


def mask_columns(starts_of, row, q_cols, k_cols):
    place = lax.broadcasted_iota(jnp.int32, (TILE, PAIR), 0)
    lane = lane_index(TILE)
    for tile in range(2):
        before, start = starts_of(row, tile), starts_of(row, tile + 1)
        late = jnp.where(place >= start, 1.0, 0.0)
        q_cols[tile] = jnp.where(lane == 0, late, jnp.where(lane == 1, 1.0, 0.0)).astype(jnp.bfloat16)
        early = jnp.where(place < before, -FIRM, 0.0)
        k_cols[tile, 0] = jnp.where(
            lane == 0, -FIRM, jnp.where(lane == 1, early, 0.0)
        ).astype(jnp.bfloat16)
        early = jnp.where(place < start, -FIRM, 0.0)
        k_cols[tile, 1] = jnp.where(lane == 0, early, 0.0).astype(jnp.bfloat16)


def attend_kernel(starts_ref, q_ref, k_ref, v_ref, probs_ref, out_ref, inverse_ref, q_cols, k_cols):
    row = pl.program_id(0)

    @pl.when(pl.program_id(1) == 0)
    def _():
        mask_columns(lambda r, i: starts_ref[r, i], row, q_cols, k_cols)

    lane = lane_index(TILE)
    causal = lax.broadcasted_iota(jnp.int32, (TILE, TILE), 1) <= lax.broadcasted_iota(
        jnp.int32, (TILE, TILE), 0
    )
    ones = jnp.ones((TILE, PAIR), jnp.bfloat16)
    for tile in range(2):
        queries = q_ref[0, pl.ds(tile * TILE, TILE)]
        keys = [
            jnp.concatenate([k_ref[0, pl.ds((tile + w) * TILE, TILE)], k_cols[tile, w]], axis=1)
            for w in range(2)
        ]
        values = [
            jnp.concatenate([v_ref[0, pl.ds((tile + w) * TILE, TILE)], ones], axis=1)
            for w in range(2)
        ]
        mixed, inverse = [], []
        for head in range(2):
            mine = (lane < HD) if head == 0 else (lane >= HD)
            left = jnp.concatenate([jnp.where(mine, queries, jnp.bfloat16(0)), q_cols[tile]], axis=1)
            far = dot_nt(left, keys[0])
            near = jnp.where(causal, dot_nt(left, keys[1]), -FIRM)
            top = jnp.max(jnp.maximum(far, near), axis=-1, keepdims=True)
            far = jnp.exp(far - top).astype(jnp.bfloat16)
            near = jnp.exp(near - top).astype(jnp.bfloat16)
            probs_ref[0, 0, tile, head, 0] = far
            probs_ref[0, 0, tile, head, 1] = near
            total = dot_nn(far, values[0]) + dot_nn(near, values[1])
            share = 1.0 / total[:, PAIR:]
            mixed.append(total[:, :PAIR] * share)
            inverse.append(share)
        out_ref[0, pl.ds(tile * TILE, TILE)] = jnp.where(lane < HD, mixed[0], mixed[1]).astype(
            jnp.bfloat16
        )
        inverse_ref[0, pl.ds(tile * TILE, TILE)] = jnp.where(lane < HD, inverse[0], inverse[1])


def attend(starts, q, k, v):
    rows, local, width = q.shape
    pairs = width // PAIR
    by_pair = lambda r, j: (r, 0, j)
    return pl.pallas_call(
        attend_kernel,
        grid=(rows, pairs),
        in_specs=[
            pl.BlockSpec(memory_space=pltpu.SMEM),
            pl.BlockSpec((1, local, PAIR), by_pair),
            pl.BlockSpec((1, local + TILE, PAIR), by_pair),
            pl.BlockSpec((1, local + TILE, PAIR), by_pair),
        ],
        out_specs=[
            pl.BlockSpec((1, 1, 2, 2, 2, TILE, TILE), lambda r, j: (r, j, 0, 0, 0, 0, 0)),
            pl.BlockSpec((1, local, PAIR), by_pair),
            pl.BlockSpec((1, local, PAIR), by_pair),
        ],
        out_shape=[
            jax.ShapeDtypeStruct((rows, pairs, 2, 2, 2, TILE, TILE), jnp.bfloat16),
            jax.ShapeDtypeStruct((rows, local, width), jnp.bfloat16),
            jax.ShapeDtypeStruct((rows, local, width), jnp.float32),
        ],
        scratch_shapes=[
            pltpu.VMEM((2, TILE, PAIR), jnp.bfloat16),
            pltpu.VMEM((2, 2, TILE, PAIR), jnp.bfloat16),
        ],
        compiler_params=pltpu.CompilerParams(vmem_limit_bytes=VMEM_LIMIT),
    )(starts, q, k, v)


def attend_grad_kernel(
    probs_ref, q_ref, k_ref, v_ref, grad_ref, out_ref, inverse_ref, dq_ref, dk_ref, dv_ref, dk_sum, dv_sum
):
    lane = lane_index(TILE)
    ones = jnp.ones((TILE, PAIR), jnp.bfloat16)
    for tile in range(2):
        span = pl.ds(tile * TILE, TILE)
        queries = q_ref[0, span]
        scaled = (grad_ref[0, span].astype(jnp.float32) * inverse_ref[0, span]).astype(jnp.bfloat16)
        product = scaled.astype(jnp.float32) * out_ref[0, span].astype(jnp.float32)
        d_queries = []
        for head in range(2):
            mine = (lane < HD) if head == 0 else (lane >= HD)
            delta = -jnp.sum(jnp.where(mine, product, 0.0), axis=-1, keepdims=True)
            high = delta.astype(jnp.bfloat16).astype(jnp.float32)
            extra = jnp.where(lane == 0, high, jnp.where(lane == 1, delta - high, 0.0))
            grads = jnp.where(mine, scaled, jnp.bfloat16(0))
            mine_queries = jnp.where(mine, queries, jnp.bfloat16(0))
            left = jnp.concatenate([grads, extra.astype(jnp.bfloat16)], axis=1)
            d_query = None
            for w in range(2):
                at = pl.ds((tile + w) * TILE, TILE)
                right = jnp.concatenate([v_ref[0, at], ones], axis=1)
                probs = probs_ref[0, 0, tile, head, w]
                d_score = (probs.astype(jnp.float32) * dot_nt(left, right)).astype(jnp.bfloat16)
                part = dot_nn(d_score, k_ref[0, at])
                d_query = part if w == 0 else d_query + part
                d_key = dot_tn(d_score, mine_queries)
                d_value = dot_tn(probs, grads)
                if head == 0 and (w == 1 or tile == 0):
                    dk_sum[at] = d_key
                    dv_sum[at] = d_value
                else:
                    dk_sum[at] += d_key
                    dv_sum[at] += d_value
            d_queries.append(d_query)
        dq = jnp.where(lane < HD, d_queries[0], d_queries[1]) * (1.0 / math.sqrt(HD))
        dq_ref[0, span] = dq.astype(jnp.bfloat16)
    dk_ref[0] = dk_sum[...].astype(jnp.bfloat16)
    dv_ref[0] = dv_sum[...].astype(jnp.bfloat16)


def attend_grad(probs, q, k, v, grad, out, inverse):
    rows, local, width = q.shape
    pairs = width // PAIR
    by_pair = lambda r, j: (r, 0, j)
    small = pl.BlockSpec((1, local, PAIR), by_pair)
    large = pl.BlockSpec((1, local + TILE, PAIR), by_pair)
    return pl.pallas_call(
        attend_grad_kernel,
        grid=(rows, pairs),
        in_specs=[
            pl.BlockSpec((1, 1, 2, 2, 2, TILE, TILE), lambda r, j: (r, j, 0, 0, 0, 0, 0)),
            small,
            large,
            large,
            small,
            small,
            small,
        ],
        out_specs=[small, large, large],
        out_shape=[
            jax.ShapeDtypeStruct(q.shape, jnp.bfloat16),
            jax.ShapeDtypeStruct(k.shape, jnp.bfloat16),
            jax.ShapeDtypeStruct(k.shape, jnp.bfloat16),
        ],
        scratch_shapes=[
            pltpu.VMEM((local + TILE, PAIR), jnp.float32),
            pltpu.VMEM((local + TILE, PAIR), jnp.float32),
        ],
        compiler_params=pltpu.CompilerParams(vmem_limit_bytes=VMEM_LIMIT),
    )(probs, q, k, v, grad, out, inverse)


def gelu_pair(v):
    square = v * v
    half = 0.5 + 0.5 * jnp.tanh(v * (GELU_SCALE + (GELU_SCALE * 0.044715) * square))
    hidden = v * half
    slope = half + hidden * (1.0 - half) * (2.0 * GELU_SCALE + (6.0 * GELU_SCALE * 0.044715) * square)
    return hidden, slope


MLP_TILE = 256
CHUNK = 768


def mlp_kernel(
    x_hbm, att_hbm, dy_hbm, attn_hbm, fc_hbm, proj_hbm, vectors,
    out_hbm, middle_grad_hbm, att_grad_hbm, attn_grad_hbm, fc_grad_hbm, proj_grad_hbm, sums_ref,
    x, att, dy, attn, fc, proj, hidden, pre_grad, normed, branch, out, middle_grad, att_grad,
    attn_grad, fc_grad, proj_grad, in_sem, out_sem,
):
    tokens, width = x.shape
    chunks = fc.shape[1] // CHUNK
    tiles = tokens // MLP_TILE
    loads = [
        pltpu.make_async_copy(src, dst, in_sem.at[i])
        for i, (src, dst) in enumerate(
            ((att_hbm, att), (attn_hbm, attn), (x_hbm, x), (fc_hbm, fc), (dy_hbm, dy), (proj_hbm, proj))
        )
    ]
    for load in loads:
        load.start()
    sums_ref[...] = jnp.zeros_like(sums_ref)
    for load in loads[:3]:
        load.wait()

    def tile_step(t, carry):
        span = pl.ds(pl.multiple_of(t * MLP_TILE, MLP_TILE), MLP_TILE)
        middle = x[span].astype(jnp.float32) + dot_nn(att[span], attn[...]) + vectors[4:5]
        normal, scale = normalize(middle)
        low = (normal * vectors[5:6] + vectors[6:7]).astype(jnp.bfloat16)
        normed[span] = low

        @pl.when(t == 0)
        def _():
            for load in loads[3:]:
                load.wait()

        upstream = dy[span]
        result = middle + vectors[7:8]
        back = None
        for j in range(chunks):
            columns = pl.ds(j * CHUNK, CHUNK)
            pre = dot_nn(low, fc[:, columns]) + vectors[8 + j : 9 + j]
            value, slope = gelu_pair(pre)
            value = value.astype(jnp.bfloat16)
            hidden[span, columns] = value
            grad = dot_nt(upstream, proj[columns]) * slope
            grad = grad.astype(jnp.bfloat16)
            pre_grad[span, columns] = grad
            sums_ref[4 + j : 5 + j] += column_sum(grad.astype(jnp.float32))
            result = result + dot_nn(value, proj[columns])
            part = dot_nt(grad, fc[:, columns])
            back = part if back is None else back + part
        out[span] = result.astype(jnp.bfloat16)
        upstream = upstream.astype(jnp.float32)
        sums_ref[0:1] += column_sum(upstream)
        sums_ref[1:2] += column_sum(back * normal)
        sums_ref[2:3] += column_sum(back)
        total = upstream + norm_grad(back, vectors[5:6], normal, scale)
        middle_grad[span] = total
        total = total.astype(jnp.bfloat16)
        branch[span] = total
        sums_ref[3:4] += column_sum(total.astype(jnp.float32))
        att_grad[span] = dot_nt(total, attn[...]).astype(jnp.bfloat16)
        return carry

    lax.fori_loop(0, tiles, tile_step, 0)
    stores = []

    def store(src, dst):
        copy = pltpu.make_async_copy(src, dst, out_sem.at[len(stores)])
        copy.start()
        stores.append(copy)

    store(out, out_hbm)
    store(middle_grad, middle_grad_hbm)
    store(att_grad, att_grad_hbm)
    for j in range(chunks):
        columns = pl.ds(j * CHUNK, CHUNK)
        proj_grad[columns] = dot_tn(hidden[:, columns], dy[...]).astype(jnp.bfloat16)
        store(proj_grad.at[columns], proj_grad_hbm.at[columns])
    for j in range(chunks):
        columns = pl.ds(j * CHUNK, CHUNK)
        fc_grad[:, columns] = dot_tn(normed[...], pre_grad[:, columns]).astype(jnp.bfloat16)
        store(fc_grad.at[:, columns], fc_grad_hbm.at[:, columns])
    attn_grad[...] = dot_tn(att[...], branch[...]).astype(jnp.bfloat16)
    store(attn_grad, attn_grad_hbm)
    for copy in stores:
        copy.wait()


def mlp(x, att, dy, attn, fc, proj, vectors):
    tokens, width = x.shape
    hidden = fc.shape[1]
    low, full = jnp.bfloat16, jnp.float32
    anywhere = pl.BlockSpec(memory_space=pl.ANY)
    vmem = pl.BlockSpec(memory_space=pltpu.VMEM)
    return pl.pallas_call(
        mlp_kernel,
        in_specs=[anywhere] * 6 + [vmem],
        out_specs=[anywhere] * 6 + [vmem],
        out_shape=[
            jax.ShapeDtypeStruct((tokens, width), low),
            jax.ShapeDtypeStruct((tokens, width), full),
            jax.ShapeDtypeStruct((tokens, width), low),
            jax.ShapeDtypeStruct(attn.shape, low),
            jax.ShapeDtypeStruct(fc.shape, low),
            jax.ShapeDtypeStruct(proj.shape, low),
            jax.ShapeDtypeStruct((8, width), full),
        ],
        scratch_shapes=[
            pltpu.VMEM((tokens, width), low),
            pltpu.VMEM((tokens, width), low),
            pltpu.VMEM((tokens, width), low),
            pltpu.VMEM(attn.shape, low),
            pltpu.VMEM(fc.shape, low),
            pltpu.VMEM(proj.shape, low),
            pltpu.VMEM((tokens, hidden), low),
            pltpu.VMEM((tokens, hidden), low),
            pltpu.VMEM((tokens, width), low),
            pltpu.VMEM((tokens, width), low),
            pltpu.VMEM((tokens, width), low),
            pltpu.VMEM((tokens, width), full),
            pltpu.VMEM((tokens, width), low),
            pltpu.VMEM(attn.shape, low),
            pltpu.VMEM(fc.shape, low),
            pltpu.VMEM(proj.shape, low),
            pltpu.SemaphoreType.DMA((6,)),
            pltpu.SemaphoreType.DMA((12,)),
        ],
        compiler_params=pltpu.CompilerParams(vmem_limit_bytes=VMEM_LIMIT),
    )(x, att, dy, attn, fc, proj, vectors)


def project_grad_kernel(normed, dq, dk, dv, weight, weight_grad, prev_grad, sums):
    rows, extended, width = normed.shape
    local = dq.shape[1]
    third = [pl.ds(i * width, width) for i in range(3)]
    for r in range(rows):
        head = pl.ds(0, TILE)
        prev_grad[r] = (
            dot_nt(dk[r, head], weight[:, third[1]]) + dot_nt(dv[r, head], weight[:, third[2]])
        ).astype(jnp.bfloat16)
    total = None
    for i, grads in enumerate((dq, dk, dv)):
        total = None
        for r in range(rows):
            left = normed[r, TILE:] if i == 0 else normed[r]
            part = dot_tn(left, grads[r])
            total = part if total is None else total + part
        weight_grad[:, third[i]] = total.astype(jnp.bfloat16)
    sums[...] = jnp.zeros_like(sums)
    for r in range(rows):
        sums[0:1] += column_sum(dq[r].astype(jnp.float32))
        sums[1:2] += column_sum(dv[r].astype(jnp.float32))


def project_grad(normed, dq, dk, dv, weight):
    rows, extended, width = normed.shape
    vmem = pl.BlockSpec(memory_space=pltpu.VMEM)
    return pl.pallas_call(
        project_grad_kernel,
        in_specs=[vmem] * 5,
        out_specs=[vmem] * 3,
        out_shape=[
            jax.ShapeDtypeStruct(weight.shape, jnp.bfloat16),
            jax.ShapeDtypeStruct((rows, TILE, width), jnp.bfloat16),
            jax.ShapeDtypeStruct((8, width), jnp.float32),
        ],
        compiler_params=pltpu.CompilerParams(vmem_limit_bytes=VMEM_LIMIT),
    )(normed, dq, dk, dv, weight)


def tokens_grad_kernel(x_ref, dq, dk, dv, weight, late, middle_grad, vectors, out_ref, sums):
    row, tile = pl.program_id(0), pl.program_id(1)
    width = x_ref.shape[-1]

    @pl.when((row == 0) & (tile == 0))
    def _():
        sums[...] = jnp.zeros_like(sums)

    back = dot_nt(dq[0], weight[:, :width])
    back = back + dot_nt(dk[0], weight[:, width : 2 * width])
    back = back + dot_nt(dv[0], weight[:, 2 * width :])
    back = back + jnp.where(tile == pl.num_programs(1) - 1, late[0].astype(jnp.float32), 0.0)
    normal, scale = normalize(x_ref[0].astype(jnp.float32))
    sums[0:1] += column_sum(back * normal)
    sums[1:2] += column_sum(back)
    out_ref[0] = middle_grad[0] + norm_grad(back, vectors[0:1], normal, scale)


def tokens_grad_of(x, dq, dk, dv, weight, late, middle_grad, vectors):
    rows, local, width = x.shape
    block = lambda shift: pl.BlockSpec((1, TILE, width), lambda r, t: (r, t + shift, 0))
    whole = lambda v: pl.BlockSpec(v.shape, lambda r, t: (0, 0))
    return pl.pallas_call(
        tokens_grad_kernel,
        grid=(rows, local // TILE),
        in_specs=[
            block(0),
            block(0),
            block(1),
            block(1),
            whole(weight),
            pl.BlockSpec((1, TILE, width), lambda r, t: (r, 0, 0)),
            block(0),
            whole(vectors),
        ],
        out_specs=[block(0), pl.BlockSpec((8, width), lambda r, t: (0, 0))],
        out_shape=[
            jax.ShapeDtypeStruct(x.shape, jnp.float32),
            jax.ShapeDtypeStruct((8, width), jnp.float32),
        ],
        compiler_params=pltpu.CompilerParams(vmem_limit_bytes=VMEM_LIMIT),
    )(x, dq, dk, dv, weight, late, middle_grad, vectors)


def spread_vectors(slots, size, fc_size, width):
    outer = slots.shape[0]
    zeros = jnp.zeros((8, width - PAIR), jnp.float32)
    first, second = None, None
    for d in range(outer * 8):
        index = (d // 8, (d // 4) % 2, (d // 2) % 2, d % 2)
        top = jnp.concatenate([slots[index + (slice(0, 8),)], zeros], axis=1)
        low = jnp.concatenate([slots[index + (slice(8, 16),)], zeros], axis=1)
        top = pltpu.roll(top, d * size, 1) if d else top
        row, lane = divmod(d * fc_size, width)
        low = pltpu.roll(low, lane, 1) if lane else low
        low = pltpu.roll(low, row, 0) if row else low
        first = top if first is None else first + top
        second = low if second is None else second + low
    return first, second


def join_rows(target, slots, columns):
    outer, rows = slots.shape[0], slots.shape[-2]

    def body(a, carry):
        for y in range(2):
            for c in range(2):
                both = [slots[a, y, c, s, :, columns].astype(jnp.float32) for s in range(2)]
                start = pl.multiple_of(((a * 2 + y) * 2 + c) * (2 * rows), 2 * rows)
                joined = jnp.concatenate(both, axis=0).astype(target.dtype)
                target[pl.ds(start, 2 * rows), columns] = joined
        return carry

    lax.fori_loop(0, outer, body, 0)


VECTORS = 9


FORWARD_ORDERS = (0, 0, 1, 1, 1, 1, 1, 1, 1, 0, 0, 1, 1, 0, 1)
PREV_AFTER, EAGER = (2, 5), 99
FORWARD_PLAN = {'ln': [(1, 0), (1, 1), (1, 2), (1, 3), (2, 0), (1, 4), (2, 1), (2, 2), (1, 5), (2, 3), (1, 6), (3, 0), (2, 4), (1, 7), (4, 0)], 'q': [(3, 1), (3, 2), (3, 3), (2, 5), (1, 8), (2, 6), (1, 9), (4, 1), (2, 7), (4, 2), (3, 4)], 'k': [(4, 3), (4, 4), (1, 10)], 'v': [(3, 5), (1, 11), (3, 6), (4, 5), (2, 9), (4, 6)], 'b0': [(1, 12)], 'b3': [(1, 13), (3, 7)], 'b4': [(2, 10)], 'b5': [(4, 7), (1, 14), (2, 8), (2, 13), (2, 11)], 'a2': [(3, 8), (3, 9)], 'a4': [(4, 8), (2, 12), (4, 9)], 'a5': [(3, 11)], 'm1': [(3, 10), (4, 11)], 'm2': [(2, 14), (4, 10)], 'm4': [(3, 12)], 'm7': [(4, 12), (3, 13)], 'w1': [(3, 14)], 'w2': [(4, 13)], 'end': [(4, 14)]}


def forward_kernel(outer, pieces, *refs):
    tokens_hbm, dy_hbm, starts_ref = refs[:3]
    vector_refs = refs[3 : 3 + VECTORS]
    shards = refs[3 + VECTORS : 7 + VECTORS]
    (
        normed_hbm, q_hbm, k_hbm, v_hbm, probs_hbm, att_hbm, hidden_hbm, slope_hbm, middle_hbm,
        normed2_hbm, qkv_hbm, attn_hbm, fc_hbm, proj_slots, terms_hbm, vectors,
    ) = refs[7 + VECTORS : 23 + VECTORS]
    (
        own, vector_slots, qkv_slots, attn_slots, fc_slots, qkv, attn, fc, x, normed, q, k, v, probs, att,
        hidden, slope, middle, normed2, dy, terms, q_cols, k_cols,
        move_sem, out_sem, probs_sem, terms_sem, own_sem, send_sem, recv_sem,
    ) = refs[23 + VECTORS :]
    rows, local, width = q.shape
    a, y, c, s = place()
    size, fc_size = vector_refs[0].shape[1], vector_refs[-1].shape[1]
    pairs, chunks = width // PAIR, fc.shape[1] // CHUNK

    load = pltpu.make_async_copy(tokens_hbm, x.at[:, pl.ds(TILE, local)], move_sem.at[0])
    load_dy = pltpu.make_async_copy(dy_hbm, dy, move_sem.at[3])
    load.start()
    own[...] = jnp.zeros_like(own)
    for i, ref in enumerate(vector_refs):
        own[i : i + 1, : ref.shape[1]] = ref[...].astype(jnp.float32)
    greet(outer)
    prev = remote(
        tokens_hbm.at[:, pl.ds(local - TILE, TILE)],
        x.at[:, pl.ds(0, TILE)],
        move_sem.at[1],
        move_sem.at[2],
        device(a, y, c, 1 - s),
    )
    work = Gather(
        outer,
        pieces,
        (own,) + shards,
        (vector_slots, qkv_slots, attn_slots, fc_slots, proj_slots),
        own_sem,
        send_sem,
        recv_sem,
        EAGER,
    )
    work.start()
    load_dy.start()

    def start_prev():
        @pl.when(s == 0)
        def _():
            prev.start()

    work.after = {PREV_AFTER: start_prev}
    comm, comm_at = sites_of(work, FORWARD_PLAN)
    stores = []

    def store(src, dst):
        copy = pltpu.make_async_copy(src, dst, out_sem.at[len(stores)])
        copy.start()
        stores.append(copy)

    def starts_of(r, i):
        tile = 2 * s - 1 + i
        start = starts_ref[r, jnp.maximum(tile, 0)]
        return jnp.where(tile < 0, TILE, start - tile * TILE)

    @pl.when(s == 0)
    def _():
        for r in range(rows):
            x[r, 0:TILE] = jnp.zeros((TILE, width), x.dtype)

    for r in range(rows):
        mask_columns(starts_of, r, q_cols.at[r], k_cols.at[r])
    load.wait()
    comm("ln")
    first, second = spread_vectors(vector_slots, size, fc_size, width)
    vectors[0:8], vectors[8:16] = first, second

    def norm_tile(r, span):
        normal, _ = normalize(x[r, span].astype(jnp.float32))
        normed[r, span] = (normal * vectors[0:1] + vectors[1:2]).astype(jnp.bfloat16)

    def norm_step(n, carry):
        r, t = n // (local // TILE), lax.rem(n, local // TILE) + 1
        norm_tile(r, pl.ds(pl.multiple_of(t * TILE, TILE), TILE))
        return carry

    lax.fori_loop(0, rows * (local // TILE), norm_step, 0)
    third = [slice(i * width, (i + 1) * width) for i in range(3)]
    for i, site in enumerate(("q", "k", "v")):
        comm(site)
        join_rows(qkv, qkv_slots, third[i])

        def row_step(r, carry):
            value = dot_nn(normed[r, TILE:], qkv[:, third[i]])
            if i == 0:
                value = (value + vectors[2:3]).astype(jnp.bfloat16)
                q[r] = value * jnp.bfloat16(1.0 / math.sqrt(HD))
            elif i == 1:
                k[r, TILE:] = value.astype(jnp.bfloat16)
            else:
                v[r, TILE:] = (value + vectors[3:4]).astype(jnp.bfloat16)
            return carry

        lax.fori_loop(0, rows, row_step, 0)
    store(q, q_hbm)
    store(qkv, qkv_hbm)
    lane = lane_index(TILE)
    causal = lax.broadcasted_iota(jnp.int32, (TILE, 2 * TILE), 0) <= (
        lax.broadcasted_iota(jnp.int32, (TILE, 2 * TILE), 1) & (TILE - 1)
    )

    def probs_copy(slot, r, j, tile):
        part = probs_hbm.at[r, j, :, pl.ds(tile * 4 * TILE, 4 * TILE)]
        return pltpu.make_async_copy(probs.at[slot], part, probs_sem.at[slot])

    def attend_pair(r, j, tile, slot):
        pair = pl.ds(pl.multiple_of(j * PAIR, PAIR), PAIR)
        queries = q[r, tile * TILE : (tile + 1) * TILE, pair]
        left = []
        for head in range(2):
            mine = (lane < HD) if head == 0 else (lane >= HD)
            mine = jnp.where(mine, queries, jnp.bfloat16(0))
            left.append(jnp.concatenate([mine, q_cols[r, tile]], axis=1))
        left = jnp.concatenate(left, axis=0)
        scores = []
        for w in range(2):
            keys = k[r, (tile + w) * TILE : (tile + w + 1) * TILE, pair]
            scores.append(dot_nt(jnp.concatenate([keys, k_cols[r, tile, w]], axis=1), left))
        far, near = scores[0], jnp.where(causal, scores[1], -FIRM)
        top = jnp.max(jnp.maximum(far, near), axis=0, keepdims=True)
        far, near = jnp.exp(far - top), jnp.exp(near - top)
        share = 1.0 / jnp.sum(far + near, axis=0, keepdims=True)
        far, near = (far * share).astype(jnp.bfloat16), (near * share).astype(jnp.bfloat16)
        probs[slot, :, 0 : 2 * TILE], probs[slot, :, 2 * TILE :] = far, near
        values = v[r, tile * TILE : (tile + 2) * TILE, pair]
        mixed = []
        for head in range(2):
            part = slice(head * TILE, (head + 1) * TILE)
            mixed.append(dot_tn(jnp.concatenate([far[:, part], near[:, part]], axis=0), values))
        span = pl.ds(pl.multiple_of(r * local + tile * TILE, TILE), TILE)
        att[span, pair] = jnp.where(lane < HD, mixed[0], mixed[1]).astype(jnp.bfloat16)

    def attend_step(n, tile, index):
        r, j = n // (pairs // 2), lax.rem(n, pairs // 2) * 2
        slot = lax.rem(n, 2) * 2

        @pl.when(n + index * rows * pairs // 2 >= 2)
        def _():
            for i in range(2):
                probs_copy(slot + i, r, j + i, tile).wait()

        for i in range(2):
            attend_pair(r, j + i, tile, slot + i)
        for i in range(2):
            probs_copy(slot + i, r, j + i, tile).start()

    def late_step(n, carry):
        comm_at(n, "b", rows * pairs // 2)
        attend_step(n, 1, 0)
        return carry

    lax.fori_loop(0, rows * pairs // 2, late_step, 0)
    comm("prev")

    @pl.when(s == 1)
    def _():
        prev.wait_recv()

    for r in range(rows):
        norm_tile(r, slice(0, TILE))
        k[r, 0:TILE] = dot_nn(normed[r, 0:TILE], qkv[:, third[1]]).astype(jnp.bfloat16)
        value = dot_nn(normed[r, 0:TILE], qkv[:, third[2]]) + vectors[3:4]
        v[r, 0:TILE] = value.astype(jnp.bfloat16)
    store(normed, normed_hbm)
    store(k, k_hbm)
    store(v, v_hbm)

    def early_step(n, carry):
        comm_at(n, "a", rows * pairs // 2)
        attend_step(n, 0, 1)
        return carry

    lax.fori_loop(0, rows * pairs // 2, early_step, 0)
    store(att, att_hbm)
    comm("asm")
    join_rows(attn, attn_slots, slice(0, width))
    store(attn, attn_hbm)

    def mlp_step(n, carry):
        r, j = n // chunks, lax.rem(n, chunks)
        span = pl.ds(pl.multiple_of(r * local, TILE), local)
        units = pl.ds(pl.multiple_of(j * CHUNK, CHUNK), CHUNK)

        @pl.when(j == 0)
        def _():
            value = x[r, TILE:].astype(jnp.float32) + dot_nn(att[span], attn[...]) + vectors[4:5]
            middle[span] = value
            normal, _ = normalize(value)
            normed2[span] = (normal * vectors[5:6] + vectors[6:7]).astype(jnp.bfloat16)

        comm_at(n, "m", rows * chunks)

        @pl.when(r == 0)
        def _():
            join_rows(fc, fc_slots, units)

        bias = vectors[8:9]
        for i in range(1, chunks):
            bias = jnp.where(j == i, vectors[8 + i : 9 + i], bias)
        value, back = gelu_pair(dot_nn(normed2[span], fc[:, units]) + bias)
        hidden[span, units] = value.astype(jnp.bfloat16)
        slope[span, units] = back.astype(jnp.bfloat16)
        return carry

    lax.fori_loop(0, rows * chunks, mlp_step, 0)
    store(slope, slope_hbm)
    store(hidden, hidden_hbm)
    store(middle, middle_hbm)
    store(normed2, normed2_hbm)
    store(fc, fc_hbm)
    load_dy.wait()
    share = terms.shape[-2]
    each = CHUNK // (8 * share)

    def terms_copy(j):
        slot = lax.rem(j, 2)
        return pltpu.make_async_copy(
            terms.at[slot], terms_hbm.at[pl.ds(j * each, each)], terms_sem.at[slot]
        )

    def weight_step(j, carry):
        comm_at(j, "w", chunks)
        units = pl.ds(pl.multiple_of(j * CHUNK, CHUNK), CHUNK)
        grad = dot_tn(hidden[:, units], dy[...]).astype(jnp.bfloat16)

        @pl.when(j >= 2)
        def _():
            terms_copy(j - 2).wait()

        terms[lax.rem(j, 2)] = grad.reshape((each, 2, 2, 2, share, width))
        terms_copy(j).start()
        return carry

    lax.fori_loop(0, chunks, weight_step, 0)
    comm("end")
    work.end()
    for j in range(chunks - 2, chunks):
        terms_copy(j).wait()
    for n in range(4):
        probs_copy(n, 0, n, 0).wait()
    for copy in stores:
        copy.wait()

    @pl.when(s == 0)
    def _():
        prev.wait_send()


def forward(outer, tokens, dy, starts, vectors, weights):
    rows, local, width = tokens.shape
    devices = outer * 8
    low, full = jnp.bfloat16, jnp.float32
    pairs = width // PAIR
    qkv_weight, attn_weight, fc_weight, proj_weight = weights
    hidden = fc_weight.shape[1]
    half = width // 2
    pieces = [(0, 0, PAIR)] + [(1, i * half, half) for i in range(6)] + [(2, 0, width)]
    pieces += [(3, j * CHUNK, CHUNK) for j in range(hidden // CHUNK)]
    pieces += [(4, j * 2 * PAIR, 2 * PAIR) for j in range(width // (2 * PAIR))]
    pieces = [piece + (order,) for piece, order in zip(pieces, FORWARD_ORDERS)]
    anywhere = pl.BlockSpec(memory_space=pl.ANY)
    vmem = pl.BlockSpec(memory_space=pltpu.VMEM)
    extended = (rows, local + TILE, width)
    flat = (rows * local, width)
    whole = [(devices * weight.shape[0], weight.shape[1]) for weight in weights]
    slots = [(outer, 2, 2, 2) + weight.shape for weight in weights]
    shape = jax.ShapeDtypeStruct
    results = pl.pallas_call(
        functools.partial(forward_kernel, outer, pieces),
        in_specs=[anywhere] * 2 + [pl.BlockSpec(memory_space=pltpu.SMEM)] + [vmem] * (VECTORS + 4),
        out_specs=[anywhere] * 15 + [vmem],
        out_shape=[
            shape(extended, low),
            shape(tokens.shape, low),
            shape(extended, low),
            shape(extended, low),
            shape((rows, pairs, TILE, 8 * TILE), low),
            shape(flat, low),
            shape((rows * local, hidden), low),
            shape((rows * local, hidden), low),
            shape(flat, full),
            shape(flat, low),
            shape(whole[0], low),
            shape(whole[1], low),
            shape(whole[2], low),
            shape(slots[3], low),
            shape(slots[3], low),
            shape((16, width), full),
        ],
        scratch_shapes=[
            pltpu.VMEM((16, PAIR), full),
            pltpu.VMEM((outer, 2, 2, 2, 16, PAIR), full),
            pltpu.VMEM(slots[0], low),
            pltpu.VMEM(slots[1], low),
            pltpu.VMEM(slots[2], low),
            pltpu.VMEM(whole[0], low),
            pltpu.VMEM(whole[1], low),
            pltpu.VMEM(whole[2], low),
            pltpu.VMEM(extended, low),
            pltpu.VMEM(extended, low),
            pltpu.VMEM(tokens.shape, low),
            pltpu.VMEM(extended, low),
            pltpu.VMEM(extended, low),
            pltpu.VMEM((4, TILE, 4 * TILE), low),
            pltpu.VMEM(flat, low),
            pltpu.VMEM((rows * local, hidden), low),
            pltpu.VMEM((rows * local, hidden), low),
            pltpu.VMEM(flat, full),
            pltpu.VMEM(flat, low),
            pltpu.VMEM(flat, low),
            pltpu.VMEM((2, CHUNK // (8 * proj_weight.shape[0])) + slots[3][1:], low),
            pltpu.VMEM((rows, 2, TILE, PAIR), low),
            pltpu.VMEM((rows, 2, 2, TILE, PAIR), low),
            pltpu.SemaphoreType.DMA((4,)),
            pltpu.SemaphoreType.DMA((12,)),
            pltpu.SemaphoreType.DMA((4,)),
            pltpu.SemaphoreType.DMA((2,)),
        ]
        + Gather.semaphores(outer, 5, len(pieces)),
        compiler_params=pltpu.CompilerParams(
            collective_id=2, has_side_effects=True, vmem_limit_bytes=VMEM_LIMIT
        ),
    )(tokens, dy, starts, *[vector.reshape(1, -1) for vector in vectors], *weights)
    return results


def shares_out(rows, columns):
    return jax.ShapeDtypeStruct((rows, columns), jnp.float32)


def column_pieces(array, columns, parts, orders):
    step = columns // parts
    return [(array, j * step, step, orders[j % len(orders)]) for j in range(parts)]


def pack_columns(values, start, lanes):
    width = values.shape[1]
    moved = pltpu.roll(values, (width - start) % width, 1) if start % width else values
    return jnp.where(lane_index(values.shape[0]) < lanes, moved[:, :PAIR], 0.0)


def mlp_backward(refs, fc_terms, attn_terms, vectors, att, att_grad, middle, sums, work, comm, comm_at):
    slope_hbm, normed_hbm, dy_hbm, attn_hbm, fc_hbm, proj_hbm, load_middle, load_att = refs

    def body(dy, slope, normed, attn, fc, proj, branch, stage, proj_sem, slope_sem, fc_sem, in_sem, stage_sem):
        tokens, width = dy.shape
        chunks = fc.shape[1] // CHUNK
        block = tokens // 2
        spans = [pl.ds(j * CHUNK, CHUNK) for j in range(chunks)]
        share = fc_terms.shape[-2]

        copies = lambda src, dst, sem: [
            pltpu.make_async_copy(src.at[:, span], dst.at[:, span], sem.at[j])
            for j, span in enumerate(spans)
        ]
        load_proj = [
            pltpu.make_async_copy(proj_hbm.at[span], proj.at[span], proj_sem.at[j])
            for j, span in enumerate(spans)
        ]
        load_slope, load_fc = copies(slope_hbm, slope, slope_sem), copies(fc_hbm, fc, fc_sem)
        others = ((dy_hbm, dy), (normed_hbm, normed), (attn_hbm, attn))
        load_dy, load_normed, load_attn = [
            pltpu.make_async_copy(src, dst, in_sem.at[i]) for i, (src, dst) in enumerate(others)
        ]
        load_dy.start()
        for j in range(chunks):
            load_proj[j].start()
            load_slope[j].start()
        load_normed.start()
        for j in range(chunks):
            load_fc[j].start()
        for load in (load_middle, load_attn, load_att):
            load.start()
        comm("start")
        load_dy.wait()

        def grad_step(n, carry):
            t, j = n // chunks, lax.rem(n, chunks)
            span = pl.ds(pl.multiple_of(t * block, block), block)
            units = pl.ds(pl.multiple_of(j * CHUNK, CHUNK), CHUNK)
            for i in range(chunks):

                @pl.when(n == i)
                def _():
                    load_proj[i].wait()
                    load_slope[i].wait()

            comm_at(n, "m", 2 * chunks)
            grad = dot_nt(dy[span], proj[units]) * slope[span, units].astype(jnp.float32)
            grad = grad.astype(jnp.bfloat16)
            slope[span, units] = grad
            total = column_sum(grad.astype(jnp.float32))
            for i in range(chunks):
                sums[12 + i : 13 + i] += jnp.where(j == i, total, 0.0)
            return carry

        lax.fori_loop(0, 2 * chunks, grad_step, 0)
        load_normed.wait()
        waited = set()

        def stage_copy(n):
            to = fc_terms.at[:, :, :, :, :, spans[n]] if n < chunks else attn_terms
            return pltpu.make_async_copy(stage.at[n % 2], to, stage_sem.at[n])

        def settle(n):
            if n not in waited:
                waited.add(n)
                stage_copy(n).wait()

        def put(n, grad):
            if n >= 2:
                settle(n - 2)
            stage[n % 2] = grad.astype(jnp.bfloat16).reshape(stage.shape[1:])
            stage_copy(n).start()

        for p, piece in enumerate(work.pieces):
            if piece[0] in (1, 2):
                work.before[p] = functools.partial(settle, piece[1] // CHUNK if piece[0] == 1 else chunks)
        for j in range(chunks):
            comm(f"w{j}")
            put(j, dot_tn(normed[...], slope[:, spans[j]]))

        def back_step(t, carry):
            span = pl.ds(pl.multiple_of(t * block, block), block)
            back = None
            for j in range(chunks):

                @pl.when(t == 0)
                def _():
                    load_fc[j].wait()

                comm_at(t, "o", 2, chunks, j)
                more = dot_nt(slope[span, spans[j]], fc[:, spans[j]])
                back = more if back is None else back + more

            @pl.when(t == 0)
            def _():
                load_middle.wait()
                load_attn.wait()

            upstream = dy[span].astype(jnp.float32)
            value = middle[span]
            normal, scale = normalize(value)
            sums[4:5] += column_sum(upstream)
            sums[5:6] += column_sum(back * normal)
            sums[6:7] += column_sum(back)
            total = upstream + norm_grad(back, vectors[5:6], normal, scale)
            middle[span] = total
            total = total.astype(jnp.bfloat16)
            branch[span] = total
            sums[7:8] += column_sum(total.astype(jnp.float32))
            att_grad[span] = dot_nt(total, attn[...]).astype(jnp.bfloat16)
            return carry

        lax.fori_loop(0, 2, back_step, 0)
        load_att.wait()
        comm("attn")
        put(chunks, dot_tn(att[...], branch[...]))
        comm("rest")
        for n in range(chunks + 1):
            settle(n)

    tokens, width = att.shape
    hidden, chunks = fc_hbm.shape[1], fc_hbm.shape[1] // CHUNK
    low = jnp.bfloat16
    dma = lambda n: pltpu.SemaphoreType.DMA((n,))
    pl.run_scoped(
        body,
        pltpu.VMEM((tokens, width), low),
        pltpu.VMEM((tokens, hidden), low),
        pltpu.VMEM((tokens, width), low),
        pltpu.VMEM(attn_hbm.shape, low),
        pltpu.VMEM(fc_hbm.shape, low),
        pltpu.VMEM(proj_hbm.shape, low),
        pltpu.VMEM((tokens, width), low),
        pltpu.VMEM((2,) + attn_terms.shape, low),
        dma(chunks),
        dma(chunks),
        dma(chunks),
        dma(3),
        dma(chunks + 1),
    )


def backward_kernel(outer, pieces, places, *refs):
    (
        hidden_hbm, slope_hbm, middle_hbm, normed2_hbm, att_hbm, dy_hbm, attn_hbm, fc_hbm, proj_hbm, proj_terms,
        probs_hbm, q_hbm, k_hbm, v_hbm, normed_hbm, x_hbm, weight_hbm, vectors,
        out_hbm, tokens_grad_hbm, fc_terms, attn_terms, proj_share, fc_share, attn_share, qkv_share, vector_share,
        flat_att, flat_grad, flat_middle, prev, late, vector_terms, vector_got, sums,
        main_sem, late_sem, vector_send, vector_recv, *rest,
    ) = refs
    rows, local, width = q_hbm.shape
    pairs = width // PAIR
    a, y, c, s = place()
    load_middle = pltpu.make_async_copy(middle_hbm, flat_middle, main_sem.at[0])
    load_att = pltpu.make_async_copy(att_hbm, flat_att, main_sem.at[1])
    sums[...] = jnp.zeros_like(sums)
    greet_all(outer)
    work = Scatter(
        outer, pieces, [proj_terms, fc_terms, attn_terms, None],
        [proj_share, fc_share, attn_share, qkv_share], rest[:-3], *rest[-3:], places,
    )
    comm, comm_at = sites_of(work, BACKWARD_PLAN)
    mlp_refs = (
        slope_hbm, normed2_hbm, dy_hbm, attn_hbm, fc_hbm, proj_hbm, load_middle, load_att,
    )
    mlp_backward(
        mlp_refs, fc_terms, attn_terms, vectors, flat_att, flat_grad, flat_middle, sums,
        work, comm, comm_at,
    )
    low, full = jnp.bfloat16, jnp.float32
    extended = (rows, local + TILE, width)
    dma = lambda *n: pltpu.SemaphoreType.DMA(n)
    pl.run_scoped(
        functools.partial(
            attend_backward, outer, work, comm, comm_at,
            (probs_hbm, q_hbm, k_hbm, v_hbm, normed_hbm, x_hbm, weight_hbm, hidden_hbm, proj_hbm, middle_hbm),
            vectors, tokens_grad_hbm, out_hbm,
            vector_share, flat_att, flat_grad, flat_middle, prev, late, vector_terms, vector_got, sums,
            late_sem, vector_send, vector_recv,
        ),
        pltpu.VMEM(q_hbm.shape, low),
        pltpu.VMEM(extended, low),
        pltpu.VMEM(extended, low),
        pltpu.VMEM(extended, low),
        pltpu.VMEM(weight_hbm.shape, low),
        pltpu.VMEM((6, TILE, 2 * TILE), low),
        pltpu.VMEM((4, TILE, 6 * TILE), low),
        pltpu.VMEM(q_hbm.shape, low),
        pltpu.VMEM(extended, low),
        pltpu.VMEM(extended, low),
        pltpu.VMEM((rows, TILE, width), full),
        pltpu.VMEM((outer, 2, 2, 2, weight_hbm.shape[0] // (outer * 8), weight_hbm.shape[1]), low),
        dma(3, rows),
        dma(3),
        dma(6),
        dma(4),
        dma(rows * local // TILE),
        dma(4),
        dma(2, 4),
        dma(2),
        dma(2),
    )


def attend_backward(
    outer, work, comm, comm_at, arrays, vectors, tokens_grad_hbm, out_hbm, vector_share, att, grad, middle,
    prev, late, vector_terms, vector_got, sums, late_sem, vector_send, vector_recv,
    q, k, v, normed, weight, far_probs, near_probs, dq, dk, dv, dq_part, qkv_terms,
    in_sem, after_sem, far_sem, near_sem, out_sem, proj_sem, hidden_sem, middle_sem, result_sem,
):
    probs_hbm, q_hbm, k_hbm, v_hbm, normed_hbm, x_hbm, weight_hbm, hidden_hbm, proj_hbm, middle_hbm = arrays
    rows, local, width = q.shape
    pairs = width // PAIR
    a, y, c, s = place()
    work.terms[3] = qkv_terms
    loads = [
        [pltpu.make_async_copy(src.at[r], dst.at[r], in_sem.at[i, r]) for r in range(rows)]
        for i, (src, dst) in enumerate(((q_hbm, q), (k_hbm, k), (v_hbm, v)))
    ]
    load_weight = pltpu.make_async_copy(weight_hbm, weight, after_sem.at[0])
    load_normed = pltpu.make_async_copy(normed_hbm, normed, after_sem.at[1])
    load_x = pltpu.make_async_copy(x_hbm, q, after_sem.at[2])
    wide = 2 * TILE

    def far_copy(n):
        part = probs_hbm.at[n // pairs, lax.rem(n, pairs), :, pl.ds(0, wide)]
        slot = lax.rem(n, 6)
        return pltpu.make_async_copy(part, far_probs.at[slot], far_sem.at[slot])

    def near_copy(n):
        slot = lax.rem(n, 4)
        part = probs_hbm.at[lax.rem(n, rows), n // rows, :, pl.ds(wide, 3 * wide)]
        return pltpu.make_async_copy(part, near_probs.at[slot], near_sem.at[slot])

    for r in range(rows):
        for load in loads:
            load[r].start()
        if r == 0:
            for n in range(6):
                far_copy(n).start()
    load_weight.start()
    load_normed.start()
    for n in range(4):
        near_copy(n).start()
    lane = lane_index(TILE)
    ones = jnp.ones((TILE, PAIR), jnp.bfloat16)

    def sides(r, pair, tile):
        span = pl.ds(pl.multiple_of(r * local + tile * TILE, TILE), TILE)
        grads, queries = grad[span, pair], q[r, tile * TILE : (tile + 1) * TILE, pair]
        product = grads.astype(jnp.float32) * att[span, pair].astype(jnp.float32)
        left, mine_grads, mine_queries = [], [], []
        for head in range(2):
            mine = (lane < HD) if head == 0 else (lane >= HD)
            delta = -jnp.sum(jnp.where(mine, product, 0.0), axis=-1, keepdims=True)
            high = delta.astype(jnp.bfloat16).astype(jnp.float32)
            extra = jnp.where(lane == 0, high, jnp.where(lane == 1, delta - high, 0.0))
            mine_grads.append(jnp.where(mine, grads, jnp.bfloat16(0)))
            mine_queries.append(jnp.where(mine, queries, jnp.bfloat16(0)))
            left.append(jnp.concatenate([mine_grads[-1], extra.astype(jnp.bfloat16)], axis=1))
        return [jnp.concatenate(part, axis=0) for part in (left, mine_grads, mine_queries)]

    def unit(r, pair, tile, side, chances):
        values = jnp.concatenate([v[r, tile * TILE : (tile + 1) * TILE, pair], ones], axis=1)
        d_score = (chances.astype(jnp.float32) * dot_nt(values, side[0])).astype(jnp.bfloat16)
        span = slice(tile * TILE, (tile + 1) * TILE)
        dk[r, span, pair] = dot_nn(d_score, side[2]).astype(jnp.bfloat16)
        dv[r, span, pair] = dot_nn(chances, side[1]).astype(jnp.bfloat16)
        return d_score

    def heads(parts):
        return jnp.where(lane < HD, parts[0], parts[1])

    far_steps = rows * pairs // 2

    def far_step(n, carry):
        r, j = n // (pairs // 2), lax.rem(n, pairs // 2) * 2
        for row in range(rows):

            @pl.when(n == row * (pairs // 2))
            def _():
                for load in loads:
                    load[row].wait()

        comm_at(n, "f", far_steps)
        for i in range(2):
            far_copy(2 * n + i).wait()
        for i in range(2):
            pair = pl.ds(pl.multiple_of((j + i) * PAIR, PAIR), PAIR)
            d_score = unit(r, pair, 0, sides(r, pair, 0), far_probs[lax.rem(2 * n + i, 6)])
            keys = k[r, 0:TILE, pair]
            dq_part[r, :, pair] = heads(
                [dot_tn(d_score[:, h * TILE : (h + 1) * TILE], keys) for h in range(2)]
            )

        @pl.when(2 * n + 6 < rows * pairs)
        def _():
            for i in range(2):
                far_copy(2 * n + 6 + i).start()

        return carry

    lax.fori_loop(0, far_steps, far_step, 0)
    load_weight.wait()
    comm("mm")
    third = [slice(i * width, (i + 1) * width) for i in range(3)]
    for r in range(rows):
        head = slice(0, TILE)
        prev[r] = (
            dot_nt(dk[r, head], weight[:, third[1]]) + dot_nt(dv[r, head], weight[:, third[2]])
        ).astype(jnp.bfloat16)
    late_copy = remote(prev, late, late_sem.at[0], late_sem.at[1], device(a, y, c, 1 - s))

    @pl.when(s == 1)
    def _():
        late_copy.start()
        late[...] = jnp.zeros_like(late)

    load_normed.wait()
    near_steps = rows * pairs // 2

    def near_pair(r, j, slot):
        pair = pl.ds(pl.multiple_of(j * PAIR, PAIR), PAIR)
        scale = 1.0 / math.sqrt(HD)
        one, two = sides(r, pair, 0), sides(r, pair, 1)
        both = [jnp.concatenate(part, axis=0) for part in zip(one, two)]
        first = unit(r, pair, 1, both, near_probs[slot, :, 0 : 2 * wide])
        second = unit(r, pair, 2, two, near_probs[slot, :, 2 * wide :])
        keys = k[r, TILE : 3 * TILE, pair]
        part = heads([dot_tn(first[:, h * TILE : (h + 1) * TILE], keys[:TILE]) for h in range(2)])
        dq[r, 0:TILE, pair] = ((dq_part[r, :, pair] + part) * scale).astype(jnp.bfloat16)
        crossed = jnp.concatenate([first[:, wide:], second], axis=0)
        part = heads([dot_tn(crossed[:, h * TILE : (h + 1) * TILE], keys) for h in range(2)])
        dq[r, TILE : 2 * TILE, pair] = (part * scale).astype(jnp.bfloat16)

    def near_step(n, carry):
        comm_at(n, "n", near_steps)
        for r in range(rows):
            near_copy(n * rows + r).wait()
        near_pair(0, n, lax.rem(n * rows, 4))
        comm_at(n, "h", near_steps)
        for r in range(1, rows):
            near_pair(r, n, lax.rem(n * rows + r, 4))

        @pl.when(n + 2 < near_steps)
        def _():
            for r in range(rows):
                near_copy((n + 2) * rows + r).start()

        @pl.when(lax.rem(n, 2) == 1)
        def _():
            comm_at(n, "g", near_steps)
            block = pl.ds(pl.multiple_of((n // 2) * (2 * PAIR), 2 * PAIR), 2 * PAIR)
            share = qkv_terms.shape[-2]
            for i, grads in enumerate((dq, dk, dv)):
                total = None
                for row in range(rows):
                    left = normed[row, TILE:] if i == 0 else normed[row]
                    part = dot_tn(left, grads[row, :, block])
                    total = part if total is None else total + part
                to = pl.ds(pl.multiple_of((n // 2) * width + i * 2 * PAIR, 2 * PAIR), 2 * PAIR)
                qkv_terms[:, :, :, :, :, to] = total.astype(jnp.bfloat16).reshape(
                    (outer, 2, 2, 2, share, 2 * PAIR)
                )

        return carry

    lax.fori_loop(0, near_steps, near_step, 0)
    load_x.start()
    chunks = hidden_hbm.shape[1] // CHUNK
    places = [(k, 0), (k, 1), (v, 0), (v, 1)]
    load_proj = [
        pltpu.make_async_copy(
            proj_hbm.at[pl.ds(j * CHUNK, CHUNK)], places[j][0].at[places[j][1]], proj_sem.at[j]
        )
        for j in range(chunks)
    ]

    def tile_of(u):
        return pl.ds(pl.multiple_of(u * TILE, TILE), TILE)

    def hidden_copy(u, j):
        lanes = pl.ds(pl.multiple_of(lax.rem(u, 2) * CHUNK, CHUNK), CHUNK)
        src = hidden_hbm.at[tile_of(u), pl.ds(j * CHUNK, CHUNK)]
        return pltpu.make_async_copy(src, near_probs.at[j, :, lanes], hidden_sem.at[lax.rem(u, 2), j])

    def middle_copy(u):
        slot = lax.rem(u, 2)
        return pltpu.make_async_copy(middle_hbm.at[tile_of(u)], dq_part.at[slot], middle_sem.at[slot])

    def result_copy(u):
        slot = lax.rem(u, 2)
        src = normed.at[slot, pl.ds(0, TILE)]
        return pltpu.make_async_copy(src, out_hbm.at[tile_of(u)], result_sem.at[slot])

    for load in load_proj:
        load.start()
    for u in range(2):
        middle_copy(u).start()
        for j in range(chunks):
            hidden_copy(u, j).start()
    for r in range(rows):
        sums[2:3] += column_sum(dq[r].astype(jnp.float32))
        sums[3:4] += column_sum(dv[r].astype(jnp.float32))
    load_x.wait()
    stores = []
    tiles = local // TILE
    for t in range(tiles):
        if t == tiles - 1:
            comm(f"t{t * rows}")

            @pl.when(s == 0)
            def _():
                late_copy.wait_recv()

        def token_step(r, carry):
            for row in range(rows):
                if t < tiles - 1 or row > 0:

                    @pl.when(r == row)
                    def _():
                        comm(f"t{t * rows + row}")

            span = slice(t * TILE, (t + 1) * TILE)
            keys = slice((t + 1) * TILE, (t + 2) * TILE)
            back = dot_nt(dq[r, span], weight[:, third[0]])
            back = back + dot_nt(dk[r, keys], weight[:, third[1]])
            back = back + dot_nt(dv[r, keys], weight[:, third[2]])
            if t == tiles - 1:
                back = back + late[r].astype(jnp.float32)
            normal, scale = normalize(q[r, span].astype(jnp.float32))
            sums[0:1] += column_sum(back * normal)
            sums[1:2] += column_sum(back)
            flat = pl.ds(pl.multiple_of(r * local + t * TILE, TILE), TILE)
            middle[flat] = middle[flat] + norm_grad(back, vectors[0:1], normal, scale)
            return carry

        lax.fori_loop(0, rows, token_step, 0)
        for r in range(rows):
            store = pltpu.make_async_copy(
                middle.at[pl.ds(r * local + t * TILE, TILE)],
                tokens_grad_hbm.at[r, pl.ds(t * TILE, TILE)],
                out_sem.at[t * rows + r],
            )
            store.start()
            stores.append(store)
    size = width // (outer * 8)
    fc_size = 4 * size
    total, fc_total = sums[0:8], sums[8:16]
    for d in range(outer * 8):
        row, start = divmod(d * fc_size, width)
        index = (d // 8, (d // 4) % 2, (d // 2) % 2, d % 2)
        vector_terms[index + (slice(0, 8),)] = pack_columns(total, d * size, size)
        vector_terms[index + (slice(8, 16),)] = pack_columns(
            jnp.broadcast_to(fc_total[4 + row : 5 + row], (8, width)), start, fc_size
        )
    vector_copies = [
        remote(
            vector_terms.at[to], vector_got.at[n], vector_send.at[n], vector_recv.at[n], device(*to)
        )
        for n, (to, _) in enumerate(everyone(outer))
    ]
    for copy in vector_copies:
        copy.start()
    for load in load_proj:
        load.wait()
    out_tiles = rows * local // TILE

    def out_step(u, carry):
        comm_at(u, "u", out_tiles)
        slot = lax.rem(u, 2)
        middle_copy(u).wait()
        result = dq_part[slot] + vectors[7:8]
        for j in range(chunks):
            hidden_copy(u, j).wait()
            lanes = pl.ds(pl.multiple_of(slot * CHUNK, CHUNK), CHUNK)
            result = result + dot_nn(near_probs[j, :, lanes], places[j][0][places[j][1]])

        @pl.when(u >= 2)
        def _():
            result_copy(u - 2).wait()

        normed[slot, 0:TILE] = result.astype(jnp.bfloat16)
        result_copy(u).start()

        @pl.when(u + 2 < out_tiles)
        def _():
            middle_copy(u + 2).start()
            for j in range(chunks):
                hidden_copy(u + 2, j).start()

        return carry

    lax.fori_loop(0, out_tiles, out_step, 0)
    for u in range(out_tiles - 2, out_tiles):
        result_copy(u).wait()
    comm("end")
    value = vector_terms[a, y, c, s]
    for n, copy in enumerate(vector_copies):
        copy.wait_recv()
        value = value + vector_got[n]
    vector_share[...] = value
    work.end()
    for copy in vector_copies:
        copy.wait_send()
    for store in stores:
        store.wait()

    @pl.when(s == 1)
    def _():
        late_copy.wait_send()


BACKWARD_ORDERS = (0, 1, 1, 0, 1, 1, 0, 1, 0, 1, 1, 0, 1, 1, 1, 0, 1, 0, 1)
BACKWARD_PLAN = {'start': [(0, 0), (0, 1), (0, 2)], 'm3': [(1, 0)], 'm4': [(1, 1), (1, 2)], 'w2': [(0, 3), (0, 4)], 'w3': [(2, 0), (0, 5), (0, 6)], 'o0': [(2, 1), (1, 3), (1, 4), (0, 7), (0, 8)], 'o1': [(0, 9), (0, 10)], 'o2': [(1, 5), (1, 6)], 'o4': [(1, 7), (1, 8), (1, 9), (3, 1), (2, 2), (1, 10)], 'o7': [(2, 3)], 'attn': [(3, 0), (2, 6)], 'rest': [(4, 1), (2, 4)], 'f0': [(2, 5), (2, 8), (0, 11), (0, 12)], 'f3': [(4, 0), (3, 2), (2, 7)], 'mm': [(3, 4), (1, 11)], 'n0': [(3, 5), (2, 9), (1, 12), (3, 7)], 'n1': [(4, 2), (2, 10)], 'h1': [(3, 3), (2, 11), (4, 4)], 'g1': [(3, 6)], 'n2': [(4, 5), (4, 7), (3, 8), (0, 13), (0, 14)], 'h2': [(4, 3)], 'n3': [(2, 12)], 'h3': [(4, 6)], 'g3': [(4, 8), (3, 11), (1, 13), (1, 14)], 'n4': [(0, 15), (0, 16)], 'n5': [(4, 11)], 'g5': [(2, 13), (1, 15), (1, 16)], 't0': [(0, 17), (0, 18)], 't1': [(3, 9), (3, 10), (2, 14)], 't2': [(3, 12), (2, 16), (1, 17), (1, 18), (3, 13)], 't3': [(4, 9)], 'u0': [(4, 10), (2, 15)], 'u1': [(4, 12), (4, 13), (3, 14), (3, 16), (2, 18)], 'u2': [(3, 15), (2, 17)], 'u3': [(4, 14), (3, 18)], 'end': [(4, 15), (4, 16), (3, 17), (4, 18), (4, 17)]}


def backward(outer, hidden, slope, middle, normed2, att, dy, attn, fc, proj, proj_terms, probs, q, k, v, normed, x, weight, vectors):
    rows, local, width = q.shape
    devices = outer * 8
    low, full = jnp.bfloat16, jnp.float32
    share = weight.shape[0] // devices
    units = fc.shape[1]
    anywhere = pl.BlockSpec(memory_space=pl.ANY)
    vmem = pl.BlockSpec(memory_space=pltpu.VMEM)
    blocks = weight.shape[1] // width
    pieces = column_pieces(0, width, 3, (0,))
    pieces += column_pieces(1, units, 2 * units // width, (0,)) + column_pieces(2, width, 2, (0,))
    first = len(pieces)
    pieces += column_pieces(3, weight.shape[1], 2 * blocks, (0,))
    pieces = [piece[:3] + (order,) for piece, order in zip(pieces, BACKWARD_ORDERS)]
    part, half = width // 3, width // 2
    places = {}
    for b in range(blocks):
        for h in range(2):
            begin, end = h * half, (h + 1) * half
            places[first + 2 * b + h] = [
                (max(i * part, begin) - begin, min((i + 1) * part, end) - max(i * part, begin),
                 i * width + b * part + max(i * part, begin) - i * part)
                for i in range(blocks)
                if max(i * part, begin) < min((i + 1) * part, end)
            ]
    shapes = [(units // devices, width, low), (share, units, low), (share, width, low), (share, weight.shape[1], low)]
    slots = lambda columns: jax.ShapeDtypeStruct((outer, 2, 2, 2, share, columns), low)
    flat = dy.shape
    return pl.pallas_call(
        functools.partial(backward_kernel, outer, pieces, places),
        in_specs=[anywhere] * 17 + [vmem],
        out_specs=[anywhere] * 4 + [vmem] * 5,
        out_shape=[
            jax.ShapeDtypeStruct(flat, low),
            jax.ShapeDtypeStruct(x.shape, full),
            slots(units),
            slots(width),
        ]
        + [shares_out(shape[0], shape[1]) for shape in shapes]
        + [shares_out(16, PAIR)],
        scratch_shapes=[
            pltpu.VMEM(flat, low),
            pltpu.VMEM(flat, low),
            pltpu.VMEM(flat, full),
            pltpu.VMEM((rows, TILE, width), low),
            pltpu.VMEM((rows, TILE, width), low),
            pltpu.VMEM((outer, 2, 2, 2, 16, PAIR), full),
            pltpu.VMEM((devices - 1, 16, PAIR), full),
            pltpu.VMEM((16, width), full),
            pltpu.SemaphoreType.DMA((2,)),
            pltpu.SemaphoreType.DMA((2,)),
            pltpu.SemaphoreType.DMA((devices - 1,)),
            pltpu.SemaphoreType.DMA((devices - 1,)),
        ]
        + Scatter.scratch(outer, shapes, pieces),
        compiler_params=pltpu.CompilerParams(
            collective_id=4, has_side_effects=True, vmem_limit_bytes=VMEM_LIMIT
        ),
    )(
        hidden, slope, middle, normed2, att, dy, attn, fc, proj, proj_terms,
        probs, q, k, v, normed, x, weight, vectors,
    )


def gather_weights(outer, weights, vectors, fc_bias):
    devices = outer * 8
    shards = [pack_vectors(vectors + [fc_bias])]
    shards += [w.reshape(pack_shape(w.shape)) for w in weights]
    full = gather_all(outer, shards, cut([shard.shape for shard in shards]))
    packed = full[0].reshape(devices, -1)
    count, size = len(vectors), vectors[0].shape[0]
    first = packed[:, : count * size].reshape(devices, count, size)
    first = jnp.swapaxes(first, 0, 1).reshape(count, devices * size)
    second = packed[:, count * size : count * size + fc_bias.shape[0]].reshape(-1, devices * size)
    whole = [f.reshape(devices * w.shape[0], w.shape[1]) for f, w in zip(full[1:], weights)]
    return whole, jnp.concatenate([first, second], axis=0)


def scatter_grads(outer, weight_terms, vector_terms, fc_bias_term):
    devices = outer * 8
    count, width = vector_terms.shape
    first = jnp.swapaxes(vector_terms.reshape(count, devices, width // devices), 0, 1)
    first = first.reshape(devices, -1)
    second = fc_bias_term.reshape(devices, -1)
    packed = pack_vectors([first, second])
    terms = [packed.reshape((outer, 2, 2, 2) + packed.shape[1:])]
    shapes = [(term.shape[0] // devices, term.shape[1]) for term in weight_terms]
    for term, shape in zip(weight_terms, shapes):
        terms.append(term.reshape((outer, 2, 2, 2) + pack_shape(shape)))
    shares = scatter_all(outer, terms, cut([term.shape[-2:] for term in terms]))
    flat = shares[0].reshape(-1)
    size = width // devices
    vectors = [flat[i * size : (i + 1) * size] for i in range(count)]
    fc_bias = flat[count * size : count * size + second.shape[1]]
    return [share.reshape(shape) for share, shape in zip(shares[1:], shapes)], vectors, fc_bias


def shards(
    tokens_in,
    doc_starts,
    norm1_gain,
    norm1_bias,
    qkv_weight,
    query_bias,
    value_bias,
    attn_weight,
    attn_bias,
    norm2_gain,
    norm2_bias,
    fc_weight,
    fc_bias,
    proj_weight,
    proj_bias,
    out_grad,
):
    outer = lax.axis_size("batch") // 4
    rows, local, width = tokens_in.shape
    seq = lax.axis_index("seq")
    weights = [qkv_weight, attn_weight, fc_weight, proj_weight]
    vectors = [norm1_gain, norm1_bias, query_bias, value_bias, attn_bias, norm2_gain, norm2_bias, proj_bias]
    flat = lambda value: value.reshape(rows * local, width)
    block = lambda value: value.reshape(rows, local, width)
    dy = flat(out_grad)
    devices = 8 * outer
    if qkv_weight.shape[0] % 8 == 0 and proj_weight.shape[0] % 16 == 0 and CHUNK % (8 * proj_weight.shape[0]) == 0:
        (
            normed, q, k, v, probs, att, hidden, slope, middle, normed2, qkv, attn, fc, proj, proj_terms, vectors,
        ) = forward(outer, tokens_in, dy, doc_starts, vectors + [fc_bias], weights)
        proj = proj.reshape(devices * proj_weight.shape[0], width)
        out, tokens_grad, _, _, proj_share, fc_share, attn_share, qkv_share, packed = backward(
            outer, hidden, slope, middle, normed2, att, dy, attn, fc, proj, proj_terms,
            probs, q, k, v, normed, tokens_in, qkv, vectors,
        )
        size = width // devices
        weights = [qkv_share, attn_share, fc_share, proj_share]
        shares = [packed[i, :size] for i in range(8)]
        fc_bias_share = packed[8, : 4 * size]
    else:
        first = 2 * seq
        padded = jnp.pad(doc_starts, ((0, 0), (1, 0)))
        starts = lax.dynamic_slice_in_dim(padded, first, 3, 1)
        starts = starts - TILE * (first - 1 + jnp.arange(3, dtype=jnp.int32))
        prev = lax.ppermute(tokens_in[:, local - TILE :], "seq", [(0, 1)])
        (qkv, attn, fc, proj), vectors = gather_weights(outer, weights, vectors, fc_bias)
        normed, q, k, v = project(tokens_in, prev, qkv, vectors)
        probs, att, inverse = attend(starts, q, k, v)
        out, middle_grad, att_grad, attn_grad, fc_grad, proj_grad, mlp_sums = mlp(
            flat(tokens_in), flat(att), dy, attn, fc, proj, vectors
        )
        dq, dk, dv = attend_grad(probs, q, k, v, block(att_grad), att, inverse)
        qkv_grad, prev_grad, project_sums = project_grad(normed, dq, dk, dv, qkv)
        late = lax.ppermute(prev_grad, "seq", [(1, 0)])
        tokens_grad, norm_sums = tokens_grad_of(
            tokens_in, dq, dk, dv, qkv, late, block(middle_grad), vectors
        )
        sums = jnp.concatenate([norm_sums[:2], project_sums[:2], mlp_sums[:4]], axis=0)
        weights, shares, fc_bias_share = scatter_grads(
            outer, [qkv_grad, attn_grad, fc_grad, proj_grad], sums, mlp_sums[4:]
        )
    gain1, bias1, query, value, proj_b, gain2, bias2, attn_b = shares
    return (
        out.reshape(rows, local, width),
        tokens_grad,
        gain1,
        bias1,
        weights[0],
        query,
        value,
        weights[1],
        attn_b,
        gain2,
        bias2,
        weights[2],
        fc_bias_share,
        weights[3],
        proj_b,
    )


def solution(mesh):
    return jax.shard_map(
        shards,
        mesh=mesh,
        in_specs=(
            P("batch", "seq", None),
            P("batch", None),
            P(("batch", "seq")),
            P(("batch", "seq")),
            P(("batch", "seq"), None),
            P(("batch", "seq")),
            P(("batch", "seq")),
            P(("batch", "seq"), None),
            P(("batch", "seq")),
            P(("batch", "seq")),
            P(("batch", "seq")),
            P(("batch", "seq"), None),
            P(("batch", "seq")),
            P(("batch", "seq"), None),
            P(("batch", "seq")),
            P("batch", "seq", None),
        ),
        out_specs=(
            P("batch", "seq", None),
            P("batch", "seq", None),
            P(("batch", "seq")),
            P(("batch", "seq")),
            P(("batch", "seq"), None),
            P(("batch", "seq")),
            P(("batch", "seq")),
            P(("batch", "seq"), None),
            P(("batch", "seq")),
            P(("batch", "seq")),
            P(("batch", "seq")),
            P(("batch", "seq"), None),
            P(("batch", "seq")),
            P(("batch", "seq"), None),
            P(("batch", "seq")),
        ),
        check_vma=False,
    )
```

```python
import functools
import math

import jax
import jax.numpy as jnp
from jax import lax
from jax.experimental import pallas as pl
from jax.experimental.pallas import tpu as pltpu
from jax.sharding import PartitionSpec as P

HD = 64
EPSILON = 1e-05
GELU_SCALE = 0.7978845608028654
MESH_ID = pl.DeviceIdType.MESH
VMEM_LIMIT = 62 * 2**20
EVERY = slice(None)


def place():
    batch, seq = lax.axis_index("batch"), lax.axis_index("seq")
    return (batch // 4, (batch // 2) % 2, batch % 2, seq)


def device(a, y, c, s):
    return (a * 4 + y * 2 + c, s)


def greet(outer):
    a, y, c, s = place()
    barrier = pltpu.get_barrier_semaphore()
    others = [device(lax.rem(a + k, outer), y, c, s) for k in range(1, outer)]
    others += [device(a, 1 - y, c, s), device(a, y, c, 1 - s), device(a, y, 1 - c, s)]
    for other in others:
        pl.semaphore_signal(barrier, inc=1, device_id=other, device_id_type=MESH_ID)
    pl.semaphore_wait(barrier, len(others))


def everyone(outer):
    a, y, c, s = place()
    devices = outer * 8
    me = ((a * 2 + y) * 2 + c) * 2 + s
    split = lambda d: (d // 8, (d // 4) % 2, (d // 2) % 2, d % 2)
    return [
        (split(lax.rem(me + k, devices)), split(lax.rem(me + devices - k, devices)))
        for k in range(1, devices)
    ]


def greet_all(outer):
    barrier = pltpu.get_barrier_semaphore()
    others = everyone(outer)
    for other, _ in others:
        pl.semaphore_signal(barrier, inc=1, device_id=device(*other), device_id_type=MESH_ID)
    pl.semaphore_wait(barrier, len(others))


def remote(src, dst, send_sem, recv_sem, other):
    return pltpu.make_async_remote_copy(
        src_ref=src,
        dst_ref=dst,
        send_sem=send_sem,
        recv_sem=recv_sem,
        device_id=other,
        device_id_type=MESH_ID,
    )


def sites_of(work, plan):
    def comm(name):
        for phase, p in plan.get(name, ()):
            work.act(phase, p)
            if (phase, p) in work.after:
                work.after[(phase, p)]()

    def comm_at(n, name, count, stride=1, offset=0):
        for i in range(count):
            site = f"{name}{i * stride + offset}"
            if site in plan:

                @pl.when(n == i)
                def _():
                    comm(site)

    return comm, comm_at


class Gather:
    def __init__(self, outer, pieces, shards, outs, own_sem, send_sem, recv_sem, eager=99):
        self.outer, self.pieces, self.shards, self.outs = outer, pieces, shards, outs
        self.own_sem, self.send_sem, self.recv_sem = own_sem, send_sem, recv_sem
        self.eager, self.after = eager, {}
        self.place = place()

    def sems(self, p, k):
        return self.send_sem.at[p, k], self.recv_sem.at[p, k]

    def own(self, i):
        return pltpu.make_async_copy(
            self.shards[i], self.outs[i].at[self.place], self.own_sem.at[i]
        )

    def first(self, p, k):
        i, start, width, order = self.pieces[p]
        a, y, c, s = self.place
        columns = pl.ds(start, width)
        src = self.shards[i].at[:, columns]
        dst = self.outs[i].at[a, y, c, s, :, columns]
        if k == 0:
            return remote(src, dst, *self.sems(p, 0), self.near(order))
        return remote(src, dst, *self.sems(p, k), device(lax.rem(a + k, self.outer), y, c, s))

    def near(self, order):
        a, y, c, s = self.place
        return device(a, 1 - y, c, s) if order == 0 else device(a, y, c, 1 - s)

    def second(self, p, k):
        i, start, width, order = self.pieces[p]
        a, y, c, s = self.place
        source = lax.rem(a + self.outer - k, self.outer)
        block = self.outs[i].at[source, y, c, s, :, pl.ds(start, width)]
        return remote(block, block, *self.sems(p, self.outer - 1 + k), self.near(order))

    def third(self, p):
        i, start, width, order = self.pieces[p]
        a, y, c, s = self.place
        index = (EVERY, EVERY, c, s) if order == 0 else (EVERY, y, c, EVERY)
        block = self.outs[i].at[index + (EVERY, pl.ds(start, width))]
        return remote(block, block, *self.sems(p, 2 * self.outer - 1), self.near(1 - order))

    def fourth(self, p):
        i, start, width, order = self.pieces[p]
        a, y, c, s = self.place
        block = self.outs[i].at[EVERY, EVERY, c, EVERY, EVERY, pl.ds(start, width)]
        return remote(block, block, *self.sems(p, 2 * self.outer), device(a, y, 1 - c, s))

    def start(self):
        for p in range(len(self.pieces)):
            for k in range(1, self.outer):
                self.first(p, k).start()
            if p < self.eager:
                self.first(p, 0).start()
        for i in range(len(self.shards)):
            self.own(i).start()

    def act(self, phase, p):
        outer = self.outer
        if phase == 1:
            if p >= self.eager:
                self.first(p, 0).start()
            for k in range(1, outer):
                self.first(p, k).wait_recv()
                self.second(p, k).start()
        elif phase == 2:
            if p == 0:
                for n in range(len(self.shards)):
                    self.own(n).wait()
            self.first(p, 0).wait_recv()
            for k in range(1, outer):
                self.second(p, k).wait_recv()
            self.third(p).start()
        elif phase == 3:
            self.third(p).wait_recv()
            self.fourth(p).start()
        else:
            self.fourth(p).wait_recv()

    def end(self):
        for p in range(len(self.pieces)):
            for k in range(self.outer):
                self.first(p, k).wait_send()
            for k in range(1, self.outer):
                self.second(p, k).wait_send()
            self.third(p).wait_send()
            self.fourth(p).wait_send()

    @staticmethod
    def semaphores(outer, arrays, pieces):
        return [
            pltpu.SemaphoreType.DMA((arrays,)),
            pltpu.SemaphoreType.DMA((pieces, 2 * outer + 1)),
            pltpu.SemaphoreType.DMA((pieces, 2 * outer + 1)),
        ]


def add_slots(target, other):
    target[...] = target[...] + other[...]


class Scatter:
    def __init__(self, outer, pieces, terms, outs, slots, own_sem, send_sem, recv_sem, places=None):
        self.outer, self.pieces, self.terms, self.outs = outer, pieces, terms, outs
        n = len(pieces)
        self.held, self.got = slots[:n], [slots[k * n : (k + 1) * n] for k in range(1, 5)]
        self.own_sem, self.send_sem, self.recv_sem = own_sem, send_sem, recv_sem
        self.places, self.before, self.after = places or {}, {}, {}
        self.place = place()

    def sems(self, p, k):
        return self.send_sem.at[p, k], self.recv_sem.at[p, k]

    def own(self, p):
        i, start, width, order = self.pieces[p]
        a, y, c, s = self.place
        block = self.terms[i].at[EVERY, EVERY, c, EVERY, EVERY, pl.ds(start, width)]
        return pltpu.make_async_copy(block, self.held[p], self.own_sem.at[p])

    def first(self, p):
        i, start, width, order = self.pieces[p]
        a, y, c, s = self.place
        block = self.terms[i].at[EVERY, EVERY, 1 - c, EVERY, EVERY, pl.ds(start, width)]
        return remote(block, self.got[0][p], *self.sems(p, 0), device(a, y, 1 - c, s))

    def second(self, p):
        a, y, c, s = self.place
        if self.pieces[p][3] == 0:
            src, other = self.held[p].at[:, :, 1 - s], device(a, y, c, 1 - s)
        else:
            src, other = self.held[p].at[:, 1 - y], device(a, 1 - y, c, s)
        return remote(src, self.got[1][p], *self.sems(p, 1), other)

    def third(self, p):
        a, y, c, s = self.place
        if self.pieces[p][3] == 0:
            src, other = self.held[p].at[:, 1 - y, s], device(a, 1 - y, c, s)
        else:
            src, other = self.held[p].at[:, y, 1 - s], device(a, y, c, 1 - s)
        return remote(src, self.got[2][p], *self.sems(p, 2), other)

    def fourth(self, p, k):
        a, y, c, s = self.place
        to = lax.rem(a + k, self.outer)
        src = self.held[p].at[to, y, s]
        return remote(src, self.got[3][p].at[k - 1], *self.sems(p, 2 + k), device(to, y, c, s))

    def act(self, phase, p):
        outer = self.outer
        a, y, c, s = self.place
        i, start, width, order = self.pieces[p]
        if phase == 0:
            if p in self.before:
                self.before[p]()
            self.own(p).start()
            self.first(p).start()
        elif phase == 1:
            self.own(p).wait()
            self.first(p).wait_recv()
            add_slots(self.held[p], self.got[0][p])
            self.second(p).start()
        elif phase == 2:
            self.second(p).wait_recv()
            mine = (EVERY, EVERY, s) if order == 0 else (EVERY, y)
            add_slots(self.held[p].at[mine], self.got[1][p])
            self.third(p).start()
        elif phase == 3:
            self.third(p).wait_recv()
            add_slots(self.held[p].at[:, y, s], self.got[2][p])
            for k in range(1, outer):
                self.fourth(p, k).start()
        else:
            value = self.held[p][a, y, s].astype(jnp.float32)
            for k in range(1, outer):
                self.fourth(p, k).wait_recv()
                value = value + self.got[3][p][k - 1].astype(jnp.float32)
            for offset, size, to in self.places.get(p, [(0, width, start)]):
                self.outs[i][:, to : to + size] = value[:, offset : offset + size]

    def end(self):
        for p in range(len(self.pieces)):
            self.first(p).wait_send()
            self.second(p).wait_send()
            self.third(p).wait_send()
            for k in range(1, self.outer):
                self.fourth(p, k).wait_send()

    @staticmethod
    def scratch(outer, shapes, pieces):
        def slot(p, *lead):
            i, start, width, order = pieces[p]
            return pltpu.VMEM(lead + (shapes[i][0], width), shapes[i][2])

        n = range(len(pieces))
        leads = ((outer, 2, 2), (outer, 2, 2), (outer, 2), (outer,), (max(outer - 1, 1),))
        return [slot(p, *lead) for lead in leads for p in n] + [
            pltpu.SemaphoreType.DMA((len(pieces),)),
            pltpu.SemaphoreType.DMA((len(pieces), outer + 2)),
            pltpu.SemaphoreType.DMA((len(pieces), outer + 2)),
        ]


def steps_in_order(count, lags):
    first = 5 - len(lags)
    steps = [(p + lag, k + first, p) for p in range(count) for k, lag in enumerate(lags)]
    return [(p, phase) for _, phase, p in sorted(steps)]


def gather_kernel(outer, pieces, count, *refs):
    greet(outer)
    work = Gather(outer, pieces, refs[:count], refs[count : 2 * count], *refs[2 * count :])
    work.start()
    for p, phase in steps_in_order(len(pieces), (1, 2, 4, 6)):
        work.act(phase, p)
    work.end()


def gather_all(outer, shards, pieces):
    count = len(shards)
    return pl.pallas_call(
        functools.partial(gather_kernel, outer, pieces, count),
        out_shape=[
            jax.ShapeDtypeStruct((outer, 2, 2, 2) + shard.shape, shard.dtype) for shard in shards
        ],
        in_specs=[pl.BlockSpec(memory_space=pltpu.VMEM)] * count,
        out_specs=[pl.BlockSpec(memory_space=pl.ANY)] * count,
        scratch_shapes=Gather.semaphores(outer, count, len(pieces)),
        compiler_params=pltpu.CompilerParams(
            collective_id=0, has_side_effects=True, vmem_limit_bytes=VMEM_LIMIT
        ),
    )(*shards)


def scatter_kernel(outer, pieces, count, *refs):
    greet(outer)
    rest = refs[2 * count :]
    work = Scatter(outer, pieces, refs[:count], refs[count : 2 * count], rest[:-3], *rest[-3:])
    for p, phase in steps_in_order(len(pieces), (0, 1, 3, 4, 5)):
        work.act(phase, p)
    work.end()


def scatter_all(outer, terms, pieces):
    count = len(terms)
    shapes = [term.shape[-2:] + (term.dtype,) for term in terms]
    return pl.pallas_call(
        functools.partial(scatter_kernel, outer, pieces, count),
        out_shape=[jax.ShapeDtypeStruct(term.shape[-2:], jnp.float32) for term in terms],
        in_specs=[pl.BlockSpec(memory_space=pl.ANY)] * count,
        out_specs=[pl.BlockSpec(memory_space=pltpu.VMEM)] * count,
        scratch_shapes=Scatter.scratch(outer, shapes, pieces),
        compiler_params=pltpu.CompilerParams(
            collective_id=1, has_side_effects=True, vmem_limit_bytes=VMEM_LIMIT
        ),
    )(*terms)


def cut(shape_list):
    pieces = []
    for i, (rows, columns) in enumerate(shape_list):
        parts, blocks = 1, columns // 128
        if rows % 8 == 0:
            fits = [k for k in range(1, blocks + 1) if blocks % k == 0 and rows * columns // k <= 25000]
            parts = min(fits) if fits else 1
        width = columns // parts
        for k in range(parts):
            pieces.append((i, k * width, width, len(pieces) % 2))
    return pieces


def pack_shape(shape):
    rows, columns = shape
    return shape if rows % 8 == 0 else (rows * columns // 128, 128)


def pack_vectors(parts):
    joined = jnp.concatenate([part.astype(jnp.float32) for part in parts], axis=-1)
    size = -(-joined.shape[-1] // 1024) * 1024
    pad = [(0, 0)] * (joined.ndim - 1) + [(0, size - joined.shape[-1])]
    return jnp.pad(joined, pad).reshape(joined.shape[:-1] + (size // 128, 128))


TILE = 256
PAIR = 128
FIRM = 1e30


def dot_nn(left, right):
    return lax.dot_general(left, right, (((1,), (0,)), ((), ())), preferred_element_type=jnp.float32)


def dot_nt(left, right):
    return lax.dot_general(left, right, (((1,), (1,)), ((), ())), preferred_element_type=jnp.float32)


def dot_tn(left, right):
    return lax.dot_general(left, right, (((0,), (0,)), ((), ())), preferred_element_type=jnp.float32)


def normalize(values):
    average = jnp.mean(values, axis=-1, keepdims=True)
    centered = values - average
    variance = jnp.mean(centered * centered, axis=-1, keepdims=True)
    scale = lax.rsqrt(variance + EPSILON)
    return centered * scale, scale


def norm_grad(upstream, gain, normal, scale):
    inner = upstream * gain
    first = jnp.mean(inner, axis=-1, keepdims=True)
    second = jnp.mean(inner * normal, axis=-1, keepdims=True)
    return scale * (inner - first - normal * second)


def column_sum(values):
    return jnp.sum(values, axis=0, keepdims=True)


def project_kernel(x_ref, prev_ref, weight_ref, vectors_ref, normed_ref, q_ref, k_ref, v_ref):
    tile = pl.program_id(1)
    width = x_ref.shape[-1]
    x = jnp.where(tile == 0, prev_ref[0], x_ref[0]).astype(jnp.float32)
    normal, _ = normalize(x)
    normed = (normal * vectors_ref[0:1] + vectors_ref[1:2]).astype(jnp.bfloat16)
    normed_ref[0] = normed

    @pl.when(tile > 0)
    def _():
        queries = dot_nn(normed, weight_ref[:, :width]) + vectors_ref[2:3]
        q_ref[0] = queries.astype(jnp.bfloat16) * jnp.bfloat16(1.0 / math.sqrt(HD))

    k_ref[0] = dot_nn(normed, weight_ref[:, width : 2 * width]).astype(jnp.bfloat16)
    values = dot_nn(normed, weight_ref[:, 2 * width :]) + vectors_ref[3:4]
    v_ref[0] = values.astype(jnp.bfloat16)


def project(tokens, prev, weight, vectors):
    rows, local, width = tokens.shape
    tiles = local // TILE
    here = lambda r, t: (r, jnp.maximum(t - 1, 0), 0)
    extended = jax.ShapeDtypeStruct((rows, local + TILE, width), jnp.bfloat16)
    return pl.pallas_call(
        project_kernel,
        grid=(rows, tiles + 1),
        in_specs=[
            pl.BlockSpec((1, TILE, width), here),
            pl.BlockSpec((1, TILE, width), lambda r, t: (r, 0, 0)),
            pl.BlockSpec(weight.shape, lambda r, t: (0, 0)),
            pl.BlockSpec(vectors.shape, lambda r, t: (0, 0)),
        ],
        out_specs=[
            pl.BlockSpec((1, TILE, width), lambda r, t: (r, t, 0)),
            pl.BlockSpec((1, TILE, width), here),
            pl.BlockSpec((1, TILE, width), lambda r, t: (r, t, 0)),
            pl.BlockSpec((1, TILE, width), lambda r, t: (r, t, 0)),
        ],
        out_shape=[extended, jax.ShapeDtypeStruct(tokens.shape, jnp.bfloat16), extended, extended],
        compiler_params=pltpu.CompilerParams(vmem_limit_bytes=VMEM_LIMIT),
    )(tokens, prev, weight, vectors)


def lane_index(rows):
    return lax.broadcasted_iota(jnp.int32, (rows, PAIR), 1)


def mask_columns(starts_of, row, q_cols, k_cols):
    place = lax.broadcasted_iota(jnp.int32, (TILE, PAIR), 0)
    lane = lane_index(TILE)
    for tile in range(2):
        before, start = starts_of(row, tile), starts_of(row, tile + 1)
        late = jnp.where(place >= start, 1.0, 0.0)
        q_cols[tile] = jnp.where(lane == 0, late, jnp.where(lane == 1, 1.0, 0.0)).astype(jnp.bfloat16)
        early = jnp.where(place < before, -FIRM, 0.0)
        k_cols[tile, 0] = jnp.where(
            lane == 0, -FIRM, jnp.where(lane == 1, early, 0.0)
        ).astype(jnp.bfloat16)
        early = jnp.where(place < start, -FIRM, 0.0)
        k_cols[tile, 1] = jnp.where(lane == 0, early, 0.0).astype(jnp.bfloat16)


def attend_kernel(starts_ref, q_ref, k_ref, v_ref, probs_ref, out_ref, inverse_ref, q_cols, k_cols):
    row = pl.program_id(0)

    @pl.when(pl.program_id(1) == 0)
    def _():
        mask_columns(lambda r, i: starts_ref[r, i], row, q_cols, k_cols)

    lane = lane_index(TILE)
    causal = lax.broadcasted_iota(jnp.int32, (TILE, TILE), 1) <= lax.broadcasted_iota(
        jnp.int32, (TILE, TILE), 0
    )
    ones = jnp.ones((TILE, PAIR), jnp.bfloat16)
    for tile in range(2):
        queries = q_ref[0, pl.ds(tile * TILE, TILE)]
        keys = [
            jnp.concatenate([k_ref[0, pl.ds((tile + w) * TILE, TILE)], k_cols[tile, w]], axis=1)
            for w in range(2)
        ]
        values = [
            jnp.concatenate([v_ref[0, pl.ds((tile + w) * TILE, TILE)], ones], axis=1)
            for w in range(2)
        ]
        mixed, inverse = [], []
        for head in range(2):
            mine = (lane < HD) if head == 0 else (lane >= HD)
            left = jnp.concatenate([jnp.where(mine, queries, jnp.bfloat16(0)), q_cols[tile]], axis=1)
            far = dot_nt(left, keys[0])
            near = jnp.where(causal, dot_nt(left, keys[1]), -FIRM)
            top = jnp.max(jnp.maximum(far, near), axis=-1, keepdims=True)
            far = jnp.exp(far - top).astype(jnp.bfloat16)
            near = jnp.exp(near - top).astype(jnp.bfloat16)
            probs_ref[0, 0, tile, head, 0] = far
            probs_ref[0, 0, tile, head, 1] = near
            total = dot_nn(far, values[0]) + dot_nn(near, values[1])
            share = 1.0 / total[:, PAIR:]
            mixed.append(total[:, :PAIR] * share)
            inverse.append(share)
        out_ref[0, pl.ds(tile * TILE, TILE)] = jnp.where(lane < HD, mixed[0], mixed[1]).astype(
            jnp.bfloat16
        )
        inverse_ref[0, pl.ds(tile * TILE, TILE)] = jnp.where(lane < HD, inverse[0], inverse[1])


def attend(starts, q, k, v):
    rows, local, width = q.shape
    pairs = width // PAIR
    by_pair = lambda r, j: (r, 0, j)
    return pl.pallas_call(
        attend_kernel,
        grid=(rows, pairs),
        in_specs=[
            pl.BlockSpec(memory_space=pltpu.SMEM),
            pl.BlockSpec((1, local, PAIR), by_pair),
            pl.BlockSpec((1, local + TILE, PAIR), by_pair),
            pl.BlockSpec((1, local + TILE, PAIR), by_pair),
        ],
        out_specs=[
            pl.BlockSpec((1, 1, 2, 2, 2, TILE, TILE), lambda r, j: (r, j, 0, 0, 0, 0, 0)),
            pl.BlockSpec((1, local, PAIR), by_pair),
            pl.BlockSpec((1, local, PAIR), by_pair),
        ],
        out_shape=[
            jax.ShapeDtypeStruct((rows, pairs, 2, 2, 2, TILE, TILE), jnp.bfloat16),
            jax.ShapeDtypeStruct((rows, local, width), jnp.bfloat16),
            jax.ShapeDtypeStruct((rows, local, width), jnp.float32),
        ],
        scratch_shapes=[
            pltpu.VMEM((2, TILE, PAIR), jnp.bfloat16),
            pltpu.VMEM((2, 2, TILE, PAIR), jnp.bfloat16),
        ],
        compiler_params=pltpu.CompilerParams(vmem_limit_bytes=VMEM_LIMIT),
    )(starts, q, k, v)


def attend_grad_kernel(
    probs_ref, q_ref, k_ref, v_ref, grad_ref, out_ref, inverse_ref, dq_ref, dk_ref, dv_ref, dk_sum, dv_sum
):
    lane = lane_index(TILE)
    ones = jnp.ones((TILE, PAIR), jnp.bfloat16)
    for tile in range(2):
        span = pl.ds(tile * TILE, TILE)
        queries = q_ref[0, span]
        scaled = (grad_ref[0, span].astype(jnp.float32) * inverse_ref[0, span]).astype(jnp.bfloat16)
        product = scaled.astype(jnp.float32) * out_ref[0, span].astype(jnp.float32)
        d_queries = []
        for head in range(2):
            mine = (lane < HD) if head == 0 else (lane >= HD)
            delta = -jnp.sum(jnp.where(mine, product, 0.0), axis=-1, keepdims=True)
            high = delta.astype(jnp.bfloat16).astype(jnp.float32)
            extra = jnp.where(lane == 0, high, jnp.where(lane == 1, delta - high, 0.0))
            grads = jnp.where(mine, scaled, jnp.bfloat16(0))
            mine_queries = jnp.where(mine, queries, jnp.bfloat16(0))
            left = jnp.concatenate([grads, extra.astype(jnp.bfloat16)], axis=1)
            d_query = None
            for w in range(2):
                at = pl.ds((tile + w) * TILE, TILE)
                right = jnp.concatenate([v_ref[0, at], ones], axis=1)
                probs = probs_ref[0, 0, tile, head, w]
                d_score = (probs.astype(jnp.float32) * dot_nt(left, right)).astype(jnp.bfloat16)
                part = dot_nn(d_score, k_ref[0, at])
                d_query = part if w == 0 else d_query + part
                d_key = dot_tn(d_score, mine_queries)
                d_value = dot_tn(probs, grads)
                if head == 0 and (w == 1 or tile == 0):
                    dk_sum[at] = d_key
                    dv_sum[at] = d_value
                else:
                    dk_sum[at] += d_key
                    dv_sum[at] += d_value
            d_queries.append(d_query)
        dq = jnp.where(lane < HD, d_queries[0], d_queries[1]) * (1.0 / math.sqrt(HD))
        dq_ref[0, span] = dq.astype(jnp.bfloat16)
    dk_ref[0] = dk_sum[...].astype(jnp.bfloat16)
    dv_ref[0] = dv_sum[...].astype(jnp.bfloat16)


def attend_grad(probs, q, k, v, grad, out, inverse):
    rows, local, width = q.shape
    pairs = width // PAIR
    by_pair = lambda r, j: (r, 0, j)
    small = pl.BlockSpec((1, local, PAIR), by_pair)
    large = pl.BlockSpec((1, local + TILE, PAIR), by_pair)
    return pl.pallas_call(
        attend_grad_kernel,
        grid=(rows, pairs),
        in_specs=[
            pl.BlockSpec((1, 1, 2, 2, 2, TILE, TILE), lambda r, j: (r, j, 0, 0, 0, 0, 0)),
            small,
            large,
            large,
            small,
            small,
            small,
        ],
        out_specs=[small, large, large],
        out_shape=[
            jax.ShapeDtypeStruct(q.shape, jnp.bfloat16),
            jax.ShapeDtypeStruct(k.shape, jnp.bfloat16),
            jax.ShapeDtypeStruct(k.shape, jnp.bfloat16),
        ],
        scratch_shapes=[
            pltpu.VMEM((local + TILE, PAIR), jnp.float32),
            pltpu.VMEM((local + TILE, PAIR), jnp.float32),
        ],
        compiler_params=pltpu.CompilerParams(vmem_limit_bytes=VMEM_LIMIT),
    )(probs, q, k, v, grad, out, inverse)


def gelu_pair(v):
    square = v * v
    half = 0.5 + 0.5 * jnp.tanh(v * (GELU_SCALE + (GELU_SCALE * 0.044715) * square))
    hidden = v * half
    slope = half + hidden * (1.0 - half) * (2.0 * GELU_SCALE + (6.0 * GELU_SCALE * 0.044715) * square)
    return hidden, slope


MLP_TILE = 256
CHUNK = 768


def mlp_kernel(
    x_hbm, att_hbm, dy_hbm, attn_hbm, fc_hbm, proj_hbm, vectors,
    out_hbm, middle_grad_hbm, att_grad_hbm, attn_grad_hbm, fc_grad_hbm, proj_grad_hbm, sums_ref,
    x, att, dy, attn, fc, proj, hidden, pre_grad, normed, branch, out, middle_grad, att_grad,
    attn_grad, fc_grad, proj_grad, in_sem, out_sem,
):
    tokens, width = x.shape
    chunks = fc.shape[1] // CHUNK
    tiles = tokens // MLP_TILE
    loads = [
        pltpu.make_async_copy(src, dst, in_sem.at[i])
        for i, (src, dst) in enumerate(
            ((att_hbm, att), (attn_hbm, attn), (x_hbm, x), (fc_hbm, fc), (dy_hbm, dy), (proj_hbm, proj))
        )
    ]
    for load in loads:
        load.start()
    sums_ref[...] = jnp.zeros_like(sums_ref)
    for load in loads[:3]:
        load.wait()

    def tile_step(t, carry):
        span = pl.ds(pl.multiple_of(t * MLP_TILE, MLP_TILE), MLP_TILE)
        middle = x[span].astype(jnp.float32) + dot_nn(att[span], attn[...]) + vectors[4:5]
        normal, scale = normalize(middle)
        low = (normal * vectors[5:6] + vectors[6:7]).astype(jnp.bfloat16)
        normed[span] = low

        @pl.when(t == 0)
        def _():
            for load in loads[3:]:
                load.wait()

        upstream = dy[span]
        result = middle + vectors[7:8]
        back = None
        for j in range(chunks):
            columns = pl.ds(j * CHUNK, CHUNK)
            pre = dot_nn(low, fc[:, columns]) + vectors[8 + j : 9 + j]
            value, slope = gelu_pair(pre)
            value = value.astype(jnp.bfloat16)
            hidden[span, columns] = value
            grad = dot_nt(upstream, proj[columns]) * slope
            grad = grad.astype(jnp.bfloat16)
            pre_grad[span, columns] = grad
            sums_ref[4 + j : 5 + j] += column_sum(grad.astype(jnp.float32))
            result = result + dot_nn(value, proj[columns])
            part = dot_nt(grad, fc[:, columns])
            back = part if back is None else back + part
        out[span] = result.astype(jnp.bfloat16)
        upstream = upstream.astype(jnp.float32)
        sums_ref[0:1] += column_sum(upstream)
        sums_ref[1:2] += column_sum(back * normal)
        sums_ref[2:3] += column_sum(back)
        total = upstream + norm_grad(back, vectors[5:6], normal, scale)
        middle_grad[span] = total
        total = total.astype(jnp.bfloat16)
        branch[span] = total
        sums_ref[3:4] += column_sum(total.astype(jnp.float32))
        att_grad[span] = dot_nt(total, attn[...]).astype(jnp.bfloat16)
        return carry

    lax.fori_loop(0, tiles, tile_step, 0)
    stores = []

    def store(src, dst):
        copy = pltpu.make_async_copy(src, dst, out_sem.at[len(stores)])
        copy.start()
        stores.append(copy)

    store(out, out_hbm)
    store(middle_grad, middle_grad_hbm)
    store(att_grad, att_grad_hbm)
    for j in range(chunks):
        columns = pl.ds(j * CHUNK, CHUNK)
        proj_grad[columns] = dot_tn(hidden[:, columns], dy[...]).astype(jnp.bfloat16)
        store(proj_grad.at[columns], proj_grad_hbm.at[columns])
    for j in range(chunks):
        columns = pl.ds(j * CHUNK, CHUNK)
        fc_grad[:, columns] = dot_tn(normed[...], pre_grad[:, columns]).astype(jnp.bfloat16)
        store(fc_grad.at[:, columns], fc_grad_hbm.at[:, columns])
    attn_grad[...] = dot_tn(att[...], branch[...]).astype(jnp.bfloat16)
    store(attn_grad, attn_grad_hbm)
    for copy in stores:
        copy.wait()


def mlp(x, att, dy, attn, fc, proj, vectors):
    tokens, width = x.shape
    hidden = fc.shape[1]
    low, full = jnp.bfloat16, jnp.float32
    anywhere = pl.BlockSpec(memory_space=pl.ANY)
    vmem = pl.BlockSpec(memory_space=pltpu.VMEM)
    return pl.pallas_call(
        mlp_kernel,
        in_specs=[anywhere] * 6 + [vmem],
        out_specs=[anywhere] * 6 + [vmem],
        out_shape=[
            jax.ShapeDtypeStruct((tokens, width), low),
            jax.ShapeDtypeStruct((tokens, width), full),
            jax.ShapeDtypeStruct((tokens, width), low),
            jax.ShapeDtypeStruct(attn.shape, low),
            jax.ShapeDtypeStruct(fc.shape, low),
            jax.ShapeDtypeStruct(proj.shape, low),
            jax.ShapeDtypeStruct((8, width), full),
        ],
        scratch_shapes=[
            pltpu.VMEM((tokens, width), low),
            pltpu.VMEM((tokens, width), low),
            pltpu.VMEM((tokens, width), low),
            pltpu.VMEM(attn.shape, low),
            pltpu.VMEM(fc.shape, low),
            pltpu.VMEM(proj.shape, low),
            pltpu.VMEM((tokens, hidden), low),
            pltpu.VMEM((tokens, hidden), low),
            pltpu.VMEM((tokens, width), low),
            pltpu.VMEM((tokens, width), low),
            pltpu.VMEM((tokens, width), low),
            pltpu.VMEM((tokens, width), full),
            pltpu.VMEM((tokens, width), low),
            pltpu.VMEM(attn.shape, low),
            pltpu.VMEM(fc.shape, low),
            pltpu.VMEM(proj.shape, low),
            pltpu.SemaphoreType.DMA((6,)),
            pltpu.SemaphoreType.DMA((12,)),
        ],
        compiler_params=pltpu.CompilerParams(vmem_limit_bytes=VMEM_LIMIT),
    )(x, att, dy, attn, fc, proj, vectors)


def project_grad_kernel(normed, dq, dk, dv, weight, weight_grad, prev_grad, sums):
    rows, extended, width = normed.shape
    local = dq.shape[1]
    third = [pl.ds(i * width, width) for i in range(3)]
    for r in range(rows):
        head = pl.ds(0, TILE)
        prev_grad[r] = (
            dot_nt(dk[r, head], weight[:, third[1]]) + dot_nt(dv[r, head], weight[:, third[2]])
        ).astype(jnp.bfloat16)
    total = None
    for i, grads in enumerate((dq, dk, dv)):
        total = None
        for r in range(rows):
            left = normed[r, TILE:] if i == 0 else normed[r]
            part = dot_tn(left, grads[r])
            total = part if total is None else total + part
        weight_grad[:, third[i]] = total.astype(jnp.bfloat16)
    sums[...] = jnp.zeros_like(sums)
    for r in range(rows):
        sums[0:1] += column_sum(dq[r].astype(jnp.float32))
        sums[1:2] += column_sum(dv[r].astype(jnp.float32))


def project_grad(normed, dq, dk, dv, weight):
    rows, extended, width = normed.shape
    vmem = pl.BlockSpec(memory_space=pltpu.VMEM)
    return pl.pallas_call(
        project_grad_kernel,
        in_specs=[vmem] * 5,
        out_specs=[vmem] * 3,
        out_shape=[
            jax.ShapeDtypeStruct(weight.shape, jnp.bfloat16),
            jax.ShapeDtypeStruct((rows, TILE, width), jnp.bfloat16),
            jax.ShapeDtypeStruct((8, width), jnp.float32),
        ],
        compiler_params=pltpu.CompilerParams(vmem_limit_bytes=VMEM_LIMIT),
    )(normed, dq, dk, dv, weight)


def tokens_grad_kernel(x_ref, dq, dk, dv, weight, late, middle_grad, vectors, out_ref, sums):
    row, tile = pl.program_id(0), pl.program_id(1)
    width = x_ref.shape[-1]

    @pl.when((row == 0) & (tile == 0))
    def _():
        sums[...] = jnp.zeros_like(sums)

    back = dot_nt(dq[0], weight[:, :width])
    back = back + dot_nt(dk[0], weight[:, width : 2 * width])
    back = back + dot_nt(dv[0], weight[:, 2 * width :])
    back = back + jnp.where(tile == pl.num_programs(1) - 1, late[0].astype(jnp.float32), 0.0)
    normal, scale = normalize(x_ref[0].astype(jnp.float32))
    sums[0:1] += column_sum(back * normal)
    sums[1:2] += column_sum(back)
    out_ref[0] = middle_grad[0] + norm_grad(back, vectors[0:1], normal, scale)


def tokens_grad_of(x, dq, dk, dv, weight, late, middle_grad, vectors):
    rows, local, width = x.shape
    block = lambda shift: pl.BlockSpec((1, TILE, width), lambda r, t: (r, t + shift, 0))
    whole = lambda v: pl.BlockSpec(v.shape, lambda r, t: (0, 0))
    return pl.pallas_call(
        tokens_grad_kernel,
        grid=(rows, local // TILE),
        in_specs=[
            block(0),
            block(0),
            block(1),
            block(1),
            whole(weight),
            pl.BlockSpec((1, TILE, width), lambda r, t: (r, 0, 0)),
            block(0),
            whole(vectors),
        ],
        out_specs=[block(0), pl.BlockSpec((8, width), lambda r, t: (0, 0))],
        out_shape=[
            jax.ShapeDtypeStruct(x.shape, jnp.float32),
            jax.ShapeDtypeStruct((8, width), jnp.float32),
        ],
        compiler_params=pltpu.CompilerParams(vmem_limit_bytes=VMEM_LIMIT),
    )(x, dq, dk, dv, weight, late, middle_grad, vectors)


def spread_vectors(slots, size, fc_size, width):
    outer = slots.shape[0]
    zeros = jnp.zeros((8, width - PAIR), jnp.float32)
    first, second = None, None
    for d in range(outer * 8):
        index = (d // 8, (d // 4) % 2, (d // 2) % 2, d % 2)
        top = jnp.concatenate([slots[index + (slice(0, 8),)], zeros], axis=1)
        low = jnp.concatenate([slots[index + (slice(8, 16),)], zeros], axis=1)
        top = pltpu.roll(top, d * size, 1) if d else top
        row, lane = divmod(d * fc_size, width)
        low = pltpu.roll(low, lane, 1) if lane else low
        low = pltpu.roll(low, row, 0) if row else low
        first = top if first is None else first + top
        second = low if second is None else second + low
    return first, second


def join_rows(target, slots, columns):
    outer, rows = slots.shape[0], slots.shape[-2]

    def body(a, carry):
        for y in range(2):
            for c in range(2):
                both = [slots[a, y, c, s, :, columns].astype(jnp.float32) for s in range(2)]
                start = pl.multiple_of(((a * 2 + y) * 2 + c) * (2 * rows), 2 * rows)
                joined = jnp.concatenate(both, axis=0).astype(target.dtype)
                target[pl.ds(start, 2 * rows), columns] = joined
        return carry

    lax.fori_loop(0, outer, body, 0)


VECTORS = 9


FORWARD_ORDERS = (0, 1, 1, 1, 1, 1, 1, 1, 1, 0, 0, 1, 0, 1, 0)
PREV_AFTER, EAGER = (2, 4), 12
FORWARD_PLAN = {'ln': [(1, 0), (1, 1), (1, 2), (2, 0), (1, 3), (2, 1), (1, 4), (2, 2), (1, 5), (3, 0), (1, 6), (2, 3), (2, 4), (4, 0)], 'q': [(3, 1), (2, 5), (2, 6), (1, 7), (3, 2), (1, 8), (4, 1), (4, 2)], 'k': [(3, 3), (1, 9), (3, 4), (1, 10), (4, 3), (4, 4)], 'v': [(3, 5), (1, 11), (3, 6), (1, 12), (4, 5), (2, 9), (4, 6)], 'b0': [(2, 7), (2, 10)], 'b1': [(1, 13)], 'b2': [(2, 8), (2, 12)], 'b3': [(2, 11)], 'b4': [(1, 14)], 'a0': [(3, 7), (3, 9)], 'a3': [(4, 7), (3, 8)], 'a4': [(4, 9), (3, 10)], 'asm': [(4, 8)], 'm0': [(4, 10), (2, 13)], 'm1': [(3, 11)], 'm3': [(2, 14), (4, 11)], 'm5': [(3, 12)], 'w0': [(4, 12), (3, 13)], 'w2': [(3, 14)], 'w3': [(4, 13)], 'end': [(4, 14)]}


def forward_kernel(outer, pieces, *refs):
    tokens_hbm, dy_hbm, starts_ref = refs[:3]
    vector_refs = refs[3 : 3 + VECTORS]
    shards = refs[3 + VECTORS : 7 + VECTORS]
    (
        normed_hbm, q_hbm, k_hbm, v_hbm, probs_hbm, att_hbm, hidden_hbm, slope_hbm, middle_hbm,
        normed2_hbm, qkv_hbm, attn_hbm, fc_hbm, proj_slots, terms_hbm, vectors,
    ) = refs[7 + VECTORS : 23 + VECTORS]
    (
        own, vector_slots, qkv_slots, attn_slots, fc_slots, qkv, attn, fc, x, normed, q, k, v, probs, att,
        hidden, slope, middle, normed2, dy, terms, q_cols, k_cols,
        move_sem, out_sem, probs_sem, terms_sem, own_sem, send_sem, recv_sem,
    ) = refs[23 + VECTORS :]
    rows, local, width = q.shape
    a, y, c, s = place()
    size, fc_size = vector_refs[0].shape[1], vector_refs[-1].shape[1]
    pairs, chunks = width // PAIR, fc.shape[1] // CHUNK

    load = pltpu.make_async_copy(tokens_hbm, x.at[:, pl.ds(TILE, local)], move_sem.at[0])
    load_dy = pltpu.make_async_copy(dy_hbm, dy, move_sem.at[3])
    load.start()
    own[...] = jnp.zeros_like(own)
    for i, ref in enumerate(vector_refs):
        own[i : i + 1, : ref.shape[1]] = ref[...].astype(jnp.float32)
    greet(outer)
    prev = remote(
        tokens_hbm.at[:, pl.ds(local - TILE, TILE)],
        x.at[:, pl.ds(0, TILE)],
        move_sem.at[1],
        move_sem.at[2],
        device(a, y, c, 1 - s),
    )
    work = Gather(
        outer,
        pieces,
        (own,) + shards,
        (vector_slots, qkv_slots, attn_slots, fc_slots, proj_slots),
        own_sem,
        send_sem,
        recv_sem,
        EAGER,
    )
    work.start()
    load_dy.start()

    def start_prev():
        @pl.when(s == 0)
        def _():
            prev.start()

    work.after = {PREV_AFTER: start_prev}
    comm, comm_at = sites_of(work, FORWARD_PLAN)
    stores = []

    def store(src, dst):
        copy = pltpu.make_async_copy(src, dst, out_sem.at[len(stores)])
        copy.start()
        stores.append(copy)

    def starts_of(r, i):
        tile = 2 * s - 1 + i
        start = starts_ref[r, jnp.maximum(tile, 0)]
        return jnp.where(tile < 0, TILE, start - tile * TILE)

    @pl.when(s == 0)
    def _():
        for r in range(rows):
            x[r, 0:TILE] = jnp.zeros((TILE, width), x.dtype)

    for r in range(rows):
        mask_columns(starts_of, r, q_cols.at[r], k_cols.at[r])
    load.wait()
    comm("ln")
    first, second = spread_vectors(vector_slots, size, fc_size, width)
    vectors[0:8], vectors[8:16] = first, second

    def norm_tile(r, span):
        normal, _ = normalize(x[r, span].astype(jnp.float32))
        normed[r, span] = (normal * vectors[0:1] + vectors[1:2]).astype(jnp.bfloat16)

    def norm_step(n, carry):
        r, t = n // (local // TILE), lax.rem(n, local // TILE) + 1
        norm_tile(r, pl.ds(pl.multiple_of(t * TILE, TILE), TILE))
        return carry

    lax.fori_loop(0, rows * (local // TILE), norm_step, 0)
    third = [slice(i * width, (i + 1) * width) for i in range(3)]
    for i, site in enumerate(("q", "k", "v")):
        comm(site)
        join_rows(qkv, qkv_slots, third[i])

        def row_step(r, carry):
            value = dot_nn(normed[r, TILE:], qkv[:, third[i]])
            if i == 0:
                value = (value + vectors[2:3]).astype(jnp.bfloat16)
                q[r] = value * jnp.bfloat16(1.0 / math.sqrt(HD))
            elif i == 1:
                k[r, TILE:] = value.astype(jnp.bfloat16)
            else:
                v[r, TILE:] = (value + vectors[3:4]).astype(jnp.bfloat16)
            return carry

        lax.fori_loop(0, rows, row_step, 0)
    store(q, q_hbm)
    store(qkv, qkv_hbm)
    lane = lane_index(TILE)
    causal = lax.broadcasted_iota(jnp.int32, (TILE, 2 * TILE), 0) <= (
        lax.broadcasted_iota(jnp.int32, (TILE, 2 * TILE), 1) & (TILE - 1)
    )

    def probs_copy(slot, r, j, tile):
        part = probs_hbm.at[r, j, :, pl.ds(tile * 4 * TILE, 4 * TILE)]
        return pltpu.make_async_copy(probs.at[slot], part, probs_sem.at[slot])

    def attend_pair(r, j, tile, slot):
        pair = pl.ds(pl.multiple_of(j * PAIR, PAIR), PAIR)
        queries = q[r, tile * TILE : (tile + 1) * TILE, pair]
        left = []
        for head in range(2):
            mine = (lane < HD) if head == 0 else (lane >= HD)
            mine = jnp.where(mine, queries, jnp.bfloat16(0))
            left.append(jnp.concatenate([mine, q_cols[r, tile]], axis=1))
        left = jnp.concatenate(left, axis=0)
        scores = []
        for w in range(2):
            keys = k[r, (tile + w) * TILE : (tile + w + 1) * TILE, pair]
            scores.append(dot_nt(jnp.concatenate([keys, k_cols[r, tile, w]], axis=1), left))
        far, near = scores[0], jnp.where(causal, scores[1], -FIRM)
        top = jnp.max(jnp.maximum(far, near), axis=0, keepdims=True)
        far, near = jnp.exp(far - top), jnp.exp(near - top)
        share = 1.0 / jnp.sum(far + near, axis=0, keepdims=True)
        far, near = (far * share).astype(jnp.bfloat16), (near * share).astype(jnp.bfloat16)
        probs[slot, :, 0 : 2 * TILE], probs[slot, :, 2 * TILE :] = far, near
        values = v[r, tile * TILE : (tile + 2) * TILE, pair]
        mixed = []
        for head in range(2):
            part = slice(head * TILE, (head + 1) * TILE)
            mixed.append(dot_tn(jnp.concatenate([far[:, part], near[:, part]], axis=0), values))
        span = pl.ds(pl.multiple_of(r * local + tile * TILE, TILE), TILE)
        att[span, pair] = jnp.where(lane < HD, mixed[0], mixed[1]).astype(jnp.bfloat16)

    def attend_step(n, tile, index):
        r, j = n // (pairs // 2), lax.rem(n, pairs // 2) * 2
        slot = lax.rem(n, 2) * 2

        @pl.when(n + index * rows * pairs // 2 >= 2)
        def _():
            for i in range(2):
                probs_copy(slot + i, r, j + i, tile).wait()

        for i in range(2):
            attend_pair(r, j + i, tile, slot + i)
        for i in range(2):
            probs_copy(slot + i, r, j + i, tile).start()

    def late_step(n, carry):
        comm_at(n, "b", rows * pairs // 2)
        attend_step(n, 1, 0)
        return carry

    lax.fori_loop(0, rows * pairs // 2, late_step, 0)
    comm("prev")

    @pl.when(s == 1)
    def _():
        prev.wait_recv()

    for r in range(rows):
        norm_tile(r, slice(0, TILE))
        k[r, 0:TILE] = dot_nn(normed[r, 0:TILE], qkv[:, third[1]]).astype(jnp.bfloat16)
        value = dot_nn(normed[r, 0:TILE], qkv[:, third[2]]) + vectors[3:4]
        v[r, 0:TILE] = value.astype(jnp.bfloat16)
    store(normed, normed_hbm)
    store(k, k_hbm)
    store(v, v_hbm)

    def early_step(n, carry):
        comm_at(n, "a", rows * pairs // 2)
        attend_step(n, 0, 1)
        return carry

    lax.fori_loop(0, rows * pairs // 2, early_step, 0)
    store(att, att_hbm)
    comm("asm")
    join_rows(attn, attn_slots, slice(0, width))
    store(attn, attn_hbm)

    def mlp_step(n, carry):
        r, j = n // chunks, lax.rem(n, chunks)
        span = pl.ds(pl.multiple_of(r * local, TILE), local)
        units = pl.ds(pl.multiple_of(j * CHUNK, CHUNK), CHUNK)

        @pl.when(j == 0)
        def _():
            value = x[r, TILE:].astype(jnp.float32) + dot_nn(att[span], attn[...]) + vectors[4:5]
            middle[span] = value
            normal, _ = normalize(value)
            normed2[span] = (normal * vectors[5:6] + vectors[6:7]).astype(jnp.bfloat16)

        comm_at(n, "m", rows * chunks)

        @pl.when(r == 0)
        def _():
            join_rows(fc, fc_slots, units)

        bias = vectors[8:9]
        for i in range(1, chunks):
            bias = jnp.where(j == i, vectors[8 + i : 9 + i], bias)
        value, back = gelu_pair(dot_nn(normed2[span], fc[:, units]) + bias)
        hidden[span, units] = value.astype(jnp.bfloat16)
        slope[span, units] = back.astype(jnp.bfloat16)
        return carry

    lax.fori_loop(0, rows * chunks, mlp_step, 0)
    store(slope, slope_hbm)
    store(hidden, hidden_hbm)
    store(middle, middle_hbm)
    store(normed2, normed2_hbm)
    store(fc, fc_hbm)
    load_dy.wait()
    share = terms.shape[-2]
    each = CHUNK // (8 * share)

    def terms_copy(j):
        slot = lax.rem(j, 2)
        return pltpu.make_async_copy(
            terms.at[slot], terms_hbm.at[pl.ds(j * each, each)], terms_sem.at[slot]
        )

    def weight_step(j, carry):
        comm_at(j, "w", chunks)
        units = pl.ds(pl.multiple_of(j * CHUNK, CHUNK), CHUNK)
        grad = dot_tn(hidden[:, units], dy[...]).astype(jnp.bfloat16)

        @pl.when(j >= 2)
        def _():
            terms_copy(j - 2).wait()

        terms[lax.rem(j, 2)] = grad.reshape((each, 2, 2, 2, share, width))
        terms_copy(j).start()
        return carry

    lax.fori_loop(0, chunks, weight_step, 0)
    comm("end")
    work.end()
    for j in range(chunks - 2, chunks):
        terms_copy(j).wait()
    for n in range(4):
        probs_copy(n, 0, n, 0).wait()
    for copy in stores:
        copy.wait()

    @pl.when(s == 0)
    def _():
        prev.wait_send()


def forward(outer, tokens, dy, starts, vectors, weights):
    rows, local, width = tokens.shape
    devices = outer * 8
    low, full = jnp.bfloat16, jnp.float32
    pairs = width // PAIR
    qkv_weight, attn_weight, fc_weight, proj_weight = weights
    hidden = fc_weight.shape[1]
    half = width // 2
    pieces = [(0, 0, PAIR)] + [(1, i * half, half) for i in range(6)] + [(2, 0, width)]
    pieces += [(3, j * CHUNK, CHUNK) for j in range(hidden // CHUNK)]
    pieces += [(4, j * 2 * PAIR, 2 * PAIR) for j in range(width // (2 * PAIR))]
    pieces = [piece + (order,) for piece, order in zip(pieces, FORWARD_ORDERS)]
    anywhere = pl.BlockSpec(memory_space=pl.ANY)
    vmem = pl.BlockSpec(memory_space=pltpu.VMEM)
    extended = (rows, local + TILE, width)
    flat = (rows * local, width)
    whole = [(devices * weight.shape[0], weight.shape[1]) for weight in weights]
    slots = [(outer, 2, 2, 2) + weight.shape for weight in weights]
    shape = jax.ShapeDtypeStruct
    results = pl.pallas_call(
        functools.partial(forward_kernel, outer, pieces),
        in_specs=[anywhere] * 2 + [pl.BlockSpec(memory_space=pltpu.SMEM)] + [vmem] * (VECTORS + 4),
        out_specs=[anywhere] * 15 + [vmem],
        out_shape=[
            shape(extended, low),
            shape(tokens.shape, low),
            shape(extended, low),
            shape(extended, low),
            shape((rows, pairs, TILE, 8 * TILE), low),
            shape(flat, low),
            shape((rows * local, hidden), low),
            shape((rows * local, hidden), low),
            shape(flat, full),
            shape(flat, low),
            shape(whole[0], low),
            shape(whole[1], low),
            shape(whole[2], low),
            shape(slots[3], low),
            shape(slots[3], low),
            shape((16, width), full),
        ],
        scratch_shapes=[
            pltpu.VMEM((16, PAIR), full),
            pltpu.VMEM((outer, 2, 2, 2, 16, PAIR), full),
            pltpu.VMEM(slots[0], low),
            pltpu.VMEM(slots[1], low),
            pltpu.VMEM(slots[2], low),
            pltpu.VMEM(whole[0], low),
            pltpu.VMEM(whole[1], low),
            pltpu.VMEM(whole[2], low),
            pltpu.VMEM(extended, low),
            pltpu.VMEM(extended, low),
            pltpu.VMEM(tokens.shape, low),
            pltpu.VMEM(extended, low),
            pltpu.VMEM(extended, low),
            pltpu.VMEM((4, TILE, 4 * TILE), low),
            pltpu.VMEM(flat, low),
            pltpu.VMEM((rows * local, hidden), low),
            pltpu.VMEM((rows * local, hidden), low),
            pltpu.VMEM(flat, full),
            pltpu.VMEM(flat, low),
            pltpu.VMEM(flat, low),
            pltpu.VMEM((2, CHUNK // (8 * proj_weight.shape[0])) + slots[3][1:], low),
            pltpu.VMEM((rows, 2, TILE, PAIR), low),
            pltpu.VMEM((rows, 2, 2, TILE, PAIR), low),
            pltpu.SemaphoreType.DMA((4,)),
            pltpu.SemaphoreType.DMA((12,)),
            pltpu.SemaphoreType.DMA((4,)),
            pltpu.SemaphoreType.DMA((2,)),
        ]
        + Gather.semaphores(outer, 5, len(pieces)),
        compiler_params=pltpu.CompilerParams(
            collective_id=2, has_side_effects=True, vmem_limit_bytes=VMEM_LIMIT
        ),
    )(tokens, dy, starts, *[vector.reshape(1, -1) for vector in vectors], *weights)
    return results


def shares_out(rows, columns):
    return jax.ShapeDtypeStruct((rows, columns), jnp.float32)


def column_pieces(array, columns, parts, orders):
    step = columns // parts
    return [(array, j * step, step, orders[j % len(orders)]) for j in range(parts)]


def pack_columns(values, start, lanes):
    width = values.shape[1]
    moved = pltpu.roll(values, (width - start) % width, 1) if start % width else values
    return jnp.where(lane_index(values.shape[0]) < lanes, moved[:, :PAIR], 0.0)


def mlp_backward(refs, fc_terms, attn_terms, vectors, att, att_grad, middle, sums, work, comm, comm_at):
    slope_hbm, normed_hbm, dy_hbm, attn_hbm, fc_hbm, proj_hbm, load_middle, load_att = refs

    def body(dy, slope, normed, attn, fc, proj, branch, stage, proj_sem, slope_sem, fc_sem, in_sem, stage_sem):
        tokens, width = dy.shape
        chunks = fc.shape[1] // CHUNK
        block = tokens // 2
        spans = [pl.ds(j * CHUNK, CHUNK) for j in range(chunks)]
        share = fc_terms.shape[-2]

        copies = lambda src, dst, sem: [
            pltpu.make_async_copy(src.at[:, span], dst.at[:, span], sem.at[j])
            for j, span in enumerate(spans)
        ]
        load_proj = [
            pltpu.make_async_copy(proj_hbm.at[span], proj.at[span], proj_sem.at[j])
            for j, span in enumerate(spans)
        ]
        load_slope, load_fc = copies(slope_hbm, slope, slope_sem), copies(fc_hbm, fc, fc_sem)
        others = ((dy_hbm, dy), (normed_hbm, normed), (attn_hbm, attn))
        load_dy, load_normed, load_attn = [
            pltpu.make_async_copy(src, dst, in_sem.at[i]) for i, (src, dst) in enumerate(others)
        ]
        load_dy.start()
        for j in range(chunks):
            load_proj[j].start()
            load_slope[j].start()
        load_normed.start()
        for j in range(chunks):
            load_fc[j].start()
        for load in (load_middle, load_attn, load_att):
            load.start()
        comm("start")
        load_dy.wait()

        def grad_step(n, carry):
            t, j = n // chunks, lax.rem(n, chunks)
            span = pl.ds(pl.multiple_of(t * block, block), block)
            units = pl.ds(pl.multiple_of(j * CHUNK, CHUNK), CHUNK)
            for i in range(chunks):

                @pl.when(n == i)
                def _():
                    load_proj[i].wait()
                    load_slope[i].wait()

            comm_at(n, "m", 2 * chunks)
            grad = dot_nt(dy[span], proj[units]) * slope[span, units].astype(jnp.float32)
            grad = grad.astype(jnp.bfloat16)
            slope[span, units] = grad
            total = column_sum(grad.astype(jnp.float32))
            for i in range(chunks):
                sums[12 + i : 13 + i] += jnp.where(j == i, total, 0.0)
            return carry

        lax.fori_loop(0, 2 * chunks, grad_step, 0)
        load_normed.wait()
        waited = set()

        def stage_copy(n):
            to = fc_terms.at[:, :, :, :, :, spans[n]] if n < chunks else attn_terms
            return pltpu.make_async_copy(stage.at[n % 2], to, stage_sem.at[n])

        def settle(n):
            if n not in waited:
                waited.add(n)
                stage_copy(n).wait()

        def put(n, grad):
            if n >= 2:
                settle(n - 2)
            stage[n % 2] = grad.astype(jnp.bfloat16).reshape(stage.shape[1:])
            stage_copy(n).start()

        for p, piece in enumerate(work.pieces):
            if piece[0] in (1, 2):
                work.before[p] = functools.partial(settle, piece[1] // CHUNK if piece[0] == 1 else chunks)
        for j in range(chunks):
            comm(f"w{j}")
            put(j, dot_tn(normed[...], slope[:, spans[j]]))

        def back_step(t, carry):
            span = pl.ds(pl.multiple_of(t * block, block), block)
            back = None
            for j in range(chunks):

                @pl.when(t == 0)
                def _():
                    load_fc[j].wait()

                comm_at(t, "o", 2, chunks, j)
                more = dot_nt(slope[span, spans[j]], fc[:, spans[j]])
                back = more if back is None else back + more

            @pl.when(t == 0)
            def _():
                load_middle.wait()
                load_attn.wait()

            upstream = dy[span].astype(jnp.float32)
            value = middle[span]
            normal, scale = normalize(value)
            sums[4:5] += column_sum(upstream)
            sums[5:6] += column_sum(back * normal)
            sums[6:7] += column_sum(back)
            total = upstream + norm_grad(back, vectors[5:6], normal, scale)
            middle[span] = total
            total = total.astype(jnp.bfloat16)
            branch[span] = total
            sums[7:8] += column_sum(total.astype(jnp.float32))
            att_grad[span] = dot_nt(total, attn[...]).astype(jnp.bfloat16)
            return carry

        lax.fori_loop(0, 2, back_step, 0)
        load_att.wait()
        comm("attn")
        put(chunks, dot_tn(att[...], branch[...]))
        comm("rest")
        for n in range(chunks + 1):
            settle(n)

    tokens, width = att.shape
    hidden, chunks = fc_hbm.shape[1], fc_hbm.shape[1] // CHUNK
    low = jnp.bfloat16
    dma = lambda n: pltpu.SemaphoreType.DMA((n,))
    pl.run_scoped(
        body,
        pltpu.VMEM((tokens, width), low),
        pltpu.VMEM((tokens, hidden), low),
        pltpu.VMEM((tokens, width), low),
        pltpu.VMEM(attn_hbm.shape, low),
        pltpu.VMEM(fc_hbm.shape, low),
        pltpu.VMEM(proj_hbm.shape, low),
        pltpu.VMEM((tokens, width), low),
        pltpu.VMEM((2,) + attn_terms.shape, low),
        dma(chunks),
        dma(chunks),
        dma(chunks),
        dma(3),
        dma(chunks + 1),
    )


def backward_kernel(outer, pieces, places, *refs):
    (
        hidden_hbm, slope_hbm, middle_hbm, normed2_hbm, att_hbm, dy_hbm, attn_hbm, fc_hbm, proj_hbm, proj_terms,
        probs_hbm, q_hbm, k_hbm, v_hbm, normed_hbm, x_hbm, weight_hbm, vectors,
        out_hbm, tokens_grad_hbm, fc_terms, attn_terms, proj_share, fc_share, attn_share, qkv_share, vector_share,
        flat_att, flat_grad, flat_middle, prev, late, vector_terms, vector_got, sums,
        main_sem, late_sem, vector_send, vector_recv, *rest,
    ) = refs
    rows, local, width = q_hbm.shape
    pairs = width // PAIR
    a, y, c, s = place()
    load_middle = pltpu.make_async_copy(middle_hbm, flat_middle, main_sem.at[0])
    load_att = pltpu.make_async_copy(att_hbm, flat_att, main_sem.at[1])
    sums[...] = jnp.zeros_like(sums)
    greet_all(outer)
    work = Scatter(
        outer, pieces, [proj_terms, fc_terms, attn_terms, None],
        [proj_share, fc_share, attn_share, qkv_share], rest[:-3], *rest[-3:], places,
    )
    comm, comm_at = sites_of(work, BACKWARD_PLAN)
    mlp_refs = (
        slope_hbm, normed2_hbm, dy_hbm, attn_hbm, fc_hbm, proj_hbm, load_middle, load_att,
    )
    mlp_backward(
        mlp_refs, fc_terms, attn_terms, vectors, flat_att, flat_grad, flat_middle, sums,
        work, comm, comm_at,
    )
    low, full = jnp.bfloat16, jnp.float32
    extended = (rows, local + TILE, width)
    dma = lambda *n: pltpu.SemaphoreType.DMA(n)
    pl.run_scoped(
        functools.partial(
            attend_backward, outer, work, comm, comm_at,
            (probs_hbm, q_hbm, k_hbm, v_hbm, normed_hbm, x_hbm, weight_hbm, hidden_hbm, proj_hbm, middle_hbm),
            vectors, tokens_grad_hbm, out_hbm,
            vector_share, flat_att, flat_grad, flat_middle, prev, late, vector_terms, vector_got, sums,
            late_sem, vector_send, vector_recv,
        ),
        pltpu.VMEM(q_hbm.shape, low),
        pltpu.VMEM(extended, low),
        pltpu.VMEM(extended, low),
        pltpu.VMEM(extended, low),
        pltpu.VMEM(weight_hbm.shape, low),
        pltpu.VMEM((6, TILE, 2 * TILE), low),
        pltpu.VMEM((4, TILE, 6 * TILE), low),
        pltpu.VMEM(q_hbm.shape, low),
        pltpu.VMEM(extended, low),
        pltpu.VMEM(extended, low),
        pltpu.VMEM((rows, TILE, width), full),
        pltpu.VMEM((outer, 2, 2, 2, weight_hbm.shape[0] // (outer * 8), weight_hbm.shape[1]), low),
        dma(3, rows),
        dma(3),
        dma(6),
        dma(4),
        dma(rows * local // TILE),
        dma(4),
        dma(2, 4),
        dma(2),
        dma(2),
    )


def attend_backward(
    outer, work, comm, comm_at, arrays, vectors, tokens_grad_hbm, out_hbm, vector_share, att, grad, middle,
    prev, late, vector_terms, vector_got, sums, late_sem, vector_send, vector_recv,
    q, k, v, normed, weight, far_probs, near_probs, dq, dk, dv, dq_part, qkv_terms,
    in_sem, after_sem, far_sem, near_sem, out_sem, proj_sem, hidden_sem, middle_sem, result_sem,
):
    probs_hbm, q_hbm, k_hbm, v_hbm, normed_hbm, x_hbm, weight_hbm, hidden_hbm, proj_hbm, middle_hbm = arrays
    rows, local, width = q.shape
    pairs = width // PAIR
    a, y, c, s = place()
    work.terms[3] = qkv_terms
    loads = [
        [pltpu.make_async_copy(src.at[r], dst.at[r], in_sem.at[i, r]) for r in range(rows)]
        for i, (src, dst) in enumerate(((q_hbm, q), (k_hbm, k), (v_hbm, v)))
    ]
    load_weight = pltpu.make_async_copy(weight_hbm, weight, after_sem.at[0])
    load_normed = pltpu.make_async_copy(normed_hbm, normed, after_sem.at[1])
    load_x = pltpu.make_async_copy(x_hbm, q, after_sem.at[2])
    wide = 2 * TILE

    def far_copy(n):
        part = probs_hbm.at[n // pairs, lax.rem(n, pairs), :, pl.ds(0, wide)]
        slot = lax.rem(n, 6)
        return pltpu.make_async_copy(part, far_probs.at[slot], far_sem.at[slot])

    def near_copy(n):
        slot = lax.rem(n, 4)
        part = probs_hbm.at[lax.rem(n, rows), n // rows, :, pl.ds(wide, 3 * wide)]
        return pltpu.make_async_copy(part, near_probs.at[slot], near_sem.at[slot])

    for r in range(rows):
        for load in loads:
            load[r].start()
        if r == 0:
            for n in range(6):
                far_copy(n).start()
    load_weight.start()
    load_normed.start()
    for n in range(4):
        near_copy(n).start()
    lane = lane_index(TILE)
    ones = jnp.ones((TILE, PAIR), jnp.bfloat16)

    def sides(r, pair, tile):
        span = pl.ds(pl.multiple_of(r * local + tile * TILE, TILE), TILE)
        grads, queries = grad[span, pair], q[r, tile * TILE : (tile + 1) * TILE, pair]
        product = grads.astype(jnp.float32) * att[span, pair].astype(jnp.float32)
        left, mine_grads, mine_queries = [], [], []
        for head in range(2):
            mine = (lane < HD) if head == 0 else (lane >= HD)
            delta = -jnp.sum(jnp.where(mine, product, 0.0), axis=-1, keepdims=True)
            high = delta.astype(jnp.bfloat16).astype(jnp.float32)
            extra = jnp.where(lane == 0, high, jnp.where(lane == 1, delta - high, 0.0))
            mine_grads.append(jnp.where(mine, grads, jnp.bfloat16(0)))
            mine_queries.append(jnp.where(mine, queries, jnp.bfloat16(0)))
            left.append(jnp.concatenate([mine_grads[-1], extra.astype(jnp.bfloat16)], axis=1))
        return [jnp.concatenate(part, axis=0) for part in (left, mine_grads, mine_queries)]

    def unit(r, pair, tile, side, chances):
        values = jnp.concatenate([v[r, tile * TILE : (tile + 1) * TILE, pair], ones], axis=1)
        d_score = (chances.astype(jnp.float32) * dot_nt(values, side[0])).astype(jnp.bfloat16)
        span = slice(tile * TILE, (tile + 1) * TILE)
        dk[r, span, pair] = dot_nn(d_score, side[2]).astype(jnp.bfloat16)
        dv[r, span, pair] = dot_nn(chances, side[1]).astype(jnp.bfloat16)
        return d_score

    def heads(parts):
        return jnp.where(lane < HD, parts[0], parts[1])

    far_steps = rows * pairs // 2

    def far_step(n, carry):
        r, j = n // (pairs // 2), lax.rem(n, pairs // 2) * 2
        for row in range(rows):

            @pl.when(n == row * (pairs // 2))
            def _():
                for load in loads:
                    load[row].wait()

        comm_at(n, "f", far_steps)
        for i in range(2):
            far_copy(2 * n + i).wait()
        for i in range(2):
            pair = pl.ds(pl.multiple_of((j + i) * PAIR, PAIR), PAIR)
            d_score = unit(r, pair, 0, sides(r, pair, 0), far_probs[lax.rem(2 * n + i, 6)])
            keys = k[r, 0:TILE, pair]
            dq_part[r, :, pair] = heads(
                [dot_tn(d_score[:, h * TILE : (h + 1) * TILE], keys) for h in range(2)]
            )

        @pl.when(2 * n + 6 < rows * pairs)
        def _():
            for i in range(2):
                far_copy(2 * n + 6 + i).start()

        return carry

    lax.fori_loop(0, far_steps, far_step, 0)
    load_weight.wait()
    comm("mm")
    third = [slice(i * width, (i + 1) * width) for i in range(3)]
    for r in range(rows):
        head = slice(0, TILE)
        prev[r] = (
            dot_nt(dk[r, head], weight[:, third[1]]) + dot_nt(dv[r, head], weight[:, third[2]])
        ).astype(jnp.bfloat16)
    late_copy = remote(prev, late, late_sem.at[0], late_sem.at[1], device(a, y, c, 1 - s))

    @pl.when(s == 1)
    def _():
        late_copy.start()
        late[...] = jnp.zeros_like(late)

    load_normed.wait()
    near_steps = rows * pairs // 2

    def near_pair(r, j, slot):
        pair = pl.ds(pl.multiple_of(j * PAIR, PAIR), PAIR)
        scale = 1.0 / math.sqrt(HD)
        one, two = sides(r, pair, 0), sides(r, pair, 1)
        both = [jnp.concatenate(part, axis=0) for part in zip(one, two)]
        first = unit(r, pair, 1, both, near_probs[slot, :, 0 : 2 * wide])
        second = unit(r, pair, 2, two, near_probs[slot, :, 2 * wide :])
        keys = k[r, TILE : 3 * TILE, pair]
        part = heads([dot_tn(first[:, h * TILE : (h + 1) * TILE], keys[:TILE]) for h in range(2)])
        dq[r, 0:TILE, pair] = ((dq_part[r, :, pair] + part) * scale).astype(jnp.bfloat16)
        crossed = jnp.concatenate([first[:, wide:], second], axis=0)
        part = heads([dot_tn(crossed[:, h * TILE : (h + 1) * TILE], keys) for h in range(2)])
        dq[r, TILE : 2 * TILE, pair] = (part * scale).astype(jnp.bfloat16)

    def near_step(n, carry):
        comm_at(n, "n", near_steps)
        for r in range(rows):
            near_copy(n * rows + r).wait()
        near_pair(0, n, lax.rem(n * rows, 4))
        comm_at(n, "h", near_steps)
        for r in range(1, rows):
            near_pair(r, n, lax.rem(n * rows + r, 4))

        @pl.when(n + 2 < near_steps)
        def _():
            for r in range(rows):
                near_copy((n + 2) * rows + r).start()

        @pl.when(lax.rem(n, 2) == 1)
        def _():
            comm_at(n, "g", near_steps)
            block = pl.ds(pl.multiple_of((n // 2) * (2 * PAIR), 2 * PAIR), 2 * PAIR)
            share = qkv_terms.shape[-2]
            for i, grads in enumerate((dq, dk, dv)):
                total = None
                for row in range(rows):
                    left = normed[row, TILE:] if i == 0 else normed[row]
                    part = dot_tn(left, grads[row, :, block])
                    total = part if total is None else total + part
                to = pl.ds(pl.multiple_of((n // 2) * width + i * 2 * PAIR, 2 * PAIR), 2 * PAIR)
                qkv_terms[:, :, :, :, :, to] = total.astype(jnp.bfloat16).reshape(
                    (outer, 2, 2, 2, share, 2 * PAIR)
                )

        return carry

    lax.fori_loop(0, near_steps, near_step, 0)
    load_x.start()
    chunks = hidden_hbm.shape[1] // CHUNK
    places = [(k, 0), (k, 1), (v, 0), (v, 1)]
    load_proj = [
        pltpu.make_async_copy(
            proj_hbm.at[pl.ds(j * CHUNK, CHUNK)], places[j][0].at[places[j][1]], proj_sem.at[j]
        )
        for j in range(chunks)
    ]

    def tile_of(u):
        return pl.ds(pl.multiple_of(u * TILE, TILE), TILE)

    def hidden_copy(u, j):
        lanes = pl.ds(pl.multiple_of(lax.rem(u, 2) * CHUNK, CHUNK), CHUNK)
        src = hidden_hbm.at[tile_of(u), pl.ds(j * CHUNK, CHUNK)]
        return pltpu.make_async_copy(src, near_probs.at[j, :, lanes], hidden_sem.at[lax.rem(u, 2), j])

    def middle_copy(u):
        slot = lax.rem(u, 2)
        return pltpu.make_async_copy(middle_hbm.at[tile_of(u)], dq_part.at[slot], middle_sem.at[slot])

    def result_copy(u):
        slot = lax.rem(u, 2)
        src = normed.at[slot, pl.ds(0, TILE)]
        return pltpu.make_async_copy(src, out_hbm.at[tile_of(u)], result_sem.at[slot])

    for load in load_proj:
        load.start()
    for u in range(2):
        middle_copy(u).start()
        for j in range(chunks):
            hidden_copy(u, j).start()
    for r in range(rows):
        sums[2:3] += column_sum(dq[r].astype(jnp.float32))
        sums[3:4] += column_sum(dv[r].astype(jnp.float32))
    load_x.wait()
    stores = []
    tiles = local // TILE
    for t in range(tiles):
        if t == tiles - 1:
            comm(f"t{t * rows}")

            @pl.when(s == 0)
            def _():
                late_copy.wait_recv()

        def token_step(r, carry):
            for row in range(rows):
                if t < tiles - 1 or row > 0:

                    @pl.when(r == row)
                    def _():
                        comm(f"t{t * rows + row}")

            span = slice(t * TILE, (t + 1) * TILE)
            keys = slice((t + 1) * TILE, (t + 2) * TILE)
            back = dot_nt(dq[r, span], weight[:, third[0]])
            back = back + dot_nt(dk[r, keys], weight[:, third[1]])
            back = back + dot_nt(dv[r, keys], weight[:, third[2]])
            if t == tiles - 1:
                back = back + late[r].astype(jnp.float32)
            normal, scale = normalize(q[r, span].astype(jnp.float32))
            sums[0:1] += column_sum(back * normal)
            sums[1:2] += column_sum(back)
            flat = pl.ds(pl.multiple_of(r * local + t * TILE, TILE), TILE)
            middle[flat] = middle[flat] + norm_grad(back, vectors[0:1], normal, scale)
            return carry

        lax.fori_loop(0, rows, token_step, 0)
        for r in range(rows):
            store = pltpu.make_async_copy(
                middle.at[pl.ds(r * local + t * TILE, TILE)],
                tokens_grad_hbm.at[r, pl.ds(t * TILE, TILE)],
                out_sem.at[t * rows + r],
            )
            store.start()
            stores.append(store)
    size = width // (outer * 8)
    fc_size = 4 * size
    total, fc_total = sums[0:8], sums[8:16]
    for d in range(outer * 8):
        row, start = divmod(d * fc_size, width)
        index = (d // 8, (d // 4) % 2, (d // 2) % 2, d % 2)
        vector_terms[index + (slice(0, 8),)] = pack_columns(total, d * size, size)
        vector_terms[index + (slice(8, 16),)] = pack_columns(
            jnp.broadcast_to(fc_total[4 + row : 5 + row], (8, width)), start, fc_size
        )
    vector_copies = [
        remote(
            vector_terms.at[to], vector_got.at[n], vector_send.at[n], vector_recv.at[n], device(*to)
        )
        for n, (to, _) in enumerate(everyone(outer))
    ]
    for copy in vector_copies:
        copy.start()
    for load in load_proj:
        load.wait()
    out_tiles = rows * local // TILE

    def out_step(u, carry):
        comm_at(u, "u", out_tiles)
        slot = lax.rem(u, 2)
        middle_copy(u).wait()
        result = dq_part[slot] + vectors[7:8]
        for j in range(chunks):
            hidden_copy(u, j).wait()
            lanes = pl.ds(pl.multiple_of(slot * CHUNK, CHUNK), CHUNK)
            result = result + dot_nn(near_probs[j, :, lanes], places[j][0][places[j][1]])

        @pl.when(u >= 2)
        def _():
            result_copy(u - 2).wait()

        normed[slot, 0:TILE] = result.astype(jnp.bfloat16)
        result_copy(u).start()

        @pl.when(u + 2 < out_tiles)
        def _():
            middle_copy(u + 2).start()
            for j in range(chunks):
                hidden_copy(u + 2, j).start()

        return carry

    lax.fori_loop(0, out_tiles, out_step, 0)
    for u in range(out_tiles - 2, out_tiles):
        result_copy(u).wait()
    comm("end")
    value = vector_terms[a, y, c, s]
    for n, copy in enumerate(vector_copies):
        copy.wait_recv()
        value = value + vector_got[n]
    vector_share[...] = value
    work.end()
    for copy in vector_copies:
        copy.wait_send()
    for store in stores:
        store.wait()

    @pl.when(s == 1)
    def _():
        late_copy.wait_send()


BACKWARD_ORDERS = (0, 1, 1, 0, 1, 1, 0, 1, 0, 1, 1, 0, 1, 1, 1, 0, 1, 0, 1)
BACKWARD_PLAN = {'start': [(0, 0), (0, 1), (0, 2)], 'm3': [(1, 0)], 'm4': [(1, 1), (1, 2)], 'w2': [(0, 3), (0, 4)], 'w3': [(2, 0), (0, 5), (0, 6)], 'o0': [(2, 1), (1, 3), (1, 4), (0, 7), (0, 8)], 'o1': [(0, 9), (0, 10)], 'o2': [(1, 5), (1, 6)], 'o4': [(1, 7), (1, 8), (1, 9), (3, 1), (2, 2), (1, 10)], 'o7': [(2, 3)], 'attn': [(3, 0), (2, 6)], 'rest': [(4, 1), (2, 4)], 'f0': [(2, 5), (2, 8), (0, 11), (0, 12)], 'f3': [(4, 0), (3, 2), (2, 7)], 'mm': [(3, 4), (1, 11)], 'n0': [(3, 5), (2, 9), (1, 12), (3, 7)], 'n1': [(4, 2), (2, 10)], 'h1': [(3, 3), (2, 11), (4, 4)], 'g1': [(3, 6)], 'n2': [(4, 5), (4, 7), (3, 8), (0, 13), (0, 14)], 'h2': [(4, 3)], 'n3': [(2, 12)], 'h3': [(4, 6)], 'g3': [(4, 8), (3, 11), (1, 13), (1, 14)], 'n4': [(0, 15), (0, 16)], 'n5': [(4, 11)], 'g5': [(2, 13), (1, 15), (1, 16)], 't0': [(0, 17), (0, 18)], 't1': [(3, 9), (3, 10), (2, 14)], 't2': [(3, 12), (2, 16), (1, 17), (1, 18), (3, 13)], 't3': [(4, 9)], 'u0': [(4, 10), (2, 15)], 'u1': [(4, 12), (4, 13), (3, 14), (3, 16), (2, 18)], 'u2': [(3, 15), (2, 17)], 'u3': [(4, 14), (3, 18)], 'end': [(4, 15), (4, 16), (3, 17), (4, 18), (4, 17)]}


def backward(outer, hidden, slope, middle, normed2, att, dy, attn, fc, proj, proj_terms, probs, q, k, v, normed, x, weight, vectors):
    rows, local, width = q.shape
    devices = outer * 8
    low, full = jnp.bfloat16, jnp.float32
    share = weight.shape[0] // devices
    units = fc.shape[1]
    anywhere = pl.BlockSpec(memory_space=pl.ANY)
    vmem = pl.BlockSpec(memory_space=pltpu.VMEM)
    blocks = weight.shape[1] // width
    pieces = column_pieces(0, width, 3, (0,))
    pieces += column_pieces(1, units, 2 * units // width, (0,)) + column_pieces(2, width, 2, (0,))
    first = len(pieces)
    pieces += column_pieces(3, weight.shape[1], 2 * blocks, (0,))
    pieces = [piece[:3] + (order,) for piece, order in zip(pieces, BACKWARD_ORDERS)]
    part, half = width // 3, width // 2
    places = {}
    for b in range(blocks):
        for h in range(2):
            begin, end = h * half, (h + 1) * half
            places[first + 2 * b + h] = [
                (max(i * part, begin) - begin, min((i + 1) * part, end) - max(i * part, begin),
                 i * width + b * part + max(i * part, begin) - i * part)
                for i in range(blocks)
                if max(i * part, begin) < min((i + 1) * part, end)
            ]
    shapes = [(units // devices, width, low), (share, units, low), (share, width, low), (share, weight.shape[1], low)]
    slots = lambda columns: jax.ShapeDtypeStruct((outer, 2, 2, 2, share, columns), low)
    flat = dy.shape
    return pl.pallas_call(
        functools.partial(backward_kernel, outer, pieces, places),
        in_specs=[anywhere] * 17 + [vmem],
        out_specs=[anywhere] * 4 + [vmem] * 5,
        out_shape=[
            jax.ShapeDtypeStruct(flat, low),
            jax.ShapeDtypeStruct(x.shape, full),
            slots(units),
            slots(width),
        ]
        + [shares_out(shape[0], shape[1]) for shape in shapes]
        + [shares_out(16, PAIR)],
        scratch_shapes=[
            pltpu.VMEM(flat, low),
            pltpu.VMEM(flat, low),
            pltpu.VMEM(flat, full),
            pltpu.VMEM((rows, TILE, width), low),
            pltpu.VMEM((rows, TILE, width), low),
            pltpu.VMEM((outer, 2, 2, 2, 16, PAIR), full),
            pltpu.VMEM((devices - 1, 16, PAIR), full),
            pltpu.VMEM((16, width), full),
            pltpu.SemaphoreType.DMA((2,)),
            pltpu.SemaphoreType.DMA((2,)),
            pltpu.SemaphoreType.DMA((devices - 1,)),
            pltpu.SemaphoreType.DMA((devices - 1,)),
        ]
        + Scatter.scratch(outer, shapes, pieces),
        compiler_params=pltpu.CompilerParams(
            collective_id=4, has_side_effects=True, vmem_limit_bytes=VMEM_LIMIT
        ),
    )(
        hidden, slope, middle, normed2, att, dy, attn, fc, proj, proj_terms,
        probs, q, k, v, normed, x, weight, vectors,
    )


def gather_weights(outer, weights, vectors, fc_bias):
    devices = outer * 8
    shards = [pack_vectors(vectors + [fc_bias])]
    shards += [w.reshape(pack_shape(w.shape)) for w in weights]
    full = gather_all(outer, shards, cut([shard.shape for shard in shards]))
    packed = full[0].reshape(devices, -1)
    count, size = len(vectors), vectors[0].shape[0]
    first = packed[:, : count * size].reshape(devices, count, size)
    first = jnp.swapaxes(first, 0, 1).reshape(count, devices * size)
    second = packed[:, count * size : count * size + fc_bias.shape[0]].reshape(-1, devices * size)
    whole = [f.reshape(devices * w.shape[0], w.shape[1]) for f, w in zip(full[1:], weights)]
    return whole, jnp.concatenate([first, second], axis=0)


def scatter_grads(outer, weight_terms, vector_terms, fc_bias_term):
    devices = outer * 8
    count, width = vector_terms.shape
    first = jnp.swapaxes(vector_terms.reshape(count, devices, width // devices), 0, 1)
    first = first.reshape(devices, -1)
    second = fc_bias_term.reshape(devices, -1)
    packed = pack_vectors([first, second])
    terms = [packed.reshape((outer, 2, 2, 2) + packed.shape[1:])]
    shapes = [(term.shape[0] // devices, term.shape[1]) for term in weight_terms]
    for term, shape in zip(weight_terms, shapes):
        terms.append(term.reshape((outer, 2, 2, 2) + pack_shape(shape)))
    shares = scatter_all(outer, terms, cut([term.shape[-2:] for term in terms]))
    flat = shares[0].reshape(-1)
    size = width // devices
    vectors = [flat[i * size : (i + 1) * size] for i in range(count)]
    fc_bias = flat[count * size : count * size + second.shape[1]]
    return [share.reshape(shape) for share, shape in zip(shares[1:], shapes)], vectors, fc_bias


def shards(
    tokens_in,
    doc_starts,
    norm1_gain,
    norm1_bias,
    qkv_weight,
    query_bias,
    value_bias,
    attn_weight,
    attn_bias,
    norm2_gain,
    norm2_bias,
    fc_weight,
    fc_bias,
    proj_weight,
    proj_bias,
    out_grad,
):
    outer = lax.axis_size("batch") // 4
    rows, local, width = tokens_in.shape
    seq = lax.axis_index("seq")
    weights = [qkv_weight, attn_weight, fc_weight, proj_weight]
    vectors = [norm1_gain, norm1_bias, query_bias, value_bias, attn_bias, norm2_gain, norm2_bias, proj_bias]
    flat = lambda value: value.reshape(rows * local, width)
    block = lambda value: value.reshape(rows, local, width)
    dy = flat(out_grad)
    devices = 8 * outer
    if qkv_weight.shape[0] % 8 == 0 and proj_weight.shape[0] % 16 == 0 and CHUNK % (8 * proj_weight.shape[0]) == 0:
        (
            normed, q, k, v, probs, att, hidden, slope, middle, normed2, qkv, attn, fc, proj, proj_terms, vectors,
        ) = forward(outer, tokens_in, dy, doc_starts, vectors + [fc_bias], weights)
        proj = proj.reshape(devices * proj_weight.shape[0], width)
        out, tokens_grad, _, _, proj_share, fc_share, attn_share, qkv_share, packed = backward(
            outer, hidden, slope, middle, normed2, att, dy, attn, fc, proj, proj_terms,
            probs, q, k, v, normed, tokens_in, qkv, vectors,
        )
        size = width // devices
        weights = [qkv_share, attn_share, fc_share, proj_share]
        shares = [packed[i, :size] for i in range(8)]
        fc_bias_share = packed[8, : 4 * size]
    else:
        first = 2 * seq
        padded = jnp.pad(doc_starts, ((0, 0), (1, 0)))
        starts = lax.dynamic_slice_in_dim(padded, first, 3, 1)
        starts = starts - TILE * (first - 1 + jnp.arange(3, dtype=jnp.int32))
        prev = lax.ppermute(tokens_in[:, local - TILE :], "seq", [(0, 1)])
        (qkv, attn, fc, proj), vectors = gather_weights(outer, weights, vectors, fc_bias)
        normed, q, k, v = project(tokens_in, prev, qkv, vectors)
        probs, att, inverse = attend(starts, q, k, v)
        out, middle_grad, att_grad, attn_grad, fc_grad, proj_grad, mlp_sums = mlp(
            flat(tokens_in), flat(att), dy, attn, fc, proj, vectors
        )
        dq, dk, dv = attend_grad(probs, q, k, v, block(att_grad), att, inverse)
        qkv_grad, prev_grad, project_sums = project_grad(normed, dq, dk, dv, qkv)
        late = lax.ppermute(prev_grad, "seq", [(1, 0)])
        tokens_grad, norm_sums = tokens_grad_of(
            tokens_in, dq, dk, dv, qkv, late, block(middle_grad), vectors
        )
        sums = jnp.concatenate([norm_sums[:2], project_sums[:2], mlp_sums[:4]], axis=0)
        weights, shares, fc_bias_share = scatter_grads(
            outer, [qkv_grad, attn_grad, fc_grad, proj_grad], sums, mlp_sums[4:]
        )
    gain1, bias1, query, value, proj_b, gain2, bias2, attn_b = shares
    return (
        out.reshape(rows, local, width),
        tokens_grad,
        gain1,
        bias1,
        weights[0],
        query,
        value,
        weights[1],
        attn_b,
        gain2,
        bias2,
        weights[2],
        fc_bias_share,
        weights[3],
        proj_b,
    )


def solution(mesh):
    return jax.shard_map(
        shards,
        mesh=mesh,
        in_specs=(
            P("batch", "seq", None),
            P("batch", None),
            P(("batch", "seq")),
            P(("batch", "seq")),
            P(("batch", "seq"), None),
            P(("batch", "seq")),
            P(("batch", "seq")),
            P(("batch", "seq"), None),
            P(("batch", "seq")),
            P(("batch", "seq")),
            P(("batch", "seq")),
            P(("batch", "seq"), None),
            P(("batch", "seq")),
            P(("batch", "seq"), None),
            P(("batch", "seq")),
            P("batch", "seq", None),
        ),
        out_specs=(
            P("batch", "seq", None),
            P("batch", "seq", None),
            P(("batch", "seq")),
            P(("batch", "seq")),
            P(("batch", "seq"), None),
            P(("batch", "seq")),
            P(("batch", "seq")),
            P(("batch", "seq"), None),
            P(("batch", "seq")),
            P(("batch", "seq")),
            P(("batch", "seq")),
            P(("batch", "seq"), None),
            P(("batch", "seq")),
            P(("batch", "seq"), None),
            P(("batch", "seq")),
        ),
        check_vma=False,
    )
```

```python
import functools
import math

import jax
import jax.numpy as jnp
from jax import lax
from jax.experimental import pallas as pl
from jax.experimental.pallas import tpu as pltpu
from jax.sharding import PartitionSpec as P

HD = 64
EPSILON = 1e-05
GELU_SCALE = 0.7978845608028654
MESH_ID = pl.DeviceIdType.MESH
VMEM_LIMIT = 62 * 2**20
EVERY = slice(None)


def place():
    batch, seq = lax.axis_index("batch"), lax.axis_index("seq")
    return (batch // 4, (batch // 2) % 2, batch % 2, seq)


def device(a, y, c, s):
    return (a * 4 + y * 2 + c, s)


def greet(outer):
    a, y, c, s = place()
    barrier = pltpu.get_barrier_semaphore()
    others = [device(lax.rem(a + k, outer), y, c, s) for k in range(1, outer)]
    others += [device(a, 1 - y, c, s), device(a, y, c, 1 - s), device(a, y, 1 - c, s)]
    for other in others:
        pl.semaphore_signal(barrier, inc=1, device_id=other, device_id_type=MESH_ID)
    pl.semaphore_wait(barrier, len(others))


def everyone(outer):
    a, y, c, s = place()
    devices = outer * 8
    me = ((a * 2 + y) * 2 + c) * 2 + s
    split = lambda d: (d // 8, (d // 4) % 2, (d // 2) % 2, d % 2)
    return [
        (split(lax.rem(me + k, devices)), split(lax.rem(me + devices - k, devices)))
        for k in range(1, devices)
    ]


def greet_all(outer):
    barrier = pltpu.get_barrier_semaphore()
    others = everyone(outer)
    for other, _ in others:
        pl.semaphore_signal(barrier, inc=1, device_id=device(*other), device_id_type=MESH_ID)
    pl.semaphore_wait(barrier, len(others))


def remote(src, dst, send_sem, recv_sem, other):
    return pltpu.make_async_remote_copy(
        src_ref=src,
        dst_ref=dst,
        send_sem=send_sem,
        recv_sem=recv_sem,
        device_id=other,
        device_id_type=MESH_ID,
    )


def sites_of(work, plan):
    def comm(name):
        for phase, p in plan.get(name, ()):
            work.act(phase, p)
            if (phase, p) in work.after:
                work.after[(phase, p)]()

    def comm_at(n, name, count, stride=1, offset=0):
        for i in range(count):
            site = f"{name}{i * stride + offset}"
            if site in plan:

                @pl.when(n == i)
                def _():
                    comm(site)

    return comm, comm_at


class Gather:
    def __init__(self, outer, pieces, shards, outs, own_sem, send_sem, recv_sem, eager=99):
        self.outer, self.pieces, self.shards, self.outs = outer, pieces, shards, outs
        self.own_sem, self.send_sem, self.recv_sem = own_sem, send_sem, recv_sem
        self.eager, self.after = eager, {}
        self.place = place()

    def sems(self, p, k):
        return self.send_sem.at[p, k], self.recv_sem.at[p, k]

    def own(self, i):
        return pltpu.make_async_copy(
            self.shards[i], self.outs[i].at[self.place], self.own_sem.at[i]
        )

    def first(self, p, k):
        i, start, width, order = self.pieces[p]
        a, y, c, s = self.place
        columns = pl.ds(start, width)
        src = self.shards[i].at[:, columns]
        dst = self.outs[i].at[a, y, c, s, :, columns]
        if k == 0:
            return remote(src, dst, *self.sems(p, 0), self.near(order))
        return remote(src, dst, *self.sems(p, k), device(lax.rem(a + k, self.outer), y, c, s))

    def near(self, order):
        a, y, c, s = self.place
        return device(a, 1 - y, c, s) if order == 0 else device(a, y, c, 1 - s)

    def second(self, p, k):
        i, start, width, order = self.pieces[p]
        a, y, c, s = self.place
        source = lax.rem(a + self.outer - k, self.outer)
        block = self.outs[i].at[source, y, c, s, :, pl.ds(start, width)]
        return remote(block, block, *self.sems(p, self.outer - 1 + k), self.near(order))

    def third(self, p):
        i, start, width, order = self.pieces[p]
        a, y, c, s = self.place
        index = (EVERY, EVERY, c, s) if order == 0 else (EVERY, y, c, EVERY)
        block = self.outs[i].at[index + (EVERY, pl.ds(start, width))]
        return remote(block, block, *self.sems(p, 2 * self.outer - 1), self.near(1 - order))

    def fourth(self, p):
        i, start, width, order = self.pieces[p]
        a, y, c, s = self.place
        block = self.outs[i].at[EVERY, EVERY, c, EVERY, EVERY, pl.ds(start, width)]
        return remote(block, block, *self.sems(p, 2 * self.outer), device(a, y, 1 - c, s))

    def start(self):
        for p in range(len(self.pieces)):
            for k in range(1, self.outer):
                self.first(p, k).start()
            if p < self.eager:
                self.first(p, 0).start()
        for i in range(len(self.shards)):
            self.own(i).start()

    def act(self, phase, p):
        outer = self.outer
        if phase == 1:
            if p >= self.eager:
                self.first(p, 0).start()
            for k in range(1, outer):
                self.first(p, k).wait_recv()
                self.second(p, k).start()
        elif phase == 2:
            if p == 0:
                for n in range(len(self.shards)):
                    self.own(n).wait()
            self.first(p, 0).wait_recv()
            for k in range(1, outer):
                self.second(p, k).wait_recv()
            self.third(p).start()
        elif phase == 3:
            self.third(p).wait_recv()
            self.fourth(p).start()
        else:
            self.fourth(p).wait_recv()

    def end(self):
        for p in range(len(self.pieces)):
            for k in range(self.outer):
                self.first(p, k).wait_send()
            for k in range(1, self.outer):
                self.second(p, k).wait_send()
            self.third(p).wait_send()
            self.fourth(p).wait_send()

    @staticmethod
    def semaphores(outer, arrays, pieces):
        return [
            pltpu.SemaphoreType.DMA((arrays,)),
            pltpu.SemaphoreType.DMA((pieces, 2 * outer + 1)),
            pltpu.SemaphoreType.DMA((pieces, 2 * outer + 1)),
        ]


def add_slots(target, other):
    target[...] = target[...] + other[...]


class Scatter:
    def __init__(self, outer, pieces, terms, outs, slots, own_sem, send_sem, recv_sem, places=None):
        self.outer, self.pieces, self.terms, self.outs = outer, pieces, terms, outs
        n = len(pieces)
        self.held, self.got = slots[:n], [slots[k * n : (k + 1) * n] for k in range(1, 5)]
        self.own_sem, self.send_sem, self.recv_sem = own_sem, send_sem, recv_sem
        self.places, self.before, self.after = places or {}, {}, {}
        self.place = place()

    def sems(self, p, k):
        return self.send_sem.at[p, k], self.recv_sem.at[p, k]

    def own(self, p):
        i, start, width, order = self.pieces[p]
        a, y, c, s = self.place
        block = self.terms[i].at[EVERY, EVERY, c, EVERY, EVERY, pl.ds(start, width)]
        return pltpu.make_async_copy(block, self.held[p], self.own_sem.at[p])

    def first(self, p):
        i, start, width, order = self.pieces[p]
        a, y, c, s = self.place
        block = self.terms[i].at[EVERY, EVERY, 1 - c, EVERY, EVERY, pl.ds(start, width)]
        return remote(block, self.got[0][p], *self.sems(p, 0), device(a, y, 1 - c, s))

    def second(self, p):
        a, y, c, s = self.place
        if self.pieces[p][3] == 0:
            src, other = self.held[p].at[:, :, 1 - s], device(a, y, c, 1 - s)
        else:
            src, other = self.held[p].at[:, 1 - y], device(a, 1 - y, c, s)
        return remote(src, self.got[1][p], *self.sems(p, 1), other)

    def third(self, p):
        a, y, c, s = self.place
        if self.pieces[p][3] == 0:
            src, other = self.held[p].at[:, 1 - y, s], device(a, 1 - y, c, s)
        else:
            src, other = self.held[p].at[:, y, 1 - s], device(a, y, c, 1 - s)
        return remote(src, self.got[2][p], *self.sems(p, 2), other)

    def fourth(self, p, k):
        a, y, c, s = self.place
        to = lax.rem(a + k, self.outer)
        src = self.held[p].at[to, y, s]
        return remote(src, self.got[3][p].at[k - 1], *self.sems(p, 2 + k), device(to, y, c, s))

    def act(self, phase, p):
        outer = self.outer
        a, y, c, s = self.place
        i, start, width, order = self.pieces[p]
        if phase == 0:
            if p in self.before:
                self.before[p]()
            self.own(p).start()
            self.first(p).start()
        elif phase == 1:
            self.own(p).wait()
            self.first(p).wait_recv()
            add_slots(self.held[p], self.got[0][p])
            self.second(p).start()
        elif phase == 2:
            self.second(p).wait_recv()
            mine = (EVERY, EVERY, s) if order == 0 else (EVERY, y)
            add_slots(self.held[p].at[mine], self.got[1][p])
            self.third(p).start()
        elif phase == 3:
            self.third(p).wait_recv()
            add_slots(self.held[p].at[:, y, s], self.got[2][p])
            for k in range(1, outer):
                self.fourth(p, k).start()
        else:
            value = self.held[p][a, y, s].astype(jnp.float32)
            for k in range(1, outer):
                self.fourth(p, k).wait_recv()
                value = value + self.got[3][p][k - 1].astype(jnp.float32)
            for offset, size, to in self.places.get(p, [(0, width, start)]):
                self.outs[i][:, to : to + size] = value[:, offset : offset + size]

    def end(self):
        for p in range(len(self.pieces)):
            self.first(p).wait_send()
            self.second(p).wait_send()
            self.third(p).wait_send()
            for k in range(1, self.outer):
                self.fourth(p, k).wait_send()

    @staticmethod
    def scratch(outer, shapes, pieces):
        def slot(p, *lead):
            i, start, width, order = pieces[p]
            return pltpu.VMEM(lead + (shapes[i][0], width), shapes[i][2])

        n = range(len(pieces))
        leads = ((outer, 2, 2), (outer, 2, 2), (outer, 2), (outer,), (max(outer - 1, 1),))
        return [slot(p, *lead) for lead in leads for p in n] + [
            pltpu.SemaphoreType.DMA((len(pieces),)),
            pltpu.SemaphoreType.DMA((len(pieces), outer + 2)),
            pltpu.SemaphoreType.DMA((len(pieces), outer + 2)),
        ]


def steps_in_order(count, lags):
    first = 5 - len(lags)
    steps = [(p + lag, k + first, p) for p in range(count) for k, lag in enumerate(lags)]
    return [(p, phase) for _, phase, p in sorted(steps)]


def gather_kernel(outer, pieces, count, *refs):
    greet(outer)
    work = Gather(outer, pieces, refs[:count], refs[count : 2 * count], *refs[2 * count :])
    work.start()
    for p, phase in steps_in_order(len(pieces), (1, 2, 4, 6)):
        work.act(phase, p)
    work.end()


def gather_all(outer, shards, pieces):
    count = len(shards)
    return pl.pallas_call(
        functools.partial(gather_kernel, outer, pieces, count),
        out_shape=[
            jax.ShapeDtypeStruct((outer, 2, 2, 2) + shard.shape, shard.dtype) for shard in shards
        ],
        in_specs=[pl.BlockSpec(memory_space=pltpu.VMEM)] * count,
        out_specs=[pl.BlockSpec(memory_space=pl.ANY)] * count,
        scratch_shapes=Gather.semaphores(outer, count, len(pieces)),
        compiler_params=pltpu.CompilerParams(
            collective_id=0, has_side_effects=True, vmem_limit_bytes=VMEM_LIMIT
        ),
    )(*shards)


def scatter_kernel(outer, pieces, count, *refs):
    greet(outer)
    rest = refs[2 * count :]
    work = Scatter(outer, pieces, refs[:count], refs[count : 2 * count], rest[:-3], *rest[-3:])
    for p, phase in steps_in_order(len(pieces), (0, 1, 3, 4, 5)):
        work.act(phase, p)
    work.end()


def scatter_all(outer, terms, pieces):
    count = len(terms)
    shapes = [term.shape[-2:] + (term.dtype,) for term in terms]
    return pl.pallas_call(
        functools.partial(scatter_kernel, outer, pieces, count),
        out_shape=[jax.ShapeDtypeStruct(term.shape[-2:], jnp.float32) for term in terms],
        in_specs=[pl.BlockSpec(memory_space=pl.ANY)] * count,
        out_specs=[pl.BlockSpec(memory_space=pltpu.VMEM)] * count,
        scratch_shapes=Scatter.scratch(outer, shapes, pieces),
        compiler_params=pltpu.CompilerParams(
            collective_id=1, has_side_effects=True, vmem_limit_bytes=VMEM_LIMIT
        ),
    )(*terms)


def cut(shape_list):
    pieces = []
    for i, (rows, columns) in enumerate(shape_list):
        parts, blocks = 1, columns // 128
        if rows % 8 == 0:
            fits = [k for k in range(1, blocks + 1) if blocks % k == 0 and rows * columns // k <= 25000]
            parts = min(fits) if fits else 1
        width = columns // parts
        for k in range(parts):
            pieces.append((i, k * width, width, len(pieces) % 2))
    return pieces


def pack_shape(shape):
    rows, columns = shape
    return shape if rows % 8 == 0 else (rows * columns // 128, 128)


def pack_vectors(parts):
    joined = jnp.concatenate([part.astype(jnp.float32) for part in parts], axis=-1)
    size = -(-joined.shape[-1] // 1024) * 1024
    pad = [(0, 0)] * (joined.ndim - 1) + [(0, size - joined.shape[-1])]
    return jnp.pad(joined, pad).reshape(joined.shape[:-1] + (size // 128, 128))


TILE = 256
PAIR = 128
FIRM = 1e30


def dot_nn(left, right):
    return lax.dot_general(left, right, (((1,), (0,)), ((), ())), preferred_element_type=jnp.float32)


def dot_nt(left, right):
    return lax.dot_general(left, right, (((1,), (1,)), ((), ())), preferred_element_type=jnp.float32)


def dot_tn(left, right):
    return lax.dot_general(left, right, (((0,), (0,)), ((), ())), preferred_element_type=jnp.float32)


def normalize(values):
    average = jnp.mean(values, axis=-1, keepdims=True)
    centered = values - average
    variance = jnp.mean(centered * centered, axis=-1, keepdims=True)
    scale = lax.rsqrt(variance + EPSILON)
    return centered * scale, scale


def norm_grad(upstream, gain, normal, scale):
    inner = upstream * gain
    first = jnp.mean(inner, axis=-1, keepdims=True)
    second = jnp.mean(inner * normal, axis=-1, keepdims=True)
    return scale * (inner - first - normal * second)


def column_sum(values):
    return jnp.sum(values, axis=0, keepdims=True)


def project_kernel(x_ref, prev_ref, weight_ref, vectors_ref, normed_ref, q_ref, k_ref, v_ref):
    tile = pl.program_id(1)
    width = x_ref.shape[-1]
    x = jnp.where(tile == 0, prev_ref[0], x_ref[0]).astype(jnp.float32)
    normal, _ = normalize(x)
    normed = (normal * vectors_ref[0:1] + vectors_ref[1:2]).astype(jnp.bfloat16)
    normed_ref[0] = normed

    @pl.when(tile > 0)
    def _():
        queries = dot_nn(normed, weight_ref[:, :width]) + vectors_ref[2:3]
        q_ref[0] = queries.astype(jnp.bfloat16) * jnp.bfloat16(1.0 / math.sqrt(HD))

    k_ref[0] = dot_nn(normed, weight_ref[:, width : 2 * width]).astype(jnp.bfloat16)
    values = dot_nn(normed, weight_ref[:, 2 * width :]) + vectors_ref[3:4]
    v_ref[0] = values.astype(jnp.bfloat16)


def project(tokens, prev, weight, vectors):
    rows, local, width = tokens.shape
    tiles = local // TILE
    here = lambda r, t: (r, jnp.maximum(t - 1, 0), 0)
    extended = jax.ShapeDtypeStruct((rows, local + TILE, width), jnp.bfloat16)
    return pl.pallas_call(
        project_kernel,
        grid=(rows, tiles + 1),
        in_specs=[
            pl.BlockSpec((1, TILE, width), here),
            pl.BlockSpec((1, TILE, width), lambda r, t: (r, 0, 0)),
            pl.BlockSpec(weight.shape, lambda r, t: (0, 0)),
            pl.BlockSpec(vectors.shape, lambda r, t: (0, 0)),
        ],
        out_specs=[
            pl.BlockSpec((1, TILE, width), lambda r, t: (r, t, 0)),
            pl.BlockSpec((1, TILE, width), here),
            pl.BlockSpec((1, TILE, width), lambda r, t: (r, t, 0)),
            pl.BlockSpec((1, TILE, width), lambda r, t: (r, t, 0)),
        ],
        out_shape=[extended, jax.ShapeDtypeStruct(tokens.shape, jnp.bfloat16), extended, extended],
        compiler_params=pltpu.CompilerParams(vmem_limit_bytes=VMEM_LIMIT),
    )(tokens, prev, weight, vectors)


def lane_index(rows):
    return lax.broadcasted_iota(jnp.int32, (rows, PAIR), 1)


def mask_columns(starts_of, row, q_cols, k_cols):
    place = lax.broadcasted_iota(jnp.int32, (TILE, PAIR), 0)
    lane = lane_index(TILE)
    for tile in range(2):
        before, start = starts_of(row, tile), starts_of(row, tile + 1)
        late = jnp.where(place >= start, 1.0, 0.0)
        q_cols[tile] = jnp.where(lane == 0, late, jnp.where(lane == 1, 1.0, 0.0)).astype(jnp.bfloat16)
        early = jnp.where(place < before, -FIRM, 0.0)
        k_cols[tile, 0] = jnp.where(
            lane == 0, -FIRM, jnp.where(lane == 1, early, 0.0)
        ).astype(jnp.bfloat16)
        early = jnp.where(place < start, -FIRM, 0.0)
        k_cols[tile, 1] = jnp.where(lane == 0, early, 0.0).astype(jnp.bfloat16)


def attend_kernel(starts_ref, q_ref, k_ref, v_ref, probs_ref, out_ref, inverse_ref, q_cols, k_cols):
    row = pl.program_id(0)

    @pl.when(pl.program_id(1) == 0)
    def _():
        mask_columns(lambda r, i: starts_ref[r, i], row, q_cols, k_cols)

    lane = lane_index(TILE)
    causal = lax.broadcasted_iota(jnp.int32, (TILE, TILE), 1) <= lax.broadcasted_iota(
        jnp.int32, (TILE, TILE), 0
    )
    ones = jnp.ones((TILE, PAIR), jnp.bfloat16)
    for tile in range(2):
        queries = q_ref[0, pl.ds(tile * TILE, TILE)]
        keys = [
            jnp.concatenate([k_ref[0, pl.ds((tile + w) * TILE, TILE)], k_cols[tile, w]], axis=1)
            for w in range(2)
        ]
        values = [
            jnp.concatenate([v_ref[0, pl.ds((tile + w) * TILE, TILE)], ones], axis=1)
            for w in range(2)
        ]
        mixed, inverse = [], []
        for head in range(2):
            mine = (lane < HD) if head == 0 else (lane >= HD)
            left = jnp.concatenate([jnp.where(mine, queries, jnp.bfloat16(0)), q_cols[tile]], axis=1)
            far = dot_nt(left, keys[0])
            near = jnp.where(causal, dot_nt(left, keys[1]), -FIRM)
            top = jnp.max(jnp.maximum(far, near), axis=-1, keepdims=True)
            far = jnp.exp(far - top).astype(jnp.bfloat16)
            near = jnp.exp(near - top).astype(jnp.bfloat16)
            probs_ref[0, 0, tile, head, 0] = far
            probs_ref[0, 0, tile, head, 1] = near
            total = dot_nn(far, values[0]) + dot_nn(near, values[1])
            share = 1.0 / total[:, PAIR:]
            mixed.append(total[:, :PAIR] * share)
            inverse.append(share)
        out_ref[0, pl.ds(tile * TILE, TILE)] = jnp.where(lane < HD, mixed[0], mixed[1]).astype(
            jnp.bfloat16
        )
        inverse_ref[0, pl.ds(tile * TILE, TILE)] = jnp.where(lane < HD, inverse[0], inverse[1])


def attend(starts, q, k, v):
    rows, local, width = q.shape
    pairs = width // PAIR
    by_pair = lambda r, j: (r, 0, j)
    return pl.pallas_call(
        attend_kernel,
        grid=(rows, pairs),
        in_specs=[
            pl.BlockSpec(memory_space=pltpu.SMEM),
            pl.BlockSpec((1, local, PAIR), by_pair),
            pl.BlockSpec((1, local + TILE, PAIR), by_pair),
            pl.BlockSpec((1, local + TILE, PAIR), by_pair),
        ],
        out_specs=[
            pl.BlockSpec((1, 1, 2, 2, 2, TILE, TILE), lambda r, j: (r, j, 0, 0, 0, 0, 0)),
            pl.BlockSpec((1, local, PAIR), by_pair),
            pl.BlockSpec((1, local, PAIR), by_pair),
        ],
        out_shape=[
            jax.ShapeDtypeStruct((rows, pairs, 2, 2, 2, TILE, TILE), jnp.bfloat16),
            jax.ShapeDtypeStruct((rows, local, width), jnp.bfloat16),
            jax.ShapeDtypeStruct((rows, local, width), jnp.float32),
        ],
        scratch_shapes=[
            pltpu.VMEM((2, TILE, PAIR), jnp.bfloat16),
            pltpu.VMEM((2, 2, TILE, PAIR), jnp.bfloat16),
        ],
        compiler_params=pltpu.CompilerParams(vmem_limit_bytes=VMEM_LIMIT),
    )(starts, q, k, v)


def attend_grad_kernel(
    probs_ref, q_ref, k_ref, v_ref, grad_ref, out_ref, inverse_ref, dq_ref, dk_ref, dv_ref, dk_sum, dv_sum
):
    lane = lane_index(TILE)
    ones = jnp.ones((TILE, PAIR), jnp.bfloat16)
    for tile in range(2):
        span = pl.ds(tile * TILE, TILE)
        queries = q_ref[0, span]
        scaled = (grad_ref[0, span].astype(jnp.float32) * inverse_ref[0, span]).astype(jnp.bfloat16)
        product = scaled.astype(jnp.float32) * out_ref[0, span].astype(jnp.float32)
        d_queries = []
        for head in range(2):
            mine = (lane < HD) if head == 0 else (lane >= HD)
            delta = -jnp.sum(jnp.where(mine, product, 0.0), axis=-1, keepdims=True)
            high = delta.astype(jnp.bfloat16).astype(jnp.float32)
            extra = jnp.where(lane == 0, high, jnp.where(lane == 1, delta - high, 0.0))
            grads = jnp.where(mine, scaled, jnp.bfloat16(0))
            mine_queries = jnp.where(mine, queries, jnp.bfloat16(0))
            left = jnp.concatenate([grads, extra.astype(jnp.bfloat16)], axis=1)
            d_query = None
            for w in range(2):
                at = pl.ds((tile + w) * TILE, TILE)
                right = jnp.concatenate([v_ref[0, at], ones], axis=1)
                probs = probs_ref[0, 0, tile, head, w]
                d_score = (probs.astype(jnp.float32) * dot_nt(left, right)).astype(jnp.bfloat16)
                part = dot_nn(d_score, k_ref[0, at])
                d_query = part if w == 0 else d_query + part
                d_key = dot_tn(d_score, mine_queries)
                d_value = dot_tn(probs, grads)
                if head == 0 and (w == 1 or tile == 0):
                    dk_sum[at] = d_key
                    dv_sum[at] = d_value
                else:
                    dk_sum[at] += d_key
                    dv_sum[at] += d_value
            d_queries.append(d_query)
        dq = jnp.where(lane < HD, d_queries[0], d_queries[1]) * (1.0 / math.sqrt(HD))
        dq_ref[0, span] = dq.astype(jnp.bfloat16)
    dk_ref[0] = dk_sum[...].astype(jnp.bfloat16)
    dv_ref[0] = dv_sum[...].astype(jnp.bfloat16)


def attend_grad(probs, q, k, v, grad, out, inverse):
    rows, local, width = q.shape
    pairs = width // PAIR
    by_pair = lambda r, j: (r, 0, j)
    small = pl.BlockSpec((1, local, PAIR), by_pair)
    large = pl.BlockSpec((1, local + TILE, PAIR), by_pair)
    return pl.pallas_call(
        attend_grad_kernel,
        grid=(rows, pairs),
        in_specs=[
            pl.BlockSpec((1, 1, 2, 2, 2, TILE, TILE), lambda r, j: (r, j, 0, 0, 0, 0, 0)),
            small,
            large,
            large,
            small,
            small,
            small,
        ],
        out_specs=[small, large, large],
        out_shape=[
            jax.ShapeDtypeStruct(q.shape, jnp.bfloat16),
            jax.ShapeDtypeStruct(k.shape, jnp.bfloat16),
            jax.ShapeDtypeStruct(k.shape, jnp.bfloat16),
        ],
        scratch_shapes=[
            pltpu.VMEM((local + TILE, PAIR), jnp.float32),
            pltpu.VMEM((local + TILE, PAIR), jnp.float32),
        ],
        compiler_params=pltpu.CompilerParams(vmem_limit_bytes=VMEM_LIMIT),
    )(probs, q, k, v, grad, out, inverse)


def gelu_pair(v):
    square = v * v
    half = 0.5 + 0.5 * jnp.tanh(v * (GELU_SCALE + (GELU_SCALE * 0.044715) * square))
    hidden = v * half
    slope = half + hidden * (1.0 - half) * (2.0 * GELU_SCALE + (6.0 * GELU_SCALE * 0.044715) * square)
    return hidden, slope


MLP_TILE = 256
CHUNK = 768


def mlp_kernel(
    x_hbm, att_hbm, dy_hbm, attn_hbm, fc_hbm, proj_hbm, vectors,
    out_hbm, middle_grad_hbm, att_grad_hbm, attn_grad_hbm, fc_grad_hbm, proj_grad_hbm, sums_ref,
    x, att, dy, attn, fc, proj, hidden, pre_grad, normed, branch, out, middle_grad, att_grad,
    attn_grad, fc_grad, proj_grad, in_sem, out_sem,
):
    tokens, width = x.shape
    chunks = fc.shape[1] // CHUNK
    tiles = tokens // MLP_TILE
    loads = [
        pltpu.make_async_copy(src, dst, in_sem.at[i])
        for i, (src, dst) in enumerate(
            ((att_hbm, att), (attn_hbm, attn), (x_hbm, x), (fc_hbm, fc), (dy_hbm, dy), (proj_hbm, proj))
        )
    ]
    for load in loads:
        load.start()
    sums_ref[...] = jnp.zeros_like(sums_ref)
    for load in loads[:3]:
        load.wait()

    def tile_step(t, carry):
        span = pl.ds(pl.multiple_of(t * MLP_TILE, MLP_TILE), MLP_TILE)
        middle = x[span].astype(jnp.float32) + dot_nn(att[span], attn[...]) + vectors[4:5]
        normal, scale = normalize(middle)
        low = (normal * vectors[5:6] + vectors[6:7]).astype(jnp.bfloat16)
        normed[span] = low

        @pl.when(t == 0)
        def _():
            for load in loads[3:]:
                load.wait()

        upstream = dy[span]
        result = middle + vectors[7:8]
        back = None
        for j in range(chunks):
            columns = pl.ds(j * CHUNK, CHUNK)
            pre = dot_nn(low, fc[:, columns]) + vectors[8 + j : 9 + j]
            value, slope = gelu_pair(pre)
            value = value.astype(jnp.bfloat16)
            hidden[span, columns] = value
            grad = dot_nt(upstream, proj[columns]) * slope
            grad = grad.astype(jnp.bfloat16)
            pre_grad[span, columns] = grad
            sums_ref[4 + j : 5 + j] += column_sum(grad.astype(jnp.float32))
            result = result + dot_nn(value, proj[columns])
            part = dot_nt(grad, fc[:, columns])
            back = part if back is None else back + part
        out[span] = result.astype(jnp.bfloat16)
        upstream = upstream.astype(jnp.float32)
        sums_ref[0:1] += column_sum(upstream)
        sums_ref[1:2] += column_sum(back * normal)
        sums_ref[2:3] += column_sum(back)
        total = upstream + norm_grad(back, vectors[5:6], normal, scale)
        middle_grad[span] = total
        total = total.astype(jnp.bfloat16)
        branch[span] = total
        sums_ref[3:4] += column_sum(total.astype(jnp.float32))
        att_grad[span] = dot_nt(total, attn[...]).astype(jnp.bfloat16)
        return carry

    lax.fori_loop(0, tiles, tile_step, 0)
    stores = []

    def store(src, dst):
        copy = pltpu.make_async_copy(src, dst, out_sem.at[len(stores)])
        copy.start()
        stores.append(copy)

    store(out, out_hbm)
    store(middle_grad, middle_grad_hbm)
    store(att_grad, att_grad_hbm)
    for j in range(chunks):
        columns = pl.ds(j * CHUNK, CHUNK)
        proj_grad[columns] = dot_tn(hidden[:, columns], dy[...]).astype(jnp.bfloat16)
        store(proj_grad.at[columns], proj_grad_hbm.at[columns])
    for j in range(chunks):
        columns = pl.ds(j * CHUNK, CHUNK)
        fc_grad[:, columns] = dot_tn(normed[...], pre_grad[:, columns]).astype(jnp.bfloat16)
        store(fc_grad.at[:, columns], fc_grad_hbm.at[:, columns])
    attn_grad[...] = dot_tn(att[...], branch[...]).astype(jnp.bfloat16)
    store(attn_grad, attn_grad_hbm)
    for copy in stores:
        copy.wait()


def mlp(x, att, dy, attn, fc, proj, vectors):
    tokens, width = x.shape
    hidden = fc.shape[1]
    low, full = jnp.bfloat16, jnp.float32
    anywhere = pl.BlockSpec(memory_space=pl.ANY)
    vmem = pl.BlockSpec(memory_space=pltpu.VMEM)
    return pl.pallas_call(
        mlp_kernel,
        in_specs=[anywhere] * 6 + [vmem],
        out_specs=[anywhere] * 6 + [vmem],
        out_shape=[
            jax.ShapeDtypeStruct((tokens, width), low),
            jax.ShapeDtypeStruct((tokens, width), full),
            jax.ShapeDtypeStruct((tokens, width), low),
            jax.ShapeDtypeStruct(attn.shape, low),
            jax.ShapeDtypeStruct(fc.shape, low),
            jax.ShapeDtypeStruct(proj.shape, low),
            jax.ShapeDtypeStruct((8, width), full),
        ],
        scratch_shapes=[
            pltpu.VMEM((tokens, width), low),
            pltpu.VMEM((tokens, width), low),
            pltpu.VMEM((tokens, width), low),
            pltpu.VMEM(attn.shape, low),
            pltpu.VMEM(fc.shape, low),
            pltpu.VMEM(proj.shape, low),
            pltpu.VMEM((tokens, hidden), low),
            pltpu.VMEM((tokens, hidden), low),
            pltpu.VMEM((tokens, width), low),
            pltpu.VMEM((tokens, width), low),
            pltpu.VMEM((tokens, width), low),
            pltpu.VMEM((tokens, width), full),
            pltpu.VMEM((tokens, width), low),
            pltpu.VMEM(attn.shape, low),
            pltpu.VMEM(fc.shape, low),
            pltpu.VMEM(proj.shape, low),
            pltpu.SemaphoreType.DMA((6,)),
            pltpu.SemaphoreType.DMA((12,)),
        ],
        compiler_params=pltpu.CompilerParams(vmem_limit_bytes=VMEM_LIMIT),
    )(x, att, dy, attn, fc, proj, vectors)


def project_grad_kernel(normed, dq, dk, dv, weight, weight_grad, prev_grad, sums):
    rows, extended, width = normed.shape
    local = dq.shape[1]
    third = [pl.ds(i * width, width) for i in range(3)]
    for r in range(rows):
        head = pl.ds(0, TILE)
        prev_grad[r] = (
            dot_nt(dk[r, head], weight[:, third[1]]) + dot_nt(dv[r, head], weight[:, third[2]])
        ).astype(jnp.bfloat16)
    total = None
    for i, grads in enumerate((dq, dk, dv)):
        total = None
        for r in range(rows):
            left = normed[r, TILE:] if i == 0 else normed[r]
            part = dot_tn(left, grads[r])
            total = part if total is None else total + part
        weight_grad[:, third[i]] = total.astype(jnp.bfloat16)
    sums[...] = jnp.zeros_like(sums)
    for r in range(rows):
        sums[0:1] += column_sum(dq[r].astype(jnp.float32))
        sums[1:2] += column_sum(dv[r].astype(jnp.float32))


def project_grad(normed, dq, dk, dv, weight):
    rows, extended, width = normed.shape
    vmem = pl.BlockSpec(memory_space=pltpu.VMEM)
    return pl.pallas_call(
        project_grad_kernel,
        in_specs=[vmem] * 5,
        out_specs=[vmem] * 3,
        out_shape=[
            jax.ShapeDtypeStruct(weight.shape, jnp.bfloat16),
            jax.ShapeDtypeStruct((rows, TILE, width), jnp.bfloat16),
            jax.ShapeDtypeStruct((8, width), jnp.float32),
        ],
        compiler_params=pltpu.CompilerParams(vmem_limit_bytes=VMEM_LIMIT),
    )(normed, dq, dk, dv, weight)


def tokens_grad_kernel(x_ref, dq, dk, dv, weight, late, middle_grad, vectors, out_ref, sums):
    row, tile = pl.program_id(0), pl.program_id(1)
    width = x_ref.shape[-1]

    @pl.when((row == 0) & (tile == 0))
    def _():
        sums[...] = jnp.zeros_like(sums)

    back = dot_nt(dq[0], weight[:, :width])
    back = back + dot_nt(dk[0], weight[:, width : 2 * width])
    back = back + dot_nt(dv[0], weight[:, 2 * width :])
    back = back + jnp.where(tile == pl.num_programs(1) - 1, late[0].astype(jnp.float32), 0.0)
    normal, scale = normalize(x_ref[0].astype(jnp.float32))
    sums[0:1] += column_sum(back * normal)
    sums[1:2] += column_sum(back)
    out_ref[0] = middle_grad[0] + norm_grad(back, vectors[0:1], normal, scale)


def tokens_grad_of(x, dq, dk, dv, weight, late, middle_grad, vectors):
    rows, local, width = x.shape
    block = lambda shift: pl.BlockSpec((1, TILE, width), lambda r, t: (r, t + shift, 0))
    whole = lambda v: pl.BlockSpec(v.shape, lambda r, t: (0, 0))
    return pl.pallas_call(
        tokens_grad_kernel,
        grid=(rows, local // TILE),
        in_specs=[
            block(0),
            block(0),
            block(1),
            block(1),
            whole(weight),
            pl.BlockSpec((1, TILE, width), lambda r, t: (r, 0, 0)),
            block(0),
            whole(vectors),
        ],
        out_specs=[block(0), pl.BlockSpec((8, width), lambda r, t: (0, 0))],
        out_shape=[
            jax.ShapeDtypeStruct(x.shape, jnp.float32),
            jax.ShapeDtypeStruct((8, width), jnp.float32),
        ],
        compiler_params=pltpu.CompilerParams(vmem_limit_bytes=VMEM_LIMIT),
    )(x, dq, dk, dv, weight, late, middle_grad, vectors)


def spread_vectors(slots, size, fc_size, width):
    outer = slots.shape[0]
    zeros = jnp.zeros((8, width - PAIR), jnp.float32)
    first, second = None, None
    for d in range(outer * 8):
        index = (d // 8, (d // 4) % 2, (d // 2) % 2, d % 2)
        top = jnp.concatenate([slots[index + (slice(0, 8),)], zeros], axis=1)
        low = jnp.concatenate([slots[index + (slice(8, 16),)], zeros], axis=1)
        top = pltpu.roll(top, d * size, 1) if d else top
        row, lane = divmod(d * fc_size, width)
        low = pltpu.roll(low, lane, 1) if lane else low
        low = pltpu.roll(low, row, 0) if row else low
        first = top if first is None else first + top
        second = low if second is None else second + low
    return first, second


def join_rows(target, slots, columns):
    outer, rows = slots.shape[0], slots.shape[-2]

    def body(a, carry):
        for y in range(2):
            for c in range(2):
                both = [slots[a, y, c, s, :, columns].astype(jnp.float32) for s in range(2)]
                start = pl.multiple_of(((a * 2 + y) * 2 + c) * (2 * rows), 2 * rows)
                joined = jnp.concatenate(both, axis=0).astype(target.dtype)
                target[pl.ds(start, 2 * rows), columns] = joined
        return carry

    lax.fori_loop(0, outer, body, 0)


VECTORS = 9


FORWARD_ORDERS = (0, 1, 1, 1, 1, 1, 1, 1, 1, 0, 0, 1, 0, 1, 0)
PREV_AFTER, EAGER = (2, 4), 12
FORWARD_PLAN = {'ln': [(1, 0), (1, 1), (1, 2), (2, 0), (1, 3), (2, 1), (1, 4), (2, 2), (1, 5), (3, 0), (1, 6), (2, 3), (2, 4), (4, 0)], 'q': [(3, 1), (2, 5), (2, 6), (1, 7), (3, 2), (1, 8), (4, 1), (4, 2)], 'k': [(3, 3), (1, 9), (3, 4), (1, 10), (4, 3), (4, 4)], 'v': [(3, 5), (1, 11), (3, 6), (1, 12), (4, 5), (2, 9), (4, 6)], 'b0': [(2, 7), (2, 10)], 'b1': [(1, 13)], 'b2': [(2, 8), (2, 12)], 'b3': [(2, 11)], 'b4': [(1, 14)], 'a0': [(3, 7), (3, 9)], 'a3': [(4, 7), (3, 8)], 'a4': [(4, 9), (3, 10)], 'asm': [(4, 8)], 'm0': [(4, 10), (2, 13)], 'm1': [(3, 11)], 'm3': [(2, 14), (4, 11)], 'm5': [(3, 12)], 'w0': [(4, 12), (3, 13)], 'w2': [(3, 14)], 'w3': [(4, 13)], 'end': [(4, 14)]}


def forward_kernel(outer, pieces, *refs):
    tokens_hbm, dy_hbm, starts_ref = refs[:3]
    vector_refs = refs[3 : 3 + VECTORS]
    shards = refs[3 + VECTORS : 7 + VECTORS]
    (
        normed_hbm, q_hbm, k_hbm, v_hbm, probs_hbm, att_hbm, hidden_hbm, slope_hbm, middle_hbm,
        normed2_hbm, qkv_hbm, attn_hbm, fc_hbm, proj_slots, terms_hbm, vectors,
    ) = refs[7 + VECTORS : 23 + VECTORS]
    (
        own, vector_slots, qkv_slots, attn_slots, fc_slots, qkv, attn, fc, x, normed, q, k, v, probs, att,
        hidden, slope, middle, normed2, dy, terms, q_cols, k_cols,
        move_sem, out_sem, probs_sem, terms_sem, own_sem, send_sem, recv_sem,
    ) = refs[23 + VECTORS :]
    rows, local, width = q.shape
    a, y, c, s = place()
    size, fc_size = vector_refs[0].shape[1], vector_refs[-1].shape[1]
    pairs, chunks = width // PAIR, fc.shape[1] // CHUNK

    load = pltpu.make_async_copy(tokens_hbm, x.at[:, pl.ds(TILE, local)], move_sem.at[0])
    load_dy = pltpu.make_async_copy(dy_hbm, dy, move_sem.at[3])
    load.start()
    own[...] = jnp.zeros_like(own)
    for i, ref in enumerate(vector_refs):
        own[i : i + 1, : ref.shape[1]] = ref[...].astype(jnp.float32)
    greet(outer)
    prev = remote(
        tokens_hbm.at[:, pl.ds(local - TILE, TILE)],
        x.at[:, pl.ds(0, TILE)],
        move_sem.at[1],
        move_sem.at[2],
        device(a, y, c, 1 - s),
    )
    work = Gather(
        outer,
        pieces,
        (own,) + shards,
        (vector_slots, qkv_slots, attn_slots, fc_slots, proj_slots),
        own_sem,
        send_sem,
        recv_sem,
        EAGER,
    )
    work.start()
    load_dy.start()

    def start_prev():
        @pl.when(s == 0)
        def _():
            prev.start()

    work.after = {PREV_AFTER: start_prev}
    comm, comm_at = sites_of(work, FORWARD_PLAN)
    stores = []

    def store(src, dst):
        copy = pltpu.make_async_copy(src, dst, out_sem.at[len(stores)])
        copy.start()
        stores.append(copy)

    def starts_of(r, i):
        tile = 2 * s - 1 + i
        start = starts_ref[r, jnp.maximum(tile, 0)]
        return jnp.where(tile < 0, TILE, start - tile * TILE)

    @pl.when(s == 0)
    def _():
        for r in range(rows):
            x[r, 0:TILE] = jnp.zeros((TILE, width), x.dtype)

    for r in range(rows):
        mask_columns(starts_of, r, q_cols.at[r], k_cols.at[r])
    load.wait()
    comm("ln")
    first, second = spread_vectors(vector_slots, size, fc_size, width)
    vectors[0:8], vectors[8:16] = first, second

    def norm_tile(r, span):
        normal, _ = normalize(x[r, span].astype(jnp.float32))
        normed[r, span] = (normal * vectors[0:1] + vectors[1:2]).astype(jnp.bfloat16)

    def norm_step(n, carry):
        r, t = n // (local // TILE), lax.rem(n, local // TILE) + 1
        norm_tile(r, pl.ds(pl.multiple_of(t * TILE, TILE), TILE))
        return carry

    lax.fori_loop(0, rows * (local // TILE), norm_step, 0)
    third = [slice(i * width, (i + 1) * width) for i in range(3)]
    for i, site in enumerate(("q", "k", "v")):
        comm(site)
        join_rows(qkv, qkv_slots, third[i])

        def row_step(r, carry):
            value = dot_nn(normed[r, TILE:], qkv[:, third[i]])
            if i == 0:
                value = (value + vectors[2:3]).astype(jnp.bfloat16)
                q[r] = value * jnp.bfloat16(1.0 / math.sqrt(HD))
            elif i == 1:
                k[r, TILE:] = value.astype(jnp.bfloat16)
            else:
                v[r, TILE:] = (value + vectors[3:4]).astype(jnp.bfloat16)
            return carry

        lax.fori_loop(0, rows, row_step, 0)
    store(q, q_hbm)
    store(qkv, qkv_hbm)
    lane = lane_index(TILE)
    causal = lax.broadcasted_iota(jnp.int32, (TILE, 2 * TILE), 0) <= (
        lax.broadcasted_iota(jnp.int32, (TILE, 2 * TILE), 1) & (TILE - 1)
    )

    def probs_copy(slot, r, j, tile):
        part = probs_hbm.at[r, j, :, pl.ds(tile * 4 * TILE, 4 * TILE)]
        return pltpu.make_async_copy(probs.at[slot], part, probs_sem.at[slot])

    def attend_pair(r, j, tile, slot):
        pair = pl.ds(pl.multiple_of(j * PAIR, PAIR), PAIR)
        queries = q[r, tile * TILE : (tile + 1) * TILE, pair]
        left = []
        for head in range(2):
            mine = (lane < HD) if head == 0 else (lane >= HD)
            mine = jnp.where(mine, queries, jnp.bfloat16(0))
            left.append(jnp.concatenate([mine, q_cols[r, tile]], axis=1))
        left = jnp.concatenate(left, axis=0)
        scores = []
        for w in range(2):
            keys = k[r, (tile + w) * TILE : (tile + w + 1) * TILE, pair]
            scores.append(dot_nt(jnp.concatenate([keys, k_cols[r, tile, w]], axis=1), left))
        far, near = scores[0], jnp.where(causal, scores[1], -FIRM)
        top = jnp.max(jnp.maximum(far, near), axis=0, keepdims=True)
        far, near = jnp.exp(far - top), jnp.exp(near - top)
        share = 1.0 / jnp.sum(far + near, axis=0, keepdims=True)
        far, near = (far * share).astype(jnp.bfloat16), (near * share).astype(jnp.bfloat16)
        probs[slot, :, 0 : 2 * TILE], probs[slot, :, 2 * TILE :] = far, near
        values = v[r, tile * TILE : (tile + 2) * TILE, pair]
        mixed = []
        for head in range(2):
            part = slice(head * TILE, (head + 1) * TILE)
            mixed.append(dot_tn(jnp.concatenate([far[:, part], near[:, part]], axis=0), values))
        span = pl.ds(pl.multiple_of(r * local + tile * TILE, TILE), TILE)
        att[span, pair] = jnp.where(lane < HD, mixed[0], mixed[1]).astype(jnp.bfloat16)

    def attend_step(n, tile, index):
        r, j = n // (pairs // 2), lax.rem(n, pairs // 2) * 2
        slot = lax.rem(n, 2) * 2

        @pl.when(n + index * rows * pairs // 2 >= 2)
        def _():
            for i in range(2):
                probs_copy(slot + i, r, j + i, tile).wait()

        for i in range(2):
            attend_pair(r, j + i, tile, slot + i)
        for i in range(2):
            probs_copy(slot + i, r, j + i, tile).start()

    def late_step(n, carry):
        comm_at(n, "b", rows * pairs // 2)
        attend_step(n, 1, 0)
        return carry

    lax.fori_loop(0, rows * pairs // 2, late_step, 0)
    comm("prev")

    @pl.when(s == 1)
    def _():
        prev.wait_recv()

    for r in range(rows):
        norm_tile(r, slice(0, TILE))
        k[r, 0:TILE] = dot_nn(normed[r, 0:TILE], qkv[:, third[1]]).astype(jnp.bfloat16)
        value = dot_nn(normed[r, 0:TILE], qkv[:, third[2]]) + vectors[3:4]
        v[r, 0:TILE] = value.astype(jnp.bfloat16)
    store(normed, normed_hbm)
    store(k, k_hbm)
    store(v, v_hbm)

    def early_step(n, carry):
        comm_at(n, "a", rows * pairs // 2)
        attend_step(n, 0, 1)
        return carry

    lax.fori_loop(0, rows * pairs // 2, early_step, 0)
    store(att, att_hbm)
    comm("asm")
    join_rows(attn, attn_slots, slice(0, width))
    store(attn, attn_hbm)

    def mlp_step(n, carry):
        r, j = n // chunks, lax.rem(n, chunks)
        span = pl.ds(pl.multiple_of(r * local, TILE), local)
        units = pl.ds(pl.multiple_of(j * CHUNK, CHUNK), CHUNK)

        @pl.when(j == 0)
        def _():
            value = x[r, TILE:].astype(jnp.float32) + dot_nn(att[span], attn[...]) + vectors[4:5]
            middle[span] = value
            normal, _ = normalize(value)
            normed2[span] = (normal * vectors[5:6] + vectors[6:7]).astype(jnp.bfloat16)

        comm_at(n, "m", rows * chunks)

        @pl.when(r == 0)
        def _():
            join_rows(fc, fc_slots, units)

        bias = vectors[8:9]
        for i in range(1, chunks):
            bias = jnp.where(j == i, vectors[8 + i : 9 + i], bias)
        value, back = gelu_pair(dot_nn(normed2[span], fc[:, units]) + bias)
        hidden[span, units] = value.astype(jnp.bfloat16)
        slope[span, units] = back.astype(jnp.bfloat16)
        return carry

    lax.fori_loop(0, rows * chunks, mlp_step, 0)
    store(slope, slope_hbm)
    store(hidden, hidden_hbm)
    store(middle, middle_hbm)
    store(normed2, normed2_hbm)
    store(fc, fc_hbm)
    load_dy.wait()
    share = terms.shape[-2]
    each = CHUNK // (8 * share)

    def terms_copy(j):
        slot = lax.rem(j, 2)
        return pltpu.make_async_copy(
            terms.at[slot], terms_hbm.at[pl.ds(j * each, each)], terms_sem.at[slot]
        )

    def weight_step(j, carry):
        comm_at(j, "w", chunks)
        units = pl.ds(pl.multiple_of(j * CHUNK, CHUNK), CHUNK)
        grad = dot_tn(hidden[:, units], dy[...]).astype(jnp.bfloat16)

        @pl.when(j >= 2)
        def _():
            terms_copy(j - 2).wait()

        terms[lax.rem(j, 2)] = grad.reshape((each, 2, 2, 2, share, width))
        terms_copy(j).start()
        return carry

    lax.fori_loop(0, chunks, weight_step, 0)
    comm("end")
    work.end()
    for j in range(chunks - 2, chunks):
        terms_copy(j).wait()
    for n in range(4):
        probs_copy(n, 0, n, 0).wait()
    for copy in stores:
        copy.wait()

    @pl.when(s == 0)
    def _():
        prev.wait_send()


def forward(outer, tokens, dy, starts, vectors, weights):
    rows, local, width = tokens.shape
    devices = outer * 8
    low, full = jnp.bfloat16, jnp.float32
    pairs = width // PAIR
    qkv_weight, attn_weight, fc_weight, proj_weight = weights
    hidden = fc_weight.shape[1]
    half = width // 2
    pieces = [(0, 0, PAIR)] + [(1, i * half, half) for i in range(6)] + [(2, 0, width)]
    pieces += [(3, j * CHUNK, CHUNK) for j in range(hidden // CHUNK)]
    pieces += [(4, j * 2 * PAIR, 2 * PAIR) for j in range(width // (2 * PAIR))]
    pieces = [piece + (order,) for piece, order in zip(pieces, FORWARD_ORDERS)]
    anywhere = pl.BlockSpec(memory_space=pl.ANY)
    vmem = pl.BlockSpec(memory_space=pltpu.VMEM)
    extended = (rows, local + TILE, width)
    flat = (rows * local, width)
    whole = [(devices * weight.shape[0], weight.shape[1]) for weight in weights]
    slots = [(outer, 2, 2, 2) + weight.shape for weight in weights]
    shape = jax.ShapeDtypeStruct
    results = pl.pallas_call(
        functools.partial(forward_kernel, outer, pieces),
        in_specs=[anywhere] * 2 + [pl.BlockSpec(memory_space=pltpu.SMEM)] + [vmem] * (VECTORS + 4),
        out_specs=[anywhere] * 15 + [vmem],
        out_shape=[
            shape(extended, low),
            shape(tokens.shape, low),
            shape(extended, low),
            shape(extended, low),
            shape((rows, pairs, TILE, 8 * TILE), low),
            shape(flat, low),
            shape((rows * local, hidden), low),
            shape((rows * local, hidden), low),
            shape(flat, full),
            shape(flat, low),
            shape(whole[0], low),
            shape(whole[1], low),
            shape(whole[2], low),
            shape(slots[3], low),
            shape(slots[3], low),
            shape((16, width), full),
        ],
        scratch_shapes=[
            pltpu.VMEM((16, PAIR), full),
            pltpu.VMEM((outer, 2, 2, 2, 16, PAIR), full),
            pltpu.VMEM(slots[0], low),
            pltpu.VMEM(slots[1], low),
            pltpu.VMEM(slots[2], low),
            pltpu.VMEM(whole[0], low),
            pltpu.VMEM(whole[1], low),
            pltpu.VMEM(whole[2], low),
            pltpu.VMEM(extended, low),
            pltpu.VMEM(extended, low),
            pltpu.VMEM(tokens.shape, low),
            pltpu.VMEM(extended, low),
            pltpu.VMEM(extended, low),
            pltpu.VMEM((4, TILE, 4 * TILE), low),
            pltpu.VMEM(flat, low),
            pltpu.VMEM((rows * local, hidden), low),
            pltpu.VMEM((rows * local, hidden), low),
            pltpu.VMEM(flat, full),
            pltpu.VMEM(flat, low),
            pltpu.VMEM(flat, low),
            pltpu.VMEM((2, CHUNK // (8 * proj_weight.shape[0])) + slots[3][1:], low),
            pltpu.VMEM((rows, 2, TILE, PAIR), low),
            pltpu.VMEM((rows, 2, 2, TILE, PAIR), low),
            pltpu.SemaphoreType.DMA((4,)),
            pltpu.SemaphoreType.DMA((12,)),
            pltpu.SemaphoreType.DMA((4,)),
            pltpu.SemaphoreType.DMA((2,)),
        ]
        + Gather.semaphores(outer, 5, len(pieces)),
        compiler_params=pltpu.CompilerParams(
            collective_id=2, has_side_effects=True, vmem_limit_bytes=VMEM_LIMIT
        ),
    )(tokens, dy, starts, *[vector.reshape(1, -1) for vector in vectors], *weights)
    return results


def shares_out(rows, columns):
    return jax.ShapeDtypeStruct((rows, columns), jnp.float32)


def column_pieces(array, columns, parts, orders):
    step = columns // parts
    return [(array, j * step, step, orders[j % len(orders)]) for j in range(parts)]


def pack_columns(values, start, lanes):
    width = values.shape[1]
    moved = pltpu.roll(values, (width - start) % width, 1) if start % width else values
    return jnp.where(lane_index(values.shape[0]) < lanes, moved[:, :PAIR], 0.0)


def mlp_backward(refs, fc_terms, attn_terms, vectors, att, att_grad, middle, sums, work, comm, comm_at):
    slope_hbm, normed_hbm, dy_hbm, attn_hbm, fc_hbm, proj_hbm, load_middle, load_att = refs

    def body(dy, slope, normed, attn, fc, proj, branch, stage, proj_sem, slope_sem, fc_sem, in_sem, stage_sem):
        tokens, width = dy.shape
        chunks = fc.shape[1] // CHUNK
        block = tokens // 2
        spans = [pl.ds(j * CHUNK, CHUNK) for j in range(chunks)]
        share = fc_terms.shape[-2]

        copies = lambda src, dst, sem: [
            pltpu.make_async_copy(src.at[:, span], dst.at[:, span], sem.at[j])
            for j, span in enumerate(spans)
        ]
        load_proj = [
            pltpu.make_async_copy(proj_hbm.at[span], proj.at[span], proj_sem.at[j])
            for j, span in enumerate(spans)
        ]
        load_slope, load_fc = copies(slope_hbm, slope, slope_sem), copies(fc_hbm, fc, fc_sem)
        others = ((dy_hbm, dy), (normed_hbm, normed), (attn_hbm, attn))
        load_dy, load_normed, load_attn = [
            pltpu.make_async_copy(src, dst, in_sem.at[i]) for i, (src, dst) in enumerate(others)
        ]
        load_dy.start()
        for j in range(chunks):
            load_proj[j].start()
            load_slope[j].start()
        load_normed.start()
        for j in range(chunks):
            load_fc[j].start()
        for load in (load_middle, load_attn, load_att):
            load.start()
        comm("start")
        load_dy.wait()

        def grad_step(j, carry):
            units = pl.ds(pl.multiple_of(j * CHUNK, CHUNK), CHUNK)
            for i in range(chunks):

                @pl.when(j == i)
                def _():
                    load_proj[i].wait()
                    load_slope[i].wait()

            comm_at(j, "m", chunks)
            grad = dot_nt(dy[...], proj[units]) * slope[:, units].astype(jnp.float32)
            grad = grad.astype(jnp.bfloat16)
            slope[:, units] = grad
            total = column_sum(grad.astype(jnp.float32))
            for i in range(chunks):
                sums[12 + i : 13 + i] += jnp.where(j == i, total, 0.0)
            return carry

        lax.fori_loop(0, chunks, grad_step, 0)
        for i in range(chunks, 2 * chunks):
            comm(f"m{i}")
        load_normed.wait()
        waited = set()

        def stage_copy(n):
            to = fc_terms.at[:, :, :, :, :, spans[n]] if n < chunks else attn_terms
            return pltpu.make_async_copy(stage.at[n % 2], to, stage_sem.at[n])

        def settle(n):
            if n not in waited:
                waited.add(n)
                stage_copy(n).wait()

        def put(n, grad):
            if n >= 2:
                settle(n - 2)
            stage[n % 2] = grad.astype(jnp.bfloat16).reshape(stage.shape[1:])
            stage_copy(n).start()

        for p, piece in enumerate(work.pieces):
            if piece[0] in (1, 2):
                work.before[p] = functools.partial(settle, piece[1] // CHUNK if piece[0] == 1 else chunks)
        for j in range(chunks):
            comm(f"w{j}")
            put(j, dot_tn(normed[...], slope[:, spans[j]]))

        def back_step(t, carry):
            span = pl.ds(pl.multiple_of(t * block, block), block)
            back = None
            for j in range(chunks):

                @pl.when(t == 0)
                def _():
                    load_fc[j].wait()

                comm_at(t, "o", 2, chunks, j)
                more = dot_nt(slope[span, spans[j]], fc[:, spans[j]])
                back = more if back is None else back + more

            @pl.when(t == 0)
            def _():
                load_middle.wait()
                load_attn.wait()

            upstream = dy[span].astype(jnp.float32)
            value = middle[span]
            normal, scale = normalize(value)
            sums[4:5] += column_sum(upstream)
            sums[5:6] += column_sum(back * normal)
            sums[6:7] += column_sum(back)
            total = upstream + norm_grad(back, vectors[5:6], normal, scale)
            middle[span] = total
            total = total.astype(jnp.bfloat16)
            branch[span] = total
            sums[7:8] += column_sum(total.astype(jnp.float32))
            att_grad[span] = dot_nt(total, attn[...]).astype(jnp.bfloat16)
            return carry

        lax.fori_loop(0, 2, back_step, 0)
        load_att.wait()
        comm("attn")
        put(chunks, dot_tn(att[...], branch[...]))
        comm("rest")
        for n in range(chunks + 1):
            settle(n)

    tokens, width = att.shape
    hidden, chunks = fc_hbm.shape[1], fc_hbm.shape[1] // CHUNK
    low = jnp.bfloat16
    dma = lambda n: pltpu.SemaphoreType.DMA((n,))
    pl.run_scoped(
        body,
        pltpu.VMEM((tokens, width), low),
        pltpu.VMEM((tokens, hidden), low),
        pltpu.VMEM((tokens, width), low),
        pltpu.VMEM(attn_hbm.shape, low),
        pltpu.VMEM(fc_hbm.shape, low),
        pltpu.VMEM(proj_hbm.shape, low),
        pltpu.VMEM((tokens, width), low),
        pltpu.VMEM((2,) + attn_terms.shape, low),
        dma(chunks),
        dma(chunks),
        dma(chunks),
        dma(3),
        dma(chunks + 1),
    )


def backward_kernel(outer, pieces, places, *refs):
    (
        hidden_hbm, slope_hbm, middle_hbm, normed2_hbm, att_hbm, dy_hbm, attn_hbm, fc_hbm, proj_hbm, proj_terms,
        probs_hbm, q_hbm, k_hbm, v_hbm, normed_hbm, x_hbm, weight_hbm, vectors,
        out_hbm, tokens_grad_hbm, fc_terms, attn_terms, proj_share, fc_share, attn_share, qkv_share, vector_share,
        flat_att, flat_grad, flat_middle, prev, late, vector_terms, vector_got, sums,
        main_sem, late_sem, vector_send, vector_recv, *rest,
    ) = refs
    rows, local, width = q_hbm.shape
    pairs = width // PAIR
    a, y, c, s = place()
    load_middle = pltpu.make_async_copy(middle_hbm, flat_middle, main_sem.at[0])
    load_att = pltpu.make_async_copy(att_hbm, flat_att, main_sem.at[1])
    sums[...] = jnp.zeros_like(sums)
    greet_all(outer)
    work = Scatter(
        outer, pieces, [proj_terms, fc_terms, attn_terms, None],
        [proj_share, fc_share, attn_share, qkv_share], rest[:-3], *rest[-3:], places,
    )
    comm, comm_at = sites_of(work, BACKWARD_PLAN)
    mlp_refs = (
        slope_hbm, normed2_hbm, dy_hbm, attn_hbm, fc_hbm, proj_hbm, load_middle, load_att,
    )
    mlp_backward(
        mlp_refs, fc_terms, attn_terms, vectors, flat_att, flat_grad, flat_middle, sums,
        work, comm, comm_at,
    )
    low, full = jnp.bfloat16, jnp.float32
    extended = (rows, local + TILE, width)
    dma = lambda *n: pltpu.SemaphoreType.DMA(n)
    pl.run_scoped(
        functools.partial(
            attend_backward, outer, work, comm, comm_at,
            (probs_hbm, q_hbm, k_hbm, v_hbm, normed_hbm, x_hbm, weight_hbm, hidden_hbm, proj_hbm, middle_hbm),
            vectors, tokens_grad_hbm, out_hbm,
            vector_share, flat_att, flat_grad, flat_middle, prev, late, vector_terms, vector_got, sums,
            late_sem, vector_send, vector_recv,
        ),
        pltpu.VMEM(q_hbm.shape, low),
        pltpu.VMEM(extended, low),
        pltpu.VMEM(extended, low),
        pltpu.VMEM(extended, low),
        pltpu.VMEM(weight_hbm.shape, low),
        pltpu.VMEM((6, TILE, 2 * TILE), low),
        pltpu.VMEM((4, TILE, 6 * TILE), low),
        pltpu.VMEM(q_hbm.shape, low),
        pltpu.VMEM(extended, low),
        pltpu.VMEM(extended, low),
        pltpu.VMEM((rows, TILE, width), full),
        pltpu.VMEM((outer, 2, 2, 2, weight_hbm.shape[0] // (outer * 8), weight_hbm.shape[1]), low),
        dma(3, rows),
        dma(3),
        dma(6),
        dma(4),
        dma(rows * local // TILE),
        dma(4),
        dma(2, 4),
        dma(2),
        dma(2),
    )


def attend_backward(
    outer, work, comm, comm_at, arrays, vectors, tokens_grad_hbm, out_hbm, vector_share, att, grad, middle,
    prev, late, vector_terms, vector_got, sums, late_sem, vector_send, vector_recv,
    q, k, v, normed, weight, far_probs, near_probs, dq, dk, dv, dq_part, qkv_terms,
    in_sem, after_sem, far_sem, near_sem, out_sem, proj_sem, hidden_sem, middle_sem, result_sem,
):
    probs_hbm, q_hbm, k_hbm, v_hbm, normed_hbm, x_hbm, weight_hbm, hidden_hbm, proj_hbm, middle_hbm = arrays
    rows, local, width = q.shape
    pairs = width // PAIR
    a, y, c, s = place()
    work.terms[3] = qkv_terms
    loads = [
        [pltpu.make_async_copy(src.at[r], dst.at[r], in_sem.at[i, r]) for r in range(rows)]
        for i, (src, dst) in enumerate(((q_hbm, q), (k_hbm, k), (v_hbm, v)))
    ]
    load_weight = pltpu.make_async_copy(weight_hbm, weight, after_sem.at[0])
    load_normed = pltpu.make_async_copy(normed_hbm, normed, after_sem.at[1])
    load_x = pltpu.make_async_copy(x_hbm, q, after_sem.at[2])
    wide = 2 * TILE

    def far_copy(n):
        part = probs_hbm.at[n // pairs, lax.rem(n, pairs), :, pl.ds(0, wide)]
        slot = lax.rem(n, 6)
        return pltpu.make_async_copy(part, far_probs.at[slot], far_sem.at[slot])

    def near_copy(n):
        slot = lax.rem(n, 4)
        part = probs_hbm.at[lax.rem(n, rows), n // rows, :, pl.ds(wide, 3 * wide)]
        return pltpu.make_async_copy(part, near_probs.at[slot], near_sem.at[slot])

    for r in range(rows):
        for load in loads:
            load[r].start()
        if r == 0:
            for n in range(6):
                far_copy(n).start()
    load_weight.start()
    load_normed.start()
    for n in range(4):
        near_copy(n).start()
    lane = lane_index(TILE)
    ones = jnp.ones((TILE, PAIR), jnp.bfloat16)

    def sides(r, pair, tile):
        span = pl.ds(pl.multiple_of(r * local + tile * TILE, TILE), TILE)
        grads, queries = grad[span, pair], q[r, tile * TILE : (tile + 1) * TILE, pair]
        product = grads.astype(jnp.float32) * att[span, pair].astype(jnp.float32)
        left, mine_grads, mine_queries = [], [], []
        for head in range(2):
            mine = (lane < HD) if head == 0 else (lane >= HD)
            delta = -jnp.sum(jnp.where(mine, product, 0.0), axis=-1, keepdims=True)
            high = delta.astype(jnp.bfloat16).astype(jnp.float32)
            extra = jnp.where(lane == 0, high, jnp.where(lane == 1, delta - high, 0.0))
            mine_grads.append(jnp.where(mine, grads, jnp.bfloat16(0)))
            mine_queries.append(jnp.where(mine, queries, jnp.bfloat16(0)))
            left.append(jnp.concatenate([mine_grads[-1], extra.astype(jnp.bfloat16)], axis=1))
        return [jnp.concatenate(part, axis=0) for part in (left, mine_grads, mine_queries)]

    def unit(r, pair, tile, side, chances):
        values = jnp.concatenate([v[r, tile * TILE : (tile + 1) * TILE, pair], ones], axis=1)
        d_score = (chances.astype(jnp.float32) * dot_nt(values, side[0])).astype(jnp.bfloat16)
        span = slice(tile * TILE, (tile + 1) * TILE)
        dk[r, span, pair] = dot_nn(d_score, side[2]).astype(jnp.bfloat16)
        dv[r, span, pair] = dot_nn(chances, side[1]).astype(jnp.bfloat16)
        return d_score

    def heads(parts):
        return jnp.where(lane < HD, parts[0], parts[1])

    far_steps = rows * pairs // 2

    def far_step(n, carry):
        r, j = n // (pairs // 2), lax.rem(n, pairs // 2) * 2
        for row in range(rows):

            @pl.when(n == row * (pairs // 2))
            def _():
                for load in loads:
                    load[row].wait()

        comm_at(n, "f", far_steps)
        for i in range(2):
            far_copy(2 * n + i).wait()
        for i in range(2):
            pair = pl.ds(pl.multiple_of((j + i) * PAIR, PAIR), PAIR)
            d_score = unit(r, pair, 0, sides(r, pair, 0), far_probs[lax.rem(2 * n + i, 6)])
            keys = k[r, 0:TILE, pair]
            dq_part[r, :, pair] = heads(
                [dot_tn(d_score[:, h * TILE : (h + 1) * TILE], keys) for h in range(2)]
            )

        @pl.when(2 * n + 6 < rows * pairs)
        def _():
            for i in range(2):
                far_copy(2 * n + 6 + i).start()

        return carry

    lax.fori_loop(0, far_steps, far_step, 0)
    load_weight.wait()
    comm("mm")
    third = [slice(i * width, (i + 1) * width) for i in range(3)]
    for r in range(rows):
        head = slice(0, TILE)
        prev[r] = (
            dot_nt(dk[r, head], weight[:, third[1]]) + dot_nt(dv[r, head], weight[:, third[2]])
        ).astype(jnp.bfloat16)
    late_copy = remote(prev, late, late_sem.at[0], late_sem.at[1], device(a, y, c, 1 - s))

    @pl.when(s == 1)
    def _():
        late_copy.start()
        late[...] = jnp.zeros_like(late)

    load_normed.wait()
    near_steps = rows * pairs // 2

    def near_pair(r, j, slot):
        pair = pl.ds(pl.multiple_of(j * PAIR, PAIR), PAIR)
        scale = 1.0 / math.sqrt(HD)
        one, two = sides(r, pair, 0), sides(r, pair, 1)
        both = [jnp.concatenate(part, axis=0) for part in zip(one, two)]
        first = unit(r, pair, 1, both, near_probs[slot, :, 0 : 2 * wide])
        second = unit(r, pair, 2, two, near_probs[slot, :, 2 * wide :])
        keys = k[r, TILE : 3 * TILE, pair]
        part = heads([dot_tn(first[:, h * TILE : (h + 1) * TILE], keys[:TILE]) for h in range(2)])
        dq[r, 0:TILE, pair] = ((dq_part[r, :, pair] + part) * scale).astype(jnp.bfloat16)
        crossed = jnp.concatenate([first[:, wide:], second], axis=0)
        part = heads([dot_tn(crossed[:, h * TILE : (h + 1) * TILE], keys) for h in range(2)])
        dq[r, TILE : 2 * TILE, pair] = (part * scale).astype(jnp.bfloat16)

    def near_step(n, carry):
        comm_at(n, "n", near_steps)
        for r in range(rows):
            near_copy(n * rows + r).wait()
        near_pair(0, n, lax.rem(n * rows, 4))
        comm_at(n, "h", near_steps)
        for r in range(1, rows):
            near_pair(r, n, lax.rem(n * rows + r, 4))

        @pl.when(n + 2 < near_steps)
        def _():
            for r in range(rows):
                near_copy((n + 2) * rows + r).start()

        @pl.when(lax.rem(n, 2) == 1)
        def _():
            comm_at(n, "g", near_steps)
            block = pl.ds(pl.multiple_of((n // 2) * (2 * PAIR), 2 * PAIR), 2 * PAIR)
            share = qkv_terms.shape[-2]
            for i, grads in enumerate((dq, dk, dv)):
                total = None
                for row in range(rows):
                    left = normed[row, TILE:] if i == 0 else normed[row]
                    part = dot_tn(left, grads[row, :, block])
                    total = part if total is None else total + part
                to = pl.ds(pl.multiple_of((n // 2) * width + i * 2 * PAIR, 2 * PAIR), 2 * PAIR)
                qkv_terms[:, :, :, :, :, to] = total.astype(jnp.bfloat16).reshape(
                    (outer, 2, 2, 2, share, 2 * PAIR)
                )

        return carry

    lax.fori_loop(0, near_steps, near_step, 0)
    load_x.start()
    chunks = hidden_hbm.shape[1] // CHUNK
    places = [(k, 0), (k, 1), (v, 0), (v, 1)]
    load_proj = [
        pltpu.make_async_copy(
            proj_hbm.at[pl.ds(j * CHUNK, CHUNK)], places[j][0].at[places[j][1]], proj_sem.at[j]
        )
        for j in range(chunks)
    ]

    def tile_of(u):
        return pl.ds(pl.multiple_of(u * TILE, TILE), TILE)

    def hidden_copy(u, j):
        lanes = pl.ds(pl.multiple_of(lax.rem(u, 2) * CHUNK, CHUNK), CHUNK)
        src = hidden_hbm.at[tile_of(u), pl.ds(j * CHUNK, CHUNK)]
        return pltpu.make_async_copy(src, near_probs.at[j, :, lanes], hidden_sem.at[lax.rem(u, 2), j])

    def middle_copy(u):
        slot = lax.rem(u, 2)
        return pltpu.make_async_copy(middle_hbm.at[tile_of(u)], dq_part.at[slot], middle_sem.at[slot])

    def result_copy(u):
        slot = lax.rem(u, 2)
        src = normed.at[slot, pl.ds(0, TILE)]
        return pltpu.make_async_copy(src, out_hbm.at[tile_of(u)], result_sem.at[slot])

    for load in load_proj:
        load.start()
    for u in range(2):
        middle_copy(u).start()
        for j in range(chunks):
            hidden_copy(u, j).start()
    for r in range(rows):
        sums[2:3] += column_sum(dq[r].astype(jnp.float32))
        sums[3:4] += column_sum(dv[r].astype(jnp.float32))
    load_x.wait()
    tiles = local // TILE

    def token_step(r, carry):
        for row in range(rows):

            @pl.when(r == row)
            def _():
                for t in range(tiles):
                    comm(f"t{row * tiles + t}")
                if row == 0:

                    @pl.when(s == 0)
                    def _():
                        late_copy.wait_recv()

        back = dot_nt(dq[r], weight[:, third[0]])
        back = back + dot_nt(dk[r, TILE:], weight[:, third[1]])
        back = back + dot_nt(dv[r, TILE:], weight[:, third[2]])
        last = slice(local - TILE, local)
        back = jnp.concatenate([back[: local - TILE], back[last] + late[r].astype(jnp.float32)], axis=0)
        normal, scale = normalize(q[r].astype(jnp.float32))
        sums[0:1] += column_sum(back * normal)
        sums[1:2] += column_sum(back)
        flat = pl.ds(pl.multiple_of(r * local, local), local)
        middle[flat] = middle[flat] + norm_grad(back, vectors[0:1], normal, scale)
        pltpu.make_async_copy(middle.at[flat], tokens_grad_hbm.at[r], out_sem.at[r]).start()
        return carry

    lax.fori_loop(0, rows, token_step, 0)
    stores = [
        pltpu.make_async_copy(middle.at[pl.ds(r * local, local)], tokens_grad_hbm.at[r], out_sem.at[r])
        for r in range(rows)
    ]
    size = width // (outer * 8)
    fc_size = 4 * size
    total, fc_total = sums[0:8], sums[8:16]
    for d in range(outer * 8):
        row, start = divmod(d * fc_size, width)
        index = (d // 8, (d // 4) % 2, (d // 2) % 2, d % 2)
        vector_terms[index + (slice(0, 8),)] = pack_columns(total, d * size, size)
        vector_terms[index + (slice(8, 16),)] = pack_columns(
            jnp.broadcast_to(fc_total[4 + row : 5 + row], (8, width)), start, fc_size
        )
    vector_copies = [
        remote(
            vector_terms.at[to], vector_got.at[n], vector_send.at[n], vector_recv.at[n], device(*to)
        )
        for n, (to, _) in enumerate(everyone(outer))
    ]
    for copy in vector_copies:
        copy.start()
    for load in load_proj:
        load.wait()
    out_tiles = rows * local // TILE

    def out_step(u, carry):
        comm_at(u, "u", out_tiles)
        slot = lax.rem(u, 2)
        middle_copy(u).wait()
        result = dq_part[slot] + vectors[7:8]
        for j in range(chunks):
            hidden_copy(u, j).wait()
            lanes = pl.ds(pl.multiple_of(slot * CHUNK, CHUNK), CHUNK)
            result = result + dot_nn(near_probs[j, :, lanes], places[j][0][places[j][1]])

        @pl.when(u >= 2)
        def _():
            result_copy(u - 2).wait()

        normed[slot, 0:TILE] = result.astype(jnp.bfloat16)
        result_copy(u).start()

        @pl.when(u + 2 < out_tiles)
        def _():
            middle_copy(u + 2).start()
            for j in range(chunks):
                hidden_copy(u + 2, j).start()

        return carry

    lax.fori_loop(0, out_tiles, out_step, 0)
    for u in range(out_tiles - 2, out_tiles):
        result_copy(u).wait()
    comm("end")
    value = vector_terms[a, y, c, s]
    for n, copy in enumerate(vector_copies):
        copy.wait_recv()
        value = value + vector_got[n]
    vector_share[...] = value
    work.end()
    for copy in vector_copies:
        copy.wait_send()
    for store in stores:
        store.wait()

    @pl.when(s == 1)
    def _():
        late_copy.wait_send()


BACKWARD_ORDERS = (0, 1, 1, 0, 1, 1, 0, 1, 0, 1, 1, 0, 1, 1, 1, 0, 1, 0, 1)
BACKWARD_PLAN = {'start': [(0, 0), (0, 1), (0, 2)], 'm3': [(1, 0)], 'm4': [(1, 1), (1, 2)], 'w2': [(0, 3), (0, 4)], 'w3': [(2, 0), (0, 5), (0, 6)], 'o0': [(2, 1), (1, 3), (1, 4), (0, 7), (0, 8)], 'o1': [(0, 9), (0, 10)], 'o2': [(1, 5), (1, 6)], 'o4': [(1, 7), (1, 8), (1, 9), (3, 1), (2, 2), (1, 10)], 'o7': [(2, 3)], 'attn': [(3, 0), (2, 6)], 'rest': [(4, 1), (2, 4)], 'f0': [(2, 5), (2, 8), (0, 11), (0, 12)], 'f3': [(4, 0), (3, 2), (2, 7)], 'mm': [(3, 4), (1, 11)], 'n0': [(3, 5), (2, 9), (1, 12), (3, 7)], 'n1': [(4, 2), (2, 10)], 'h1': [(3, 3), (2, 11), (4, 4)], 'g1': [(3, 6)], 'n2': [(4, 5), (4, 7), (3, 8), (0, 13), (0, 14)], 'h2': [(4, 3)], 'n3': [(2, 12)], 'h3': [(4, 6)], 'g3': [(4, 8), (3, 11), (1, 13), (1, 14)], 'n4': [(0, 15), (0, 16)], 'n5': [(4, 11)], 'g5': [(2, 13), (1, 15), (1, 16)], 't0': [(0, 17), (0, 18)], 't1': [(3, 9), (3, 10), (2, 14)], 't2': [(3, 12), (2, 16), (1, 17), (1, 18), (3, 13)], 't3': [(4, 9)], 'u0': [(4, 10), (2, 15)], 'u1': [(4, 12), (4, 13), (3, 14), (3, 16), (2, 18)], 'u2': [(3, 15), (2, 17)], 'u3': [(4, 14), (3, 18)], 'end': [(4, 15), (4, 16), (3, 17), (4, 18), (4, 17)]}


def backward(outer, hidden, slope, middle, normed2, att, dy, attn, fc, proj, proj_terms, probs, q, k, v, normed, x, weight, vectors):
    rows, local, width = q.shape
    devices = outer * 8
    low, full = jnp.bfloat16, jnp.float32
    share = weight.shape[0] // devices
    units = fc.shape[1]
    anywhere = pl.BlockSpec(memory_space=pl.ANY)
    vmem = pl.BlockSpec(memory_space=pltpu.VMEM)
    blocks = weight.shape[1] // width
    pieces = column_pieces(0, width, 3, (0,))
    pieces += column_pieces(1, units, 2 * units // width, (0,)) + column_pieces(2, width, 2, (0,))
    first = len(pieces)
    pieces += column_pieces(3, weight.shape[1], 2 * blocks, (0,))
    pieces = [piece[:3] + (order,) for piece, order in zip(pieces, BACKWARD_ORDERS)]
    part, half = width // 3, width // 2
    places = {}
    for b in range(blocks):
        for h in range(2):
            begin, end = h * half, (h + 1) * half
            places[first + 2 * b + h] = [
                (max(i * part, begin) - begin, min((i + 1) * part, end) - max(i * part, begin),
                 i * width + b * part + max(i * part, begin) - i * part)
                for i in range(blocks)
                if max(i * part, begin) < min((i + 1) * part, end)
            ]
    shapes = [(units // devices, width, low), (share, units, low), (share, width, low), (share, weight.shape[1], low)]
    slots = lambda columns: jax.ShapeDtypeStruct((outer, 2, 2, 2, share, columns), low)
    flat = dy.shape
    return pl.pallas_call(
        functools.partial(backward_kernel, outer, pieces, places),
        in_specs=[anywhere] * 17 + [vmem],
        out_specs=[anywhere] * 4 + [vmem] * 5,
        out_shape=[
            jax.ShapeDtypeStruct(flat, low),
            jax.ShapeDtypeStruct(x.shape, full),
            slots(units),
            slots(width),
        ]
        + [shares_out(shape[0], shape[1]) for shape in shapes]
        + [shares_out(16, PAIR)],
        scratch_shapes=[
            pltpu.VMEM(flat, low),
            pltpu.VMEM(flat, low),
            pltpu.VMEM(flat, full),
            pltpu.VMEM((rows, TILE, width), low),
            pltpu.VMEM((rows, TILE, width), low),
            pltpu.VMEM((outer, 2, 2, 2, 16, PAIR), full),
            pltpu.VMEM((devices - 1, 16, PAIR), full),
            pltpu.VMEM((16, width), full),
            pltpu.SemaphoreType.DMA((2,)),
            pltpu.SemaphoreType.DMA((2,)),
            pltpu.SemaphoreType.DMA((devices - 1,)),
            pltpu.SemaphoreType.DMA((devices - 1,)),
        ]
        + Scatter.scratch(outer, shapes, pieces),
        compiler_params=pltpu.CompilerParams(
            collective_id=4, has_side_effects=True, vmem_limit_bytes=VMEM_LIMIT
        ),
    )(
        hidden, slope, middle, normed2, att, dy, attn, fc, proj, proj_terms,
        probs, q, k, v, normed, x, weight, vectors,
    )


def gather_weights(outer, weights, vectors, fc_bias):
    devices = outer * 8
    shards = [pack_vectors(vectors + [fc_bias])]
    shards += [w.reshape(pack_shape(w.shape)) for w in weights]
    full = gather_all(outer, shards, cut([shard.shape for shard in shards]))
    packed = full[0].reshape(devices, -1)
    count, size = len(vectors), vectors[0].shape[0]
    first = packed[:, : count * size].reshape(devices, count, size)
    first = jnp.swapaxes(first, 0, 1).reshape(count, devices * size)
    second = packed[:, count * size : count * size + fc_bias.shape[0]].reshape(-1, devices * size)
    whole = [f.reshape(devices * w.shape[0], w.shape[1]) for f, w in zip(full[1:], weights)]
    return whole, jnp.concatenate([first, second], axis=0)


def scatter_grads(outer, weight_terms, vector_terms, fc_bias_term):
    devices = outer * 8
    count, width = vector_terms.shape
    first = jnp.swapaxes(vector_terms.reshape(count, devices, width // devices), 0, 1)
    first = first.reshape(devices, -1)
    second = fc_bias_term.reshape(devices, -1)
    packed = pack_vectors([first, second])
    terms = [packed.reshape((outer, 2, 2, 2) + packed.shape[1:])]
    shapes = [(term.shape[0] // devices, term.shape[1]) for term in weight_terms]
    for term, shape in zip(weight_terms, shapes):
        terms.append(term.reshape((outer, 2, 2, 2) + pack_shape(shape)))
    shares = scatter_all(outer, terms, cut([term.shape[-2:] for term in terms]))
    flat = shares[0].reshape(-1)
    size = width // devices
    vectors = [flat[i * size : (i + 1) * size] for i in range(count)]
    fc_bias = flat[count * size : count * size + second.shape[1]]
    return [share.reshape(shape) for share, shape in zip(shares[1:], shapes)], vectors, fc_bias


def shards(
    tokens_in,
    doc_starts,
    norm1_gain,
    norm1_bias,
    qkv_weight,
    query_bias,
    value_bias,
    attn_weight,
    attn_bias,
    norm2_gain,
    norm2_bias,
    fc_weight,
    fc_bias,
    proj_weight,
    proj_bias,
    out_grad,
):
    outer = lax.axis_size("batch") // 4
    rows, local, width = tokens_in.shape
    seq = lax.axis_index("seq")
    weights = [qkv_weight, attn_weight, fc_weight, proj_weight]
    vectors = [norm1_gain, norm1_bias, query_bias, value_bias, attn_bias, norm2_gain, norm2_bias, proj_bias]
    flat = lambda value: value.reshape(rows * local, width)
    block = lambda value: value.reshape(rows, local, width)
    dy = flat(out_grad)
    devices = 8 * outer
    if qkv_weight.shape[0] % 8 == 0 and proj_weight.shape[0] % 16 == 0 and CHUNK % (8 * proj_weight.shape[0]) == 0:
        (
            normed, q, k, v, probs, att, hidden, slope, middle, normed2, qkv, attn, fc, proj, proj_terms, vectors,
        ) = forward(outer, tokens_in, dy, doc_starts, vectors + [fc_bias], weights)
        proj = proj.reshape(devices * proj_weight.shape[0], width)
        out, tokens_grad, _, _, proj_share, fc_share, attn_share, qkv_share, packed = backward(
            outer, hidden, slope, middle, normed2, att, dy, attn, fc, proj, proj_terms,
            probs, q, k, v, normed, tokens_in, qkv, vectors,
        )
        size = width // devices
        weights = [qkv_share, attn_share, fc_share, proj_share]
        shares = [packed[i, :size] for i in range(8)]
        fc_bias_share = packed[8, : 4 * size]
    else:
        first = 2 * seq
        padded = jnp.pad(doc_starts, ((0, 0), (1, 0)))
        starts = lax.dynamic_slice_in_dim(padded, first, 3, 1)
        starts = starts - TILE * (first - 1 + jnp.arange(3, dtype=jnp.int32))
        prev = lax.ppermute(tokens_in[:, local - TILE :], "seq", [(0, 1)])
        (qkv, attn, fc, proj), vectors = gather_weights(outer, weights, vectors, fc_bias)
        normed, q, k, v = project(tokens_in, prev, qkv, vectors)
        probs, att, inverse = attend(starts, q, k, v)
        out, middle_grad, att_grad, attn_grad, fc_grad, proj_grad, mlp_sums = mlp(
            flat(tokens_in), flat(att), dy, attn, fc, proj, vectors
        )
        dq, dk, dv = attend_grad(probs, q, k, v, block(att_grad), att, inverse)
        qkv_grad, prev_grad, project_sums = project_grad(normed, dq, dk, dv, qkv)
        late = lax.ppermute(prev_grad, "seq", [(1, 0)])
        tokens_grad, norm_sums = tokens_grad_of(
            tokens_in, dq, dk, dv, qkv, late, block(middle_grad), vectors
        )
        sums = jnp.concatenate([norm_sums[:2], project_sums[:2], mlp_sums[:4]], axis=0)
        weights, shares, fc_bias_share = scatter_grads(
            outer, [qkv_grad, attn_grad, fc_grad, proj_grad], sums, mlp_sums[4:]
        )
    gain1, bias1, query, value, proj_b, gain2, bias2, attn_b = shares
    return (
        out.reshape(rows, local, width),
        tokens_grad,
        gain1,
        bias1,
        weights[0],
        query,
        value,
        weights[1],
        attn_b,
        gain2,
        bias2,
        weights[2],
        fc_bias_share,
        weights[3],
        proj_b,
    )


def solution(mesh):
    return jax.shard_map(
        shards,
        mesh=mesh,
        in_specs=(
            P("batch", "seq", None),
            P("batch", None),
            P(("batch", "seq")),
            P(("batch", "seq")),
            P(("batch", "seq"), None),
            P(("batch", "seq")),
            P(("batch", "seq")),
            P(("batch", "seq"), None),
            P(("batch", "seq")),
            P(("batch", "seq")),
            P(("batch", "seq")),
            P(("batch", "seq"), None),
            P(("batch", "seq")),
            P(("batch", "seq"), None),
            P(("batch", "seq")),
            P("batch", "seq", None),
        ),
        out_specs=(
            P("batch", "seq", None),
            P("batch", "seq", None),
            P(("batch", "seq")),
            P(("batch", "seq")),
            P(("batch", "seq"), None),
            P(("batch", "seq")),
            P(("batch", "seq")),
            P(("batch", "seq"), None),
            P(("batch", "seq")),
            P(("batch", "seq")),
            P(("batch", "seq")),
            P(("batch", "seq"), None),
            P(("batch", "seq")),
            P(("batch", "seq"), None),
            P(("batch", "seq")),
        ),
        check_vma=False,
    )
```
